128 devices in a mesh: shot: 16 (over y, x), rcv: 8 (over z, core).
Axes of the slice: x: 4, y: 4, z: 4, core: 2. Of those that a mesh axis runs over, the one named last changes fastest.
Arguments:
- traces: bfloat16 [81920, 1024], P(('shot', 'rcv')), may hold values from -216 to 216
- src_index: int32 [81920], P(('shot', 'rcv')), may hold values from 0 to 2047, as said below
- rcv_index: int32 [81920], P(('shot', 'rcv')), may hold values from 0 to 2047, as said below
- off_index: int32 [81920], P(('shot', 'rcv')), may hold values from 0 to 127
- send_rows: int32 [128, 16, 80], P(('shot', 'rcv')), may hold values from 0 to 639, as said below
- send_counts: int32 [128, 16], P(('shot', 'rcv')), may hold values from 0 to 80, as said below
- recv_bins: int32 [128, 16, 80], P(('shot', 'rcv')), may hold values from 0 to 31
Outputs:
- source_terms: float32 [2048, 512], P('shot')
- receiver_terms: float32 [8, 256, 512], P('rcv', 'shot')
- offset_terms: float32 [128, 512], replicated
- cmp_terms: float32 [512, 512], P('shot')
The draws below stay inside these ranges and needn't reach their ends.
Inputs may be any that keep to these rules, and one draw needn't show every extreme that they name: `send_counts`: each device's 16 counts add up to 640; in every draw every device of some rcv index has 80 toward one shot index. `send_rows`: for each device and shot index, the first send_counts entries are rows of that device's traces; over all shot indices they name each of its 640 rows exactly once; later entries are arbitrary rows. `src_index`: A trace's source lies in the block of 128 sources of its device's shot index. `rcv_index`: A trace's receiver lies in the block of 256 receivers of its device's rcv index.
All inputs are finite; a program needn't handle non-finite values.
Results may differ from the reference program's by a relative error of at most 0.0017.
Values sent between devices are 32-bit elements; how exact they have to be, the bound alone decides.
No kernel may reach another device: no remote copies, remote signals or barrier semaphores. Data moves between devices by JAX's collectives and lax.ppermute only.
A program may use at most 64 MiB of HBM per device.

```python
import jax
import jax.numpy as jnp

SAMPLES = 1024
FREQS = 512
TR_DEV = 640
OFFSETS = 128
ITERS = 2
TRACES = 81920
CAP = 80
SRC_G = 128
RCV_G = 256
CMP_G = 32
NSRC = 2048
NRCV = 2048
NCMP = 512
N_SHOT = 16
N_RCV = 8
DEVICES = 128


def trace_lists(key):
    mean_load = TR_DEV // N_SHOT
    capacity = 2 * mean_load
    rest_load = TR_DEV - capacity
    base_load = rest_load // (N_SHOT - 1)
    extra_load = rest_load - base_load * (N_SHOT - 1)
    heavy = jax.random.randint(jax.random.fold_in(key, 11), (N_RCV,), 0, N_SHOT)
    jitter = jax.random.randint(jax.random.fold_in(key, 12), (DEVICES, N_SHOT - 1), 0, base_load // 2 + 1)
    position = jnp.arange(N_SHOT - 1, dtype=jnp.int32)
    others = base_load + (position < extra_load).astype(jnp.int32)[None, :] + jitter - jnp.roll(jitter, -1, axis=1)
    device_ids = jnp.arange(DEVICES, dtype=jnp.int32)
    heavy_dev = heavy[device_ids % N_RCV]
    owner_ids = jnp.arange(N_SHOT, dtype=jnp.int32)[None, :]
    place = jnp.clip((owner_ids - heavy_dev[:, None] - 1) % N_SHOT, 0, N_SHOT - 2)
    counts = jnp.where(owner_ids == heavy_dev[:, None], capacity, jnp.take_along_axis(others, place, axis=1))
    starts = jnp.cumsum(counts, axis=1) - counts
    orders = jax.vmap(lambda subkey: jax.random.permutation(subkey, TR_DEV))(jax.random.split(jax.random.fold_in(key, 13), DEVICES))
    slot_ids = jnp.arange(capacity, dtype=jnp.int32)[None, None, :]
    spots = jnp.clip(starts[:, :, None] + slot_ids, 0, TR_DEV - 1).reshape(DEVICES, N_SHOT * capacity)
    picked = jnp.take_along_axis(orders, spots, axis=1).reshape(DEVICES, N_SHOT, capacity)
    filler = jax.random.randint(jax.random.fold_in(key, 14), (DEVICES, N_SHOT, capacity), 0, TR_DEV)
    rows = jnp.where(slot_ids < counts[:, :, None], picked, filler)
    return (rows.astype(jnp.int32), counts.astype(jnp.int32))


def draw_send_rows(key, part):
    rows, counts = trace_lists(key)
    return rows


def draw_send_counts(key, part):
    rows, counts = trace_lists(key)
    return counts


def draw_src_index(key, part):
    key = jax.random.fold_in(key, 3)
    device_ids = jnp.arange(TRACES, dtype=jnp.int32) // TR_DEV
    block = device_ids // N_RCV
    return (block * SRC_G + jax.random.randint(key, (TRACES,), 0, SRC_G)).astype(jnp.int32)


def draw_rcv_index(key, part):
    key = jax.random.fold_in(key, 4)
    device_ids = jnp.arange(TRACES, dtype=jnp.int32) // TR_DEV
    block = device_ids % N_RCV
    return (block * RCV_G + jax.random.randint(key, (TRACES,), 0, RCV_G)).astype(jnp.int32)


def draw_traces(key, part):
    key = jax.random.fold_in(key, 1)
    noise_key = jax.random.fold_in(key, 21)
    amp_key = jax.random.fold_in(key, 22)
    rows = jnp.arange(TRACES, dtype=jnp.float32)
    rise = jnp.exp(1.5 * rows / TRACES)[:, None]
    amplitude = jnp.exp(jax.random.uniform(amp_key, (TRACES, 1)) * jnp.log(10.0))
    noise = jnp.clip(jax.random.normal(noise_key, (TRACES, SAMPLES)), -3.0, 3.0)
    earlier = jnp.concatenate([jnp.zeros((TRACES, 1), jnp.float32), noise[:, :-1]], axis=1)
    wave = noise + 0.6 * earlier
    return (amplitude * rise * wave).astype(jnp.bfloat16)


def with_ends(values, own_key, low, high):
    extent = values.shape
    index_at = [jax.random.randint(jax.random.fold_in(own_key, axis), (), 0, extent[axis]) for axis in range(len(extent))]
    values = values.at[tuple(index_at)].set(low)
    longest = extent.index(max(extent))
    index_at[longest] = (index_at[longest] + 1) % extent[longest]
    return values.at[tuple(index_at)].set(high)


def setup_inputs(seed: int = 0) -> dict:
    seeds = jax.random.split(jax.random.key(seed), 8)
    traces = draw_traces(jax.random.fold_in(seeds[7], 71), 0)
    src_index = draw_src_index(jax.random.fold_in(seeds[7], 71), 0)
    rcv_index = draw_rcv_index(jax.random.fold_in(seeds[7], 71), 0)
    off_index = with_ends(jax.random.randint(seeds[3], (TRACES,), 0, OFFSETS), jax.random.fold_in(seeds[3], 1), 0, OFFSETS - 1).astype(jnp.int32)
    send_rows = draw_send_rows(jax.random.fold_in(seeds[7], 71), 0)
    send_counts = draw_send_counts(jax.random.fold_in(seeds[7], 71), 0)
    recv_bins = with_ends(jax.random.randint(seeds[6], (DEVICES, N_SHOT, CAP), 0, CMP_G), jax.random.fold_in(seeds[6], 1), 0, CMP_G - 1).astype(jnp.int32)
    return {"traces": traces, "src_index": src_index, "rcv_index": rcv_index, "off_index": off_index, "send_rows": send_rows, "send_counts": send_counts, "recv_bins": recv_bins}


def fourier_basis(samples, freq_count):
    sample_ids = jnp.arange(samples, dtype=jnp.int32)[:, None]
    freq_ids = jnp.arange(freq_count, dtype=jnp.int32)[None, :]
    angle = (sample_ids * freq_ids % samples).astype(jnp.float32) * (2.0 * jnp.pi / samples)
    factor = 1.0 / jnp.sqrt(jnp.float32(samples))
    return jnp.concatenate([jnp.cos(angle) * factor, jnp.sin(angle) * factor], axis=1).astype(jnp.bfloat16)

def forward_apply(tables, src_index, rcv_index, off_index, cmp_index):
    source_tab, receiver_tab, offset_tab, cmp_tab = tables
    result = jnp.take(source_tab, src_index, axis=0) + jnp.take(receiver_tab, rcv_index, axis=0)
    result = result + jnp.take(offset_tab, off_index, axis=0)
    return result + jnp.take(cmp_tab, cmp_index, axis=0)

def adjoint_apply(values, src_index, rcv_index, off_index, cmp_index):
    return (jax.ops.segment_sum(values, src_index, num_segments=NSRC), jax.ops.segment_sum(values, rcv_index, num_segments=NRCV), jax.ops.segment_sum(values, off_index, num_segments=OFFSETS), jax.ops.segment_sum(values, cmp_index, num_segments=NCMP))

def table_norm(tables):
    total = jnp.float32(0.0)
    for member in tables:
        total = total + jnp.sum(member * member)
    return jnp.sqrt(total)

def reference(traces, src_index, rcv_index, off_index, send_rows, send_counts, recv_bins):
    fourier = fourier_basis(SAMPLES, FREQS)
    spectra = jnp.dot(traces, fourier, preferred_element_type=jnp.float32)
    real_part = spectra[:, :FREQS]
    imag_part = spectra[:, FREQS:]
    log_spectra = jnp.log1p(real_part * real_part + imag_part * imag_part)
    sender_bins = recv_bins.reshape(N_SHOT, N_RCV, N_SHOT, CAP).transpose(2, 1, 0, 3).reshape(DEVICES, N_SHOT, CAP)
    slot_ids = jnp.arange(CAP, dtype=jnp.int32)
    owner_ids = jnp.arange(N_SHOT, dtype=jnp.int32)
    device_ids = jnp.arange(DEVICES, dtype=jnp.int32)
    slot_live = slot_ids[None, None, :] < send_counts[:, :, None]
    target = jnp.where(slot_live, device_ids[:, None, None] * TR_DEV + send_rows, TRACES).astype(jnp.int32)
    bin_value = (owner_ids[None, :, None] * CMP_G + sender_bins).astype(jnp.int32)
    cmp_index = jnp.zeros((TRACES,), jnp.int32).at[target.reshape(-1)].set(bin_value.reshape(-1), mode='drop')
    indices = (src_index, rcv_index, off_index, cmp_index)
    beta_val = jnp.sqrt(jnp.sum(log_spectra * log_spectra))
    left_vec = log_spectra / beta_val
    right_raw = adjoint_apply(left_vec, *indices)
    alpha_val = table_norm(right_raw)
    right_vec = jax.tree.map(lambda member: member / alpha_val, right_raw)
    search = right_vec
    solution = jax.tree.map(jnp.zeros_like, right_vec)
    phibar = beta_val
    rhobar = alpha_val
    for iteration in range(ITERS):
        left_raw = forward_apply(right_vec, *indices) - alpha_val * left_vec
        beta_val = jnp.sqrt(jnp.sum(left_raw * left_raw))
        left_vec = left_raw / beta_val
        image = adjoint_apply(left_vec, *indices)
        right_raw = jax.tree.map(lambda member, former: member - beta_val * former, image, right_vec)
        alpha_val = table_norm(right_raw)
        right_vec = jax.tree.map(lambda member: member / alpha_val, right_raw)
        rho_val = jnp.sqrt(rhobar * rhobar + beta_val * beta_val)
        cosine = rhobar / rho_val
        sine_val = beta_val / rho_val
        theta_val = sine_val * alpha_val
        rhobar = -cosine * alpha_val
        phi_val = cosine * phibar
        phibar = sine_val * phibar
        solution = jax.tree.map(lambda member, former: member + phi_val / rho_val * former, solution, search)
        search = jax.tree.map(lambda member, former: member - theta_val / rho_val * former, right_vec, search)
    source_tab, receiver_tab, offset_tab, cmp_tab = solution
    return (source_tab, receiver_tab.reshape(N_RCV, RCV_G, FREQS), offset_tab, cmp_tab)
```

```python
import functools

import ml_dtypes
import numpy as np

import jax
import jax.numpy as jnp
from jax import lax
from jax.experimental import pallas as pl
from jax.experimental.pallas import tpu as pltpu
from jax.sharding import PartitionSpec as P

SAMPLES = 1024
FREQS = 512
TR_DEV = 640
N_SHOT = 16
N_RCV = 8
DEVICES = 128
CAP = 80
SRC_G = 128
RCV_G = 256
CMP_G = 32
SLICE = FREQS // N_SHOT
LANES = 128
OFF_TILE = 16
CMP_TILE = 17
LIVE_TILES = 21
LIVE_ROWS = LIVE_TILES * SLICE
SHARE = -(-LIVE_ROWS // (8 * N_RCV)) * 8
TAB_ROWS = N_RCV * SHARE
RCV_TILES = 2
ROWS = SRC_G + RCV_G + 128 + 512
SHARED = ROWS - SRC_G
SO = 2 * LANES
SOR = SO + RCV_G
OR = LANES + RCV_G
HALF = N_SHOT // 2
COUNT_STEPS = HALF // 2
CHUNKS = 4
CHUNK_ROWS = N_SHOT * SRC_G // CHUNKS
TRACE_TILES = TR_DEV // LANES
BINS_AT = TRACE_TILES * SLICE
INDEX_AT = BINS_AT + N_SHOT
INDEX_ROWS = 24
DATA_ROWS = INDEX_AT + INDEX_ROWS
STEPS = 2
OWN_ROWS = 2 * SLICE + SLICE // 2
PACK = LANES // CMP_G

VMEM = pltpu.VMEM
F32 = jnp.float32
BF16 = jnp.bfloat16


def fourier_rows():
    phase = np.arange(FREQS)[:, None] * np.arange(SAMPLES)[None, :] % SAMPLES
    angle = phase * (2.0 * np.pi / SAMPLES)
    waves = np.stack([np.cos(angle), np.sin(angle)]).reshape(2, STEPS, -1, SAMPLES)
    table = waves.transpose(1, 0, 2, 3).reshape(2 * FREQS, SAMPLES) / np.sqrt(SAMPLES)
    return table.astype(np.float32).astype(ml_dtypes.bfloat16)


def params(mib=48):
    return pltpu.CompilerParams(vmem_limit_bytes=mib * 2**20)


def cost(micros):
    return pl.CostEstimate(flops=int(micros * 1e9), bytes_accessed=int(micros * 3e6), transcendentals=0)


ANYWHERE = pl.BlockSpec(memory_space=pltpu.HBM)


def in_hbm(*arrays):
    return [pltpu.with_memory_space_constraint(array, pltpu.HBM) for array in arrays]


def nt_dot(left, right):
    return lax.dot_general(left, right, (((1,), (1,)), ((), ())), preferred_element_type=F32)


def split_rows(values):
    high = values.astype(BF16)
    low = (values - high.astype(F32)).astype(BF16)
    return jnp.concatenate([high, low], axis=0)


def at(tile):
    if isinstance(tile, int):
        return slice(tile * SLICE, (tile + 1) * SLICE)
    return pl.ds(pl.multiple_of(tile * SLICE, SLICE), SLICE)


def join_rows(both):
    half = both.shape[0] // 2
    return both[:half] + both[half:]


def flip(table):
    wide = jnp.concatenate(
        [table.astype(F32), jnp.zeros((N_SHOT, LANES - CAP), F32)], axis=1
    )
    return wide.T[:CAP].astype(jnp.int32)


def index_tiles(send_rows, send_counts, src, rcv, off):
    slots = lax.broadcasted_iota(jnp.int32, (CAP, N_SHOT), 0)
    targets = jnp.where(slots < send_counts[...], flip(send_rows[...]), -1)
    trace_ids = lax.broadcasted_iota(jnp.int32, (CAP, TR_DEV), 1)
    places = lax.broadcasted_iota(jnp.int32, (CAP, TR_DEV), 0)
    total = jnp.zeros((CAP, TR_DEV), jnp.int32)
    for owner in range(N_SHOT):
        hit = targets[:, owner : owner + 1] == trace_ids
        total = total + jnp.where(hit, places + owner * LANES, 0)
    slot_row = jnp.sum(total, axis=0, keepdims=True)
    rows = [src[...] & (SRC_G - 1), rcv[...] & (RCV_G - 1), off[...]]
    rows = [row.reshape(1, TR_DEV) for row in rows] + [slot_row]
    table = jnp.concatenate(rows, axis=0).astype(F32)
    tiles = [table[:, q * LANES : (q + 1) * LANES] for q in range(TRACE_TILES)]
    tiles.append(jnp.zeros((INDEX_ROWS - 4 * TRACE_TILES, LANES), F32))
    return jnp.concatenate(tiles, axis=0)


def spectra_kernel(traces, waves, *refs):
    given, out, own, basis, extra = refs[:6], refs[6], refs[7], refs[8], refs[9]
    small, sems, small_sems = refs[10:16], refs[16], refs[17]
    indices = [
        pltpu.make_async_copy(a, b, small_sems.at[k]) for k, (a, b) in enumerate(zip(given, small))
    ]
    for copy in indices:
        copy.start()
    pieces = []
    for k in range(TRACE_TILES):
        span = slice(k * LANES, (k + 1) * LANES)
        pieces.append((traces.at[span], own.at[span]))
    size = 2 * FREQS // STEPS // 2
    for k in range(2 * STEPS):
        span = slice(k * size, (k + 1) * size)
        pieces.append((waves.at[span], basis.at[span]))
    copies = [pltpu.make_async_copy(a, b, sems.at[k]) for k, (a, b) in enumerate(pieces)]
    for copy in copies:
        copy.start()
    for copy in indices:
        copy.wait()
    send_rows, send_counts, bins, src, rcv, off = small
    pad = jnp.zeros((N_SHOT, LANES - CAP), F32)
    extra[:N_SHOT] = jnp.concatenate([bins[...].astype(F32), pad], axis=1)
    extra[N_SHOT:] = index_tiles(send_rows, send_counts, src, rcv, off)
    for part in range(N_SHOT):
        out[part, BINS_AT:, :] = extra[...]
    for copy in copies[:TRACE_TILES]:
        copy.wait()
    half = FREQS // STEPS
    for step in range(STEPS):
        for copy in copies[TRACE_TILES + 2 * step : TRACE_TILES + 2 * step + 2]:
            copy.wait()
        parts = nt_dot(basis[2 * half * step : 2 * half * (step + 1)], own[...])
        logs = jnp.log1p(parts[:half] * parts[:half] + parts[half:] * parts[half:])
        for part in range(half // SLICE):
            for q in range(TRACE_TILES):
                out[step * (half // SLICE) + part, q * SLICE : (q + 1) * SLICE, :] = logs[
                    part * SLICE : (part + 1) * SLICE, q * LANES : (q + 1) * LANES
                ]


def log_spectra(traces, basis, *small):
    return pl.pallas_call(
        spectra_kernel,
        in_specs=[ANYWHERE] * (2 + len(small)),
        out_shape=jax.ShapeDtypeStruct((N_SHOT, DATA_ROWS, LANES), F32),
        scratch_shapes=[
            VMEM((TR_DEV, SAMPLES), BF16),
            VMEM((2 * FREQS, SAMPLES), BF16),
            VMEM((DATA_ROWS - BINS_AT, LANES), F32),
        ]
        + [VMEM(array.shape, jnp.int32) for array in small]
        + [
            pltpu.SemaphoreType.DMA((TRACE_TILES + 2 * STEPS,)),
            pltpu.SemaphoreType.DMA((len(small),)),
        ],
        compiler_params=params(24),
        cost_estimate=cost(5),
        name="spectra",
    )(*in_hbm(traces, basis, *small))


def fill_ids(ids):
    ids[...] = lax.broadcasted_iota(jnp.int32, ids.shape, 0).astype(F32).astype(BF16)


def fill_hot(tiles, ids, hot):
    one = jnp.ones((1, 1), BF16)
    zero = jnp.zeros((1, 1), BF16)
    values = tiles.astype(F32)
    for q in range(TRACE_TILES):
        span = slice(q * LANES, (q + 1) * LANES)
        first = 0
        for row, size, base in ((0, SRC_G, 0), (2, 128, 0), (1, RCV_G, 0), (3, 256, 0), (3, 256, 256)):
            wanted = (values[4 * q + row : 4 * q + row + 1] - base).astype(BF16)
            hot[first : first + size, span] = jnp.where(ids[:size] == wanted, one, zero)
            first += size


def resolve_bins(data, block):
    tiles = data[block, INDEX_AT:].astype(jnp.int32)
    rows = [data[owner, pl.ds(BINS_AT + block, 1)] for owner in range(N_SHOT)]
    table = jnp.concatenate(rows, axis=0)
    owners = lax.broadcasted_iota(jnp.int32, (N_SHOT, LANES), 0)
    resolved = []
    for q in range(TRACE_TILES):
        slot = tiles[4 * q + 3 : 4 * q + 4]
        place = jnp.broadcast_to(slot & (LANES - 1), (N_SHOT, LANES))
        found = jnp.take_along_axis(table, place, axis=1, mode="promise_in_bounds")
        found = jnp.where(owners == slot >> 7, found.astype(jnp.int32) + owners * CMP_G, 0)
        resolved += [tiles[4 * q : 4 * q + 3], jnp.sum(found, axis=0, keepdims=True)]
    resolved.append(jnp.zeros((INDEX_ROWS - 4 * TRACE_TILES, LANES), jnp.int32))
    return jnp.concatenate(resolved, axis=0)


def prepare_block(data, index, ids, hot, block):
    tiles = resolve_bins(data, block)
    index[block] = tiles
    one = jnp.ones((1, 1), BF16)
    zero = jnp.zeros((1, 1), BF16)
    for q in range(TRACE_TILES):
        for place, row in enumerate((0, 2, 1, 3)):
            lane = tiles[4 * q + row : 4 * q + row + 1] & (LANES - 1)
            hit = ids[:LANES] == lane.astype(F32).astype(BF16)
            span = slice(q * LANES, (q + 1) * LANES)
            hot[place * LANES : (place + 1) * LANES, span] = jnp.where(hit, one, zero)


def add_block(data, index, hot, tab, rcv, block):
    tiles = index[block]
    values = [data[block, q * SLICE : (q + 1) * SLICE] for q in range(TRACE_TILES)]

    def of_tile(row, tile):
        picked = [
            jnp.where(tiles[4 * q + row : 4 * q + row + 1] >> 7 == tile, values[q], 0.0)
            for q in range(TRACE_TILES)
        ]
        return split_rows(jnp.concatenate(picked, axis=1))

    plain = nt_dot(split_rows(jnp.concatenate(values, axis=1)), hot[: 2 * LANES])
    tab[at(block)] = join_rows(plain[:, :LANES])
    tab[at(OFF_TILE)] += join_rows(plain[:, LANES:])
    parts = jnp.concatenate([of_tile(1, tile) for tile in range(RCV_TILES)], axis=0)
    sums = nt_dot(parts, hot[2 * LANES : 3 * LANES])
    for tile in range(RCV_TILES):
        rcv[tile] += join_rows(sums[tile * 2 * SLICE : (tile + 1) * 2 * SLICE])
    cmp_tiles = LIVE_TILES - CMP_TILE
    parts = jnp.concatenate([of_tile(3, tile) for tile in range(cmp_tiles)], axis=0)
    sums = nt_dot(parts, hot[3 * LANES :])
    for tile in range(cmp_tiles):
        tab[at(CMP_TILE + tile)] += join_rows(sums[tile * 2 * SLICE : (tile + 1) * 2 * SLICE])


def adjoint_kernel(data, tab, rcv, index, hot_even, hot_odd, ids):
    tab[OFF_TILE * SLICE :] = jnp.zeros((TAB_ROWS - OFF_TILE * SLICE, LANES), F32)
    rcv[...] = jnp.zeros((RCV_TILES, SLICE, LANES), F32)
    fill_ids(ids)
    prepare_block(data, index, ids, hot_even, 0)

    @pl.loop(0, N_SHOT // 2)
    def _(pair):
        even = 2 * pair
        prepare_block(data, index, ids, hot_odd, even + 1)
        add_block(data, index, hot_even, tab, rcv, even)
        prepare_block(data, index, ids, hot_even, jnp.minimum(even + 2, N_SHOT - 1))
        add_block(data, index, hot_odd, tab, rcv, even + 1)


EXACT = 128


def kept_part(counts):
    return (counts.astype(jnp.int32) & (EXACT - 1)).astype(jnp.int8)


def left_over(counts):
    whole = counts.astype(jnp.int32)
    return (whole - (whole & (EXACT - 1))).astype(F32).astype(BF16)


def widen(counts):
    return counts.astype(F32).astype(BF16)


def peak(counts):
    top = jnp.max(counts, axis=0, keepdims=True)
    best = top[:, :LANES]
    for start in range(LANES, counts.shape[1], LANES):
        best = jnp.maximum(best, top[:, start : start + LANES])
    return best


def block_counts(hot):
    with_cmp = nt_dot(hot[:SOR], hot[SOR:])
    with_rcv = nt_dot(hot[:SO], hot[SO:SOR])
    with_off = nt_dot(hot[:SRC_G], hot[SRC_G:SO])
    rows = jnp.concatenate([with_off, with_rcv[:SRC_G], with_cmp[:SRC_G]], axis=1)
    return rows, with_cmp[SRC_G:], with_rcv[SRC_G:]


def count_kernel(
    index, wide, kept, to_cmp_kept, to_rcv_kept, most, diag, hot_even, hot_odd, ids, to_cmp, to_rcv, *, first
):
    step = pl.program_id(0)
    even = first + 2 * step

    @pl.when(step == 0)
    def _():
        to_cmp[...] = jnp.zeros_like(to_cmp)
        to_rcv[...] = jnp.zeros_like(to_rcv)
        diag[...] = jnp.zeros_like(diag)
        most[...] = jnp.zeros_like(most)
        fill_ids(ids)
        fill_hot(index[even], ids, hot_even)

    def add(hot, place):
        rows, cmp_counts, rcv_counts = block_counts(hot)
        to_cmp[...] += cmp_counts
        to_rcv[...] += rcv_counts
        diag[...] += jnp.sum(rows, axis=0, keepdims=True)
        part = rows.astype(jnp.int32) & (EXACT - 1)
        span = slice(place * SRC_G, (place + 1) * SRC_G)
        kept[span] = part.astype(jnp.int8)
        wide[span] = part.astype(F32).astype(BF16)
        most[...] = jnp.maximum(most[...], peak(rows))

    fill_hot(index[even + 1], ids, hot_odd)
    add(hot_even, 0)
    fill_hot(index[jnp.minimum(even + 2, N_SHOT - 1)], ids, hot_even)
    add(hot_odd, 1)

    @pl.when(step == COUNT_STEPS - 1)
    def _():
        to_cmp_kept[...] = kept_part(to_cmp[...])
        to_rcv_kept[...] = kept_part(to_rcv[...])
        most[...] = jnp.maximum(most[...], jnp.maximum(peak(to_cmp[...]), peak(to_rcv[...])))


def add_left_over(most_1, most_2, index, hot, ids, to_cmp, to_rcv, use_both, use_rows):
    top = jnp.maximum(jnp.max(most_1[...]), jnp.max(most_2[...]))

    @pl.when(top >= EXACT)
    def _():
        fill_ids(ids)
        for half in range(2):
            to_cmp[...] = jnp.zeros_like(to_cmp)
            to_rcv[...] = jnp.zeros_like(to_rcv)

            @pl.loop(half * HALF, (half + 1) * HALF)
            def _(block):
                fill_hot(index[block], ids, hot)
                rows, cmp_counts, rcv_counts = block_counts(hot)
                to_cmp[...] += cmp_counts
                to_rcv[...] += rcv_counts
                use_rows(block, left_over(rows))

            use_both(left_over(to_cmp[...]), left_over(to_rcv[...]))


def widen_kernel(kept_1, kept_2, cmp_1, cmp_2, rcv_1, rcv_2, wide, to_cmp, to_rcv, held, small_cmp, small_rcv, sems):
    pieces = []
    for chunk in range(CHUNKS):
        source = kept_1 if chunk < CHUNKS // 2 else kept_2
        start = chunk % (CHUNKS // 2) * CHUNK_ROWS
        pieces.append((source.at[start : start + CHUNK_ROWS], held.at[chunk]))
    pieces += [(cmp_1, small_cmp.at[0]), (cmp_2, small_cmp.at[1])]
    pieces += [(rcv_1, small_rcv.at[0]), (rcv_2, small_rcv.at[1])]
    copies = [pltpu.make_async_copy(a, b, sems.at[k]) for k, (a, b) in enumerate(pieces)]
    for copy in copies:
        copy.start()
    for chunk in range(CHUNKS):
        copies[chunk].wait()
        wide[chunk * CHUNK_ROWS : (chunk + 1) * CHUNK_ROWS] = widen(held[chunk])
    for copy in copies[CHUNKS:]:
        copy.wait()
    to_cmp[...] = (small_cmp[0].astype(F32) + small_cmp[1].astype(F32)).astype(BF16)
    to_rcv[...] = (small_rcv[0].astype(F32) + small_rcv[1].astype(F32)).astype(BF16)


def load_halves(tab, rcv, own, shared):
    for tile in range(N_SHOT):
        own[:, tile * LANES : (tile + 1) * LANES] = split_rows(tab[at(tile)])
    shared[: 2 * SLICE, :LANES] = split_rows(tab[at(OFF_TILE)])
    for tile in range(RCV_TILES):
        shared[: 2 * SLICE, (1 + tile) * LANES : (2 + tile) * LANES] = split_rows(rcv[tile])
    for tile in range(CMP_TILE, LIVE_TILES):
        start = (tile - CMP_TILE) * LANES + OR
        shared[: 2 * SLICE, start : start + LANES] = split_rows(tab[at(tile)])


def normal_kernel(
    tab_in, rcv_in, first, last, cmp_1, cmp_2, rcv_1, rcv_2, diag_1, diag_2, most_1, most_2, index,
    tab, rcv, own_count, own, shared, to_shared, to_own, hot, ids, exact_cmp, exact_rcv,
):
    top = 2 * SLICE
    half = HALF * SRC_G
    load_halves(tab_in, rcv_in, own, shared)
    lanes = lax.broadcasted_iota(jnp.int32, (16, SHARED), 1)
    shared[top:] = jnp.where(lanes < LANES, 1.0, 0.0).astype(BF16)
    sums = jnp.dot(own[:, :half], first[...], preferred_element_type=F32)
    to_shared[...] = sums + jnp.dot(own[:, half:], last[...], preferred_element_type=F32)
    to_own[:, :half] = nt_dot(shared[...], first[...])
    to_own[:, half:] = nt_dot(shared[...], last[...])

    def others(to_cmp, to_rcv):
        cmp_sums = jnp.dot(shared[:top, :OR], to_cmp, preferred_element_type=F32)
        to_shared[:, OR:] += cmp_sums
        to_shared[:, :OR] += nt_dot(shared[:top, OR:], to_cmp)
        rcv_sums = jnp.dot(shared[:top, :LANES], to_rcv, preferred_element_type=F32)
        to_shared[:, LANES:OR] += rcv_sums
        to_shared[:, :LANES] += nt_dot(shared[:top, LANES:OR], to_rcv)

    def use_rows(block, rows):
        span = pl.ds(pl.multiple_of(block * SRC_G, SRC_G), SRC_G)
        to_shared[...] += jnp.dot(own[:, span], rows, preferred_element_type=F32)
        to_own[:, span] += nt_dot(shared[...], rows)

    def both_of(one, other):
        return (one[...].astype(F32) + other[...].astype(F32)).astype(BF16)

    others(both_of(cmp_1, cmp_2), both_of(rcv_1, rcv_2))
    add_left_over(most_1, most_2, index, hot, ids, exact_cmp, exact_rcv, others, use_rows)
    diag = diag_1[...] + diag_2[...]
    for tile in range(N_SHOT):
        span = slice(tile * LANES, (tile + 1) * LANES)
        count = to_own[top : top + 1, span]
        own_count[tile : tile + 1] = count
        tab[at(tile)] = join_rows(to_own[:top, span]) + count * tab_in[at(tile)]
    tab[at(OFF_TILE)] = join_rows(to_shared[:, :LANES]) + diag[:, :LANES] * tab_in[at(OFF_TILE)]
    for tile in range(RCV_TILES):
        span = slice((1 + tile) * LANES, (2 + tile) * LANES)
        rcv[tile] = join_rows(to_shared[:, span]) + diag[:, span] * rcv_in[tile]
    for tile in range(CMP_TILE, LIVE_TILES):
        start = (tile - CMP_TILE) * LANES + OR
        span = slice(start, start + LANES)
        tab[at(tile)] = join_rows(to_shared[:, span]) + diag[:, span] * tab_in[at(tile)]
    tab[LIVE_ROWS:] = jnp.zeros((TAB_ROWS - LIVE_ROWS, LANES), F32)


def all_sum(values):
    return jnp.sum(values, axis=tuple(range(values.ndim)), keepdims=True).reshape(1, 1)


def fold(values):
    total = values[:, :LANES]
    for start in range(LANES, values.shape[1], LANES):
        total = total + values[:, start : start + LANES]
    return total


def norm_kernel(
    tab_b, rcv_b, tab_y, rcv_y, wide, cmp_counts, rcv_counts, diag_1, diag_2, most_1, most_2, index, own_count,
    out, tab_z, rcv_z, own, shared, to_shared, hot, ids, exact_cmp, exact_rcv,
):
    shared_b = tab_b[:LIVE_ROWS]
    shared_y = tab_y[:LIVE_ROWS]
    shift = all_sum(shared_b * shared_y) / all_sum(shared_b * shared_b)
    shared_z = shared_y - shift * shared_b
    own_b = rcv_b[...]
    own_z = rcv_y[...] - shift * own_b
    tab_z[...] = shared_z
    rcv_z[...] = own_z
    load_halves(tab_z, rcv_z, own, shared)
    to_shared[...] = jnp.dot(own[...], wide[...], preferred_element_type=F32)

    def whole(tabs, own):
        return all_sum(tabs) * (1.0 / N_RCV) + all_sum(own)

    def others(to_cmp, to_rcv):
        cmp_sums = jnp.dot(shared[:, :OR], to_cmp, preferred_element_type=F32)
        to_shared[:, OR:] += cmp_sums
        rcv_sums = jnp.dot(shared[:, :LANES], to_rcv, preferred_element_type=F32)
        to_shared[:, LANES:OR] += rcv_sums

    def use_rows(block, rows):
        span = pl.ds(pl.multiple_of(block * SRC_G, SRC_G), SRC_G)
        to_shared[...] += jnp.dot(own[:, span], rows, preferred_element_type=F32)

    others(cmp_counts[...], rcv_counts[...])
    add_left_over(most_1, most_2, index, hot, ids, exact_cmp, exact_rcv, others, use_rows)
    tiles = [tab_z[at(OFF_TILE)]] + [rcv_z[tile] for tile in range(RCV_TILES)]
    tiles += [tab_z[at(tile)] for tile in range(CMP_TILE, LIVE_TILES)]
    rest = jnp.concatenate(tiles, axis=1)
    diag = diag_1[...] + diag_2[...]
    total = fold(2.0 * rest * join_rows(to_shared[...]) + diag * rest * rest)
    for tile in range(N_SHOT):
        total = total + own_count[tile : tile + 1] * tab_z[at(tile)] * tab_z[at(tile)]
    sums = (
        whole(shared_b * shared_b, own_b * own_b),
        whole(shared_b * shared_z, own_b * own_z),
        whole(shared_z * shared_z, own_z * own_z),
        all_sum(total),
        shift,
    )
    lanes = lax.broadcasted_iota(jnp.int32, (1, LANES), 1)
    row = jnp.zeros((1, LANES), F32)
    for lane, value in enumerate(sums):
        row = jnp.where(lanes == lane, value, row)
    out[...] = row


def whole_spec(*shape):
    return pl.BlockSpec(shape, lambda c: (0,) * len(shape))


TAB = (TAB_ROWS, LANES)
RCV = (RCV_TILES, SLICE, LANES)
INDEX = (N_SHOT, INDEX_ROWS, LANES)
INDEX_SPEC = pl.BlockSpec((1, INDEX_ROWS, LANES), lambda c: (c, 0, 0))


def table_shapes():
    return [jax.ShapeDtypeStruct(TAB, F32), jax.ShapeDtypeStruct(RCV, F32)]


def hot_scratch():
    return [VMEM((ROWS, TR_DEV), BF16), VMEM((256, LANES), BF16)]


def adjoint_apply(data):
    return pl.pallas_call(
        adjoint_kernel,
        out_shape=table_shapes() + [jax.ShapeDtypeStruct(INDEX, jnp.int32)],
        scratch_shapes=[VMEM((4 * LANES, TR_DEV), BF16)] * 2 + [VMEM((256, LANES), BF16)],
        compiler_params=params(24),
        cost_estimate=cost(8),
        name="adjoint_apply",
    )(data)


COUNTS = (HALF * SRC_G, SHARED)
TO_CMP = (OR, SHARED - OR)
TO_RCV = (LANES, RCV_G)
IN_VMEM = pl.BlockSpec(memory_space=VMEM)


def count_call(index, first):
    rows = pl.BlockSpec((2 * SRC_G, SHARED), lambda c: (c, 0))
    small = [whole_spec(*TO_CMP), whole_spec(*TO_RCV), whole_spec(1, LANES), whole_spec(1, SHARED)]
    return pl.pallas_call(
        functools.partial(count_kernel, first=first),
        grid=(COUNT_STEPS,),
        in_specs=[whole_spec(*INDEX)],
        out_specs=[rows, rows] + small,
        out_shape=[
            jax.ShapeDtypeStruct(COUNTS, BF16),
            pltpu.HBM(COUNTS, jnp.int8),
            jax.ShapeDtypeStruct(TO_CMP, jnp.int8),
            jax.ShapeDtypeStruct(TO_RCV, jnp.int8),
            jax.ShapeDtypeStruct((1, LANES), F32),
            jax.ShapeDtypeStruct((1, SHARED), F32),
        ],
        scratch_shapes=[VMEM((ROWS, TR_DEV), BF16)] * 2
        + [VMEM((256, LANES), BF16), VMEM(TO_CMP, F32), VMEM(TO_RCV, F32)],
        compiler_params=params(24),
        cost_estimate=cost(6),
        name="count_pairs",
    )(index)


def exact_scratch():
    return hot_scratch() + [VMEM(TO_CMP, F32), VMEM(TO_RCV, F32)]


def normal_apply(tab, rcv, index, counts_1, counts_2):
    wide_1, _, cmp_1, rcv_1, most_1, diag_1 = counts_1
    wide_2, _, cmp_2, rcv_2, most_2, diag_2 = counts_2
    return pl.pallas_call(
        normal_kernel,
        out_shape=table_shapes() + [jax.ShapeDtypeStruct((N_SHOT, LANES), F32)],
        scratch_shapes=[
            VMEM((2 * SLICE, N_SHOT * SRC_G), BF16),
            VMEM((2 * SLICE + 16, SHARED), BF16),
            VMEM((2 * SLICE, SHARED), F32),
            VMEM((2 * SLICE + 16, N_SHOT * SRC_G), F32),
        ]
        + exact_scratch(),
        compiler_params=params(20),
        cost_estimate=cost(3),
        name="normal_apply",
    )(tab, rcv, wide_1, wide_2, cmp_1, cmp_2, rcv_1, rcv_2, diag_1, diag_2, most_1, most_2, index)


def widen_counts(kept_1, kept_2):
    operands = [array for pair in zip(kept_1, kept_2) for array in pair]
    return pl.pallas_call(
        widen_kernel,
        in_specs=[ANYWHERE] * 6,
        out_shape=[
            jax.ShapeDtypeStruct((N_SHOT * SRC_G, SHARED), BF16),
            jax.ShapeDtypeStruct(TO_CMP, BF16),
            jax.ShapeDtypeStruct(TO_RCV, BF16),
        ],
        scratch_shapes=[
            VMEM((CHUNKS, CHUNK_ROWS, SHARED), jnp.int8),
            VMEM((2,) + TO_CMP, jnp.int8),
            VMEM((2,) + TO_RCV, jnp.int8),
            pltpu.SemaphoreType.DMA((CHUNKS + 4,)),
        ],
        compiler_params=params(20),
        cost_estimate=cost(3),
        name="widen_counts",
    )(*in_hbm(*operands))


def norm_sums(tab_b, rcv_b, tab_y, rcv_y, own_count, index, wide, counts_1, counts_2):
    most_1, diag_1 = counts_1[4:]
    most_2, diag_2 = counts_2[4:]
    return pl.pallas_call(
        norm_kernel,
        out_shape=jax.ShapeDtypeStruct((1, LANES), F32),
        scratch_shapes=[
            VMEM((LIVE_ROWS, LANES), F32),
            VMEM(RCV, F32),
            VMEM((2 * SLICE, N_SHOT * SRC_G), BF16),
            VMEM((2 * SLICE, SHARED), BF16),
            VMEM((2 * SLICE, SHARED), F32),
        ]
        + exact_scratch(),
        compiler_params=params(20),
        cost_estimate=cost(2),
        name="norm_sums",
    )(tab_b, rcv_b, tab_y, rcv_y, *wide, diag_1, diag_2, most_1, most_2, index, own_count)


def spread_kernel(parts, out):
    total = parts[0]
    for source in range(1, N_RCV):
        total = total + parts[source]
    for dest in range(N_RCV):
        out[dest] = total


def exchange(array, axis):
    return lax.all_to_all(array, axis, split_axis=0, concat_axis=0, tiled=True)


def spread_shares(arrived):
    shape = (N_RCV, SHARE, LANES)
    spread = pl.pallas_call(
        spread_kernel,
        out_shape=jax.ShapeDtypeStruct(shape, F32),
        compiler_params=params(24),
        cost_estimate=cost(1),
        name="sum_shares",
    )(arrived.reshape(shape))
    return spread.reshape(TAB)


def pack_kernel(tab, rcv, *refs, first):
    out, rows, sems = refs[-3:]
    lanes = lax.broadcasted_iota(jnp.int32, (SLICE, LANES), 1)
    half = SLICE // 2
    copies = []
    for dest in range(N_SHOT):
        rows[dest, :SLICE] = tab[at(dest)]
        rows[dest, SLICE : 2 * SLICE] = tab[at(OFF_TILE)]
        cmp_first = dest * CMP_G
        rcv_first = dest * (RCV_G // N_SHOT)
        bins = tab[at(CMP_TILE + cmp_first // LANES)]
        cmp_part = pltpu.roll(bins, (-cmp_first) % LANES, 1)
        rcv_part = pltpu.roll(rcv[rcv_first // LANES], (CMP_G - rcv_first) % LANES, 1)
        both = jnp.where(lanes < CMP_G, cmp_part, rcv_part)
        moved = pltpu.roll(both[half:], LANES // 2, 1)
        rows[dest, 2 * SLICE :] = jnp.where(lanes[:half] < LANES // 2, both[:half], moved)
        if dest % PACK == PACK - 1:
            group = dest // PACK
            span = slice(group * PACK, (group + 1) * PACK)
            place = out.at[span, first : first + OWN_ROWS]
            copies.append(pltpu.make_async_copy(rows.at[span], place, sems.at[group]))
            copies[-1].start()
    for copy in copies:
        copy.wait()


def pack_owned(tab, rcv, former=None):
    given = [] if former is None else in_hbm(former)
    return pl.pallas_call(
        functools.partial(pack_kernel, first=OWN_ROWS * len(given)),
        in_specs=[pl.BlockSpec(memory_space=VMEM)] * 2 + [ANYWHERE] * len(given),
        out_specs=ANYWHERE,
        out_shape=pltpu.HBM((N_SHOT, 2 * OWN_ROWS, LANES), F32),
        scratch_shapes=[
            VMEM((N_SHOT, OWN_ROWS, LANES), F32),
            pltpu.SemaphoreType.DMA((N_SHOT // PACK,)),
        ],
        input_output_aliases={2: 0} if given else {},
        compiler_params=params(24),
        cost_estimate=cost(1),
        name="pack_owned",
    )(tab, rcv, *given)


def swapped(value, axis, size, bit):
    return lax.ppermute(value, axis, [(s, s ^ bit) for s in range(size)])


def gather_sums(sums):
    for bit in (1, 2, 6):
        sums = sums + swapped(sums, "rcv", N_RCV, bit)
    here = jnp.arange(N_SHOT, dtype=jnp.int32)[:, None] == lax.axis_index("shot")
    rows = jnp.where(here, sums, 0.0)
    for bit in (1, 3, 4, 12):
        rows = rows + swapped(rows, "shot", N_SHOT, bit)
    return rows


def finish_kernel(sums, owned, source, receiver, offset, cmp):
    rows = sums[...]
    norm_b, cross, norm_z, norm_az, shift = (rows[:, lane : lane + 1] for lane in range(5))
    shift = shift * (1.0 / N_RCV)

    def total(values):
        return jnp.sum(values, axis=0, keepdims=True)

    total_b = total(norm_b)
    first = total(cross + shift * norm_b) / total_b
    off = shift - first
    zz = total(norm_z + 2.0 * off * cross + off * off * norm_b)
    zaz = total(
        norm_az
        + 2.0 * off * (norm_z + shift * cross)
        + off * off * (cross + shift * norm_b)
    )
    second = zaz / zz
    det = first * second - zz / total_b
    scale_b = (first + second) / det
    scale_y = 1.0 / det

    def combine(sender, start, stop):
        part_y = owned[sender, OWN_ROWS + start : OWN_ROWS + stop]
        return scale_b * owned[sender, start:stop] - scale_y * part_y

    def spread_halves(tile):
        return jnp.concatenate([tile, pltpu.roll(tile, LANES // 2, 1)], axis=0)

    per_tile = LANES // SLICE
    for group in range(N_SHOT // per_tile):
        span = slice(group * LANES, (group + 1) * LANES)
        senders = range(group * per_tile, (group + 1) * per_tile)
        source[:, span] = jnp.concatenate([combine(i, 0, SLICE) for i in senders], axis=0).T
        offset[:, span] = jnp.concatenate(
            [combine(i, SLICE, 2 * SLICE) for i in senders], axis=0
        ).T
        rest = jnp.concatenate(
            [spread_halves(combine(i, 2 * SLICE, OWN_ROWS)) for i in senders], axis=0
        ).T
        cmp[:, span] = rest[:CMP_G]
        receiver[0, :, span] = rest[CMP_G : CMP_G + RCV_G // N_SHOT]


def finish(sums, owned):
    return pl.pallas_call(
        finish_kernel,
        out_shape=[
            jax.ShapeDtypeStruct((SRC_G, FREQS), F32),
            jax.ShapeDtypeStruct((1, RCV_G // N_SHOT, FREQS), F32),
            jax.ShapeDtypeStruct((128, FREQS), F32),
            jax.ShapeDtypeStruct((CMP_G, FREQS), F32),
        ],
        compiler_params=params(),
        name="finish",
    )(sums, owned)


def per_device(basis, traces, src_index, rcv_index, off_index, send_rows, send_counts, recv_bins):
    data = log_spectra(
        traces, basis, send_rows[0], send_counts, recv_bins[0], src_index, rcv_index, off_index
    )
    data = exchange(data, "shot")

    tab_b, rcv_b, index = adjoint_apply(data)
    arrived = exchange(tab_b, "rcv")
    counts_1 = count_call(index, 0)
    arrived, index, counts_1 = lax.optimization_barrier((arrived, index, counts_1))
    spread = spread_shares(arrived)
    spread, index = lax.optimization_barrier((spread, index))
    tab_b = exchange(spread, "rcv")
    counts = (counts_1, count_call(index, HALF))

    tab_y, rcv_y, own_count = normal_apply(tab_b, rcv_b, index, *counts)
    arrived = exchange(tab_y, "rcv")
    packed = pack_owned(tab_b, rcv_b)
    arrived, packed = lax.optimization_barrier((arrived, packed))
    spread = spread_shares(arrived)
    kept = [counts_half[1:4] for counts_half in counts]
    spread, kept = lax.optimization_barrier((spread, kept))
    tab_y = exchange(spread, "rcv")
    wide = widen_counts(*kept)
    tab_y, wide = lax.optimization_barrier((tab_y, wide))
    packed = pack_owned(tab_y, rcv_y, packed)
    tab_y, packed = lax.optimization_barrier((tab_y, packed))
    owned = exchange(packed, "shot")
    sums = norm_sums(tab_b, rcv_b, tab_y, rcv_y, own_count, index, wide, *counts)
    return tuple(finish(gather_sums(sums), owned))


def solution(mesh):
    basis = fourier_rows()
    mapped = jax.shard_map(
        per_device,
        mesh=mesh,
        in_specs=(
            P(),
            P(("shot", "rcv"), None),
            P(("shot", "rcv")),
            P(("shot", "rcv")),
            P(("shot", "rcv")),
            P(("shot", "rcv"), None, None),
            P(("shot", "rcv"), None),
            P(("shot", "rcv"), None, None),
        ),
        out_specs=(P("shot", None), P("rcv", "shot", None), P(), P("shot", None)),
        check_vma=False,
    )

    def run(*args):
        return mapped(jnp.asarray(basis), *args)

    return run
```

```python
import functools

import ml_dtypes
import numpy as np

import jax
import jax.numpy as jnp
from jax import lax
from jax.experimental import pallas as pl
from jax.experimental.pallas import tpu as pltpu
from jax.sharding import PartitionSpec as P

SAMPLES = 1024
FREQS = 512
TR_DEV = 640
N_SHOT = 16
N_RCV = 8
DEVICES = 128
CAP = 80
SRC_G = 128
RCV_G = 256
CMP_G = 32
SLICE = FREQS // N_SHOT
LANES = 128
OFF_TILE = 16
CMP_TILE = 17
LIVE_TILES = 21
LIVE_ROWS = LIVE_TILES * SLICE
SHARE = -(-LIVE_ROWS // (8 * N_RCV)) * 8
TAB_ROWS = N_RCV * SHARE
RCV_TILES = 2
ROWS = SRC_G + RCV_G + 128 + 512
SHARED = ROWS - SRC_G
SO = 2 * LANES
SOR = SO + RCV_G
OR = LANES + RCV_G
HALF = N_SHOT // 2
COUNT_STEPS = HALF // 2
CHUNKS = 4
CHUNK_ROWS = N_SHOT * SRC_G // CHUNKS
TRACE_TILES = TR_DEV // LANES
BINS_AT = TRACE_TILES * SLICE
INDEX_AT = BINS_AT + N_SHOT
INDEX_ROWS = 24
DATA_ROWS = INDEX_AT + INDEX_ROWS
STEPS = 2
TRACE_PIECES = 10
BASIS_PIECES = 16
OWN_ROWS = 2 * SLICE + SLICE // 2

VMEM = pltpu.VMEM
F32 = jnp.float32
BF16 = jnp.bfloat16
FP8 = jnp.float8_e4m3fn


def fourier_rows():
    phase = np.arange(FREQS)[:, None] * np.arange(SAMPLES)[None, :] % SAMPLES
    angle = phase * (2.0 * np.pi / SAMPLES)
    waves = np.stack([np.cos(angle), np.sin(angle)]).reshape(2, STEPS, -1, SAMPLES)
    table = waves.transpose(1, 0, 2, 3).reshape(2 * FREQS, SAMPLES) / np.sqrt(SAMPLES)
    return table.astype(np.float32).astype(ml_dtypes.bfloat16)


def params(mib=48):
    return pltpu.CompilerParams(vmem_limit_bytes=mib * 2**20)


def cost(micros):
    return pl.CostEstimate(flops=int(micros * 1e9), bytes_accessed=int(micros * 3e6), transcendentals=0)


ANYWHERE = pl.BlockSpec(memory_space=pltpu.HBM)


def in_hbm(*arrays):
    return [pltpu.with_memory_space_constraint(array, pltpu.HBM) for array in arrays]


def nt_dot(left, right):
    return lax.dot_general(left, right, (((1,), (1,)), ((), ())), preferred_element_type=F32)


def split_rows(values):
    high = values.astype(BF16)
    low = (values - high.astype(F32)).astype(BF16)
    return jnp.concatenate([high, low], axis=0)


def at(tile):
    if isinstance(tile, int):
        return slice(tile * SLICE, (tile + 1) * SLICE)
    return pl.ds(pl.multiple_of(tile * SLICE, SLICE), SLICE)


def join_rows(both):
    half = both.shape[0] // 2
    return both[:half] + both[half:]


def flip(table):
    wide = jnp.concatenate(
        [table.astype(F32), jnp.zeros((N_SHOT, LANES - CAP), F32)], axis=1
    )
    return wide.T[:CAP].astype(jnp.int32)


def index_tiles(send_rows, send_counts, src, rcv, off):
    slots = lax.broadcasted_iota(jnp.int32, (CAP, N_SHOT), 0)
    targets = jnp.where(slots < send_counts[...], flip(send_rows[...]), -1)
    trace_ids = lax.broadcasted_iota(jnp.int32, (CAP, TR_DEV), 1)
    places = lax.broadcasted_iota(jnp.int32, (CAP, TR_DEV), 0)
    total = jnp.zeros((CAP, TR_DEV), jnp.int32)
    for owner in range(N_SHOT):
        hit = targets[:, owner : owner + 1] == trace_ids
        total = total + jnp.where(hit, places + owner * LANES, 0)
    slot_row = jnp.sum(total, axis=0, keepdims=True)
    rows = [src[...] & (SRC_G - 1), rcv[...] & (RCV_G - 1), off[...]]
    rows = [row.reshape(1, TR_DEV) for row in rows] + [slot_row]
    table = jnp.concatenate(rows, axis=0).astype(F32)
    tiles = [table[:, q * LANES : (q + 1) * LANES] for q in range(TRACE_TILES)]
    tiles.append(jnp.zeros((INDEX_ROWS - 4 * TRACE_TILES, LANES), F32))
    return jnp.concatenate(tiles, axis=0)


def spectra_kernel(traces, waves, *refs):
    given, out, own, basis, extra = refs[:6], refs[6], refs[7], refs[8], refs[9]
    small, sems, small_sems = refs[10:16], refs[16], refs[17]
    indices = [
        pltpu.make_async_copy(a, b, small_sems.at[k]) for k, (a, b) in enumerate(zip(given, small))
    ]
    for copy in indices:
        copy.start()
    pieces = []
    for k in range(TRACE_PIECES):
        size = TR_DEV // TRACE_PIECES
        span = slice(k * size, (k + 1) * size)
        pieces.append((traces.at[span], own.at[span]))
    for k in range(BASIS_PIECES):
        size = 2 * FREQS // BASIS_PIECES
        span = slice(k * size, (k + 1) * size)
        pieces.append((waves.at[span], basis.at[span]))
    copies = [pltpu.make_async_copy(a, b, sems.at[k]) for k, (a, b) in enumerate(pieces)]
    early = TRACE_PIECES + BASIS_PIECES // STEPS
    for copy in copies:
        copy.start()
    for copy in indices:
        copy.wait()
    send_rows, send_counts, bins, src, rcv, off = small
    pad = jnp.zeros((N_SHOT, LANES - CAP), F32)
    extra[:N_SHOT] = jnp.concatenate([bins[...].astype(F32), pad], axis=1)
    extra[N_SHOT:] = index_tiles(send_rows, send_counts, src, rcv, off)
    for part in range(N_SHOT):
        out[part, BINS_AT:, :] = extra[...]
    for copy in copies[:early]:
        copy.wait()
    half = FREQS // STEPS
    for step in range(STEPS):
        if step == 1:
            for copy in copies[early:]:
                copy.wait()
        parts = nt_dot(basis[2 * half * step : 2 * half * (step + 1)], own[...])
        logs = jnp.log1p(parts[:half] * parts[:half] + parts[half:] * parts[half:])
        for part in range(half // SLICE):
            for q in range(TRACE_TILES):
                out[step * (half // SLICE) + part, q * SLICE : (q + 1) * SLICE, :] = logs[
                    part * SLICE : (part + 1) * SLICE, q * LANES : (q + 1) * LANES
                ]


def log_spectra(traces, basis, *small):
    return pl.pallas_call(
        spectra_kernel,
        in_specs=[ANYWHERE] * (2 + len(small)),
        out_shape=jax.ShapeDtypeStruct((N_SHOT, DATA_ROWS, LANES), F32),
        scratch_shapes=[
            VMEM((TR_DEV, SAMPLES), BF16),
            VMEM((2 * FREQS, SAMPLES), BF16),
            VMEM((DATA_ROWS - BINS_AT, LANES), F32),
        ]
        + [VMEM(array.shape, jnp.int32) for array in small]
        + [
            pltpu.SemaphoreType.DMA((TRACE_PIECES + BASIS_PIECES,)),
            pltpu.SemaphoreType.DMA((len(small),)),
        ],
        compiler_params=params(24),
        cost_estimate=cost(5),
        name="spectra",
    )(*in_hbm(traces, basis, *small))


def fill_ids(ids):
    ids[...] = lax.broadcasted_iota(jnp.int32, ids.shape, 0).astype(F32).astype(BF16)


def fill_hot(tiles, ids, hot):
    one = jnp.ones((1, 1), BF16)
    zero = jnp.zeros((1, 1), BF16)
    values = tiles.astype(F32)
    for q in range(TRACE_TILES):
        span = slice(q * LANES, (q + 1) * LANES)
        first = 0
        for row, size, base in ((0, SRC_G, 0), (2, 128, 0), (1, RCV_G, 0), (3, 256, 0), (3, 256, 256)):
            wanted = (values[4 * q + row : 4 * q + row + 1] - base).astype(BF16)
            hits = jnp.where(ids[:size] == wanted, one, zero)
            hot[first : first + size, span] = hits.astype(hot.dtype)
            first += size


def resolve_bins(data, block):
    tiles = data[block, INDEX_AT:].astype(jnp.int32)
    rows = [data[owner, pl.ds(BINS_AT + block, 1)] for owner in range(N_SHOT)]
    table = jnp.concatenate(rows, axis=0)
    owners = lax.broadcasted_iota(jnp.int32, (N_SHOT, LANES), 0)
    resolved = []
    for q in range(TRACE_TILES):
        slot = tiles[4 * q + 3 : 4 * q + 4]
        place = jnp.broadcast_to(slot & (LANES - 1), (N_SHOT, LANES))
        found = jnp.take_along_axis(table, place, axis=1, mode="promise_in_bounds")
        found = jnp.where(owners == slot >> 7, found.astype(jnp.int32) + owners * CMP_G, 0)
        resolved += [tiles[4 * q : 4 * q + 3], jnp.sum(found, axis=0, keepdims=True)]
    resolved.append(jnp.zeros((INDEX_ROWS - 4 * TRACE_TILES, LANES), jnp.int32))
    return jnp.concatenate(resolved, axis=0)


def prepare_block(data, index, ids, hot, block):
    tiles = resolve_bins(data, block)
    index[block] = tiles
    one = jnp.ones((1, 1), BF16)
    zero = jnp.zeros((1, 1), BF16)
    for q in range(TRACE_TILES):
        for place, row in enumerate((0, 2, 1, 3)):
            lane = tiles[4 * q + row : 4 * q + row + 1] & (LANES - 1)
            hit = ids[:LANES] == lane.astype(F32).astype(BF16)
            span = slice(q * LANES, (q + 1) * LANES)
            hot[place * LANES : (place + 1) * LANES, span] = jnp.where(hit, one, zero)


def add_block(data, index, hot, tab, rcv, block):
    tiles = index[block]
    values = [data[block, q * SLICE : (q + 1) * SLICE] for q in range(TRACE_TILES)]

    def of_tile(row, tile):
        picked = [
            jnp.where(tiles[4 * q + row : 4 * q + row + 1] >> 7 == tile, values[q], 0.0)
            for q in range(TRACE_TILES)
        ]
        return split_rows(jnp.concatenate(picked, axis=1))

    plain = nt_dot(split_rows(jnp.concatenate(values, axis=1)), hot[: 2 * LANES])
    tab[at(block)] = join_rows(plain[:, :LANES])
    tab[at(OFF_TILE)] += join_rows(plain[:, LANES:])
    parts = jnp.concatenate([of_tile(1, tile) for tile in range(RCV_TILES)], axis=0)
    sums = nt_dot(parts, hot[2 * LANES : 3 * LANES])
    for tile in range(RCV_TILES):
        rcv[tile] += join_rows(sums[tile * 2 * SLICE : (tile + 1) * 2 * SLICE])
    cmp_tiles = LIVE_TILES - CMP_TILE
    parts = jnp.concatenate([of_tile(3, tile) for tile in range(cmp_tiles)], axis=0)
    sums = nt_dot(parts, hot[3 * LANES :])
    for tile in range(cmp_tiles):
        tab[at(CMP_TILE + tile)] += join_rows(sums[tile * 2 * SLICE : (tile + 1) * 2 * SLICE])


def adjoint_kernel(data, tab, rcv, index, hot_even, hot_odd, ids):
    tab[OFF_TILE * SLICE :] = jnp.zeros((TAB_ROWS - OFF_TILE * SLICE, LANES), F32)
    rcv[...] = jnp.zeros((RCV_TILES, SLICE, LANES), F32)
    fill_ids(ids)
    prepare_block(data, index, ids, hot_even, 0)

    @pl.loop(0, N_SHOT // 2)
    def _(pair):
        even = 2 * pair
        prepare_block(data, index, ids, hot_odd, even + 1)
        add_block(data, index, hot_even, tab, rcv, even)
        prepare_block(data, index, ids, hot_even, jnp.minimum(even + 2, N_SHOT - 1))
        add_block(data, index, hot_odd, tab, rcv, even + 1)


EXACT = 128


def kept_part(counts):
    return (counts.astype(jnp.int32) & (EXACT - 1)).astype(F32).astype(BF16)


def left_over(counts):
    whole = counts.astype(jnp.int32)
    return (whole - (whole & (EXACT - 1))).astype(F32).astype(BF16)


def peak(counts):
    top = jnp.max(counts, axis=0, keepdims=True)
    best = top[:, :LANES]
    for start in range(LANES, counts.shape[1], LANES):
        best = jnp.maximum(best, top[:, start : start + LANES])
    return best


def block_counts(hot):
    with_cmp = nt_dot(hot[:SOR], hot[SOR:])
    with_rcv = nt_dot(hot[:SO], hot[SO:SOR])
    with_off = nt_dot(hot[:SRC_G], hot[SRC_G:SO])
    rows = jnp.concatenate([with_off, with_rcv[:SRC_G], with_cmp[:SRC_G]], axis=1)
    return rows, with_cmp[SRC_G:], with_rcv[SRC_G:]


def count_kernel(
    index, kept, to_cmp_kept, to_rcv_kept, most, diag, hot_even, hot_odd, ids, to_cmp, to_rcv, *, first
):
    step = pl.program_id(0)
    even = first + 2 * step

    @pl.when(step == 0)
    def _():
        to_cmp[...] = jnp.zeros_like(to_cmp)
        to_rcv[...] = jnp.zeros_like(to_rcv)
        diag[...] = jnp.zeros_like(diag)
        most[...] = jnp.zeros_like(most)
        fill_ids(ids)
        fill_hot(index[even], ids, hot_even)

    def add(hot, place):
        rows, cmp_counts, rcv_counts = block_counts(hot)
        to_cmp[...] += cmp_counts
        to_rcv[...] += rcv_counts
        diag[...] += jnp.sum(rows, axis=0, keepdims=True)
        kept[place * SRC_G : (place + 1) * SRC_G] = kept_part(rows)
        most[...] = jnp.maximum(most[...], peak(rows))

    fill_hot(index[even + 1], ids, hot_odd)
    add(hot_even, 0)
    fill_hot(index[jnp.minimum(even + 2, N_SHOT - 1)], ids, hot_even)
    add(hot_odd, 1)

    @pl.when(step == COUNT_STEPS - 1)
    def _():
        to_cmp_kept[...] = kept_part(to_cmp[...])
        to_rcv_kept[...] = kept_part(to_rcv[...])
        most[...] = jnp.maximum(most[...], jnp.maximum(peak(to_cmp[...]), peak(to_rcv[...])))


def add_left_over(most_1, most_2, index, hot, ids, to_cmp, to_rcv, use_both, use_rows):
    top = jnp.maximum(jnp.max(most_1[...]), jnp.max(most_2[...]))

    @pl.when(top >= EXACT)
    def _():
        fill_ids(ids)
        for half in range(2):
            to_cmp[...] = jnp.zeros_like(to_cmp)
            to_rcv[...] = jnp.zeros_like(to_rcv)

            @pl.loop(half * HALF, (half + 1) * HALF)
            def _(block):
                fill_hot(index[block], ids, hot)
                rows, cmp_counts, rcv_counts = block_counts(hot)
                to_cmp[...] += cmp_counts
                to_rcv[...] += rcv_counts
                use_rows(block, left_over(rows))

            use_both(left_over(to_cmp[...]), left_over(to_rcv[...]))


def fetch_counts(refs, held, held_cmp, held_rcv, sems):
    first, last, cmp_1, cmp_2, rcv_1, rcv_2 = refs
    pieces = []
    for block in range(N_SHOT):
        source = first if block < HALF else last
        start = block % HALF * SRC_G
        place = block * SRC_G
        pieces.append((source.at[start : start + SRC_G], held.at[place : place + SRC_G]))
    pieces += [(cmp_1, held_cmp.at[0]), (cmp_2, held_cmp.at[1])]
    pieces += [(rcv_1, held_rcv.at[0]), (rcv_2, held_rcv.at[1])]
    copies = [pltpu.make_async_copy(a, b, sems.at[k]) for k, (a, b) in enumerate(pieces)]
    for copy in copies:
        copy.start()
    return copies


def wait_chunk(copies, chunk):
    blocks = N_SHOT // CHUNKS
    for copy in copies[chunk * blocks : (chunk + 1) * blocks]:
        copy.wait()
    return slice(chunk * CHUNK_ROWS, (chunk + 1) * CHUNK_ROWS)


def sum_halves(held):
    return (held[0].astype(F32) + held[1].astype(F32)).astype(BF16)


def load_halves(tab, rcv, own, shared):
    for tile in range(N_SHOT):
        own[:, tile * LANES : (tile + 1) * LANES] = split_rows(tab[at(tile)])
    shared[: 2 * SLICE, :LANES] = split_rows(tab[at(OFF_TILE)])
    for tile in range(RCV_TILES):
        shared[: 2 * SLICE, (1 + tile) * LANES : (2 + tile) * LANES] = split_rows(rcv[tile])
    for tile in range(CMP_TILE, LIVE_TILES):
        start = (tile - CMP_TILE) * LANES + OR
        shared[: 2 * SLICE, start : start + LANES] = split_rows(tab[at(tile)])


def normal_kernel(
    first, last, cmp_1, cmp_2, rcv_1, rcv_2, tab_in, rcv_in, diag_1, diag_2, most_1, most_2, index,
    tab, rcv, own_count, own, shared, to_shared, to_own,
    held, held_cmp, held_rcv, sems, hot, ids, exact_cmp, exact_rcv,
):
    counts = (first, last, cmp_1, cmp_2, rcv_1, rcv_2)
    copies = fetch_counts(counts, held, held_cmp, held_rcv, sems)
    top = 2 * SLICE
    load_halves(tab_in, rcv_in, own, shared)
    lanes = lax.broadcasted_iota(jnp.int32, (16, SHARED), 1)
    shared[top:] = jnp.where(lanes < LANES, 1.0, 0.0).astype(BF16)
    for chunk in range(CHUNKS):
        span = wait_chunk(copies, chunk)
        sums = jnp.dot(own[:, span], held[span], preferred_element_type=F32)
        to_shared[...] = sums if chunk == 0 else to_shared[...] + sums
        to_own[:, span] = nt_dot(shared[...], held[span])

    def others(to_cmp, to_rcv):
        cmp_sums = jnp.dot(shared[:top, :OR], to_cmp, preferred_element_type=F32)
        to_shared[:, OR:] += cmp_sums
        to_shared[:, :OR] += nt_dot(shared[:top, OR:], to_cmp)
        rcv_sums = jnp.dot(shared[:top, :LANES], to_rcv, preferred_element_type=F32)
        to_shared[:, LANES:OR] += rcv_sums
        to_shared[:, :LANES] += nt_dot(shared[:top, LANES:OR], to_rcv)

    def use_rows(block, rows):
        span = pl.ds(pl.multiple_of(block * SRC_G, SRC_G), SRC_G)
        to_shared[...] += jnp.dot(own[:, span], rows, preferred_element_type=F32)
        to_own[:, span] += nt_dot(shared[...], rows)

    for copy in copies[N_SHOT:]:
        copy.wait()
    others(sum_halves(held_cmp), sum_halves(held_rcv))
    add_left_over(most_1, most_2, index, hot, ids, exact_cmp, exact_rcv, others, use_rows)
    diag = diag_1[...] + diag_2[...]
    for tile in range(N_SHOT):
        span = slice(tile * LANES, (tile + 1) * LANES)
        count = to_own[top : top + 1, span]
        own_count[tile : tile + 1] = count
        tab[at(tile)] = join_rows(to_own[:top, span]) + count * tab_in[at(tile)]
    tab[at(OFF_TILE)] = join_rows(to_shared[:, :LANES]) + diag[:, :LANES] * tab_in[at(OFF_TILE)]
    for tile in range(RCV_TILES):
        span = slice((1 + tile) * LANES, (2 + tile) * LANES)
        rcv[tile] = join_rows(to_shared[:, span]) + diag[:, span] * rcv_in[tile]
    for tile in range(CMP_TILE, LIVE_TILES):
        start = (tile - CMP_TILE) * LANES + OR
        span = slice(start, start + LANES)
        tab[at(tile)] = join_rows(to_shared[:, span]) + diag[:, span] * tab_in[at(tile)]
    tab[LIVE_ROWS:] = jnp.zeros((TAB_ROWS - LIVE_ROWS, LANES), F32)


def all_sum(values):
    return jnp.sum(values, axis=tuple(range(values.ndim)), keepdims=True).reshape(1, 1)


def fold(values):
    total = values[:, :LANES]
    for start in range(LANES, values.shape[1], LANES):
        total = total + values[:, start : start + LANES]
    return total


def norm_kernel(
    first, last, cmp_1, cmp_2, rcv_1, rcv_2,
    tab_b, rcv_b, tab_y, rcv_y, diag_1, diag_2, most_1, most_2, index, own_count,
    out, tab_z, rcv_z, own, shared, to_shared,
    held, held_cmp, held_rcv, sems, hot, ids, exact_cmp, exact_rcv,
):
    counts = (first, last, cmp_1, cmp_2, rcv_1, rcv_2)
    copies = fetch_counts(counts, held, held_cmp, held_rcv, sems)
    shared_b = tab_b[:LIVE_ROWS]
    shared_y = tab_y[:LIVE_ROWS]
    shift = all_sum(shared_b * shared_y) / all_sum(shared_b * shared_b)
    shared_z = shared_y - shift * shared_b
    own_b = rcv_b[...]
    own_z = rcv_y[...] - shift * own_b
    tab_z[...] = shared_z
    rcv_z[...] = own_z
    load_halves(tab_z, rcv_z, own, shared)
    for chunk in range(CHUNKS):
        span = wait_chunk(copies, chunk)
        sums = jnp.dot(own[:, span], held[span], preferred_element_type=F32)
        to_shared[...] = sums if chunk == 0 else to_shared[...] + sums

    def whole(tabs, own):
        return all_sum(tabs) * (1.0 / N_RCV) + all_sum(own)

    def others(to_cmp, to_rcv):
        cmp_sums = jnp.dot(shared[:, :OR], to_cmp, preferred_element_type=F32)
        to_shared[:, OR:] += cmp_sums
        rcv_sums = jnp.dot(shared[:, :LANES], to_rcv, preferred_element_type=F32)
        to_shared[:, LANES:OR] += rcv_sums

    def use_rows(block, rows):
        span = pl.ds(pl.multiple_of(block * SRC_G, SRC_G), SRC_G)
        to_shared[...] += jnp.dot(own[:, span], rows, preferred_element_type=F32)

    for copy in copies[N_SHOT:]:
        copy.wait()
    others(sum_halves(held_cmp), sum_halves(held_rcv))
    add_left_over(most_1, most_2, index, hot, ids, exact_cmp, exact_rcv, others, use_rows)
    tiles = [tab_z[at(OFF_TILE)]] + [rcv_z[tile] for tile in range(RCV_TILES)]
    tiles += [tab_z[at(tile)] for tile in range(CMP_TILE, LIVE_TILES)]
    rest = jnp.concatenate(tiles, axis=1)
    diag = diag_1[...] + diag_2[...]
    total = fold(2.0 * rest * join_rows(to_shared[...]) + diag * rest * rest)
    for tile in range(N_SHOT):
        total = total + own_count[tile : tile + 1] * tab_z[at(tile)] * tab_z[at(tile)]
    sums = (
        whole(shared_b * shared_b, own_b * own_b),
        whole(shared_b * shared_z, own_b * own_z),
        whole(shared_z * shared_z, own_z * own_z),
        all_sum(total),
        shift,
    )
    lanes = lax.broadcasted_iota(jnp.int32, (1, LANES), 1)
    row = jnp.zeros((1, LANES), F32)
    for lane, value in enumerate(sums):
        row = jnp.where(lanes == lane, value, row)
    out[...] = row


def whole_spec(*shape):
    return pl.BlockSpec(shape, lambda c: (0,) * len(shape))


TAB = (TAB_ROWS, LANES)
RCV = (RCV_TILES, SLICE, LANES)
INDEX = (N_SHOT, INDEX_ROWS, LANES)
INDEX_SPEC = pl.BlockSpec((1, INDEX_ROWS, LANES), lambda c: (c, 0, 0))


def table_shapes():
    return [jax.ShapeDtypeStruct(TAB, F32), jax.ShapeDtypeStruct(RCV, F32)]


def hot_scratch():
    return [VMEM((ROWS, TR_DEV), FP8), VMEM((256, LANES), BF16)]


def adjoint_apply(data):
    return pl.pallas_call(
        adjoint_kernel,
        out_shape=table_shapes() + [jax.ShapeDtypeStruct(INDEX, jnp.int32)],
        scratch_shapes=[VMEM((4 * LANES, TR_DEV), BF16)] * 2 + [VMEM((256, LANES), BF16)],
        compiler_params=params(24),
        cost_estimate=cost(8),
        name="adjoint_apply",
    )(data)


COUNTS = (HALF * SRC_G, SHARED)
TO_CMP = (OR, SHARED - OR)
TO_RCV = (LANES, RCV_G)
IN_VMEM = pl.BlockSpec(memory_space=VMEM)


def count_call(index, first):
    rows = pl.BlockSpec((2 * SRC_G, SHARED), lambda c: (c, 0))
    small = [whole_spec(*TO_CMP), whole_spec(*TO_RCV), whole_spec(1, LANES), whole_spec(1, SHARED)]
    return pl.pallas_call(
        functools.partial(count_kernel, first=first),
        grid=(COUNT_STEPS,),
        in_specs=[whole_spec(*INDEX)],
        out_specs=[rows] + small,
        out_shape=[
            pltpu.HBM(COUNTS, BF16),
            pltpu.HBM(TO_CMP, BF16),
            pltpu.HBM(TO_RCV, BF16),
            jax.ShapeDtypeStruct((1, LANES), F32),
            jax.ShapeDtypeStruct((1, SHARED), F32),
        ],
        scratch_shapes=[VMEM((ROWS, TR_DEV), FP8)] * 2
        + [VMEM((256, LANES), BF16), VMEM(TO_CMP, F32), VMEM(TO_RCV, F32)],
        compiler_params=params(24),
        cost_estimate=cost(6),
        name="count_pairs",
    )(index)


def count_scratch():
    return (
        [
            VMEM((N_SHOT * SRC_G, SHARED), BF16),
            VMEM((2,) + TO_CMP, BF16),
            VMEM((2,) + TO_RCV, BF16),
            pltpu.SemaphoreType.DMA((N_SHOT + 4,)),
        ]
        + hot_scratch()
        + [VMEM(TO_CMP, F32), VMEM(TO_RCV, F32)]
    )


def count_operands(counts):
    big = in_hbm(*[array for pair in zip(counts[0][:3], counts[1][:3]) for array in pair])
    (most_1, diag_1), (most_2, diag_2) = counts[0][3:], counts[1][3:]
    return big, [diag_1, diag_2, most_1, most_2]


def normal_apply(tab, rcv, index, counts):
    big, small = count_operands(counts)
    return pl.pallas_call(
        normal_kernel,
        in_specs=[ANYWHERE] * 6 + [IN_VMEM] * 7,
        out_shape=table_shapes() + [jax.ShapeDtypeStruct((N_SHOT, LANES), F32)],
        scratch_shapes=[
            VMEM((2 * SLICE, N_SHOT * SRC_G), BF16),
            VMEM((2 * SLICE + 16, SHARED), BF16),
            VMEM((2 * SLICE, SHARED), F32),
            VMEM((2 * SLICE + 16, N_SHOT * SRC_G), F32),
        ]
        + count_scratch(),
        compiler_params=params(24),
        cost_estimate=cost(3),
        name="normal_apply",
    )(*big, tab, rcv, *small, index)


def norm_sums(tab_b, rcv_b, tab_y, rcv_y, own_count, index, counts):
    big, small = count_operands(counts)
    return pl.pallas_call(
        norm_kernel,
        in_specs=[ANYWHERE] * 6 + [IN_VMEM] * 10,
        out_shape=jax.ShapeDtypeStruct((1, LANES), F32),
        scratch_shapes=[
            VMEM((LIVE_ROWS, LANES), F32),
            VMEM(RCV, F32),
            VMEM((2 * SLICE, N_SHOT * SRC_G), BF16),
            VMEM((2 * SLICE, SHARED), BF16),
            VMEM((2 * SLICE, SHARED), F32),
        ]
        + count_scratch(),
        compiler_params=params(24),
        cost_estimate=cost(2),
        name="norm_sums",
    )(*big, tab_b, rcv_b, tab_y, rcv_y, *small, index, own_count)


def spread_kernel(parts, out):
    total = parts[0]
    for source in range(1, N_RCV):
        total = total + parts[source]
    for dest in range(N_RCV):
        out[dest] = total


def exchange(array, axis):
    return lax.all_to_all(array, axis, split_axis=0, concat_axis=0, tiled=True)


def spread_shares(arrived):
    shape = (N_RCV, SHARE, LANES)
    spread = pl.pallas_call(
        spread_kernel,
        out_shape=jax.ShapeDtypeStruct(shape, F32),
        compiler_params=params(24),
        cost_estimate=cost(1),
        name="sum_shares",
    )(arrived.reshape(shape))
    return spread.reshape(TAB)


def pack_kernel(tab, rcv, *refs, first):
    out, rows, sems = refs[-3:]
    lanes = lax.broadcasted_iota(jnp.int32, (SLICE, LANES), 1)
    half = SLICE // 2
    copies = []
    for dest in range(N_SHOT):
        rows[dest, :SLICE] = tab[at(dest)]
        rows[dest, SLICE : 2 * SLICE] = tab[at(OFF_TILE)]
        cmp_first = dest * CMP_G
        rcv_first = dest * (RCV_G // N_SHOT)
        bins = tab[at(CMP_TILE + cmp_first // LANES)]
        cmp_part = pltpu.roll(bins, (-cmp_first) % LANES, 1)
        rcv_part = pltpu.roll(rcv[rcv_first // LANES], (CMP_G - rcv_first) % LANES, 1)
        both = jnp.where(lanes < CMP_G, cmp_part, rcv_part)
        moved = pltpu.roll(both[half:], LANES // 2, 1)
        rows[dest, 2 * SLICE :] = jnp.where(lanes[:half] < LANES // 2, both[:half], moved)
        place = out.at[dest, first : first + OWN_ROWS]
        copies.append(pltpu.make_async_copy(rows.at[dest], place, sems.at[dest]))
        copies[-1].start()
    for copy in copies:
        copy.wait()


def pack_owned(tab, rcv, former=None):
    given = [] if former is None else in_hbm(former)
    return pl.pallas_call(
        functools.partial(pack_kernel, first=OWN_ROWS * len(given)),
        in_specs=[pl.BlockSpec(memory_space=VMEM)] * 2 + [ANYWHERE] * len(given),
        out_specs=ANYWHERE,
        out_shape=pltpu.HBM((N_SHOT, 2 * OWN_ROWS, LANES), F32),
        scratch_shapes=[
            VMEM((N_SHOT, OWN_ROWS, LANES), F32),
            pltpu.SemaphoreType.DMA((N_SHOT,)),
        ],
        input_output_aliases={2: 0} if given else {},
        compiler_params=params(24),
        cost_estimate=cost(1),
        name="pack_owned",
    )(tab, rcv, *given)


def swapped(value, axis, size, bit):
    return lax.ppermute(value, axis, [(s, s ^ bit) for s in range(size)])


def gather_sums(sums):
    for bit in (1, 2, 6):
        sums = sums + swapped(sums, "rcv", N_RCV, bit)
    here = jnp.arange(N_SHOT, dtype=jnp.int32)[:, None] == lax.axis_index("shot")
    rows = jnp.where(here, sums, 0.0)
    for bit in (1, 3, 4, 12):
        rows = rows + swapped(rows, "shot", N_SHOT, bit)
    return rows


def finish_kernel(sums, owned, source, receiver, offset, cmp, done_so, done_rest, sems):
    rows = sums[...]
    norm_b, cross, norm_z, norm_az, shift = (rows[:, lane : lane + 1] for lane in range(5))
    shift = shift * (1.0 / N_RCV)

    def total(values):
        return jnp.sum(values, axis=0, keepdims=True)

    total_b = total(norm_b)
    first = total(cross + shift * norm_b) / total_b
    off = shift - first
    zz = total(norm_z + 2.0 * off * cross + off * off * norm_b)
    zaz = total(
        norm_az
        + 2.0 * off * (norm_z + shift * cross)
        + off * off * (cross + shift * norm_b)
    )
    second = zaz / zz
    det = first * second - zz / total_b
    scale_b = (first + second) / det
    scale_y = 1.0 / det

    def combine(sender, start, stop):
        part_y = owned[sender, OWN_ROWS + start : OWN_ROWS + stop]
        return scale_b * owned[sender, start:stop] - scale_y * part_y

    def spread_halves(tile):
        return jnp.concatenate([tile, pltpu.roll(tile, LANES // 2, 1)], axis=0)

    per_tile = LANES // SLICE
    rcv_rows = RCV_G // N_SHOT
    copies = []

    def write(block, target):
        copies.append(pltpu.make_async_copy(block, target, sems.at[len(copies)]))
        copies[-1].start()

    for group in range(N_SHOT // per_tile):
        span = slice(group * LANES, (group + 1) * LANES)
        senders = range(group * per_tile, (group + 1) * per_tile)
        for place, target in enumerate((source, offset)):
            start = place * SLICE
            table = [combine(i, start, start + SLICE) for i in senders]
            done_so[place, group] = jnp.concatenate(table, axis=0).T
            write(done_so.at[place, group], target.at[:, span])
        rest = [spread_halves(combine(i, 2 * SLICE, OWN_ROWS)) for i in senders]
        done_rest[group] = jnp.concatenate(rest, axis=0).T
        write(done_rest.at[group, :CMP_G], cmp.at[:, span])
        write(done_rest.at[group, CMP_G : CMP_G + rcv_rows], receiver.at[0, :, span])
    for copy in copies:
        copy.wait()


def finish(sums, owned):
    groups = FREQS // LANES
    return pl.pallas_call(
        finish_kernel,
        in_specs=[IN_VMEM] * 2,
        out_specs=[ANYWHERE] * 4,
        out_shape=[
            jax.ShapeDtypeStruct((SRC_G, FREQS), F32),
            jax.ShapeDtypeStruct((1, RCV_G // N_SHOT, FREQS), F32),
            jax.ShapeDtypeStruct((128, FREQS), F32),
            jax.ShapeDtypeStruct((CMP_G, FREQS), F32),
        ],
        scratch_shapes=[
            VMEM((2, groups, LANES, LANES), F32),
            VMEM((groups, LANES, LANES), F32),
            pltpu.SemaphoreType.DMA((4 * groups,)),
        ],
        compiler_params=params(24),
        name="finish",
    )(sums, owned)


def per_device(basis, traces, src_index, rcv_index, off_index, send_rows, send_counts, recv_bins):
    data = log_spectra(
        traces, basis, send_rows[0], send_counts, recv_bins[0], src_index, rcv_index, off_index
    )
    data = exchange(data, "shot")

    tab_b, rcv_b, index = adjoint_apply(data)
    arrived = exchange(tab_b, "rcv")
    counts_1 = count_call(index, 0)
    arrived, index, counts_1 = lax.optimization_barrier((arrived, index, counts_1))
    spread = spread_shares(arrived)
    spread, index = lax.optimization_barrier((spread, index))
    tab_b = exchange(spread, "rcv")
    counts = (counts_1, count_call(index, HALF))

    tab_y, rcv_y, own_count = normal_apply(tab_b, rcv_b, index, counts)
    arrived = exchange(tab_y, "rcv")
    packed = pack_owned(tab_b, rcv_b)
    arrived, packed = lax.optimization_barrier((arrived, packed))
    tab_y = exchange(spread_shares(arrived), "rcv")
    packed = pack_owned(tab_y, rcv_y, packed)
    tab_y, packed = lax.optimization_barrier((tab_y, packed))
    owned = exchange(packed, "shot")
    sums = norm_sums(tab_b, rcv_b, tab_y, rcv_y, own_count, index, counts)
    return tuple(finish(gather_sums(sums), owned))


def solution(mesh):
    basis = fourier_rows()
    mapped = jax.shard_map(
        per_device,
        mesh=mesh,
        in_specs=(
            P(),
            P(("shot", "rcv"), None),
            P(("shot", "rcv")),
            P(("shot", "rcv")),
            P(("shot", "rcv")),
            P(("shot", "rcv"), None, None),
            P(("shot", "rcv"), None),
            P(("shot", "rcv"), None, None),
        ),
        out_specs=(P("shot", None), P("rcv", "shot", None), P(), P("shot", None)),
        check_vma=False,
    )

    def run(*args):
        return mapped(jnp.asarray(basis), *args)

    return run
```

```python
import functools

import ml_dtypes
import numpy as np

import jax
import jax.numpy as jnp
from jax import lax
from jax.experimental import pallas as pl
from jax.experimental.pallas import tpu as pltpu
from jax.sharding import PartitionSpec as P

SAMPLES = 1024
FREQS = 512
TR_DEV = 640
N_SHOT = 16
N_RCV = 8
DEVICES = 128
CAP = 80
SRC_G = 128
RCV_G = 256
CMP_G = 32
SLICE = FREQS // N_SHOT
LANES = 128
OFF_TILE = 16
CMP_TILE = 17
LIVE_TILES = 21
LIVE_ROWS = LIVE_TILES * SLICE
SHARE = -(-LIVE_ROWS // (8 * N_RCV)) * 8
TAB_ROWS = N_RCV * SHARE
RCV_TILES = 2
ROWS = SRC_G + RCV_G + 128 + 512
SHARED = ROWS - SRC_G
SO = 2 * LANES
SOR = SO + RCV_G
OR = LANES + RCV_G
HALF = N_SHOT // 2
COUNT_STEPS = HALF // 2
CHUNKS = 4
CHUNK_ROWS = N_SHOT * SRC_G // CHUNKS
TRACE_TILES = TR_DEV // LANES
BINS_AT = TRACE_TILES * SLICE
INDEX_AT = BINS_AT + N_SHOT
INDEX_ROWS = 24
DATA_ROWS = INDEX_AT + INDEX_ROWS
STEPS = 2
OWN_ROWS = 2 * SLICE + SLICE // 2
PACK = LANES // CMP_G

VMEM = pltpu.VMEM
F32 = jnp.float32
BF16 = jnp.bfloat16
FP8 = jnp.float8_e4m3fn


def fourier_rows():
    phase = np.arange(FREQS)[:, None] * np.arange(SAMPLES)[None, :] % SAMPLES
    angle = phase * (2.0 * np.pi / SAMPLES)
    waves = np.stack([np.cos(angle), np.sin(angle)]).reshape(2, STEPS, -1, SAMPLES)
    table = waves.transpose(1, 0, 2, 3).reshape(2 * FREQS, SAMPLES) / np.sqrt(SAMPLES)
    return table.astype(np.float32).astype(ml_dtypes.bfloat16)


def params(mib=48):
    return pltpu.CompilerParams(vmem_limit_bytes=mib * 2**20)


def cost(micros):
    return pl.CostEstimate(flops=int(micros * 1e9), bytes_accessed=int(micros * 3e6), transcendentals=0)


ANYWHERE = pl.BlockSpec(memory_space=pltpu.HBM)


def in_hbm(*arrays):
    return [pltpu.with_memory_space_constraint(array, pltpu.HBM) for array in arrays]


def nt_dot(left, right):
    return lax.dot_general(left, right, (((1,), (1,)), ((), ())), preferred_element_type=F32)


def split_rows(values):
    high = values.astype(BF16)
    low = (values - high.astype(F32)).astype(BF16)
    return jnp.concatenate([high, low], axis=0)


def at(tile):
    if isinstance(tile, int):
        return slice(tile * SLICE, (tile + 1) * SLICE)
    return pl.ds(pl.multiple_of(tile * SLICE, SLICE), SLICE)


def join_rows(both):
    half = both.shape[0] // 2
    return both[:half] + both[half:]


def flip(table):
    wide = jnp.concatenate(
        [table.astype(F32), jnp.zeros((N_SHOT, LANES - CAP), F32)], axis=1
    )
    return wide.T[:CAP].astype(jnp.int32)


def index_tiles(send_rows, send_counts, src, rcv, off):
    slots = lax.broadcasted_iota(jnp.int32, (CAP, N_SHOT), 0)
    targets = jnp.where(slots < send_counts[...], flip(send_rows[...]), -1)
    trace_ids = lax.broadcasted_iota(jnp.int32, (CAP, TR_DEV), 1)
    places = lax.broadcasted_iota(jnp.int32, (CAP, TR_DEV), 0)
    total = jnp.zeros((CAP, TR_DEV), jnp.int32)
    for owner in range(N_SHOT):
        hit = targets[:, owner : owner + 1] == trace_ids
        total = total + jnp.where(hit, places + owner * LANES, 0)
    slot_row = jnp.sum(total, axis=0, keepdims=True)
    rows = [src[...] & (SRC_G - 1), rcv[...] & (RCV_G - 1), off[...]]
    rows = [row.reshape(1, TR_DEV) for row in rows] + [slot_row]
    table = jnp.concatenate(rows, axis=0).astype(F32)
    tiles = [table[:, q * LANES : (q + 1) * LANES] for q in range(TRACE_TILES)]
    tiles.append(jnp.zeros((INDEX_ROWS - 4 * TRACE_TILES, LANES), F32))
    return jnp.concatenate(tiles, axis=0)


def spectra_kernel(traces, waves, *refs):
    given, out, own, basis, extra = refs[:6], refs[6], refs[7], refs[8], refs[9]
    small, sems, small_sems = refs[10:16], refs[16], refs[17]
    indices = [
        pltpu.make_async_copy(a, b, small_sems.at[k]) for k, (a, b) in enumerate(zip(given, small))
    ]
    for copy in indices:
        copy.start()
    pieces = []
    for k in range(TRACE_TILES):
        span = slice(k * LANES, (k + 1) * LANES)
        pieces.append((traces.at[span], own.at[span]))
    size = 2 * FREQS // STEPS // 2
    for k in range(2 * STEPS):
        span = slice(k * size, (k + 1) * size)
        pieces.append((waves.at[span], basis.at[span]))
    copies = [pltpu.make_async_copy(a, b, sems.at[k]) for k, (a, b) in enumerate(pieces)]
    early = TRACE_TILES + 2
    for copy in copies[:early]:
        copy.start()
    for copy in indices:
        copy.wait()
    send_rows, send_counts, bins, src, rcv, off = small
    pad = jnp.zeros((N_SHOT, LANES - CAP), F32)
    extra[:N_SHOT] = jnp.concatenate([bins[...].astype(F32), pad], axis=1)
    extra[N_SHOT:] = index_tiles(send_rows, send_counts, src, rcv, off)
    for part in range(N_SHOT):
        out[part, BINS_AT:, :] = extra[...]
    for copy in copies[:early]:
        copy.wait()
    for copy in copies[early:]:
        copy.start()
    half = FREQS // STEPS
    for step in range(STEPS):
        if step == 1:
            for copy in copies[early:]:
                copy.wait()
        parts = nt_dot(basis[2 * half * step : 2 * half * (step + 1)], own[...])
        logs = jnp.log1p(parts[:half] * parts[:half] + parts[half:] * parts[half:])
        for part in range(half // SLICE):
            for q in range(TRACE_TILES):
                out[step * (half // SLICE) + part, q * SLICE : (q + 1) * SLICE, :] = logs[
                    part * SLICE : (part + 1) * SLICE, q * LANES : (q + 1) * LANES
                ]


def log_spectra(traces, basis, *small):
    return pl.pallas_call(
        spectra_kernel,
        in_specs=[ANYWHERE] * (2 + len(small)),
        out_shape=jax.ShapeDtypeStruct((N_SHOT, DATA_ROWS, LANES), F32),
        scratch_shapes=[
            VMEM((TR_DEV, SAMPLES), BF16),
            VMEM((2 * FREQS, SAMPLES), BF16),
            VMEM((DATA_ROWS - BINS_AT, LANES), F32),
        ]
        + [VMEM(array.shape, jnp.int32) for array in small]
        + [
            pltpu.SemaphoreType.DMA((TRACE_TILES + 2 * STEPS,)),
            pltpu.SemaphoreType.DMA((len(small),)),
        ],
        compiler_params=params(24),
        cost_estimate=cost(5),
        name="spectra",
    )(*in_hbm(traces, basis, *small))


def fill_ids(ids):
    ids[...] = lax.broadcasted_iota(jnp.int32, ids.shape, 0).astype(F32).astype(BF16)


def fill_hot(tiles, ids, hot):
    one = jnp.ones((1, 1), BF16)
    zero = jnp.zeros((1, 1), BF16)
    values = tiles.astype(F32)
    for q in range(TRACE_TILES):
        span = slice(q * LANES, (q + 1) * LANES)
        first = 0
        for row, size, base in ((0, SRC_G, 0), (2, 128, 0), (1, RCV_G, 0), (3, 256, 0), (3, 256, 256)):
            wanted = (values[4 * q + row : 4 * q + row + 1] - base).astype(BF16)
            hits = jnp.where(ids[:size] == wanted, one, zero)
            hot[first : first + size, span] = hits.astype(hot.dtype)
            first += size


def resolve_bins(data, block):
    tiles = data[block, INDEX_AT:].astype(jnp.int32)
    rows = [data[owner, pl.ds(BINS_AT + block, 1)] for owner in range(N_SHOT)]
    table = jnp.concatenate(rows, axis=0)
    owners = lax.broadcasted_iota(jnp.int32, (N_SHOT, LANES), 0)
    resolved = []
    for q in range(TRACE_TILES):
        slot = tiles[4 * q + 3 : 4 * q + 4]
        place = jnp.broadcast_to(slot & (LANES - 1), (N_SHOT, LANES))
        found = jnp.take_along_axis(table, place, axis=1, mode="promise_in_bounds")
        found = jnp.where(owners == slot >> 7, found.astype(jnp.int32) + owners * CMP_G, 0)
        resolved += [tiles[4 * q : 4 * q + 3], jnp.sum(found, axis=0, keepdims=True)]
    resolved.append(jnp.zeros((INDEX_ROWS - 4 * TRACE_TILES, LANES), jnp.int32))
    return jnp.concatenate(resolved, axis=0)


def prepare_block(data, index, ids, hot, block):
    tiles = resolve_bins(data, block)
    index[block] = tiles
    one = jnp.ones((1, 1), BF16)
    zero = jnp.zeros((1, 1), BF16)
    for q in range(TRACE_TILES):
        for place, row in enumerate((0, 2, 1, 3)):
            lane = tiles[4 * q + row : 4 * q + row + 1] & (LANES - 1)
            hit = ids[:LANES] == lane.astype(F32).astype(BF16)
            span = slice(q * LANES, (q + 1) * LANES)
            hot[place * LANES : (place + 1) * LANES, span] = jnp.where(hit, one, zero)


def add_block(data, index, hot, tab, rcv, block):
    tiles = index[block]
    values = [data[block, q * SLICE : (q + 1) * SLICE] for q in range(TRACE_TILES)]

    both = split_rows(jnp.concatenate(values, axis=1))
    zero = jnp.zeros((1, 1), BF16)

    def of_tiles(row, count):
        place = [tiles[4 * q + row : 4 * q + row + 1] >> 7 for q in range(TRACE_TILES)]
        place = jnp.concatenate(place, axis=1).astype(F32).astype(BF16)
        return jnp.concatenate([jnp.where(place == tile, both, zero) for tile in range(count)], axis=0)

    plain = nt_dot(both, hot[: 2 * LANES])
    tab[at(block)] = join_rows(plain[:, :LANES])
    tab[at(OFF_TILE)] += join_rows(plain[:, LANES:])
    parts = of_tiles(1, RCV_TILES)
    sums = nt_dot(parts, hot[2 * LANES : 3 * LANES])
    for tile in range(RCV_TILES):
        rcv[tile] += join_rows(sums[tile * 2 * SLICE : (tile + 1) * 2 * SLICE])
    cmp_tiles = LIVE_TILES - CMP_TILE
    parts = of_tiles(3, cmp_tiles)
    sums = nt_dot(parts, hot[3 * LANES :])
    for tile in range(cmp_tiles):
        tab[at(CMP_TILE + tile)] += join_rows(sums[tile * 2 * SLICE : (tile + 1) * 2 * SLICE])


def adjoint_kernel(data, tab, rcv, index, hot_even, hot_odd, ids):
    tab[OFF_TILE * SLICE :] = jnp.zeros((TAB_ROWS - OFF_TILE * SLICE, LANES), F32)
    rcv[...] = jnp.zeros((RCV_TILES, SLICE, LANES), F32)
    fill_ids(ids)
    prepare_block(data, index, ids, hot_even, 0)

    @pl.loop(0, N_SHOT // 2)
    def _(pair):
        even = 2 * pair
        prepare_block(data, index, ids, hot_odd, even + 1)
        add_block(data, index, hot_even, tab, rcv, even)
        prepare_block(data, index, ids, hot_even, jnp.minimum(even + 2, N_SHOT - 1))
        add_block(data, index, hot_odd, tab, rcv, even + 1)


EXACT = 128


def kept_part(counts):
    return (counts.astype(jnp.int32) & (EXACT - 1)).astype(F32).astype(BF16)


def left_over(counts):
    whole = counts.astype(jnp.int32)
    return (whole - (whole & (EXACT - 1))).astype(F32).astype(BF16)


def peak(counts):
    top = jnp.max(counts, axis=0, keepdims=True)
    best = top[:, :LANES]
    for start in range(LANES, counts.shape[1], LANES):
        best = jnp.maximum(best, top[:, start : start + LANES])
    return best


def block_counts(hot):
    with_cmp = nt_dot(hot[:SOR], hot[SOR:])
    with_rcv = nt_dot(hot[:SO], hot[SO:SOR])
    with_off = nt_dot(hot[:SRC_G], hot[SRC_G:SO])
    rows = jnp.concatenate([with_off, with_rcv[:SRC_G], with_cmp[:SRC_G]], axis=1)
    return rows, with_cmp[SRC_G:], with_rcv[SRC_G:]


def count_kernel(
    index, kept, to_cmp_kept, to_rcv_kept, most, diag, *refs, first
):
    *handed, hot_even, hot_odd, ids, to_cmp, to_rcv = refs
    step = pl.program_id(0)
    even = first + 2 * step

    @pl.when(step == 0)
    def _():
        to_cmp[...] = jnp.zeros_like(to_cmp)
        to_rcv[...] = jnp.zeros_like(to_rcv)
        diag[...] = jnp.zeros_like(diag)
        most[...] = jnp.zeros_like(most)
        fill_ids(ids)
        fill_hot(index[even], ids, hot_even)

    def add(hot, place):
        rows, cmp_counts, rcv_counts = block_counts(hot)
        to_cmp[...] += cmp_counts
        to_rcv[...] += rcv_counts
        diag[...] += jnp.sum(rows, axis=0, keepdims=True)
        part = kept_part(rows)
        for out in [kept] + handed:
            out[place * SRC_G : (place + 1) * SRC_G] = part
        most[...] = jnp.maximum(most[...], peak(rows))

    fill_hot(index[even + 1], ids, hot_odd)
    add(hot_even, 0)
    fill_hot(index[jnp.minimum(even + 2, N_SHOT - 1)], ids, hot_even)
    add(hot_odd, 1)

    @pl.when(step == COUNT_STEPS - 1)
    def _():
        to_cmp_kept[...] = (to_cmp[...].astype(jnp.int32) & (EXACT - 1)).astype(jnp.int8)
        to_rcv_kept[...] = (to_rcv[...].astype(jnp.int32) & (EXACT - 1)).astype(jnp.int8)
        most[...] = jnp.maximum(most[...], jnp.maximum(peak(to_cmp[...]), peak(to_rcv[...])))


def add_left_over(most_1, most_2, index, hot, ids, to_cmp, to_rcv, use_both, use_rows):
    top = jnp.maximum(jnp.max(most_1[...]), jnp.max(most_2[...]))

    @pl.when(top >= EXACT)
    def _():
        fill_ids(ids)
        for half in range(2):
            to_cmp[...] = jnp.zeros_like(to_cmp)
            to_rcv[...] = jnp.zeros_like(to_rcv)

            @pl.loop(half * HALF, (half + 1) * HALF)
            def _(block):
                fill_hot(index[block], ids, hot)
                rows, cmp_counts, rcv_counts = block_counts(hot)
                to_cmp[...] += cmp_counts
                to_rcv[...] += rcv_counts
                use_rows(block, left_over(rows))

            use_both(left_over(to_cmp[...]), left_over(to_rcv[...]))


def fetch_counts(refs, held, held_cmp, held_rcv, sems):
    *halves, cmp_1, cmp_2, rcv_1, rcv_2 = refs
    pieces = []
    for half, source in enumerate(halves):
        for chunk in range(CHUNKS // 2):
            start = chunk * CHUNK_ROWS
            place = held.at[half * (CHUNKS // 2) + chunk]
            pieces.append((source.at[start : start + CHUNK_ROWS], place))
    pieces += [(cmp_1, held_cmp.at[0]), (cmp_2, held_cmp.at[1])]
    pieces += [(rcv_1, held_rcv.at[0]), (rcv_2, held_rcv.at[1])]
    copies = [pltpu.make_async_copy(a, b, sems.at[k]) for k, (a, b) in enumerate(pieces)]
    for copy in copies:
        copy.start()
    return copies


def sum_halves(held):
    return (held[0].astype(F32) + held[1].astype(F32)).astype(BF16)


def load_halves(tab, rcv, own, shared):
    for tile in range(N_SHOT):
        own[:, tile * LANES : (tile + 1) * LANES] = split_rows(tab[at(tile)])
    shared[: 2 * SLICE, :LANES] = split_rows(tab[at(OFF_TILE)])
    for tile in range(RCV_TILES):
        shared[: 2 * SLICE, (1 + tile) * LANES : (2 + tile) * LANES] = split_rows(rcv[tile])
    for tile in range(CMP_TILE, LIVE_TILES):
        start = (tile - CMP_TILE) * LANES + OR
        shared[: 2 * SLICE, start : start + LANES] = split_rows(tab[at(tile)])


def normal_kernel(
    first, cmp_1, cmp_2, rcv_1, rcv_2, tab_in, rcv_in, last, diag_1, diag_2, most_1, most_2, index,
    tab, rcv, own_count, own, shared, to_shared, to_own,
    held, held_cmp, held_rcv, sems, hot, ids, exact_cmp, exact_rcv,
):
    counts = (first, cmp_1, cmp_2, rcv_1, rcv_2)
    copies = fetch_counts(counts, held, held_cmp, held_rcv, sems)
    top = 2 * SLICE
    half = HALF * SRC_G
    load_halves(tab_in, rcv_in, own, shared)
    lanes = lax.broadcasted_iota(jnp.int32, (16, SHARED), 1)
    shared[top:] = jnp.where(lanes < LANES, 1.0, 0.0).astype(BF16)
    to_shared[...] = jnp.dot(own[:, half:], last[...], preferred_element_type=F32)
    to_own[:, half:] = nt_dot(shared[...], last[...])
    for chunk in range(CHUNKS // 2):
        copies[chunk].wait()
        span = slice(chunk * CHUNK_ROWS, (chunk + 1) * CHUNK_ROWS)
        to_shared[...] += jnp.dot(own[:, span], held[chunk], preferred_element_type=F32)
        to_own[:, span] = nt_dot(shared[...], held[chunk])

    def others(to_cmp, to_rcv):
        cmp_sums = jnp.dot(shared[:top, :OR], to_cmp, preferred_element_type=F32)
        to_shared[:, OR:] += cmp_sums
        to_shared[:, :OR] += nt_dot(shared[:top, OR:], to_cmp)
        rcv_sums = jnp.dot(shared[:top, :LANES], to_rcv, preferred_element_type=F32)
        to_shared[:, LANES:OR] += rcv_sums
        to_shared[:, :LANES] += nt_dot(shared[:top, LANES:OR], to_rcv)

    def use_rows(block, rows):
        span = pl.ds(pl.multiple_of(block * SRC_G, SRC_G), SRC_G)
        to_shared[...] += jnp.dot(own[:, span], rows, preferred_element_type=F32)
        to_own[:, span] += nt_dot(shared[...], rows)

    for copy in copies[-4:]:
        copy.wait()
    others(sum_halves(held_cmp), sum_halves(held_rcv))
    add_left_over(most_1, most_2, index, hot, ids, exact_cmp, exact_rcv, others, use_rows)
    diag = diag_1[...] + diag_2[...]
    for tile in range(N_SHOT):
        span = slice(tile * LANES, (tile + 1) * LANES)
        count = to_own[top : top + 1, span]
        own_count[tile : tile + 1] = count
        tab[at(tile)] = join_rows(to_own[:top, span]) + count * tab_in[at(tile)]
    tab[at(OFF_TILE)] = join_rows(to_shared[:, :LANES]) + diag[:, :LANES] * tab_in[at(OFF_TILE)]
    for tile in range(RCV_TILES):
        span = slice((1 + tile) * LANES, (2 + tile) * LANES)
        rcv[tile] = join_rows(to_shared[:, span]) + diag[:, span] * rcv_in[tile]
    for tile in range(CMP_TILE, LIVE_TILES):
        start = (tile - CMP_TILE) * LANES + OR
        span = slice(start, start + LANES)
        tab[at(tile)] = join_rows(to_shared[:, span]) + diag[:, span] * tab_in[at(tile)]
    tab[LIVE_ROWS:] = jnp.zeros((TAB_ROWS - LIVE_ROWS, LANES), F32)


def all_sum(values):
    return jnp.sum(values, axis=tuple(range(values.ndim)), keepdims=True).reshape(1, 1)


def fold(values):
    total = values[:, :LANES]
    for start in range(LANES, values.shape[1], LANES):
        total = total + values[:, start : start + LANES]
    return total


def norm_kernel(
    first, last, cmp_1, cmp_2, rcv_1, rcv_2,
    tab_b, rcv_b, tab_y, rcv_y, diag_1, diag_2, most_1, most_2, index, own_count,
    out, tab_z, rcv_z, own, shared, to_shared,
    held, held_cmp, held_rcv, sems, hot, ids, exact_cmp, exact_rcv,
):
    counts = (first, last, cmp_1, cmp_2, rcv_1, rcv_2)
    copies = fetch_counts(counts, held, held_cmp, held_rcv, sems)
    shared_b = tab_b[:LIVE_ROWS]
    shared_y = tab_y[:LIVE_ROWS]
    shift = all_sum(shared_b * shared_y) / all_sum(shared_b * shared_b)
    shared_z = shared_y - shift * shared_b
    own_b = rcv_b[...]
    own_z = rcv_y[...] - shift * own_b
    tab_z[...] = shared_z
    rcv_z[...] = own_z
    load_halves(tab_z, rcv_z, own, shared)
    for chunk in range(CHUNKS):
        copies[chunk].wait()
        span = slice(chunk * CHUNK_ROWS, (chunk + 1) * CHUNK_ROWS)
        sums = jnp.dot(own[:, span], held[chunk], preferred_element_type=F32)
        to_shared[...] = sums if chunk == 0 else to_shared[...] + sums

    def whole(tabs, own):
        return all_sum(tabs) * (1.0 / N_RCV) + all_sum(own)

    def others(to_cmp, to_rcv):
        cmp_sums = jnp.dot(shared[:, :OR], to_cmp, preferred_element_type=F32)
        to_shared[:, OR:] += cmp_sums
        rcv_sums = jnp.dot(shared[:, :LANES], to_rcv, preferred_element_type=F32)
        to_shared[:, LANES:OR] += rcv_sums

    def use_rows(block, rows):
        span = pl.ds(pl.multiple_of(block * SRC_G, SRC_G), SRC_G)
        to_shared[...] += jnp.dot(own[:, span], rows, preferred_element_type=F32)

    for copy in copies[-4:]:
        copy.wait()
    others(sum_halves(held_cmp), sum_halves(held_rcv))
    add_left_over(most_1, most_2, index, hot, ids, exact_cmp, exact_rcv, others, use_rows)
    tiles = [tab_z[at(OFF_TILE)]] + [rcv_z[tile] for tile in range(RCV_TILES)]
    tiles += [tab_z[at(tile)] for tile in range(CMP_TILE, LIVE_TILES)]
    rest = jnp.concatenate(tiles, axis=1)
    diag = diag_1[...] + diag_2[...]
    total = fold(2.0 * rest * join_rows(to_shared[...]) + diag * rest * rest)
    for tile in range(N_SHOT):
        total = total + own_count[tile : tile + 1] * tab_z[at(tile)] * tab_z[at(tile)]
    sums = (
        whole(shared_b * shared_b, own_b * own_b),
        whole(shared_b * shared_z, own_b * own_z),
        whole(shared_z * shared_z, own_z * own_z),
        all_sum(total),
        shift,
    )
    lanes = lax.broadcasted_iota(jnp.int32, (1, LANES), 1)
    row = jnp.zeros((1, LANES), F32)
    for lane, value in enumerate(sums):
        row = jnp.where(lanes == lane, value, row)
    out[...] = row


def whole_spec(*shape):
    return pl.BlockSpec(shape, lambda c: (0,) * len(shape))


TAB = (TAB_ROWS, LANES)
RCV = (RCV_TILES, SLICE, LANES)
INDEX = (N_SHOT, INDEX_ROWS, LANES)
INDEX_SPEC = pl.BlockSpec((1, INDEX_ROWS, LANES), lambda c: (c, 0, 0))


def table_shapes():
    return [jax.ShapeDtypeStruct(TAB, F32), jax.ShapeDtypeStruct(RCV, F32)]


def hot_scratch():
    return [VMEM((ROWS, TR_DEV), FP8), VMEM((256, LANES), BF16)]


def adjoint_apply(data):
    return pl.pallas_call(
        adjoint_kernel,
        out_shape=table_shapes() + [jax.ShapeDtypeStruct(INDEX, jnp.int32)],
        scratch_shapes=[VMEM((4 * LANES, TR_DEV), BF16)] * 2 + [VMEM((256, LANES), BF16)],
        compiler_params=params(24),
        cost_estimate=cost(8),
        name="adjoint_apply",
    )(data)


COUNTS = (HALF * SRC_G, SHARED)
TO_CMP = (OR, SHARED - OR)
TO_RCV = (LANES, RCV_G)
IN_VMEM = pl.BlockSpec(memory_space=VMEM)


def count_call(index, first):
    rows = pl.BlockSpec((2 * SRC_G, SHARED), lambda c: (c, 0))
    small = [whole_spec(*TO_CMP), whole_spec(*TO_RCV), whole_spec(1, LANES), whole_spec(1, SHARED)]
    handed = [] if first == 0 else [jax.ShapeDtypeStruct(COUNTS, BF16)]
    return pl.pallas_call(
        functools.partial(count_kernel, first=first),
        grid=(COUNT_STEPS,),
        in_specs=[whole_spec(*INDEX)],
        out_specs=[rows] + small + [rows] * len(handed),
        out_shape=[
            pltpu.HBM(COUNTS, BF16),
            pltpu.HBM(TO_CMP, jnp.int8),
            pltpu.HBM(TO_RCV, jnp.int8),
            jax.ShapeDtypeStruct((1, LANES), F32),
            jax.ShapeDtypeStruct((1, SHARED), F32),
        ]
        + handed,
        scratch_shapes=[VMEM((ROWS, TR_DEV), FP8)] * 2
        + [VMEM((256, LANES), BF16), VMEM(TO_CMP, F32), VMEM(TO_RCV, F32)],
        compiler_params=params(24),
        cost_estimate=cost(6),
        name="count_pairs",
    )(index)


def count_scratch(chunks):
    return (
        [
            VMEM((chunks, CHUNK_ROWS, SHARED), BF16),
            VMEM((2,) + TO_CMP, jnp.int8),
            VMEM((2,) + TO_RCV, jnp.int8),
            pltpu.SemaphoreType.DMA((chunks + 4,)),
        ]
        + hot_scratch()
        + [VMEM(TO_CMP, F32), VMEM(TO_RCV, F32)]
    )


def count_operands(counts):
    big = in_hbm(*[array for pair in zip(counts[0][:3], counts[1][:3]) for array in pair])
    (most_1, diag_1), (most_2, diag_2) = counts[0][3:5], counts[1][3:5]
    return big, [diag_1, diag_2, most_1, most_2]


def normal_apply(tab, rcv, index, counts):
    (first, _, *rest), small = count_operands(counts)
    last = counts[1][5]
    return pl.pallas_call(
        normal_kernel,
        in_specs=[ANYWHERE] * 5 + [IN_VMEM] * 8,
        out_shape=table_shapes() + [jax.ShapeDtypeStruct((N_SHOT, LANES), F32)],
        scratch_shapes=[
            VMEM((2 * SLICE, N_SHOT * SRC_G), BF16),
            VMEM((2 * SLICE + 16, SHARED), BF16),
            VMEM((2 * SLICE, SHARED), F32),
            VMEM((2 * SLICE + 16, N_SHOT * SRC_G), F32),
        ]
        + count_scratch(CHUNKS // 2),
        compiler_params=params(24),
        cost_estimate=cost(3),
        name="normal_apply",
    )(first, *rest, tab, rcv, last, *small, index)


def norm_sums(tab_b, rcv_b, tab_y, rcv_y, own_count, index, counts):
    big, small = count_operands(counts)
    return pl.pallas_call(
        norm_kernel,
        in_specs=[ANYWHERE] * 6 + [IN_VMEM] * 10,
        out_shape=jax.ShapeDtypeStruct((1, LANES), F32),
        scratch_shapes=[
            VMEM((LIVE_ROWS, LANES), F32),
            VMEM(RCV, F32),
            VMEM((2 * SLICE, N_SHOT * SRC_G), BF16),
            VMEM((2 * SLICE, SHARED), BF16),
            VMEM((2 * SLICE, SHARED), F32),
        ]
        + count_scratch(CHUNKS),
        compiler_params=params(24),
        cost_estimate=cost(2),
        name="norm_sums",
    )(*big, tab_b, rcv_b, tab_y, rcv_y, *small, index, own_count)


def spread_kernel(parts, out):
    total = parts[0]
    for source in range(1, N_RCV):
        total = total + parts[source]
    for dest in range(N_RCV):
        out[dest] = total


def exchange(array, axis):
    return lax.all_to_all(array, axis, split_axis=0, concat_axis=0, tiled=True)


def spread_shares(arrived):
    shape = (N_RCV, SHARE, LANES)
    spread = pl.pallas_call(
        spread_kernel,
        out_shape=jax.ShapeDtypeStruct(shape, F32),
        compiler_params=params(24),
        cost_estimate=cost(1),
        name="sum_shares",
    )(arrived.reshape(shape))
    return spread.reshape(TAB)


def pack_kernel(tab, rcv, *refs, first):
    out, rows, sems = refs[-3:]
    lanes = lax.broadcasted_iota(jnp.int32, (SLICE, LANES), 1)
    half = SLICE // 2
    copies = []
    for dest in range(N_SHOT):
        rows[dest, :SLICE] = tab[at(dest)]
        rows[dest, SLICE : 2 * SLICE] = tab[at(OFF_TILE)]
        cmp_first = dest * CMP_G
        rcv_first = dest * (RCV_G // N_SHOT)
        bins = tab[at(CMP_TILE + cmp_first // LANES)]
        cmp_part = pltpu.roll(bins, (-cmp_first) % LANES, 1)
        rcv_part = pltpu.roll(rcv[rcv_first // LANES], (CMP_G - rcv_first) % LANES, 1)
        both = jnp.where(lanes < CMP_G, cmp_part, rcv_part)
        moved = pltpu.roll(both[half:], LANES // 2, 1)
        rows[dest, 2 * SLICE :] = jnp.where(lanes[:half] < LANES // 2, both[:half], moved)
        if dest % PACK == PACK - 1:
            group = dest // PACK
            span = slice(group * PACK, (group + 1) * PACK)
            place = out.at[span, first : first + OWN_ROWS]
            copies.append(pltpu.make_async_copy(rows.at[span], place, sems.at[group]))
            copies[-1].start()
    for copy in copies:
        copy.wait()


def pack_owned(tab, rcv, former=None):
    given = [] if former is None else in_hbm(former)
    return pl.pallas_call(
        functools.partial(pack_kernel, first=OWN_ROWS * len(given)),
        in_specs=[pl.BlockSpec(memory_space=VMEM)] * 2 + [ANYWHERE] * len(given),
        out_specs=ANYWHERE,
        out_shape=pltpu.HBM((N_SHOT, 2 * OWN_ROWS, LANES), F32),
        scratch_shapes=[
            VMEM((N_SHOT, OWN_ROWS, LANES), F32),
            pltpu.SemaphoreType.DMA((N_SHOT // PACK,)),
        ],
        input_output_aliases={2: 0} if given else {},
        compiler_params=params(24),
        cost_estimate=cost(1),
        name="pack_owned",
    )(tab, rcv, *given)


def swapped(value, axis, size, bit):
    return lax.ppermute(value, axis, [(s, s ^ bit) for s in range(size)])


def gather_sums(sums):
    for bit in (1, 2, 6):
        sums = sums + swapped(sums, "rcv", N_RCV, bit)
    here = jnp.arange(N_SHOT, dtype=jnp.int32)[:, None] == lax.axis_index("shot")
    rows = jnp.where(here, sums, 0.0)
    for bit in (1, 3, 4, 12):
        rows = rows + swapped(rows, "shot", N_SHOT, bit)
    return rows


def finish_kernel(sums, owned, source, receiver, offset, cmp):
    rows = sums[...]
    norm_b, cross, norm_z, norm_az, shift = (rows[:, lane : lane + 1] for lane in range(5))
    shift = shift * (1.0 / N_RCV)

    def total(values):
        return jnp.sum(values, axis=0, keepdims=True)

    total_b = total(norm_b)
    first = total(cross + shift * norm_b) / total_b
    off = shift - first
    zz = total(norm_z + 2.0 * off * cross + off * off * norm_b)
    zaz = total(
        norm_az
        + 2.0 * off * (norm_z + shift * cross)
        + off * off * (cross + shift * norm_b)
    )
    second = zaz / zz
    det = first * second - zz / total_b
    scale_b = (first + second) / det
    scale_y = 1.0 / det

    def combine(sender, start, stop):
        part_y = owned[sender, OWN_ROWS + start : OWN_ROWS + stop]
        return scale_b * owned[sender, start:stop] - scale_y * part_y

    def spread_halves(tile):
        return jnp.concatenate([tile, pltpu.roll(tile, LANES // 2, 1)], axis=0)

    per_tile = LANES // SLICE
    for group in range(N_SHOT // per_tile):
        span = slice(group * LANES, (group + 1) * LANES)
        senders = range(group * per_tile, (group + 1) * per_tile)
        source[:, span] = jnp.concatenate([combine(i, 0, SLICE) for i in senders], axis=0).T
        offset[:, span] = jnp.concatenate(
            [combine(i, SLICE, 2 * SLICE) for i in senders], axis=0
        ).T
        rest = jnp.concatenate(
            [spread_halves(combine(i, 2 * SLICE, OWN_ROWS)) for i in senders], axis=0
        ).T
        cmp[:, span] = rest[:CMP_G]
        receiver[0, :, span] = rest[CMP_G : CMP_G + RCV_G // N_SHOT]


def finish(sums, owned):
    return pl.pallas_call(
        finish_kernel,
        out_shape=[
            jax.ShapeDtypeStruct((SRC_G, FREQS), F32),
            jax.ShapeDtypeStruct((1, RCV_G // N_SHOT, FREQS), F32),
            jax.ShapeDtypeStruct((128, FREQS), F32),
            jax.ShapeDtypeStruct((CMP_G, FREQS), F32),
        ],
        compiler_params=params(),
        name="finish",
    )(sums, owned)


def per_device(basis, traces, src_index, rcv_index, off_index, send_rows, send_counts, recv_bins):
    data = log_spectra(
        traces, basis, send_rows[0], send_counts, recv_bins[0], src_index, rcv_index, off_index
    )
    data = exchange(data, "shot")

    tab_b, rcv_b, index = adjoint_apply(data)
    arrived = exchange(tab_b, "rcv")
    counts_1 = count_call(index, 0)
    arrived, index, counts_1 = lax.optimization_barrier((arrived, index, counts_1))
    spread = spread_shares(arrived)
    spread, index = lax.optimization_barrier((spread, index))
    tab_b = exchange(spread, "rcv")
    counts = (counts_1, count_call(index, HALF))

    tab_y, rcv_y, own_count = normal_apply(tab_b, rcv_b, index, counts)
    arrived = exchange(tab_y, "rcv")
    packed = pack_owned(tab_b, rcv_b)
    arrived, packed = lax.optimization_barrier((arrived, packed))
    tab_y = exchange(spread_shares(arrived), "rcv")
    packed = pack_owned(tab_y, rcv_y, packed)
    tab_y, packed = lax.optimization_barrier((tab_y, packed))
    owned = exchange(packed, "shot")
    sums = norm_sums(tab_b, rcv_b, tab_y, rcv_y, own_count, index, counts)
    return tuple(finish(gather_sums(sums), owned))


def solution(mesh):
    basis = fourier_rows()
    mapped = jax.shard_map(
        per_device,
        mesh=mesh,
        in_specs=(
            P(),
            P(("shot", "rcv"), None),
            P(("shot", "rcv")),
            P(("shot", "rcv")),
            P(("shot", "rcv")),
            P(("shot", "rcv"), None, None),
            P(("shot", "rcv"), None),
            P(("shot", "rcv"), None, None),
        ),
        out_specs=(P("shot", None), P("rcv", "shot", None), P(), P("shot", None)),
        check_vma=False,
    )

    def run(*args):
        return mapped(jnp.asarray(basis), *args)

    return run
```

```python
import functools

import ml_dtypes
import numpy as np

import jax
import jax.numpy as jnp
from jax import lax
from jax.experimental import pallas as pl
from jax.experimental.pallas import tpu as pltpu
from jax.sharding import PartitionSpec as P

SAMPLES = 1024
FREQS = 512
TR_DEV = 640
N_SHOT = 16
N_RCV = 8
DEVICES = 128
CAP = 80
SRC_G = 128
RCV_G = 256
CMP_G = 32
SLICE = FREQS // N_SHOT
LANES = 128
OFF_TILE = 16
CMP_TILE = 17
LIVE_TILES = 21
LIVE_ROWS = LIVE_TILES * SLICE
SHARE = -(-LIVE_ROWS // (8 * N_RCV)) * 8
TAB_ROWS = N_RCV * SHARE
RCV_TILES = 2
ROWS = SRC_G + RCV_G + 128 + 512
SHARED = ROWS - SRC_G
SO = 2 * LANES
SOR = SO + RCV_G
OR = LANES + RCV_G
HALF = N_SHOT // 2
COUNT_STEPS = HALF // 2
CHUNKS = 4
CHUNK_ROWS = N_SHOT * SRC_G // CHUNKS
TRACE_TILES = TR_DEV // LANES
BINS_AT = TRACE_TILES * SLICE
INDEX_AT = BINS_AT + N_SHOT
INDEX_ROWS = 24
DATA_ROWS = INDEX_AT + INDEX_ROWS
STEPS = 2
OWN_ROWS = 2 * SLICE + SLICE // 2
PACK = LANES // CMP_G

VMEM = pltpu.VMEM
F32 = jnp.float32
BF16 = jnp.bfloat16
FP8 = jnp.float8_e4m3fn


def fourier_rows():
    phase = np.arange(FREQS)[:, None] * np.arange(SAMPLES)[None, :] % SAMPLES
    angle = phase * (2.0 * np.pi / SAMPLES)
    waves = np.stack([np.cos(angle), np.sin(angle)]).reshape(2, STEPS, -1, SAMPLES)
    table = waves.transpose(1, 0, 2, 3).reshape(2 * FREQS, SAMPLES) / np.sqrt(SAMPLES)
    return table.astype(np.float32).astype(ml_dtypes.bfloat16)


def params(mib=48):
    return pltpu.CompilerParams(vmem_limit_bytes=mib * 2**20)


def cost(micros):
    return pl.CostEstimate(flops=int(micros * 1e9), bytes_accessed=int(micros * 3e6), transcendentals=0)


ANYWHERE = pl.BlockSpec(memory_space=pltpu.HBM)


def in_hbm(*arrays):
    return [pltpu.with_memory_space_constraint(array, pltpu.HBM) for array in arrays]


def nt_dot(left, right):
    return lax.dot_general(left, right, (((1,), (1,)), ((), ())), preferred_element_type=F32)


def split_rows(values):
    high = values.astype(BF16)
    low = (values - high.astype(F32)).astype(BF16)
    return jnp.concatenate([high, low], axis=0)


def at(tile):
    if isinstance(tile, int):
        return slice(tile * SLICE, (tile + 1) * SLICE)
    return pl.ds(pl.multiple_of(tile * SLICE, SLICE), SLICE)


def join_rows(both):
    half = both.shape[0] // 2
    return both[:half] + both[half:]


def flip(table):
    wide = jnp.concatenate(
        [table.astype(F32), jnp.zeros((N_SHOT, LANES - CAP), F32)], axis=1
    )
    return wide.T[:CAP].astype(jnp.int32)


def index_tiles(send_rows, send_counts, src, rcv, off):
    slots = lax.broadcasted_iota(jnp.int32, (CAP, N_SHOT), 0)
    targets = jnp.where(slots < send_counts[...], flip(send_rows[...]), -1)
    trace_ids = lax.broadcasted_iota(jnp.int32, (CAP, TR_DEV), 1)
    places = lax.broadcasted_iota(jnp.int32, (CAP, TR_DEV), 0)
    total = jnp.zeros((CAP, TR_DEV), jnp.int32)
    for owner in range(N_SHOT):
        hit = targets[:, owner : owner + 1] == trace_ids
        total = total + jnp.where(hit, places + owner * LANES, 0)
    slot_row = jnp.sum(total, axis=0, keepdims=True)
    rows = [src[...] & (SRC_G - 1), rcv[...] & (RCV_G - 1), off[...]]
    rows = [row.reshape(1, TR_DEV) for row in rows] + [slot_row]
    table = jnp.concatenate(rows, axis=0).astype(F32)
    tiles = [table[:, q * LANES : (q + 1) * LANES] for q in range(TRACE_TILES)]
    tiles.append(jnp.zeros((INDEX_ROWS - 4 * TRACE_TILES, LANES), F32))
    return jnp.concatenate(tiles, axis=0)


def spectra_kernel(traces, waves, *refs):
    given, out, own, basis, extra = refs[:6], refs[6], refs[7], refs[8], refs[9]
    small, sems, small_sems = refs[10:16], refs[16], refs[17]
    indices = [
        pltpu.make_async_copy(a, b, small_sems.at[k]) for k, (a, b) in enumerate(zip(given, small))
    ]
    for copy in indices:
        copy.start()
    pieces = []
    for k in range(TRACE_TILES):
        span = slice(k * LANES, (k + 1) * LANES)
        pieces.append((traces.at[span], own.at[span]))
    size = 2 * FREQS // STEPS // 2
    for k in range(2 * STEPS):
        span = slice(k * size, (k + 1) * size)
        pieces.append((waves.at[span], basis.at[span]))
    copies = [pltpu.make_async_copy(a, b, sems.at[k]) for k, (a, b) in enumerate(pieces)]
    early = TRACE_TILES + 2
    for copy in copies[:early]:
        copy.start()
    for copy in indices:
        copy.wait()
    send_rows, send_counts, bins, src, rcv, off = small
    pad = jnp.zeros((N_SHOT, LANES - CAP), F32)
    extra[:N_SHOT] = jnp.concatenate([bins[...].astype(F32), pad], axis=1)
    extra[N_SHOT:] = index_tiles(send_rows, send_counts, src, rcv, off)
    for part in range(N_SHOT):
        out[part, BINS_AT:, :] = extra[...]
    for copy in copies[:early]:
        copy.wait()
    for copy in copies[early:]:
        copy.start()
    half = FREQS // STEPS
    for step in range(STEPS):
        if step == 1:
            for copy in copies[early:]:
                copy.wait()
        parts = nt_dot(basis[2 * half * step : 2 * half * (step + 1)], own[...])
        logs = jnp.log1p(parts[:half] * parts[:half] + parts[half:] * parts[half:])
        for part in range(half // SLICE):
            for q in range(TRACE_TILES):
                out[step * (half // SLICE) + part, q * SLICE : (q + 1) * SLICE, :] = logs[
                    part * SLICE : (part + 1) * SLICE, q * LANES : (q + 1) * LANES
                ]


def log_spectra(traces, basis, *small):
    return pl.pallas_call(
        spectra_kernel,
        in_specs=[ANYWHERE] * (2 + len(small)),
        out_shape=jax.ShapeDtypeStruct((N_SHOT, DATA_ROWS, LANES), F32),
        scratch_shapes=[
            VMEM((TR_DEV, SAMPLES), BF16),
            VMEM((2 * FREQS, SAMPLES), BF16),
            VMEM((DATA_ROWS - BINS_AT, LANES), F32),
        ]
        + [VMEM(array.shape, jnp.int32) for array in small]
        + [
            pltpu.SemaphoreType.DMA((TRACE_TILES + 2 * STEPS,)),
            pltpu.SemaphoreType.DMA((len(small),)),
        ],
        compiler_params=params(24),
        cost_estimate=cost(5),
        name="spectra",
    )(*in_hbm(traces, basis, *small))


def fill_ids(ids):
    ids[...] = lax.broadcasted_iota(jnp.int32, ids.shape, 0).astype(F32).astype(BF16)


def fill_hot(tiles, ids, hot):
    one = jnp.ones((1, 1), BF16)
    zero = jnp.zeros((1, 1), BF16)
    values = tiles.astype(F32)
    for q in range(TRACE_TILES):
        span = slice(q * LANES, (q + 1) * LANES)
        first = 0
        for row, size, base in ((0, SRC_G, 0), (2, 128, 0), (1, RCV_G, 0), (3, 256, 0), (3, 256, 256)):
            wanted = (values[4 * q + row : 4 * q + row + 1] - base).astype(BF16)
            hits = jnp.where(ids[:size] == wanted, one, zero)
            hot[first : first + size, span] = hits.astype(hot.dtype)
            first += size


def resolve_bins(data, block):
    tiles = data[block, INDEX_AT:].astype(jnp.int32)
    rows = [data[owner, pl.ds(BINS_AT + block, 1)] for owner in range(N_SHOT)]
    table = jnp.concatenate(rows, axis=0)
    owners = lax.broadcasted_iota(jnp.int32, (N_SHOT, LANES), 0)
    resolved = []
    for q in range(TRACE_TILES):
        slot = tiles[4 * q + 3 : 4 * q + 4]
        place = jnp.broadcast_to(slot & (LANES - 1), (N_SHOT, LANES))
        found = jnp.take_along_axis(table, place, axis=1, mode="promise_in_bounds")
        found = jnp.where(owners == slot >> 7, found.astype(jnp.int32) + owners * CMP_G, 0)
        resolved += [tiles[4 * q : 4 * q + 3], jnp.sum(found, axis=0, keepdims=True)]
    resolved.append(jnp.zeros((INDEX_ROWS - 4 * TRACE_TILES, LANES), jnp.int32))
    return jnp.concatenate(resolved, axis=0)


def prepare_block(data, index, ids, hot, block):
    tiles = resolve_bins(data, block)
    index[block] = tiles
    one = jnp.ones((1, 1), BF16)
    zero = jnp.zeros((1, 1), BF16)
    for q in range(TRACE_TILES):
        for place, row in enumerate((0, 2, 1, 3)):
            lane = tiles[4 * q + row : 4 * q + row + 1] & (LANES - 1)
            hit = ids[:LANES] == lane.astype(F32).astype(BF16)
            span = slice(q * LANES, (q + 1) * LANES)
            hot[place * LANES : (place + 1) * LANES, span] = jnp.where(hit, one, zero)


def add_block(data, index, hot, tab, rcv, block):
    tiles = index[block]
    values = [data[block, q * SLICE : (q + 1) * SLICE] for q in range(TRACE_TILES)]

    both = split_rows(jnp.concatenate(values, axis=1))
    zero = jnp.zeros((1, 1), BF16)

    def of_tiles(row, count):
        place = [tiles[4 * q + row : 4 * q + row + 1] >> 7 for q in range(TRACE_TILES)]
        place = jnp.concatenate(place, axis=1).astype(F32).astype(BF16)
        return jnp.concatenate([jnp.where(place == tile, both, zero) for tile in range(count)], axis=0)

    plain = nt_dot(both, hot[: 2 * LANES])
    tab[at(block)] = join_rows(plain[:, :LANES])
    tab[at(OFF_TILE)] += join_rows(plain[:, LANES:])
    parts = of_tiles(1, RCV_TILES)
    sums = nt_dot(parts, hot[2 * LANES : 3 * LANES])
    for tile in range(RCV_TILES):
        rcv[tile] += join_rows(sums[tile * 2 * SLICE : (tile + 1) * 2 * SLICE])
    cmp_tiles = LIVE_TILES - CMP_TILE
    parts = of_tiles(3, cmp_tiles)
    sums = nt_dot(parts, hot[3 * LANES :])
    for tile in range(cmp_tiles):
        tab[at(CMP_TILE + tile)] += join_rows(sums[tile * 2 * SLICE : (tile + 1) * 2 * SLICE])


def adjoint_kernel(data, tab, rcv, index, hot_even, hot_odd, ids):
    tab[OFF_TILE * SLICE :] = jnp.zeros((TAB_ROWS - OFF_TILE * SLICE, LANES), F32)
    rcv[...] = jnp.zeros((RCV_TILES, SLICE, LANES), F32)
    fill_ids(ids)
    prepare_block(data, index, ids, hot_even, 0)

    @pl.loop(0, N_SHOT // 2)
    def _(pair):
        even = 2 * pair
        prepare_block(data, index, ids, hot_odd, even + 1)
        add_block(data, index, hot_even, tab, rcv, even)
        prepare_block(data, index, ids, hot_even, jnp.minimum(even + 2, N_SHOT - 1))
        add_block(data, index, hot_odd, tab, rcv, even + 1)


EXACT = 128


def kept_part(counts):
    return (counts.astype(jnp.int32) & (EXACT - 1)).astype(F32).astype(BF16)


def left_over(counts):
    whole = counts.astype(jnp.int32)
    return (whole - (whole & (EXACT - 1))).astype(F32).astype(BF16)


def peak(counts):
    top = jnp.max(counts, axis=0, keepdims=True)
    best = top[:, :LANES]
    for start in range(LANES, counts.shape[1], LANES):
        best = jnp.maximum(best, top[:, start : start + LANES])
    return best


def block_counts(hot):
    with_cmp = nt_dot(hot[:SOR], hot[SOR:])
    with_rcv = nt_dot(hot[:SO], hot[SO:SOR])
    with_off = nt_dot(hot[:SRC_G], hot[SRC_G:SO])
    rows = jnp.concatenate([with_off, with_rcv[:SRC_G], with_cmp[:SRC_G]], axis=1)
    return rows, with_cmp[SRC_G:], with_rcv[SRC_G:]


def count_kernel(
    index, kept, to_cmp_kept, to_rcv_kept, most, diag, hot_even, hot_odd, ids, to_cmp, to_rcv, *, first
):
    step = pl.program_id(0)
    even = first + 2 * step

    @pl.when(step == 0)
    def _():
        to_cmp[...] = jnp.zeros_like(to_cmp)
        to_rcv[...] = jnp.zeros_like(to_rcv)
        diag[...] = jnp.zeros_like(diag)
        most[...] = jnp.zeros_like(most)
        fill_ids(ids)
        fill_hot(index[even], ids, hot_even)

    def add(hot, place):
        rows, cmp_counts, rcv_counts = block_counts(hot)
        to_cmp[...] += cmp_counts
        to_rcv[...] += rcv_counts
        diag[...] += jnp.sum(rows, axis=0, keepdims=True)
        kept[place * SRC_G : (place + 1) * SRC_G] = kept_part(rows)
        most[...] = jnp.maximum(most[...], peak(rows))

    fill_hot(index[even + 1], ids, hot_odd)
    add(hot_even, 0)
    fill_hot(index[jnp.minimum(even + 2, N_SHOT - 1)], ids, hot_even)
    add(hot_odd, 1)

    @pl.when(step == COUNT_STEPS - 1)
    def _():
        to_cmp_kept[...] = kept_part(to_cmp[...])
        to_rcv_kept[...] = kept_part(to_rcv[...])
        most[...] = jnp.maximum(most[...], jnp.maximum(peak(to_cmp[...]), peak(to_rcv[...])))


def add_left_over(most_1, most_2, index, hot, ids, to_cmp, to_rcv, use_both, use_rows):
    top = jnp.maximum(jnp.max(most_1[...]), jnp.max(most_2[...]))

    @pl.when(top >= EXACT)
    def _():
        fill_ids(ids)
        for half in range(2):
            to_cmp[...] = jnp.zeros_like(to_cmp)
            to_rcv[...] = jnp.zeros_like(to_rcv)

            @pl.loop(half * HALF, (half + 1) * HALF)
            def _(block):
                fill_hot(index[block], ids, hot)
                rows, cmp_counts, rcv_counts = block_counts(hot)
                to_cmp[...] += cmp_counts
                to_rcv[...] += rcv_counts
                use_rows(block, left_over(rows))

            use_both(left_over(to_cmp[...]), left_over(to_rcv[...]))


def sum_halves(first, last):
    return (first[...].astype(F32) + last[...].astype(F32)).astype(BF16)


def load_halves(tab, rcv, own, shared):
    for tile in range(N_SHOT):
        own[:, tile * LANES : (tile + 1) * LANES] = split_rows(tab[at(tile)])
    shared[: 2 * SLICE, :LANES] = split_rows(tab[at(OFF_TILE)])
    for tile in range(RCV_TILES):
        shared[: 2 * SLICE, (1 + tile) * LANES : (2 + tile) * LANES] = split_rows(rcv[tile])
    for tile in range(CMP_TILE, LIVE_TILES):
        start = (tile - CMP_TILE) * LANES + OR
        shared[: 2 * SLICE, start : start + LANES] = split_rows(tab[at(tile)])


def normal_kernel(
    first, last, cmp_1, cmp_2, rcv_1, rcv_2, tab_in, rcv_in, diag_1, diag_2, most_1, most_2, index,
    tab, rcv, own_count, own, shared, to_shared, to_own, hot, ids, exact_cmp, exact_rcv,
):
    top = 2 * SLICE
    half = HALF * SRC_G
    load_halves(tab_in, rcv_in, own, shared)
    lanes = lax.broadcasted_iota(jnp.int32, (16, SHARED), 1)
    shared[top:] = jnp.where(lanes < LANES, 1.0, 0.0).astype(BF16)
    sums = jnp.dot(own[:, :half], first[...], preferred_element_type=F32)
    to_shared[...] = sums + jnp.dot(own[:, half:], last[...], preferred_element_type=F32)
    to_own[:, :half] = nt_dot(shared[...], first[...])
    to_own[:, half:] = nt_dot(shared[...], last[...])

    def others(to_cmp, to_rcv):
        cmp_sums = jnp.dot(shared[:top, :OR], to_cmp, preferred_element_type=F32)
        to_shared[:, OR:] += cmp_sums
        to_shared[:, :OR] += nt_dot(shared[:top, OR:], to_cmp)
        rcv_sums = jnp.dot(shared[:top, :LANES], to_rcv, preferred_element_type=F32)
        to_shared[:, LANES:OR] += rcv_sums
        to_shared[:, :LANES] += nt_dot(shared[:top, LANES:OR], to_rcv)

    def use_rows(block, rows):
        span = pl.ds(pl.multiple_of(block * SRC_G, SRC_G), SRC_G)
        to_shared[...] += jnp.dot(own[:, span], rows, preferred_element_type=F32)
        to_own[:, span] += nt_dot(shared[...], rows)

    others(sum_halves(cmp_1, cmp_2), sum_halves(rcv_1, rcv_2))
    add_left_over(most_1, most_2, index, hot, ids, exact_cmp, exact_rcv, others, use_rows)
    diag = diag_1[...] + diag_2[...]
    for tile in range(N_SHOT):
        span = slice(tile * LANES, (tile + 1) * LANES)
        count = to_own[top : top + 1, span]
        own_count[tile : tile + 1] = count
        tab[at(tile)] = join_rows(to_own[:top, span]) + count * tab_in[at(tile)]
    tab[at(OFF_TILE)] = join_rows(to_shared[:, :LANES]) + diag[:, :LANES] * tab_in[at(OFF_TILE)]
    for tile in range(RCV_TILES):
        span = slice((1 + tile) * LANES, (2 + tile) * LANES)
        rcv[tile] = join_rows(to_shared[:, span]) + diag[:, span] * rcv_in[tile]
    for tile in range(CMP_TILE, LIVE_TILES):
        start = (tile - CMP_TILE) * LANES + OR
        span = slice(start, start + LANES)
        tab[at(tile)] = join_rows(to_shared[:, span]) + diag[:, span] * tab_in[at(tile)]
    tab[LIVE_ROWS:] = jnp.zeros((TAB_ROWS - LIVE_ROWS, LANES), F32)


def all_sum(values):
    return jnp.sum(values, axis=tuple(range(values.ndim)), keepdims=True).reshape(1, 1)


def fold(values):
    total = values[:, :LANES]
    for start in range(LANES, values.shape[1], LANES):
        total = total + values[:, start : start + LANES]
    return total


def norm_kernel(
    first, last, cmp_1, cmp_2, rcv_1, rcv_2,
    tab_b, rcv_b, tab_y, rcv_y, diag_1, diag_2, most_1, most_2, index, own_count,
    out, tab_z, rcv_z, own, shared, to_shared, hot, ids, exact_cmp, exact_rcv,
):
    shared_b = tab_b[:LIVE_ROWS]
    shared_y = tab_y[:LIVE_ROWS]
    shift = all_sum(shared_b * shared_y) / all_sum(shared_b * shared_b)
    shared_z = shared_y - shift * shared_b
    own_b = rcv_b[...]
    own_z = rcv_y[...] - shift * own_b
    tab_z[...] = shared_z
    rcv_z[...] = own_z
    load_halves(tab_z, rcv_z, own, shared)
    half = HALF * SRC_G
    sums = jnp.dot(own[:, :half], first[...], preferred_element_type=F32)
    to_shared[...] = sums + jnp.dot(own[:, half:], last[...], preferred_element_type=F32)

    def whole(tabs, own):
        return all_sum(tabs) * (1.0 / N_RCV) + all_sum(own)

    def others(to_cmp, to_rcv):
        cmp_sums = jnp.dot(shared[:, :OR], to_cmp, preferred_element_type=F32)
        to_shared[:, OR:] += cmp_sums
        rcv_sums = jnp.dot(shared[:, :LANES], to_rcv, preferred_element_type=F32)
        to_shared[:, LANES:OR] += rcv_sums

    def use_rows(block, rows):
        span = pl.ds(pl.multiple_of(block * SRC_G, SRC_G), SRC_G)
        to_shared[...] += jnp.dot(own[:, span], rows, preferred_element_type=F32)

    others(sum_halves(cmp_1, cmp_2), sum_halves(rcv_1, rcv_2))
    add_left_over(most_1, most_2, index, hot, ids, exact_cmp, exact_rcv, others, use_rows)
    tiles = [tab_z[at(OFF_TILE)]] + [rcv_z[tile] for tile in range(RCV_TILES)]
    tiles += [tab_z[at(tile)] for tile in range(CMP_TILE, LIVE_TILES)]
    rest = jnp.concatenate(tiles, axis=1)
    diag = diag_1[...] + diag_2[...]
    total = fold(2.0 * rest * join_rows(to_shared[...]) + diag * rest * rest)
    for tile in range(N_SHOT):
        total = total + own_count[tile : tile + 1] * tab_z[at(tile)] * tab_z[at(tile)]
    sums = (
        whole(shared_b * shared_b, own_b * own_b),
        whole(shared_b * shared_z, own_b * own_z),
        whole(shared_z * shared_z, own_z * own_z),
        all_sum(total),
        shift,
    )
    lanes = lax.broadcasted_iota(jnp.int32, (1, LANES), 1)
    row = jnp.zeros((1, LANES), F32)
    for lane, value in enumerate(sums):
        row = jnp.where(lanes == lane, value, row)
    out[...] = row


def whole_spec(*shape):
    return pl.BlockSpec(shape, lambda c: (0,) * len(shape))


TAB = (TAB_ROWS, LANES)
RCV = (RCV_TILES, SLICE, LANES)
INDEX = (N_SHOT, INDEX_ROWS, LANES)
INDEX_SPEC = pl.BlockSpec((1, INDEX_ROWS, LANES), lambda c: (c, 0, 0))


def table_shapes():
    return [jax.ShapeDtypeStruct(TAB, F32), jax.ShapeDtypeStruct(RCV, F32)]


def hot_scratch():
    return [VMEM((ROWS, TR_DEV), FP8), VMEM((256, LANES), BF16)]


def adjoint_apply(data):
    return pl.pallas_call(
        adjoint_kernel,
        out_shape=table_shapes() + [jax.ShapeDtypeStruct(INDEX, jnp.int32)],
        scratch_shapes=[VMEM((4 * LANES, TR_DEV), BF16)] * 2 + [VMEM((256, LANES), BF16)],
        compiler_params=params(24),
        cost_estimate=cost(8),
        name="adjoint_apply",
    )(data)


COUNTS = (HALF * SRC_G, SHARED)
TO_CMP = (OR, SHARED - OR)
TO_RCV = (LANES, RCV_G)
IN_VMEM = pl.BlockSpec(memory_space=VMEM)


def count_call(index, first):
    rows = pl.BlockSpec((2 * SRC_G, SHARED), lambda c: (c, 0))
    small = [whole_spec(*TO_CMP), whole_spec(*TO_RCV), whole_spec(1, LANES), whole_spec(1, SHARED)]
    return pl.pallas_call(
        functools.partial(count_kernel, first=first),
        grid=(COUNT_STEPS,),
        in_specs=[whole_spec(*INDEX)],
        out_specs=[rows] + small,
        out_shape=[
            VMEM(COUNTS, BF16),
            VMEM(TO_CMP, BF16),
            VMEM(TO_RCV, BF16),
            jax.ShapeDtypeStruct((1, LANES), F32),
            jax.ShapeDtypeStruct((1, SHARED), F32),
        ],
        scratch_shapes=[VMEM((ROWS, TR_DEV), FP8)] * 2
        + [VMEM((256, LANES), BF16), VMEM(TO_CMP, F32), VMEM(TO_RCV, F32)],
        compiler_params=params(16),
        cost_estimate=cost(6),
        name="count_pairs",
    )(index)


def exact_scratch():
    return hot_scratch() + [VMEM(TO_CMP, F32), VMEM(TO_RCV, F32)]


def count_operands(counts):
    pairs = [array for pair in zip(counts[0][:3], counts[1][:3]) for array in pair]
    big = [pltpu.with_memory_space_constraint(array, VMEM) for array in pairs]
    (most_1, diag_1), (most_2, diag_2) = counts[0][3:], counts[1][3:]
    return big, [diag_1, diag_2, most_1, most_2]


def normal_apply(tab, rcv, index, counts):
    big, small = count_operands(counts)
    return pl.pallas_call(
        normal_kernel,
        out_shape=table_shapes() + [jax.ShapeDtypeStruct((N_SHOT, LANES), F32)],
        scratch_shapes=[
            VMEM((2 * SLICE, N_SHOT * SRC_G), BF16),
            VMEM((2 * SLICE + 16, SHARED), BF16),
            VMEM((2 * SLICE, SHARED), F32),
            VMEM((2 * SLICE + 16, N_SHOT * SRC_G), F32),
        ]
        + exact_scratch(),
        compiler_params=params(16),
        cost_estimate=cost(3),
        name="normal_apply",
    )(*big, tab, rcv, *small, index)


def norm_sums(tab_b, rcv_b, tab_y, rcv_y, own_count, index, counts):
    big, small = count_operands(counts)
    return pl.pallas_call(
        norm_kernel,
        out_shape=jax.ShapeDtypeStruct((1, LANES), F32),
        scratch_shapes=[
            VMEM((LIVE_ROWS, LANES), F32),
            VMEM(RCV, F32),
            VMEM((2 * SLICE, N_SHOT * SRC_G), BF16),
            VMEM((2 * SLICE, SHARED), BF16),
            VMEM((2 * SLICE, SHARED), F32),
        ]
        + exact_scratch(),
        compiler_params=params(16),
        cost_estimate=cost(2),
        name="norm_sums",
    )(*big, tab_b, rcv_b, tab_y, rcv_y, *small, index, own_count)


def spread_kernel(parts, out):
    total = parts[0]
    for source in range(1, N_RCV):
        total = total + parts[source]
    for dest in range(N_RCV):
        out[dest] = total


def exchange(array, axis):
    return lax.all_to_all(array, axis, split_axis=0, concat_axis=0, tiled=True)


def spread_shares(arrived):
    shape = (N_RCV, SHARE, LANES)
    spread = pl.pallas_call(
        spread_kernel,
        out_shape=jax.ShapeDtypeStruct(shape, F32),
        compiler_params=params(24),
        cost_estimate=cost(1),
        name="sum_shares",
    )(arrived.reshape(shape))
    return spread.reshape(TAB)


def pack_kernel(tab, rcv, *refs, first):
    out, rows, sems = refs[-3:]
    lanes = lax.broadcasted_iota(jnp.int32, (SLICE, LANES), 1)
    half = SLICE // 2
    copies = []
    for dest in range(N_SHOT):
        rows[dest, :SLICE] = tab[at(dest)]
        rows[dest, SLICE : 2 * SLICE] = tab[at(OFF_TILE)]
        cmp_first = dest * CMP_G
        rcv_first = dest * (RCV_G // N_SHOT)
        bins = tab[at(CMP_TILE + cmp_first // LANES)]
        cmp_part = pltpu.roll(bins, (-cmp_first) % LANES, 1)
        rcv_part = pltpu.roll(rcv[rcv_first // LANES], (CMP_G - rcv_first) % LANES, 1)
        both = jnp.where(lanes < CMP_G, cmp_part, rcv_part)
        moved = pltpu.roll(both[half:], LANES // 2, 1)
        rows[dest, 2 * SLICE :] = jnp.where(lanes[:half] < LANES // 2, both[:half], moved)
        if dest % PACK == PACK - 1:
            group = dest // PACK
            span = slice(group * PACK, (group + 1) * PACK)
            place = out.at[span, first : first + OWN_ROWS]
            copies.append(pltpu.make_async_copy(rows.at[span], place, sems.at[group]))
            copies[-1].start()
    for copy in copies:
        copy.wait()


def pack_owned(tab, rcv, former=None):
    given = [] if former is None else in_hbm(former)
    return pl.pallas_call(
        functools.partial(pack_kernel, first=OWN_ROWS * len(given)),
        in_specs=[pl.BlockSpec(memory_space=VMEM)] * 2 + [ANYWHERE] * len(given),
        out_specs=ANYWHERE,
        out_shape=pltpu.HBM((N_SHOT, 2 * OWN_ROWS, LANES), F32),
        scratch_shapes=[
            VMEM((N_SHOT, OWN_ROWS, LANES), F32),
            pltpu.SemaphoreType.DMA((N_SHOT // PACK,)),
        ],
        input_output_aliases={2: 0} if given else {},
        compiler_params=params(24),
        cost_estimate=cost(1),
        name="pack_owned",
    )(tab, rcv, *given)


def swapped(value, axis, size, bit):
    return lax.ppermute(value, axis, [(s, s ^ bit) for s in range(size)])


def gather_sums(sums):
    for bit in (1, 2, 6):
        sums = sums + swapped(sums, "rcv", N_RCV, bit)
    here = jnp.arange(N_SHOT, dtype=jnp.int32)[:, None] == lax.axis_index("shot")
    rows = jnp.where(here, sums, 0.0)
    for bit in (1, 3, 4, 12):
        rows = rows + swapped(rows, "shot", N_SHOT, bit)
    return rows


def finish_kernel(sums, owned, source, receiver, offset, cmp):
    rows = sums[...]
    norm_b, cross, norm_z, norm_az, shift = (rows[:, lane : lane + 1] for lane in range(5))
    shift = shift * (1.0 / N_RCV)

    def total(values):
        return jnp.sum(values, axis=0, keepdims=True)

    total_b = total(norm_b)
    first = total(cross + shift * norm_b) / total_b
    off = shift - first
    zz = total(norm_z + 2.0 * off * cross + off * off * norm_b)
    zaz = total(
        norm_az
        + 2.0 * off * (norm_z + shift * cross)
        + off * off * (cross + shift * norm_b)
    )
    second = zaz / zz
    det = first * second - zz / total_b
    scale_b = (first + second) / det
    scale_y = 1.0 / det

    def combine(sender, start, stop):
        part_y = owned[sender, OWN_ROWS + start : OWN_ROWS + stop]
        return scale_b * owned[sender, start:stop] - scale_y * part_y

    def spread_halves(tile):
        return jnp.concatenate([tile, pltpu.roll(tile, LANES // 2, 1)], axis=0)

    per_tile = LANES // SLICE
    for group in range(N_SHOT // per_tile):
        span = slice(group * LANES, (group + 1) * LANES)
        senders = range(group * per_tile, (group + 1) * per_tile)
        source[:, span] = jnp.concatenate([combine(i, 0, SLICE) for i in senders], axis=0).T
        offset[:, span] = jnp.concatenate(
            [combine(i, SLICE, 2 * SLICE) for i in senders], axis=0
        ).T
        rest = jnp.concatenate(
            [spread_halves(combine(i, 2 * SLICE, OWN_ROWS)) for i in senders], axis=0
        ).T
        cmp[:, span] = rest[:CMP_G]
        receiver[0, :, span] = rest[CMP_G : CMP_G + RCV_G // N_SHOT]


def finish(sums, owned):
    return pl.pallas_call(
        finish_kernel,
        out_shape=[
            jax.ShapeDtypeStruct((SRC_G, FREQS), F32),
            jax.ShapeDtypeStruct((1, RCV_G // N_SHOT, FREQS), F32),
            jax.ShapeDtypeStruct((128, FREQS), F32),
            jax.ShapeDtypeStruct((CMP_G, FREQS), F32),
        ],
        compiler_params=params(),
        name="finish",
    )(sums, owned)


def per_device(basis, traces, src_index, rcv_index, off_index, send_rows, send_counts, recv_bins):
    data = log_spectra(
        traces, basis, send_rows[0], send_counts, recv_bins[0], src_index, rcv_index, off_index
    )
    data = exchange(data, "shot")

    tab_b, rcv_b, index = adjoint_apply(data)
    arrived = exchange(tab_b, "rcv")
    counts_1 = count_call(index, 0)
    arrived, index, counts_1 = lax.optimization_barrier((arrived, index, counts_1))
    spread = spread_shares(arrived)
    spread, index = lax.optimization_barrier((spread, index))
    tab_b = exchange(spread, "rcv")
    counts = (counts_1, count_call(index, HALF))

    tab_y, rcv_y, own_count = normal_apply(tab_b, rcv_b, index, counts)
    arrived = exchange(tab_y, "rcv")
    packed = pack_owned(tab_b, rcv_b)
    arrived, packed = lax.optimization_barrier((arrived, packed))
    tab_y = exchange(spread_shares(arrived), "rcv")
    packed = pack_owned(tab_y, rcv_y, packed)
    tab_y, packed = lax.optimization_barrier((tab_y, packed))
    owned = exchange(packed, "shot")
    sums = norm_sums(tab_b, rcv_b, tab_y, rcv_y, own_count, index, counts)
    return tuple(finish(gather_sums(sums), owned))


def solution(mesh):
    basis = fourier_rows()
    mapped = jax.shard_map(
        per_device,
        mesh=mesh,
        in_specs=(
            P(),
            P(("shot", "rcv"), None),
            P(("shot", "rcv")),
            P(("shot", "rcv")),
            P(("shot", "rcv")),
            P(("shot", "rcv"), None, None),
            P(("shot", "rcv"), None),
            P(("shot", "rcv"), None, None),
        ),
        out_specs=(P("shot", None), P("rcv", "shot", None), P(), P("shot", None)),
        check_vma=False,
    )

    def run(*args):
        return mapped(jnp.asarray(basis), *args)

    return run
```

```python
import functools

import ml_dtypes
import numpy as np

import jax
import jax.numpy as jnp
from jax import lax
from jax.experimental import pallas as pl
from jax.experimental.pallas import tpu as pltpu
from jax.sharding import PartitionSpec as P

SAMPLES = 1024
FREQS = 512
TR_DEV = 640
N_SHOT = 16
N_RCV = 8
DEVICES = 128
CAP = 80
SRC_G = 128
RCV_G = 256
CMP_G = 32
SLICE = FREQS // N_SHOT
LANES = 128
OFF_TILE = 16
CMP_TILE = 17
LIVE_TILES = 21
LIVE_ROWS = LIVE_TILES * SLICE
SHARE = -(-LIVE_ROWS // (8 * N_RCV)) * 8
TAB_ROWS = N_RCV * SHARE
RCV_TILES = 2
ROWS = SRC_G + RCV_G + 128 + 512
SHARED = ROWS - SRC_G
SO = 2 * LANES
SOR = SO + RCV_G
OR = LANES + RCV_G
HALF = N_SHOT // 2
COUNT_STEPS = HALF // 2
CHUNKS = 4
CHUNK_ROWS = N_SHOT * SRC_G // CHUNKS
TRACE_TILES = TR_DEV // LANES
BINS_AT = TRACE_TILES * SLICE
INDEX_AT = BINS_AT + N_SHOT
INDEX_ROWS = 24
DATA_ROWS = INDEX_AT + INDEX_ROWS
STEPS = 2
OWN_ROWS = 2 * SLICE + SLICE // 2
PACK = LANES // CMP_G

VMEM = pltpu.VMEM
F32 = jnp.float32
BF16 = jnp.bfloat16
FP8 = jnp.float8_e4m3fn


def fourier_rows():
    phase = np.arange(FREQS)[:, None] * np.arange(SAMPLES)[None, :] % SAMPLES
    angle = phase * (2.0 * np.pi / SAMPLES)
    waves = np.stack([np.cos(angle), np.sin(angle)]).reshape(2, STEPS, -1, SAMPLES)
    table = waves.transpose(1, 0, 2, 3).reshape(2 * FREQS, SAMPLES) / np.sqrt(SAMPLES)
    return table.astype(np.float32).astype(ml_dtypes.bfloat16)


def params(mib=48):
    return pltpu.CompilerParams(vmem_limit_bytes=mib * 2**20)


def cost(micros):
    return pl.CostEstimate(flops=int(micros * 1e9), bytes_accessed=int(micros * 3e6), transcendentals=0)


ANYWHERE = pl.BlockSpec(memory_space=pltpu.HBM)


def in_hbm(*arrays):
    return [pltpu.with_memory_space_constraint(array, pltpu.HBM) for array in arrays]


def nt_dot(left, right):
    return lax.dot_general(left, right, (((1,), (1,)), ((), ())), preferred_element_type=F32)


def split_rows(values):
    high = values.astype(BF16)
    low = (values - high.astype(F32)).astype(BF16)
    return jnp.concatenate([high, low], axis=0)


def at(tile):
    if isinstance(tile, int):
        return slice(tile * SLICE, (tile + 1) * SLICE)
    return pl.ds(pl.multiple_of(tile * SLICE, SLICE), SLICE)


def join_rows(both):
    half = both.shape[0] // 2
    return both[:half] + both[half:]


def flip(table):
    wide = jnp.concatenate(
        [table.astype(F32), jnp.zeros((N_SHOT, LANES - CAP), F32)], axis=1
    )
    return wide.T[:CAP].astype(jnp.int32)


def index_tiles(send_rows, send_counts, src, rcv, off):
    slots = lax.broadcasted_iota(jnp.int32, (CAP, N_SHOT), 0)
    targets = jnp.where(slots < send_counts[...], flip(send_rows[...]), -1)
    trace_ids = lax.broadcasted_iota(jnp.int32, (CAP, TR_DEV), 1)
    places = lax.broadcasted_iota(jnp.int32, (CAP, TR_DEV), 0)
    total = jnp.zeros((CAP, TR_DEV), jnp.int32)
    for owner in range(N_SHOT):
        hit = targets[:, owner : owner + 1] == trace_ids
        total = total + jnp.where(hit, places + owner * LANES, 0)
    slot_row = jnp.sum(total, axis=0, keepdims=True)
    rows = [src[...] & (SRC_G - 1), rcv[...] & (RCV_G - 1), off[...]]
    rows = [row.reshape(1, TR_DEV) for row in rows] + [slot_row]
    table = jnp.concatenate(rows, axis=0).astype(F32)
    tiles = [table[:, q * LANES : (q + 1) * LANES] for q in range(TRACE_TILES)]
    tiles.append(jnp.zeros((INDEX_ROWS - 4 * TRACE_TILES, LANES), F32))
    return jnp.concatenate(tiles, axis=0)


def spectra_kernel(traces, waves, *refs):
    given, out, own, basis, extra = refs[:6], refs[6], refs[7], refs[8], refs[9]
    small, sems, small_sems = refs[10:16], refs[16], refs[17]
    indices = [
        pltpu.make_async_copy(a, b, small_sems.at[k]) for k, (a, b) in enumerate(zip(given, small))
    ]
    for copy in indices:
        copy.start()
    pieces = []
    for k in range(TRACE_TILES):
        span = slice(k * LANES, (k + 1) * LANES)
        pieces.append((traces.at[span], own.at[span]))
    size = 2 * FREQS // STEPS // 2
    for k in range(2 * STEPS):
        span = slice(k * size, (k + 1) * size)
        pieces.append((waves.at[span], basis.at[span]))
    copies = [pltpu.make_async_copy(a, b, sems.at[k]) for k, (a, b) in enumerate(pieces)]
    early = TRACE_TILES + 2
    for copy in copies[:early]:
        copy.start()
    for copy in indices:
        copy.wait()
    send_rows, send_counts, bins, src, rcv, off = small
    pad = jnp.zeros((N_SHOT, LANES - CAP), F32)
    extra[:N_SHOT] = jnp.concatenate([bins[...].astype(F32), pad], axis=1)
    extra[N_SHOT:] = index_tiles(send_rows, send_counts, src, rcv, off)
    for part in range(N_SHOT):
        out[part, BINS_AT:, :] = extra[...]
    for copy in copies[:early]:
        copy.wait()
    for copy in copies[early:]:
        copy.start()
    half = FREQS // STEPS
    for step in range(STEPS):
        if step == 1:
            for copy in copies[early:]:
                copy.wait()
        parts = nt_dot(basis[2 * half * step : 2 * half * (step + 1)], own[...])
        logs = jnp.log1p(parts[:half] * parts[:half] + parts[half:] * parts[half:])
        for part in range(half // SLICE):
            for q in range(TRACE_TILES):
                out[step * (half // SLICE) + part, q * SLICE : (q + 1) * SLICE, :] = logs[
                    part * SLICE : (part + 1) * SLICE, q * LANES : (q + 1) * LANES
                ]


def log_spectra(traces, basis, *small):
    return pl.pallas_call(
        spectra_kernel,
        in_specs=[ANYWHERE] * (2 + len(small)),
        out_shape=jax.ShapeDtypeStruct((N_SHOT, DATA_ROWS, LANES), F32),
        scratch_shapes=[
            VMEM((TR_DEV, SAMPLES), BF16),
            VMEM((2 * FREQS, SAMPLES), BF16),
            VMEM((DATA_ROWS - BINS_AT, LANES), F32),
        ]
        + [VMEM(array.shape, jnp.int32) for array in small]
        + [
            pltpu.SemaphoreType.DMA((TRACE_TILES + 2 * STEPS,)),
            pltpu.SemaphoreType.DMA((len(small),)),
        ],
        compiler_params=params(24),
        cost_estimate=cost(5),
        name="spectra",
    )(*in_hbm(traces, basis, *small))


def fill_ids(ids):
    ids[...] = lax.broadcasted_iota(jnp.int32, ids.shape, 0).astype(F32).astype(BF16)


def fill_hot(tiles, ids, hot):
    one = jnp.ones((1, 1), BF16)
    zero = jnp.zeros((1, 1), BF16)
    values = tiles.astype(F32)
    for q in range(TRACE_TILES):
        span = slice(q * LANES, (q + 1) * LANES)
        first = 0
        for row, size, base in ((0, SRC_G, 0), (2, 128, 0), (1, RCV_G, 0), (3, 256, 0), (3, 256, 256)):
            wanted = (values[4 * q + row : 4 * q + row + 1] - base).astype(BF16)
            hits = jnp.where(ids[:size] == wanted, one, zero)
            hot[first : first + size, span] = hits.astype(hot.dtype)
            first += size


def resolve_bins(data, block):
    tiles = data[block, INDEX_AT:].astype(jnp.int32)
    rows = [data[owner, pl.ds(BINS_AT + block, 1)] for owner in range(N_SHOT)]
    table = jnp.concatenate(rows, axis=0)
    owners = lax.broadcasted_iota(jnp.int32, (N_SHOT, LANES), 0)
    resolved = []
    for q in range(TRACE_TILES):
        slot = tiles[4 * q + 3 : 4 * q + 4]
        place = jnp.broadcast_to(slot & (LANES - 1), (N_SHOT, LANES))
        found = jnp.take_along_axis(table, place, axis=1, mode="promise_in_bounds")
        found = jnp.where(owners == slot >> 7, found.astype(jnp.int32) + owners * CMP_G, 0)
        resolved += [tiles[4 * q : 4 * q + 3], jnp.sum(found, axis=0, keepdims=True)]
    resolved.append(jnp.zeros((INDEX_ROWS - 4 * TRACE_TILES, LANES), jnp.int32))
    return jnp.concatenate(resolved, axis=0)


def prepare_block(data, index, ids, hot, block):
    tiles = resolve_bins(data, block)
    index[block] = tiles
    one = jnp.ones((1, 1), BF16)
    zero = jnp.zeros((1, 1), BF16)
    for q in range(TRACE_TILES):
        for place, row in enumerate((0, 2, 1, 3)):
            lane = tiles[4 * q + row : 4 * q + row + 1] & (LANES - 1)
            hit = ids[:LANES] == lane.astype(F32).astype(BF16)
            span = slice(q * LANES, (q + 1) * LANES)
            hot[place * LANES : (place + 1) * LANES, span] = jnp.where(hit, one, zero)


def add_block(data, index, hot, tab, rcv, block):
    tiles = index[block]
    values = [data[block, q * SLICE : (q + 1) * SLICE] for q in range(TRACE_TILES)]

    both = split_rows(jnp.concatenate(values, axis=1))
    zero = jnp.zeros((1, 1), BF16)

    def of_tiles(row, count):
        place = [tiles[4 * q + row : 4 * q + row + 1] >> 7 for q in range(TRACE_TILES)]
        place = jnp.concatenate(place, axis=1).astype(F32).astype(BF16)
        return jnp.concatenate([jnp.where(place == tile, both, zero) for tile in range(count)], axis=0)

    plain = nt_dot(both, hot[: 2 * LANES])
    tab[at(block)] = join_rows(plain[:, :LANES])
    tab[at(OFF_TILE)] += join_rows(plain[:, LANES:])
    parts = of_tiles(1, RCV_TILES)
    sums = nt_dot(parts, hot[2 * LANES : 3 * LANES])
    for tile in range(RCV_TILES):
        rcv[tile] += join_rows(sums[tile * 2 * SLICE : (tile + 1) * 2 * SLICE])
    cmp_tiles = LIVE_TILES - CMP_TILE
    parts = of_tiles(3, cmp_tiles)
    sums = nt_dot(parts, hot[3 * LANES :])
    for tile in range(cmp_tiles):
        tab[at(CMP_TILE + tile)] += join_rows(sums[tile * 2 * SLICE : (tile + 1) * 2 * SLICE])


def adjoint_kernel(data, tab, rcv, index, hot_even, hot_odd, ids):
    tab[OFF_TILE * SLICE :] = jnp.zeros((TAB_ROWS - OFF_TILE * SLICE, LANES), F32)
    rcv[...] = jnp.zeros((RCV_TILES, SLICE, LANES), F32)
    fill_ids(ids)
    prepare_block(data, index, ids, hot_even, 0)

    @pl.loop(0, N_SHOT // 2)
    def _(pair):
        even = 2 * pair
        prepare_block(data, index, ids, hot_odd, even + 1)
        add_block(data, index, hot_even, tab, rcv, even)
        prepare_block(data, index, ids, hot_even, jnp.minimum(even + 2, N_SHOT - 1))
        add_block(data, index, hot_odd, tab, rcv, even + 1)


EXACT = 128


def kept_part(counts):
    return (counts.astype(jnp.int32) & (EXACT - 1)).astype(F32).astype(BF16)


def left_over(counts):
    whole = counts.astype(jnp.int32)
    return (whole - (whole & (EXACT - 1))).astype(F32).astype(BF16)


def peak(counts):
    top = jnp.max(counts, axis=0, keepdims=True)
    best = top[:, :LANES]
    for start in range(LANES, counts.shape[1], LANES):
        best = jnp.maximum(best, top[:, start : start + LANES])
    return best


def block_counts(hot):
    with_cmp = nt_dot(hot[:SOR], hot[SOR:])
    with_rcv = nt_dot(hot[:SO], hot[SO:SOR])
    with_off = nt_dot(hot[:SRC_G], hot[SRC_G:SO])
    rows = jnp.concatenate([with_off, with_rcv[:SRC_G], with_cmp[:SRC_G]], axis=1)
    return rows, with_cmp[SRC_G:], with_rcv[SRC_G:]


def count_kernel(
    index, kept, cmp_kept, rcv_kept, most, diag, near, cmp_near, rcv_near,
    hot_even, hot_odd, ids, to_cmp, to_rcv, *, first
):
    step = pl.program_id(0)
    even = first + 2 * step

    @pl.when(step == 0)
    def _():
        to_cmp[...] = jnp.zeros_like(to_cmp)
        to_rcv[...] = jnp.zeros_like(to_rcv)
        diag[...] = jnp.zeros_like(diag)
        most[...] = jnp.zeros_like(most)
        fill_ids(ids)
        fill_hot(index[even], ids, hot_even)

    def add(hot, place):
        rows, cmp_counts, rcv_counts = block_counts(hot)
        to_cmp[...] += cmp_counts
        to_rcv[...] += rcv_counts
        diag[...] += jnp.sum(rows, axis=0, keepdims=True)
        part = kept_part(rows)
        for out in (kept, near):
            out[place * SRC_G : (place + 1) * SRC_G] = part
        most[...] = jnp.maximum(most[...], peak(rows))

    fill_hot(index[even + 1], ids, hot_odd)
    add(hot_even, 0)
    fill_hot(index[jnp.minimum(even + 2, N_SHOT - 1)], ids, hot_even)
    add(hot_odd, 1)

    @pl.when(step == COUNT_STEPS - 1)
    def _():
        cmp_kept[...] = cmp_near[...] = kept_part(to_cmp[...])
        rcv_kept[...] = rcv_near[...] = kept_part(to_rcv[...])
        most[...] = jnp.maximum(most[...], jnp.maximum(peak(to_cmp[...]), peak(to_rcv[...])))


def add_left_over(most_1, most_2, index, hot, ids, to_cmp, to_rcv, use_both, use_rows):
    top = jnp.maximum(jnp.max(most_1[...]), jnp.max(most_2[...]))

    @pl.when(top >= EXACT)
    def _():
        fill_ids(ids)
        for half in range(2):
            to_cmp[...] = jnp.zeros_like(to_cmp)
            to_rcv[...] = jnp.zeros_like(to_rcv)

            @pl.loop(half * HALF, (half + 1) * HALF)
            def _(block):
                fill_hot(index[block], ids, hot)
                rows, cmp_counts, rcv_counts = block_counts(hot)
                to_cmp[...] += cmp_counts
                to_rcv[...] += rcv_counts
                use_rows(block, left_over(rows))

            use_both(left_over(to_cmp[...]), left_over(to_rcv[...]))


def fetch_counts(refs, held, held_cmp, held_rcv, sems):
    first, last, cmp_1, cmp_2, rcv_1, rcv_2 = refs
    pieces = []
    for chunk in range(CHUNKS):
        source = first if chunk < CHUNKS // 2 else last
        start = chunk % (CHUNKS // 2) * CHUNK_ROWS
        pieces.append((source.at[start : start + CHUNK_ROWS], held.at[chunk]))
    pieces += [(cmp_1, held_cmp.at[0]), (cmp_2, held_cmp.at[1])]
    pieces += [(rcv_1, held_rcv.at[0]), (rcv_2, held_rcv.at[1])]
    copies = [pltpu.make_async_copy(a, b, sems.at[k]) for k, (a, b) in enumerate(pieces)]
    for copy in copies:
        copy.start()
    return copies


def sum_halves(first, last):
    return (first[...].astype(F32) + last[...].astype(F32)).astype(BF16)


def load_halves(tab, rcv, own, shared):
    for tile in range(N_SHOT):
        own[:, tile * LANES : (tile + 1) * LANES] = split_rows(tab[at(tile)])
    shared[: 2 * SLICE, :LANES] = split_rows(tab[at(OFF_TILE)])
    for tile in range(RCV_TILES):
        shared[: 2 * SLICE, (1 + tile) * LANES : (2 + tile) * LANES] = split_rows(rcv[tile])
    for tile in range(CMP_TILE, LIVE_TILES):
        start = (tile - CMP_TILE) * LANES + OR
        shared[: 2 * SLICE, start : start + LANES] = split_rows(tab[at(tile)])


def normal_kernel(
    first, last, cmp_1, cmp_2, rcv_1, rcv_2, tab_in, rcv_in, diag_1, diag_2, most_1, most_2, index,
    tab, rcv, own_count, own, shared, to_shared, to_own, hot, ids, exact_cmp, exact_rcv,
):
    top = 2 * SLICE
    half = HALF * SRC_G
    load_halves(tab_in, rcv_in, own, shared)
    lanes = lax.broadcasted_iota(jnp.int32, (16, SHARED), 1)
    shared[top:] = jnp.where(lanes < LANES, 1.0, 0.0).astype(BF16)
    sums = jnp.dot(own[:, :half], first[...], preferred_element_type=F32)
    to_shared[...] = sums + jnp.dot(own[:, half:], last[...], preferred_element_type=F32)
    to_own[:, :half] = nt_dot(shared[...], first[...])
    to_own[:, half:] = nt_dot(shared[...], last[...])

    def others(to_cmp, to_rcv):
        cmp_sums = jnp.dot(shared[:top, :OR], to_cmp, preferred_element_type=F32)
        to_shared[:, OR:] += cmp_sums
        to_shared[:, :OR] += nt_dot(shared[:top, OR:], to_cmp)
        rcv_sums = jnp.dot(shared[:top, :LANES], to_rcv, preferred_element_type=F32)
        to_shared[:, LANES:OR] += rcv_sums
        to_shared[:, :LANES] += nt_dot(shared[:top, LANES:OR], to_rcv)

    def use_rows(block, rows):
        span = pl.ds(pl.multiple_of(block * SRC_G, SRC_G), SRC_G)
        to_shared[...] += jnp.dot(own[:, span], rows, preferred_element_type=F32)
        to_own[:, span] += nt_dot(shared[...], rows)

    others(sum_halves(cmp_1, cmp_2), sum_halves(rcv_1, rcv_2))
    add_left_over(most_1, most_2, index, hot, ids, exact_cmp, exact_rcv, others, use_rows)
    diag = diag_1[...] + diag_2[...]
    for tile in range(N_SHOT):
        span = slice(tile * LANES, (tile + 1) * LANES)
        count = to_own[top : top + 1, span]
        own_count[tile : tile + 1] = count
        tab[at(tile)] = join_rows(to_own[:top, span]) + count * tab_in[at(tile)]
    tab[at(OFF_TILE)] = join_rows(to_shared[:, :LANES]) + diag[:, :LANES] * tab_in[at(OFF_TILE)]
    for tile in range(RCV_TILES):
        span = slice((1 + tile) * LANES, (2 + tile) * LANES)
        rcv[tile] = join_rows(to_shared[:, span]) + diag[:, span] * rcv_in[tile]
    for tile in range(CMP_TILE, LIVE_TILES):
        start = (tile - CMP_TILE) * LANES + OR
        span = slice(start, start + LANES)
        tab[at(tile)] = join_rows(to_shared[:, span]) + diag[:, span] * tab_in[at(tile)]
    tab[LIVE_ROWS:] = jnp.zeros((TAB_ROWS - LIVE_ROWS, LANES), F32)


def all_sum(values):
    return jnp.sum(values, axis=tuple(range(values.ndim)), keepdims=True).reshape(1, 1)


def fold(values):
    total = values[:, :LANES]
    for start in range(LANES, values.shape[1], LANES):
        total = total + values[:, start : start + LANES]
    return total


def norm_kernel(
    first, last, cmp_1, cmp_2, rcv_1, rcv_2,
    tab_b, rcv_b, tab_y, rcv_y, diag_1, diag_2, most_1, most_2, index, own_count,
    out, tab_z, rcv_z, own, shared, to_shared,
    held, held_cmp, held_rcv, sems, hot, ids, exact_cmp, exact_rcv,
):
    counts = (first, last, cmp_1, cmp_2, rcv_1, rcv_2)
    copies = fetch_counts(counts, held, held_cmp, held_rcv, sems)
    shared_b = tab_b[:LIVE_ROWS]
    shared_y = tab_y[:LIVE_ROWS]
    shift = all_sum(shared_b * shared_y) / all_sum(shared_b * shared_b)
    shared_z = shared_y - shift * shared_b
    own_b = rcv_b[...]
    own_z = rcv_y[...] - shift * own_b
    tab_z[...] = shared_z
    rcv_z[...] = own_z
    load_halves(tab_z, rcv_z, own, shared)
    for chunk in range(CHUNKS):
        copies[chunk].wait()
        span = slice(chunk * CHUNK_ROWS, (chunk + 1) * CHUNK_ROWS)
        sums = jnp.dot(own[:, span], held[chunk], preferred_element_type=F32)
        to_shared[...] = sums if chunk == 0 else to_shared[...] + sums

    def whole(tabs, own):
        return all_sum(tabs) * (1.0 / N_RCV) + all_sum(own)

    def others(to_cmp, to_rcv):
        cmp_sums = jnp.dot(shared[:, :OR], to_cmp, preferred_element_type=F32)
        to_shared[:, OR:] += cmp_sums
        rcv_sums = jnp.dot(shared[:, :LANES], to_rcv, preferred_element_type=F32)
        to_shared[:, LANES:OR] += rcv_sums

    def use_rows(block, rows):
        span = pl.ds(pl.multiple_of(block * SRC_G, SRC_G), SRC_G)
        to_shared[...] += jnp.dot(own[:, span], rows, preferred_element_type=F32)

    for copy in copies[CHUNKS:]:
        copy.wait()
    both_cmp = sum_halves(held_cmp.at[0], held_cmp.at[1])
    others(both_cmp, sum_halves(held_rcv.at[0], held_rcv.at[1]))
    add_left_over(most_1, most_2, index, hot, ids, exact_cmp, exact_rcv, others, use_rows)
    tiles = [tab_z[at(OFF_TILE)]] + [rcv_z[tile] for tile in range(RCV_TILES)]
    tiles += [tab_z[at(tile)] for tile in range(CMP_TILE, LIVE_TILES)]
    rest = jnp.concatenate(tiles, axis=1)
    diag = diag_1[...] + diag_2[...]
    total = fold(2.0 * rest * join_rows(to_shared[...]) + diag * rest * rest)
    for tile in range(N_SHOT):
        total = total + own_count[tile : tile + 1] * tab_z[at(tile)] * tab_z[at(tile)]
    sums = (
        whole(shared_b * shared_b, own_b * own_b),
        whole(shared_b * shared_z, own_b * own_z),
        whole(shared_z * shared_z, own_z * own_z),
        all_sum(total),
        shift,
    )
    lanes = lax.broadcasted_iota(jnp.int32, (1, LANES), 1)
    row = jnp.zeros((1, LANES), F32)
    for lane, value in enumerate(sums):
        row = jnp.where(lanes == lane, value, row)
    out[...] = row


def whole_spec(*shape):
    return pl.BlockSpec(shape, lambda c: (0,) * len(shape))


TAB = (TAB_ROWS, LANES)
RCV = (RCV_TILES, SLICE, LANES)
INDEX = (N_SHOT, INDEX_ROWS, LANES)
INDEX_SPEC = pl.BlockSpec((1, INDEX_ROWS, LANES), lambda c: (c, 0, 0))


def table_shapes():
    return [jax.ShapeDtypeStruct(TAB, F32), jax.ShapeDtypeStruct(RCV, F32)]


def hot_scratch():
    return [VMEM((ROWS, TR_DEV), FP8), VMEM((256, LANES), BF16)]


def adjoint_apply(data):
    return pl.pallas_call(
        adjoint_kernel,
        out_shape=table_shapes() + [jax.ShapeDtypeStruct(INDEX, jnp.int32)],
        scratch_shapes=[VMEM((4 * LANES, TR_DEV), BF16)] * 2 + [VMEM((256, LANES), BF16)],
        compiler_params=params(24),
        cost_estimate=cost(8),
        name="adjoint_apply",
    )(data)


COUNTS = (HALF * SRC_G, SHARED)
TO_CMP = (OR, SHARED - OR)
TO_RCV = (LANES, RCV_G)
IN_VMEM = pl.BlockSpec(memory_space=VMEM)


def count_call(index, first):
    rows = pl.BlockSpec((2 * SRC_G, SHARED), lambda c: (c, 0))
    small = [whole_spec(*TO_CMP), whole_spec(*TO_RCV), whole_spec(1, LANES), whole_spec(1, SHARED)]
    return pl.pallas_call(
        functools.partial(count_kernel, first=first),
        grid=(COUNT_STEPS,),
        in_specs=[whole_spec(*INDEX)],
        out_specs=[rows] + small + [rows] + small[:2],
        out_shape=[pltpu.HBM(shape, BF16) for shape in (COUNTS, TO_CMP, TO_RCV)]
        + [jax.ShapeDtypeStruct((1, LANES), F32), jax.ShapeDtypeStruct((1, SHARED), F32)]
        + [VMEM(shape, BF16) for shape in (COUNTS, TO_CMP, TO_RCV)],
        scratch_shapes=[VMEM((ROWS, TR_DEV), FP8)] * 2
        + [VMEM((256, LANES), BF16), VMEM(TO_CMP, F32), VMEM(TO_RCV, F32)],
        compiler_params=params(16),
        cost_estimate=cost(6),
        name="count_pairs",
    )(index)


def exact_scratch():
    return hot_scratch() + [VMEM(TO_CMP, F32), VMEM(TO_RCV, F32)]


def count_operands(counts, first, space):
    pairs = zip(counts[0][first : first + 3], counts[1][first : first + 3])
    big = [
        pltpu.with_memory_space_constraint(array, space) for pair in pairs for array in pair
    ]
    (most_1, diag_1), (most_2, diag_2) = counts[0][3:5], counts[1][3:5]
    return big, [diag_1, diag_2, most_1, most_2]


def normal_apply(tab, rcv, index, counts):
    big, small = count_operands(counts, 5, VMEM)
    return pl.pallas_call(
        normal_kernel,
        out_shape=table_shapes() + [jax.ShapeDtypeStruct((N_SHOT, LANES), F32)],
        scratch_shapes=[
            VMEM((2 * SLICE, N_SHOT * SRC_G), BF16),
            VMEM((2 * SLICE + 16, SHARED), BF16),
            VMEM((2 * SLICE, SHARED), F32),
            VMEM((2 * SLICE + 16, N_SHOT * SRC_G), F32),
        ]
        + exact_scratch(),
        compiler_params=params(16),
        cost_estimate=cost(3),
        name="normal_apply",
    )(*big, tab, rcv, *small, index)


def norm_sums(tab_b, rcv_b, tab_y, rcv_y, own_count, index, counts):
    big, small = count_operands(counts, 0, pltpu.HBM)
    return pl.pallas_call(
        norm_kernel,
        in_specs=[ANYWHERE] * 6 + [IN_VMEM] * 10,
        out_shape=jax.ShapeDtypeStruct((1, LANES), F32),
        scratch_shapes=[
            VMEM((LIVE_ROWS, LANES), F32),
            VMEM(RCV, F32),
            VMEM((2 * SLICE, N_SHOT * SRC_G), BF16),
            VMEM((2 * SLICE, SHARED), BF16),
            VMEM((2 * SLICE, SHARED), F32),
            VMEM((CHUNKS, CHUNK_ROWS, SHARED), BF16),
            VMEM((2,) + TO_CMP, BF16),
            VMEM((2,) + TO_RCV, BF16),
            pltpu.SemaphoreType.DMA((CHUNKS + 4,)),
        ]
        + exact_scratch(),
        compiler_params=params(24),
        cost_estimate=cost(2),
        name="norm_sums",
    )(*big, tab_b, rcv_b, tab_y, rcv_y, *small, index, own_count)


def spread_kernel(parts, out):
    total = parts[0]
    for source in range(1, N_RCV):
        total = total + parts[source]
    for dest in range(N_RCV):
        out[dest] = total


def exchange(array, axis):
    return lax.all_to_all(array, axis, split_axis=0, concat_axis=0, tiled=True)


def spread_shares(arrived):
    shape = (N_RCV, SHARE, LANES)
    spread = pl.pallas_call(
        spread_kernel,
        out_shape=jax.ShapeDtypeStruct(shape, F32),
        compiler_params=params(24),
        cost_estimate=cost(1),
        name="sum_shares",
    )(arrived.reshape(shape))
    return spread.reshape(TAB)


def pack_kernel(tab, rcv, *refs, first):
    out, rows, sems = refs[-3:]
    lanes = lax.broadcasted_iota(jnp.int32, (SLICE, LANES), 1)
    half = SLICE // 2
    copies = []
    for dest in range(N_SHOT):
        rows[dest, :SLICE] = tab[at(dest)]
        rows[dest, SLICE : 2 * SLICE] = tab[at(OFF_TILE)]
        cmp_first = dest * CMP_G
        rcv_first = dest * (RCV_G // N_SHOT)
        bins = tab[at(CMP_TILE + cmp_first // LANES)]
        cmp_part = pltpu.roll(bins, (-cmp_first) % LANES, 1)
        rcv_part = pltpu.roll(rcv[rcv_first // LANES], (CMP_G - rcv_first) % LANES, 1)
        both = jnp.where(lanes < CMP_G, cmp_part, rcv_part)
        moved = pltpu.roll(both[half:], LANES // 2, 1)
        rows[dest, 2 * SLICE :] = jnp.where(lanes[:half] < LANES // 2, both[:half], moved)
        if dest % PACK == PACK - 1:
            group = dest // PACK
            span = slice(group * PACK, (group + 1) * PACK)
            place = out.at[span, first : first + OWN_ROWS]
            copies.append(pltpu.make_async_copy(rows.at[span], place, sems.at[group]))
            copies[-1].start()
    for copy in copies:
        copy.wait()


def pack_owned(tab, rcv, former=None):
    given = [] if former is None else in_hbm(former)
    return pl.pallas_call(
        functools.partial(pack_kernel, first=OWN_ROWS * len(given)),
        in_specs=[pl.BlockSpec(memory_space=VMEM)] * 2 + [ANYWHERE] * len(given),
        out_specs=ANYWHERE,
        out_shape=pltpu.HBM((N_SHOT, 2 * OWN_ROWS, LANES), F32),
        scratch_shapes=[
            VMEM((N_SHOT, OWN_ROWS, LANES), F32),
            pltpu.SemaphoreType.DMA((N_SHOT // PACK,)),
        ],
        input_output_aliases={2: 0} if given else {},
        compiler_params=params(24),
        cost_estimate=cost(1),
        name="pack_owned",
    )(tab, rcv, *given)


def swapped(value, axis, size, bit):
    return lax.ppermute(value, axis, [(s, s ^ bit) for s in range(size)])


def gather_sums(sums):
    for bit in (1, 2, 6):
        sums = sums + swapped(sums, "rcv", N_RCV, bit)
    here = jnp.arange(N_SHOT, dtype=jnp.int32)[:, None] == lax.axis_index("shot")
    rows = jnp.where(here, sums, 0.0)
    for bit in (1, 3, 4, 12):
        rows = rows + swapped(rows, "shot", N_SHOT, bit)
    return rows


def finish_kernel(sums, owned, source, receiver, offset, cmp):
    rows = sums[...]
    norm_b, cross, norm_z, norm_az, shift = (rows[:, lane : lane + 1] for lane in range(5))
    shift = shift * (1.0 / N_RCV)

    def total(values):
        return jnp.sum(values, axis=0, keepdims=True)

    total_b = total(norm_b)
    first = total(cross + shift * norm_b) / total_b
    off = shift - first
    zz = total(norm_z + 2.0 * off * cross + off * off * norm_b)
    zaz = total(
        norm_az
        + 2.0 * off * (norm_z + shift * cross)
        + off * off * (cross + shift * norm_b)
    )
    second = zaz / zz
    det = first * second - zz / total_b
    scale_b = (first + second) / det
    scale_y = 1.0 / det

    def combine(sender, start, stop):
        part_y = owned[sender, OWN_ROWS + start : OWN_ROWS + stop]
        return scale_b * owned[sender, start:stop] - scale_y * part_y

    def spread_halves(tile):
        return jnp.concatenate([tile, pltpu.roll(tile, LANES // 2, 1)], axis=0)

    per_tile = LANES // SLICE
    for group in range(N_SHOT // per_tile):
        span = slice(group * LANES, (group + 1) * LANES)
        senders = range(group * per_tile, (group + 1) * per_tile)
        source[:, span] = jnp.concatenate([combine(i, 0, SLICE) for i in senders], axis=0).T
        offset[:, span] = jnp.concatenate(
            [combine(i, SLICE, 2 * SLICE) for i in senders], axis=0
        ).T
        rest = jnp.concatenate(
            [spread_halves(combine(i, 2 * SLICE, OWN_ROWS)) for i in senders], axis=0
        ).T
        cmp[:, span] = rest[:CMP_G]
        receiver[0, :, span] = rest[CMP_G : CMP_G + RCV_G // N_SHOT]


def finish(sums, owned):
    return pl.pallas_call(
        finish_kernel,
        out_shape=[
            jax.ShapeDtypeStruct((SRC_G, FREQS), F32),
            jax.ShapeDtypeStruct((1, RCV_G // N_SHOT, FREQS), F32),
            jax.ShapeDtypeStruct((128, FREQS), F32),
            jax.ShapeDtypeStruct((CMP_G, FREQS), F32),
        ],
        compiler_params=params(),
        name="finish",
    )(sums, owned)


def per_device(basis, traces, src_index, rcv_index, off_index, send_rows, send_counts, recv_bins):
    data = log_spectra(
        traces, basis, send_rows[0], send_counts, recv_bins[0], src_index, rcv_index, off_index
    )
    data = exchange(data, "shot")

    tab_b, rcv_b, index = adjoint_apply(data)
    arrived = exchange(tab_b, "rcv")
    counts_1 = count_call(index, 0)
    arrived, index, counts_1 = lax.optimization_barrier((arrived, index, counts_1))
    spread = spread_shares(arrived)
    spread, index = lax.optimization_barrier((spread, index))
    tab_b = exchange(spread, "rcv")
    counts = (counts_1, count_call(index, HALF))

    tab_y, rcv_y, own_count = normal_apply(tab_b, rcv_b, index, counts)
    arrived = exchange(tab_y, "rcv")
    packed = pack_owned(tab_b, rcv_b)
    arrived, packed = lax.optimization_barrier((arrived, packed))
    tab_y = exchange(spread_shares(arrived), "rcv")
    packed = pack_owned(tab_y, rcv_y, packed)
    tab_y, packed = lax.optimization_barrier((tab_y, packed))
    owned = exchange(packed, "shot")
    sums = norm_sums(tab_b, rcv_b, tab_y, rcv_y, own_count, index, counts)
    return tuple(finish(gather_sums(sums), owned))


def solution(mesh):
    basis = fourier_rows()
    mapped = jax.shard_map(
        per_device,
        mesh=mesh,
        in_specs=(
            P(),
            P(("shot", "rcv"), None),
            P(("shot", "rcv")),
            P(("shot", "rcv")),
            P(("shot", "rcv")),
            P(("shot", "rcv"), None, None),
            P(("shot", "rcv"), None),
            P(("shot", "rcv"), None, None),
        ),
        out_specs=(P("shot", None), P("rcv", "shot", None), P(), P("shot", None)),
        check_vma=False,
    )

    def run(*args):
        return mapped(jnp.asarray(basis), *args)

    return run
```

```python
import functools

import ml_dtypes
import numpy as np

import jax
import jax.numpy as jnp
from jax import lax
from jax.experimental import pallas as pl
from jax.experimental.pallas import tpu as pltpu
from jax.sharding import PartitionSpec as P

SAMPLES = 1024
FREQS = 512
TR_DEV = 640
N_SHOT = 16
N_RCV = 8
DEVICES = 128
CAP = 80
SRC_G = 128
RCV_G = 256
CMP_G = 32
SLICE = FREQS // N_SHOT
LANES = 128
OFF_TILE = 16
CMP_TILE = 17
LIVE_TILES = 21
LIVE_ROWS = LIVE_TILES * SLICE
SHARE = -(-LIVE_ROWS // (8 * N_RCV)) * 8
TAB_ROWS = N_RCV * SHARE
RCV_TILES = 2
ROWS = SRC_G + RCV_G + 128 + 512
SHARED = ROWS - SRC_G
SO = 2 * LANES
SOR = SO + RCV_G
OR = LANES + RCV_G
HALF = N_SHOT // 2
COUNT_STEPS = HALF // 2
CHUNKS = 4
CHUNK_ROWS = N_SHOT * SRC_G // CHUNKS
TRACE_TILES = TR_DEV // LANES
BINS_AT = TRACE_TILES * SLICE
INDEX_AT = BINS_AT + N_SHOT
INDEX_ROWS = 24
DATA_ROWS = INDEX_AT + INDEX_ROWS
STEPS = 2
OWN_ROWS = 2 * SLICE + SLICE // 2
TURNED_ROWS = 2 * LANES + CMP_G + RCV_G // N_SHOT
PACK = LANES // CMP_G

VMEM = pltpu.VMEM
F32 = jnp.float32
BF16 = jnp.bfloat16
FP8 = jnp.float8_e4m3fn


def fourier_rows():
    phase = np.arange(FREQS)[:, None] * np.arange(SAMPLES)[None, :] % SAMPLES
    angle = phase * (2.0 * np.pi / SAMPLES)
    waves = np.stack([np.cos(angle), np.sin(angle)]).reshape(2, STEPS, -1, SAMPLES)
    table = waves.transpose(1, 0, 2, 3).reshape(2 * FREQS, SAMPLES) / np.sqrt(SAMPLES)
    return table.astype(np.float32).astype(ml_dtypes.bfloat16)


def params(mib=48):
    return pltpu.CompilerParams(vmem_limit_bytes=mib * 2**20)


def cost(micros):
    return pl.CostEstimate(flops=int(micros * 1e9), bytes_accessed=int(micros * 3e6), transcendentals=0)


ANYWHERE = pl.BlockSpec(memory_space=pltpu.HBM)


def in_hbm(*arrays):
    return [pltpu.with_memory_space_constraint(array, pltpu.HBM) for array in arrays]


def nt_dot(left, right):
    return lax.dot_general(left, right, (((1,), (1,)), ((), ())), preferred_element_type=F32)


def split_rows(values):
    high = values.astype(BF16)
    low = (values - high.astype(F32)).astype(BF16)
    return jnp.concatenate([high, low], axis=0)


def at(tile):
    if isinstance(tile, int):
        return slice(tile * SLICE, (tile + 1) * SLICE)
    return pl.ds(pl.multiple_of(tile * SLICE, SLICE), SLICE)


def join_rows(both):
    half = both.shape[0] // 2
    return both[:half] + both[half:]


def flip(table):
    wide = jnp.concatenate(
        [table.astype(F32), jnp.zeros((N_SHOT, LANES - CAP), F32)], axis=1
    )
    return wide.T[:CAP].astype(jnp.int32)


def index_tiles(send_rows, send_counts, src, rcv, off):
    slots = lax.broadcasted_iota(jnp.int32, (CAP, N_SHOT), 0)
    targets = jnp.where(slots < send_counts[...], flip(send_rows[...]), -1)
    trace_ids = lax.broadcasted_iota(jnp.int32, (CAP, TR_DEV), 1)
    places = lax.broadcasted_iota(jnp.int32, (CAP, TR_DEV), 0)
    total = jnp.zeros((CAP, TR_DEV), jnp.int32)
    for owner in range(N_SHOT):
        hit = targets[:, owner : owner + 1] == trace_ids
        total = total + jnp.where(hit, places + owner * LANES, 0)
    slot_row = jnp.sum(total, axis=0, keepdims=True)
    rows = [src[...] & (SRC_G - 1), rcv[...] & (RCV_G - 1), off[...]]
    rows = [row.reshape(1, TR_DEV) for row in rows] + [slot_row]
    table = jnp.concatenate(rows, axis=0).astype(F32)
    tiles = [table[:, q * LANES : (q + 1) * LANES] for q in range(TRACE_TILES)]
    tiles.append(jnp.zeros((INDEX_ROWS - 4 * TRACE_TILES, LANES), F32))
    return jnp.concatenate(tiles, axis=0)


def spectra_kernel(traces, waves, *refs):
    given, out, own, basis, extra = refs[:6], refs[6], refs[7], refs[8], refs[9]
    small, sems, small_sems = refs[10:16], refs[16], refs[17]
    indices = [
        pltpu.make_async_copy(a, b, small_sems.at[k]) for k, (a, b) in enumerate(zip(given, small))
    ]
    for copy in indices:
        copy.start()
    pieces = []
    for k in range(TRACE_TILES):
        span = slice(k * LANES, (k + 1) * LANES)
        pieces.append((traces.at[span], own.at[span]))
    size = 2 * FREQS // STEPS // 2
    for k in range(2 * STEPS):
        span = slice(k * size, (k + 1) * size)
        pieces.append((waves.at[span], basis.at[span]))
    copies = [pltpu.make_async_copy(a, b, sems.at[k]) for k, (a, b) in enumerate(pieces)]
    early = TRACE_TILES + 2
    for copy in copies[:early]:
        copy.start()
    for copy in indices:
        copy.wait()
    send_rows, send_counts, bins, src, rcv, off = small
    pad = jnp.zeros((N_SHOT, LANES - CAP), F32)
    extra[:N_SHOT] = jnp.concatenate([bins[...].astype(F32), pad], axis=1)
    extra[N_SHOT:] = index_tiles(send_rows, send_counts, src, rcv, off)
    for part in range(N_SHOT):
        out[part, BINS_AT:, :] = extra[...]
    for copy in copies[:early]:
        copy.wait()
    for copy in copies[early:]:
        copy.start()
    half = FREQS // STEPS
    for step in range(STEPS):
        if step == 1:
            for copy in copies[early:]:
                copy.wait()
        parts = nt_dot(basis[2 * half * step : 2 * half * (step + 1)], own[...])
        logs = jnp.log1p(parts[:half] * parts[:half] + parts[half:] * parts[half:])
        for part in range(half // SLICE):
            for q in range(TRACE_TILES):
                out[step * (half // SLICE) + part, q * SLICE : (q + 1) * SLICE, :] = logs[
                    part * SLICE : (part + 1) * SLICE, q * LANES : (q + 1) * LANES
                ]


def log_spectra(traces, basis, *small):
    return pl.pallas_call(
        spectra_kernel,
        in_specs=[ANYWHERE] * (2 + len(small)),
        out_shape=jax.ShapeDtypeStruct((N_SHOT, DATA_ROWS, LANES), F32),
        scratch_shapes=[
            VMEM((TR_DEV, SAMPLES), BF16),
            VMEM((2 * FREQS, SAMPLES), BF16),
            VMEM((DATA_ROWS - BINS_AT, LANES), F32),
        ]
        + [VMEM(array.shape, jnp.int32) for array in small]
        + [
            pltpu.SemaphoreType.DMA((TRACE_TILES + 2 * STEPS,)),
            pltpu.SemaphoreType.DMA((len(small),)),
        ],
        compiler_params=params(24),
        cost_estimate=cost(5),
        name="spectra",
    )(*in_hbm(traces, basis, *small))


def fill_ids(ids):
    ids[...] = lax.broadcasted_iota(jnp.int32, ids.shape, 0).astype(F32).astype(BF16)


def fill_hot(tiles, ids, hot):
    one = jnp.ones((1, 1), BF16)
    zero = jnp.zeros((1, 1), BF16)
    values = tiles.astype(F32)
    for q in range(TRACE_TILES):
        span = slice(q * LANES, (q + 1) * LANES)
        first = 0
        for row, size, base in ((0, SRC_G, 0), (2, 128, 0), (1, RCV_G, 0), (3, 256, 0), (3, 256, 256)):
            wanted = (values[4 * q + row : 4 * q + row + 1] - base).astype(BF16)
            hits = jnp.where(ids[:size] == wanted, one, zero)
            hot[first : first + size, span] = hits.astype(hot.dtype)
            first += size


def resolve_bins(data, block):
    tiles = data[block, INDEX_AT:].astype(jnp.int32)
    rows = [data[owner, pl.ds(BINS_AT + block, 1)] for owner in range(N_SHOT)]
    table = jnp.concatenate(rows, axis=0)
    owners = lax.broadcasted_iota(jnp.int32, (N_SHOT, LANES), 0)
    resolved = []
    for q in range(TRACE_TILES):
        slot = tiles[4 * q + 3 : 4 * q + 4]
        place = jnp.broadcast_to(slot & (LANES - 1), (N_SHOT, LANES))
        found = jnp.take_along_axis(table, place, axis=1, mode="promise_in_bounds")
        found = jnp.where(owners == slot >> 7, found.astype(jnp.int32) + owners * CMP_G, 0)
        resolved += [tiles[4 * q : 4 * q + 3], jnp.sum(found, axis=0, keepdims=True)]
    resolved.append(jnp.zeros((INDEX_ROWS - 4 * TRACE_TILES, LANES), jnp.int32))
    return jnp.concatenate(resolved, axis=0)


def prepare_block(data, index, ids, hot, block):
    tiles = resolve_bins(data, block)
    index[block] = tiles
    one = jnp.ones((1, 1), BF16)
    zero = jnp.zeros((1, 1), BF16)
    for q in range(TRACE_TILES):
        for place, row in enumerate((0, 2, 1, 3)):
            lane = tiles[4 * q + row : 4 * q + row + 1] & (LANES - 1)
            hit = ids[:LANES] == lane.astype(F32).astype(BF16)
            span = slice(q * LANES, (q + 1) * LANES)
            hot[place * LANES : (place + 1) * LANES, span] = jnp.where(hit, one, zero)


def add_block(data, index, hot, tab, rcv, block):
    tiles = index[block]
    values = [data[block, q * SLICE : (q + 1) * SLICE] for q in range(TRACE_TILES)]

    both = split_rows(jnp.concatenate(values, axis=1))
    zero = jnp.zeros((1, 1), BF16)

    def of_tiles(row, count):
        place = [tiles[4 * q + row : 4 * q + row + 1] >> 7 for q in range(TRACE_TILES)]
        place = jnp.concatenate(place, axis=1).astype(F32).astype(BF16)
        return jnp.concatenate([jnp.where(place == tile, both, zero) for tile in range(count)], axis=0)

    plain = nt_dot(both, hot[: 2 * LANES])
    tab[at(block)] = join_rows(plain[:, :LANES])
    tab[at(OFF_TILE)] += join_rows(plain[:, LANES:])
    parts = of_tiles(1, RCV_TILES)
    sums = nt_dot(parts, hot[2 * LANES : 3 * LANES])
    for tile in range(RCV_TILES):
        rcv[tile] += join_rows(sums[tile * 2 * SLICE : (tile + 1) * 2 * SLICE])
    cmp_tiles = LIVE_TILES - CMP_TILE
    parts = of_tiles(3, cmp_tiles)
    sums = nt_dot(parts, hot[3 * LANES :])
    for tile in range(cmp_tiles):
        tab[at(CMP_TILE + tile)] += join_rows(sums[tile * 2 * SLICE : (tile + 1) * 2 * SLICE])


def adjoint_kernel(data, tab, rcv, index, hot_even, hot_odd, ids):
    tab[OFF_TILE * SLICE :] = jnp.zeros((TAB_ROWS - OFF_TILE * SLICE, LANES), F32)
    rcv[...] = jnp.zeros((RCV_TILES, SLICE, LANES), F32)
    fill_ids(ids)
    prepare_block(data, index, ids, hot_even, 0)

    @pl.loop(0, N_SHOT // 2)
    def _(pair):
        even = 2 * pair
        prepare_block(data, index, ids, hot_odd, even + 1)
        add_block(data, index, hot_even, tab, rcv, even)
        prepare_block(data, index, ids, hot_even, jnp.minimum(even + 2, N_SHOT - 1))
        add_block(data, index, hot_odd, tab, rcv, even + 1)


EXACT = 128


def kept_part(counts):
    return (counts.astype(jnp.int32) & (EXACT - 1)).astype(F32).astype(BF16)


def left_over(counts):
    whole = counts.astype(jnp.int32)
    return (whole - (whole & (EXACT - 1))).astype(F32).astype(BF16)


def peak(counts):
    top = jnp.max(counts, axis=0, keepdims=True)
    best = top[:, :LANES]
    for start in range(LANES, counts.shape[1], LANES):
        best = jnp.maximum(best, top[:, start : start + LANES])
    return best


def block_counts(hot):
    with_cmp = nt_dot(hot[:SOR], hot[SOR:])
    with_rcv = nt_dot(hot[:SO], hot[SO:SOR])
    with_off = nt_dot(hot[:SRC_G], hot[SRC_G:SO])
    rows = jnp.concatenate([with_off, with_rcv[:SRC_G], with_cmp[:SRC_G]], axis=1)
    return rows, with_cmp[SRC_G:], with_rcv[SRC_G:]


def count_kernel(
    index, kept, to_cmp_kept, to_rcv_kept, most, diag, hot_even, hot_odd, ids, to_cmp, to_rcv, *, first
):
    step = pl.program_id(0)
    even = first + 2 * step

    @pl.when(step == 0)
    def _():
        to_cmp[...] = jnp.zeros_like(to_cmp)
        to_rcv[...] = jnp.zeros_like(to_rcv)
        diag[...] = jnp.zeros_like(diag)
        most[...] = jnp.zeros_like(most)
        fill_ids(ids)
        fill_hot(index[even], ids, hot_even)

    def add(hot, place):
        rows, cmp_counts, rcv_counts = block_counts(hot)
        to_cmp[...] += cmp_counts
        to_rcv[...] += rcv_counts
        diag[...] += jnp.sum(rows, axis=0, keepdims=True)
        kept[place * SRC_G : (place + 1) * SRC_G] = kept_part(rows)
        most[...] = jnp.maximum(most[...], peak(rows))

    fill_hot(index[even + 1], ids, hot_odd)
    add(hot_even, 0)
    fill_hot(index[jnp.minimum(even + 2, N_SHOT - 1)], ids, hot_even)
    add(hot_odd, 1)

    @pl.when(step == COUNT_STEPS - 1)
    def _():
        to_cmp_kept[...] = (to_cmp[...].astype(jnp.int32) & (EXACT - 1)).astype(jnp.int8)
        to_rcv_kept[...] = (to_rcv[...].astype(jnp.int32) & (EXACT - 1)).astype(jnp.int8)
        most[...] = jnp.maximum(most[...], jnp.maximum(peak(to_cmp[...]), peak(to_rcv[...])))


def add_left_over(most_1, most_2, index, hot, ids, to_cmp, to_rcv, use_both, use_rows):
    top = jnp.maximum(jnp.max(most_1[...]), jnp.max(most_2[...]))

    @pl.when(top >= EXACT)
    def _():
        fill_ids(ids)
        for half in range(2):
            to_cmp[...] = jnp.zeros_like(to_cmp)
            to_rcv[...] = jnp.zeros_like(to_rcv)

            @pl.loop(half * HALF, (half + 1) * HALF)
            def _(block):
                fill_hot(index[block], ids, hot)
                rows, cmp_counts, rcv_counts = block_counts(hot)
                to_cmp[...] += cmp_counts
                to_rcv[...] += rcv_counts
                use_rows(block, left_over(rows))

            use_both(left_over(to_cmp[...]), left_over(to_rcv[...]))


def fetch_counts(refs, held, held_cmp, held_rcv, sems):
    *halves, cmp_1, cmp_2, rcv_1, rcv_2 = refs
    pieces = []
    for half, source in enumerate(halves):
        for chunk in range(CHUNKS // 2):
            start = chunk * CHUNK_ROWS
            place = held.at[half * (CHUNKS // 2) + chunk]
            pieces.append((source.at[start : start + CHUNK_ROWS], place))
    pieces += [(cmp_1, held_cmp.at[0]), (cmp_2, held_cmp.at[1])]
    pieces += [(rcv_1, held_rcv.at[0]), (rcv_2, held_rcv.at[1])]
    copies = [pltpu.make_async_copy(a, b, sems.at[k]) for k, (a, b) in enumerate(pieces)]
    for copy in copies:
        copy.start()
    return copies


def sum_halves(held):
    return (held[0].astype(F32) + held[1].astype(F32)).astype(BF16)


def load_halves(tab, rcv, own, shared):
    for tile in range(N_SHOT):
        own[:, tile * LANES : (tile + 1) * LANES] = split_rows(tab[at(tile)])
    shared[: 2 * SLICE, :LANES] = split_rows(tab[at(OFF_TILE)])
    for tile in range(RCV_TILES):
        shared[: 2 * SLICE, (1 + tile) * LANES : (2 + tile) * LANES] = split_rows(rcv[tile])
    for tile in range(CMP_TILE, LIVE_TILES):
        start = (tile - CMP_TILE) * LANES + OR
        shared[: 2 * SLICE, start : start + LANES] = split_rows(tab[at(tile)])


def normal_kernel(
    first, last, cmp_1, cmp_2, rcv_1, rcv_2, tab_in, rcv_in, diag_1, diag_2, most_1, most_2, index,
    tab, rcv, own_count, own, shared, to_shared, to_own,
    held, held_cmp, held_rcv, sems, hot, ids, exact_cmp, exact_rcv,
):
    counts = (first, last, cmp_1, cmp_2, rcv_1, rcv_2)
    copies = fetch_counts(counts, held, held_cmp, held_rcv, sems)
    top = 2 * SLICE
    load_halves(tab_in, rcv_in, own, shared)
    lanes = lax.broadcasted_iota(jnp.int32, (16, SHARED), 1)
    shared[top:] = jnp.where(lanes < LANES, 1.0, 0.0).astype(BF16)
    for chunk in range(CHUNKS):
        copies[chunk].wait()
        span = slice(chunk * CHUNK_ROWS, (chunk + 1) * CHUNK_ROWS)
        sums = jnp.dot(own[:, span], held[chunk], preferred_element_type=F32)
        to_shared[...] = sums if chunk == 0 else to_shared[...] + sums
        to_own[:, span] = nt_dot(shared[...], held[chunk])

    def others(to_cmp, to_rcv):
        cmp_sums = jnp.dot(shared[:top, :OR], to_cmp, preferred_element_type=F32)
        to_shared[:, OR:] += cmp_sums
        to_shared[:, :OR] += nt_dot(shared[:top, OR:], to_cmp)
        rcv_sums = jnp.dot(shared[:top, :LANES], to_rcv, preferred_element_type=F32)
        to_shared[:, LANES:OR] += rcv_sums
        to_shared[:, :LANES] += nt_dot(shared[:top, LANES:OR], to_rcv)

    def use_rows(block, rows):
        span = pl.ds(pl.multiple_of(block * SRC_G, SRC_G), SRC_G)
        to_shared[...] += jnp.dot(own[:, span], rows, preferred_element_type=F32)
        to_own[:, span] += nt_dot(shared[...], rows)

    for copy in copies[-4:]:
        copy.wait()
    others(sum_halves(held_cmp), sum_halves(held_rcv))
    add_left_over(most_1, most_2, index, hot, ids, exact_cmp, exact_rcv, others, use_rows)
    diag = diag_1[...] + diag_2[...]
    for tile in range(N_SHOT):
        span = slice(tile * LANES, (tile + 1) * LANES)
        count = to_own[top : top + 1, span]
        own_count[tile : tile + 1] = count
        tab[at(tile)] = join_rows(to_own[:top, span]) + count * tab_in[at(tile)]
    tab[at(OFF_TILE)] = join_rows(to_shared[:, :LANES]) + diag[:, :LANES] * tab_in[at(OFF_TILE)]
    for tile in range(RCV_TILES):
        span = slice((1 + tile) * LANES, (2 + tile) * LANES)
        rcv[tile] = join_rows(to_shared[:, span]) + diag[:, span] * rcv_in[tile]
    for tile in range(CMP_TILE, LIVE_TILES):
        start = (tile - CMP_TILE) * LANES + OR
        span = slice(start, start + LANES)
        tab[at(tile)] = join_rows(to_shared[:, span]) + diag[:, span] * tab_in[at(tile)]
    tab[LIVE_ROWS:] = jnp.zeros((TAB_ROWS - LIVE_ROWS, LANES), F32)


def all_sum(values):
    return jnp.sum(values, axis=tuple(range(values.ndim)), keepdims=True).reshape(1, 1)


def fold(values):
    total = values[:, :LANES]
    for start in range(LANES, values.shape[1], LANES):
        total = total + values[:, start : start + LANES]
    return total


def norm_kernel(
    first, last, cmp_1, cmp_2, rcv_1, rcv_2,
    tab_b, rcv_b, tab_y, rcv_y, diag_1, diag_2, most_1, most_2, index, own_count,
    out, tab_z, rcv_z, own, shared, to_shared,
    held, held_cmp, held_rcv, sems, hot, ids, exact_cmp, exact_rcv,
):
    counts = (first, last, cmp_1, cmp_2, rcv_1, rcv_2)
    copies = fetch_counts(counts, held, held_cmp, held_rcv, sems)
    shared_b = tab_b[:LIVE_ROWS]
    shared_y = tab_y[:LIVE_ROWS]
    shift = all_sum(shared_b * shared_y) / all_sum(shared_b * shared_b)
    shared_z = shared_y - shift * shared_b
    own_b = rcv_b[...]
    own_z = rcv_y[...] - shift * own_b
    tab_z[...] = shared_z
    rcv_z[...] = own_z
    load_halves(tab_z, rcv_z, own, shared)
    for chunk in range(CHUNKS):
        copies[chunk].wait()
        span = slice(chunk * CHUNK_ROWS, (chunk + 1) * CHUNK_ROWS)
        sums = jnp.dot(own[:, span], held[chunk], preferred_element_type=F32)
        to_shared[...] = sums if chunk == 0 else to_shared[...] + sums

    def whole(tabs, own):
        return all_sum(tabs) * (1.0 / N_RCV) + all_sum(own)

    def others(to_cmp, to_rcv):
        cmp_sums = jnp.dot(shared[:, :OR], to_cmp, preferred_element_type=F32)
        to_shared[:, OR:] += cmp_sums
        rcv_sums = jnp.dot(shared[:, :LANES], to_rcv, preferred_element_type=F32)
        to_shared[:, LANES:OR] += rcv_sums

    def use_rows(block, rows):
        span = pl.ds(pl.multiple_of(block * SRC_G, SRC_G), SRC_G)
        to_shared[...] += jnp.dot(own[:, span], rows, preferred_element_type=F32)

    for copy in copies[-4:]:
        copy.wait()
    others(sum_halves(held_cmp), sum_halves(held_rcv))
    add_left_over(most_1, most_2, index, hot, ids, exact_cmp, exact_rcv, others, use_rows)
    tiles = [tab_z[at(OFF_TILE)]] + [rcv_z[tile] for tile in range(RCV_TILES)]
    tiles += [tab_z[at(tile)] for tile in range(CMP_TILE, LIVE_TILES)]
    rest = jnp.concatenate(tiles, axis=1)
    diag = diag_1[...] + diag_2[...]
    total = fold(2.0 * rest * join_rows(to_shared[...]) + diag * rest * rest)
    for tile in range(N_SHOT):
        total = total + own_count[tile : tile + 1] * tab_z[at(tile)] * tab_z[at(tile)]
    sums = (
        whole(shared_b * shared_b, own_b * own_b),
        whole(shared_b * shared_z, own_b * own_z),
        whole(shared_z * shared_z, own_z * own_z),
        all_sum(total),
        shift,
    )
    lanes = lax.broadcasted_iota(jnp.int32, (1, LANES), 1)
    row = jnp.zeros((1, LANES), F32)
    for lane, value in enumerate(sums):
        row = jnp.where(lanes == lane, value, row)
    out[...] = row


def whole_spec(*shape):
    return pl.BlockSpec(shape, lambda c: (0,) * len(shape))


TAB = (TAB_ROWS, LANES)
RCV = (RCV_TILES, SLICE, LANES)
INDEX = (N_SHOT, INDEX_ROWS, LANES)
INDEX_SPEC = pl.BlockSpec((1, INDEX_ROWS, LANES), lambda c: (c, 0, 0))


def table_shapes():
    return [jax.ShapeDtypeStruct(TAB, F32), jax.ShapeDtypeStruct(RCV, F32)]


def hot_scratch():
    return [VMEM((ROWS, TR_DEV), FP8), VMEM((256, LANES), BF16)]


def adjoint_apply(data):
    return pl.pallas_call(
        adjoint_kernel,
        out_shape=table_shapes() + [jax.ShapeDtypeStruct(INDEX, jnp.int32)],
        scratch_shapes=[VMEM((4 * LANES, TR_DEV), BF16)] * 2 + [VMEM((256, LANES), BF16)],
        compiler_params=params(24),
        cost_estimate=cost(8),
        name="adjoint_apply",
    )(data)


COUNTS = (HALF * SRC_G, SHARED)
TO_CMP = (OR, SHARED - OR)
TO_RCV = (LANES, RCV_G)
IN_VMEM = pl.BlockSpec(memory_space=VMEM)


def count_call(index, first):
    rows = pl.BlockSpec((2 * SRC_G, SHARED), lambda c: (c, 0))
    small = [whole_spec(*TO_CMP), whole_spec(*TO_RCV), whole_spec(1, LANES), whole_spec(1, SHARED)]
    return pl.pallas_call(
        functools.partial(count_kernel, first=first),
        grid=(COUNT_STEPS,),
        in_specs=[whole_spec(*INDEX)],
        out_specs=[rows] + small,
        out_shape=[
            pltpu.HBM(COUNTS, BF16),
            pltpu.HBM(TO_CMP, jnp.int8),
            pltpu.HBM(TO_RCV, jnp.int8),
            jax.ShapeDtypeStruct((1, LANES), F32),
            jax.ShapeDtypeStruct((1, SHARED), F32),
        ],
        scratch_shapes=[VMEM((ROWS, TR_DEV), FP8)] * 2
        + [VMEM((256, LANES), BF16), VMEM(TO_CMP, F32), VMEM(TO_RCV, F32)],
        compiler_params=params(24),
        cost_estimate=cost(6),
        name="count_pairs",
    )(index)


def count_scratch(chunks):
    return (
        [
            VMEM((chunks, CHUNK_ROWS, SHARED), BF16),
            VMEM((2,) + TO_CMP, jnp.int8),
            VMEM((2,) + TO_RCV, jnp.int8),
            pltpu.SemaphoreType.DMA((chunks + 4,)),
        ]
        + hot_scratch()
        + [VMEM(TO_CMP, F32), VMEM(TO_RCV, F32)]
    )


def count_operands(counts):
    big = in_hbm(*[array for pair in zip(counts[0][:3], counts[1][:3]) for array in pair])
    (most_1, diag_1), (most_2, diag_2) = counts[0][3:5], counts[1][3:5]
    return big, [diag_1, diag_2, most_1, most_2]


def normal_apply(tab, rcv, index, counts):
    big, small = count_operands(counts)
    return pl.pallas_call(
        normal_kernel,
        in_specs=[ANYWHERE] * 6 + [IN_VMEM] * 7,
        out_shape=table_shapes() + [jax.ShapeDtypeStruct((N_SHOT, LANES), F32)],
        scratch_shapes=[
            VMEM((2 * SLICE, N_SHOT * SRC_G), BF16),
            VMEM((2 * SLICE + 16, SHARED), BF16),
            VMEM((2 * SLICE, SHARED), F32),
            VMEM((2 * SLICE + 16, N_SHOT * SRC_G), F32),
        ]
        + count_scratch(CHUNKS),
        compiler_params=params(24),
        cost_estimate=cost(3),
        name="normal_apply",
    )(*big, tab, rcv, *small, index)


def norm_sums(tab_b, rcv_b, tab_y, rcv_y, own_count, index, counts):
    big, small = count_operands(counts)
    return pl.pallas_call(
        norm_kernel,
        in_specs=[ANYWHERE] * 6 + [IN_VMEM] * 10,
        out_shape=jax.ShapeDtypeStruct((1, LANES), F32),
        scratch_shapes=[
            VMEM((LIVE_ROWS, LANES), F32),
            VMEM(RCV, F32),
            VMEM((2 * SLICE, N_SHOT * SRC_G), BF16),
            VMEM((2 * SLICE, SHARED), BF16),
            VMEM((2 * SLICE, SHARED), F32),
        ]
        + count_scratch(CHUNKS),
        compiler_params=params(24),
        cost_estimate=cost(2),
        name="norm_sums",
    )(*big, tab_b, rcv_b, tab_y, rcv_y, *small, index, own_count)


def spread_kernel(parts, out):
    total = parts[0]
    for source in range(1, N_RCV):
        total = total + parts[source]
    for dest in range(N_RCV):
        out[dest] = total


def exchange(array, axis):
    return lax.all_to_all(array, axis, split_axis=0, concat_axis=0, tiled=True)


def spread_shares(arrived):
    shape = (N_RCV, SHARE, LANES)
    spread = pl.pallas_call(
        spread_kernel,
        out_shape=jax.ShapeDtypeStruct(shape, F32),
        compiler_params=params(24),
        cost_estimate=cost(1),
        name="sum_shares",
    )(arrived.reshape(shape))
    return spread.reshape(TAB)


def pack_kernel(tab, rcv, *refs, first):
    out, rows, sems = refs[-3:]
    lanes = lax.broadcasted_iota(jnp.int32, (SLICE, LANES), 1)
    half = SLICE // 2
    copies = []
    for dest in range(N_SHOT):
        rows[dest, :SLICE] = tab[at(dest)]
        rows[dest, SLICE : 2 * SLICE] = tab[at(OFF_TILE)]
        cmp_first = dest * CMP_G
        rcv_first = dest * (RCV_G // N_SHOT)
        bins = tab[at(CMP_TILE + cmp_first // LANES)]
        cmp_part = pltpu.roll(bins, (-cmp_first) % LANES, 1)
        rcv_part = pltpu.roll(rcv[rcv_first // LANES], (CMP_G - rcv_first) % LANES, 1)
        both = jnp.where(lanes < CMP_G, cmp_part, rcv_part)
        moved = pltpu.roll(both[half:], LANES // 2, 1)
        rows[dest, 2 * SLICE :] = jnp.where(lanes[:half] < LANES // 2, both[:half], moved)
        if dest % PACK == PACK - 1:
            group = dest // PACK
            span = slice(group * PACK, (group + 1) * PACK)
            place = out.at[span, first : first + OWN_ROWS]
            copies.append(pltpu.make_async_copy(rows.at[span], place, sems.at[group]))
            copies[-1].start()
    for copy in copies:
        copy.wait()


def pack_owned(tab, rcv, former=None):
    given = [] if former is None else in_hbm(former)
    return pl.pallas_call(
        functools.partial(pack_kernel, first=OWN_ROWS * len(given)),
        in_specs=[pl.BlockSpec(memory_space=VMEM)] * 2 + [ANYWHERE] * len(given),
        out_specs=ANYWHERE,
        out_shape=pltpu.HBM((N_SHOT, 2 * OWN_ROWS, LANES), F32),
        scratch_shapes=[
            VMEM((N_SHOT, OWN_ROWS, LANES), F32),
            pltpu.SemaphoreType.DMA((N_SHOT // PACK,)),
        ],
        input_output_aliases={2: 0} if given else {},
        compiler_params=params(24),
        cost_estimate=cost(1),
        name="pack_owned",
    )(tab, rcv, *given)


def swapped(value, axis, size, bit):
    return lax.ppermute(value, axis, [(s, s ^ bit) for s in range(size)])


def gather_sums(sums):
    for bit in (1, 2, 6):
        sums = sums + swapped(sums, "rcv", N_RCV, bit)
    here = jnp.arange(N_SHOT, dtype=jnp.int32)[:, None] == lax.axis_index("shot")
    rows = jnp.where(here, sums, 0.0)
    for bit in (1, 3, 4, 12):
        rows = rows + swapped(rows, "shot", N_SHOT, bit)
    return rows


def turn_kernel(owned, turned):
    def spread_halves(tile):
        return jnp.concatenate([tile, pltpu.roll(tile, LANES // 2, 1)], axis=0)

    per_tile = LANES // SLICE
    for which in range(2):
        first = which * OWN_ROWS
        for group in range(N_SHOT // per_tile):
            span = slice(group * LANES, (group + 1) * LANES)
            senders = range(group * per_tile, (group + 1) * per_tile)
            for place in range(2):
                start = first + place * SLICE
                tile = [owned[i, start : start + SLICE] for i in senders]
                rows = slice(place * LANES, (place + 1) * LANES)
                turned[which, rows, span] = jnp.concatenate(tile, axis=0).T
            start = first + 2 * SLICE
            rest = [spread_halves(owned[i, start : start + SLICE // 2]) for i in senders]
            rest = jnp.concatenate(rest, axis=0).T
            turned[which, 2 * LANES :, span] = rest[: TURNED_ROWS - 2 * LANES]


def turn(owned):
    return pl.pallas_call(
        turn_kernel,
        out_shape=jax.ShapeDtypeStruct((2, TURNED_ROWS, FREQS), F32),
        compiler_params=params(16),
        cost_estimate=cost(2),
        name="turn_owned",
    )(owned)


def finish_kernel(sums, turned, source, receiver, offset, cmp):
    rows = sums[...]
    norm_b, cross, norm_z, norm_az, shift = (rows[:, lane : lane + 1] for lane in range(5))
    shift = shift * (1.0 / N_RCV)

    def total(values):
        return jnp.sum(values, axis=0, keepdims=True)

    total_b = total(norm_b)
    first = total(cross + shift * norm_b) / total_b
    off = shift - first
    zz = total(norm_z + 2.0 * off * cross + off * off * norm_b)
    zaz = total(
        norm_az
        + 2.0 * off * (norm_z + shift * cross)
        + off * off * (cross + shift * norm_b)
    )
    second = zaz / zz
    det = first * second - zz / total_b
    scale_b = (first + second) / det
    scale_y = 1.0 / det

    def combine(start, stop):
        return scale_b * turned[0, start:stop] - scale_y * turned[1, start:stop]

    source[...] = combine(0, LANES)
    offset[...] = combine(LANES, 2 * LANES)
    cmp[...] = combine(2 * LANES, 2 * LANES + CMP_G)
    receiver[0] = combine(2 * LANES + CMP_G, TURNED_ROWS)


def finish(sums, turned):
    return pl.pallas_call(
        finish_kernel,
        out_shape=[
            jax.ShapeDtypeStruct((SRC_G, FREQS), F32),
            jax.ShapeDtypeStruct((1, RCV_G // N_SHOT, FREQS), F32),
            jax.ShapeDtypeStruct((128, FREQS), F32),
            jax.ShapeDtypeStruct((CMP_G, FREQS), F32),
        ],
        compiler_params=params(16),
        cost_estimate=cost(1),
        name="finish",
    )(sums, turned)


def per_device(basis, traces, src_index, rcv_index, off_index, send_rows, send_counts, recv_bins):
    data = log_spectra(
        traces, basis, send_rows[0], send_counts, recv_bins[0], src_index, rcv_index, off_index
    )
    data = exchange(data, "shot")

    tab_b, rcv_b, index = adjoint_apply(data)
    arrived = exchange(tab_b, "rcv")
    counts_1 = count_call(index, 0)
    arrived, index, counts_1 = lax.optimization_barrier((arrived, index, counts_1))
    spread = spread_shares(arrived)
    spread, index = lax.optimization_barrier((spread, index))
    tab_b = exchange(spread, "rcv")
    counts = (counts_1, count_call(index, HALF))

    tab_y, rcv_y, own_count = normal_apply(tab_b, rcv_b, index, counts)
    arrived = exchange(tab_y, "rcv")
    packed = pack_owned(tab_b, rcv_b)
    arrived, packed = lax.optimization_barrier((arrived, packed))
    tab_y = exchange(spread_shares(arrived), "rcv")
    packed = pack_owned(tab_y, rcv_y, packed)
    tab_y, packed = lax.optimization_barrier((tab_y, packed))
    owned = exchange(packed, "shot")
    sums = norm_sums(tab_b, rcv_b, tab_y, rcv_y, own_count, index, counts)
    return tuple(finish(gather_sums(sums), turn(owned)))


def solution(mesh):
    basis = fourier_rows()
    mapped = jax.shard_map(
        per_device,
        mesh=mesh,
        in_specs=(
            P(),
            P(("shot", "rcv"), None),
            P(("shot", "rcv")),
            P(("shot", "rcv")),
            P(("shot", "rcv")),
            P(("shot", "rcv"), None, None),
            P(("shot", "rcv"), None),
            P(("shot", "rcv"), None, None),
        ),
        out_specs=(P("shot", None), P("rcv", "shot", None), P(), P("shot", None)),
        check_vma=False,
    )

    def run(*args):
        return mapped(jnp.asarray(basis), *args)

    return run
```

```python
import functools

import ml_dtypes
import numpy as np

import jax
import jax.numpy as jnp
from jax import lax
from jax.experimental import pallas as pl
from jax.experimental.pallas import tpu as pltpu
from jax.sharding import PartitionSpec as P

SAMPLES = 1024
FREQS = 512
TR_DEV = 640
N_SHOT = 16
N_RCV = 8
DEVICES = 128
CAP = 80
SRC_G = 128
RCV_G = 256
CMP_G = 32
SLICE = FREQS // N_SHOT
LANES = 128
OFF_TILE = 16
CMP_TILE = 17
LIVE_TILES = 21
LIVE_ROWS = LIVE_TILES * SLICE
SHARE = -(-LIVE_ROWS // (8 * N_RCV)) * 8
TAB_ROWS = N_RCV * SHARE
RCV_TILES = 2
ROWS = SRC_G + RCV_G + 128 + 512
SHARED = ROWS - SRC_G
SO = 2 * LANES
SOR = SO + RCV_G
OR = LANES + RCV_G
HALF = N_SHOT // 2
COUNT_STEPS = HALF // 2
CHUNKS = 4
CHUNK_ROWS = N_SHOT * SRC_G // CHUNKS
PARTS = N_SHOT // CHUNKS
TRACE_TILES = TR_DEV // LANES
BINS_AT = TRACE_TILES * SLICE
INDEX_AT = BINS_AT + N_SHOT
INDEX_ROWS = 24
DATA_ROWS = INDEX_AT + INDEX_ROWS
STEPS = 2
OWN_ROWS = 2 * SLICE + SLICE // 2
PACK = LANES // CMP_G

VMEM = pltpu.VMEM
F32 = jnp.float32
BF16 = jnp.bfloat16
FP8 = jnp.float8_e4m3fn


def fourier_rows():
    phase = np.arange(FREQS)[:, None] * np.arange(SAMPLES)[None, :] % SAMPLES
    angle = phase * (2.0 * np.pi / SAMPLES)
    waves = np.stack([np.cos(angle), np.sin(angle)]).reshape(2, STEPS, -1, SAMPLES)
    table = waves.transpose(1, 0, 2, 3).reshape(2 * FREQS, SAMPLES) / np.sqrt(SAMPLES)
    return table.astype(np.float32).astype(ml_dtypes.bfloat16)


def params(mib=48):
    return pltpu.CompilerParams(vmem_limit_bytes=mib * 2**20)


def cost(micros):
    return pl.CostEstimate(flops=int(micros * 1e9), bytes_accessed=int(micros * 3e6), transcendentals=0)


ANYWHERE = pl.BlockSpec(memory_space=pltpu.HBM)


def in_hbm(*arrays):
    return [pltpu.with_memory_space_constraint(array, pltpu.HBM) for array in arrays]


def nt_dot(left, right):
    return lax.dot_general(left, right, (((1,), (1,)), ((), ())), preferred_element_type=F32)


def split_rows(values):
    high = values.astype(BF16)
    low = (values - high.astype(F32)).astype(BF16)
    return jnp.concatenate([high, low], axis=0)


def at(tile):
    if isinstance(tile, int):
        return slice(tile * SLICE, (tile + 1) * SLICE)
    return pl.ds(pl.multiple_of(tile * SLICE, SLICE), SLICE)


def join_rows(both):
    half = both.shape[0] // 2
    return both[:half] + both[half:]


def flip(table):
    wide = jnp.concatenate(
        [table.astype(F32), jnp.zeros((N_SHOT, LANES - CAP), F32)], axis=1
    )
    return wide.T[:CAP].astype(jnp.int32)


def index_tiles(send_rows, send_counts, src, rcv, off):
    slots = lax.broadcasted_iota(jnp.int32, (CAP, N_SHOT), 0)
    targets = jnp.where(slots < send_counts[...], flip(send_rows[...]), -1)
    trace_ids = lax.broadcasted_iota(jnp.int32, (CAP, TR_DEV), 1)
    places = lax.broadcasted_iota(jnp.int32, (CAP, TR_DEV), 0)
    total = jnp.zeros((CAP, TR_DEV), jnp.int32)
    for owner in range(N_SHOT):
        hit = targets[:, owner : owner + 1] == trace_ids
        total = total + jnp.where(hit, places + owner * LANES, 0)
    slot_row = jnp.sum(total, axis=0, keepdims=True)
    rows = [src[...] & (SRC_G - 1), rcv[...] & (RCV_G - 1), off[...]]
    rows = [row.reshape(1, TR_DEV) for row in rows] + [slot_row]
    table = jnp.concatenate(rows, axis=0).astype(F32)
    tiles = [table[:, q * LANES : (q + 1) * LANES] for q in range(TRACE_TILES)]
    tiles.append(jnp.zeros((INDEX_ROWS - 4 * TRACE_TILES, LANES), F32))
    return jnp.concatenate(tiles, axis=0)


def spectra_kernel(traces, waves, *refs):
    given, out, own, basis, extra = refs[:6], refs[6], refs[7], refs[8], refs[9]
    small, sems, small_sems = refs[10:16], refs[16], refs[17]
    indices = [
        pltpu.make_async_copy(a, b, small_sems.at[k]) for k, (a, b) in enumerate(zip(given, small))
    ]
    for copy in indices:
        copy.start()
    pieces = []
    for k in range(TRACE_TILES):
        span = slice(k * LANES, (k + 1) * LANES)
        pieces.append((traces.at[span], own.at[span]))
    size = 2 * FREQS // STEPS // 2
    for k in range(2 * STEPS):
        span = slice(k * size, (k + 1) * size)
        pieces.append((waves.at[span], basis.at[span]))
    copies = [pltpu.make_async_copy(a, b, sems.at[k]) for k, (a, b) in enumerate(pieces)]
    early = TRACE_TILES + 2
    for copy in copies[:early]:
        copy.start()
    for copy in indices:
        copy.wait()
    send_rows, send_counts, bins, src, rcv, off = small
    pad = jnp.zeros((N_SHOT, LANES - CAP), F32)
    extra[:N_SHOT] = jnp.concatenate([bins[...].astype(F32), pad], axis=1)
    extra[N_SHOT:] = index_tiles(send_rows, send_counts, src, rcv, off)
    for part in range(N_SHOT):
        out[part, BINS_AT:, :] = extra[...]
    for copy in copies[:early]:
        copy.wait()
    for copy in copies[early:]:
        copy.start()
    half = FREQS // STEPS
    for step in range(STEPS):
        if step == 1:
            for copy in copies[early:]:
                copy.wait()
        parts = nt_dot(basis[2 * half * step : 2 * half * (step + 1)], own[...])
        logs = jnp.log1p(parts[:half] * parts[:half] + parts[half:] * parts[half:])
        for part in range(half // SLICE):
            for q in range(TRACE_TILES):
                out[step * (half // SLICE) + part, q * SLICE : (q + 1) * SLICE, :] = logs[
                    part * SLICE : (part + 1) * SLICE, q * LANES : (q + 1) * LANES
                ]


def log_spectra(traces, basis, *small):
    return pl.pallas_call(
        spectra_kernel,
        in_specs=[ANYWHERE] * (2 + len(small)),
        out_shape=jax.ShapeDtypeStruct((N_SHOT, DATA_ROWS, LANES), F32),
        scratch_shapes=[
            VMEM((TR_DEV, SAMPLES), BF16),
            VMEM((2 * FREQS, SAMPLES), BF16),
            VMEM((DATA_ROWS - BINS_AT, LANES), F32),
        ]
        + [VMEM(array.shape, jnp.int32) for array in small]
        + [
            pltpu.SemaphoreType.DMA((TRACE_TILES + 2 * STEPS,)),
            pltpu.SemaphoreType.DMA((len(small),)),
        ],
        compiler_params=params(24),
        cost_estimate=cost(5),
        name="spectra",
    )(*in_hbm(traces, basis, *small))


def fill_ids(ids):
    ids[...] = lax.broadcasted_iota(jnp.int32, ids.shape, 0).astype(F32).astype(BF16)


def fill_hot(tiles, ids, hot):
    one = jnp.ones((1, 1), BF16)
    zero = jnp.zeros((1, 1), BF16)
    values = tiles.astype(F32)
    for q in range(TRACE_TILES):
        span = slice(q * LANES, (q + 1) * LANES)
        first = 0
        for row, size, base in ((0, SRC_G, 0), (2, 128, 0), (1, RCV_G, 0), (3, 256, 0), (3, 256, 256)):
            wanted = (values[4 * q + row : 4 * q + row + 1] - base).astype(BF16)
            hits = jnp.where(ids[:size] == wanted, one, zero)
            hot[first : first + size, span] = hits.astype(hot.dtype)
            first += size


def resolve_bins(data, block):
    tiles = data[block, INDEX_AT:].astype(jnp.int32)
    rows = [data[owner, pl.ds(BINS_AT + block, 1)] for owner in range(N_SHOT)]
    table = jnp.concatenate(rows, axis=0)
    owners = lax.broadcasted_iota(jnp.int32, (N_SHOT, LANES), 0)
    resolved = []
    for q in range(TRACE_TILES):
        slot = tiles[4 * q + 3 : 4 * q + 4]
        place = jnp.broadcast_to(slot & (LANES - 1), (N_SHOT, LANES))
        found = jnp.take_along_axis(table, place, axis=1, mode="promise_in_bounds")
        found = jnp.where(owners == slot >> 7, found.astype(jnp.int32) + owners * CMP_G, 0)
        resolved += [tiles[4 * q : 4 * q + 3], jnp.sum(found, axis=0, keepdims=True)]
    resolved.append(jnp.zeros((INDEX_ROWS - 4 * TRACE_TILES, LANES), jnp.int32))
    return jnp.concatenate(resolved, axis=0)


def prepare_block(data, index, ids, hot, block):
    tiles = resolve_bins(data, block)
    index[block] = tiles
    one = jnp.ones((1, 1), BF16)
    zero = jnp.zeros((1, 1), BF16)
    for q in range(TRACE_TILES):
        for place, row in enumerate((0, 2, 1, 3)):
            lane = tiles[4 * q + row : 4 * q + row + 1] & (LANES - 1)
            hit = ids[:LANES] == lane.astype(F32).astype(BF16)
            span = slice(q * LANES, (q + 1) * LANES)
            hot[place * LANES : (place + 1) * LANES, span] = jnp.where(hit, one, zero)


def add_block(data, index, hot, tab, rcv, block):
    tiles = index[block]
    values = [data[block, q * SLICE : (q + 1) * SLICE] for q in range(TRACE_TILES)]

    both = split_rows(jnp.concatenate(values, axis=1))
    zero = jnp.zeros((1, 1), BF16)

    def of_tiles(row, count):
        place = [tiles[4 * q + row : 4 * q + row + 1] >> 7 for q in range(TRACE_TILES)]
        place = jnp.concatenate(place, axis=1).astype(F32).astype(BF16)
        return jnp.concatenate([jnp.where(place == tile, both, zero) for tile in range(count)], axis=0)

    plain = nt_dot(both, hot[: 2 * LANES])
    tab[at(block)] = join_rows(plain[:, :LANES])
    tab[at(OFF_TILE)] += join_rows(plain[:, LANES:])
    parts = of_tiles(1, RCV_TILES)
    sums = nt_dot(parts, hot[2 * LANES : 3 * LANES])
    for tile in range(RCV_TILES):
        rcv[tile] += join_rows(sums[tile * 2 * SLICE : (tile + 1) * 2 * SLICE])
    cmp_tiles = LIVE_TILES - CMP_TILE
    parts = of_tiles(3, cmp_tiles)
    sums = nt_dot(parts, hot[3 * LANES :])
    for tile in range(cmp_tiles):
        tab[at(CMP_TILE + tile)] += join_rows(sums[tile * 2 * SLICE : (tile + 1) * 2 * SLICE])


def adjoint_kernel(data, tab, rcv, index, hot_even, hot_odd, ids):
    tab[OFF_TILE * SLICE :] = jnp.zeros((TAB_ROWS - OFF_TILE * SLICE, LANES), F32)
    rcv[...] = jnp.zeros((RCV_TILES, SLICE, LANES), F32)
    fill_ids(ids)
    prepare_block(data, index, ids, hot_even, 0)

    @pl.loop(0, N_SHOT // 2)
    def _(pair):
        even = 2 * pair
        prepare_block(data, index, ids, hot_odd, even + 1)
        add_block(data, index, hot_even, tab, rcv, even)
        prepare_block(data, index, ids, hot_even, jnp.minimum(even + 2, N_SHOT - 1))
        add_block(data, index, hot_odd, tab, rcv, even + 1)


EXACT = 128


def kept_part(counts):
    return (counts.astype(jnp.int32) & (EXACT - 1)).astype(F32).astype(BF16)


def left_over(counts):
    whole = counts.astype(jnp.int32)
    return (whole - (whole & (EXACT - 1))).astype(F32).astype(BF16)


def peak(counts):
    top = jnp.max(counts, axis=0, keepdims=True)
    best = top[:, :LANES]
    for start in range(LANES, counts.shape[1], LANES):
        best = jnp.maximum(best, top[:, start : start + LANES])
    return best


def block_counts(hot):
    with_cmp = nt_dot(hot[:SOR], hot[SOR:])
    with_rcv = nt_dot(hot[:SO], hot[SO:SOR])
    with_off = nt_dot(hot[:SRC_G], hot[SRC_G:SO])
    rows = jnp.concatenate([with_off, with_rcv[:SRC_G], with_cmp[:SRC_G]], axis=1)
    return rows, with_cmp[SRC_G:], with_rcv[SRC_G:]


def count_kernel(
    index, kept, to_cmp_kept, to_rcv_kept, most, diag, hot_even, hot_odd, ids, to_cmp, to_rcv, *, first
):
    step = pl.program_id(0)
    even = first + 2 * step

    @pl.when(step == 0)
    def _():
        to_cmp[...] = jnp.zeros_like(to_cmp)
        to_rcv[...] = jnp.zeros_like(to_rcv)
        diag[...] = jnp.zeros_like(diag)
        most[...] = jnp.zeros_like(most)
        fill_ids(ids)
        fill_hot(index[even], ids, hot_even)

    def add(hot, place):
        rows, cmp_counts, rcv_counts = block_counts(hot)
        to_cmp[...] += cmp_counts
        to_rcv[...] += rcv_counts
        diag[...] += jnp.sum(rows, axis=0, keepdims=True)
        kept[place * SRC_G : (place + 1) * SRC_G] = kept_part(rows)
        most[...] = jnp.maximum(most[...], peak(rows))

    fill_hot(index[even + 1], ids, hot_odd)
    add(hot_even, 0)
    fill_hot(index[jnp.minimum(even + 2, N_SHOT - 1)], ids, hot_even)
    add(hot_odd, 1)

    @pl.when(step == COUNT_STEPS - 1)
    def _():
        to_cmp_kept[...] = (to_cmp[...].astype(jnp.int32) & (EXACT - 1)).astype(jnp.int8)
        to_rcv_kept[...] = (to_rcv[...].astype(jnp.int32) & (EXACT - 1)).astype(jnp.int8)
        most[...] = jnp.maximum(most[...], jnp.maximum(peak(to_cmp[...]), peak(to_rcv[...])))


def add_left_over(most_1, most_2, index, hot, ids, to_cmp, to_rcv, use_both, use_rows):
    top = jnp.maximum(jnp.max(most_1[...]), jnp.max(most_2[...]))

    @pl.when(top >= EXACT)
    def _():
        fill_ids(ids)
        for half in range(2):
            to_cmp[...] = jnp.zeros_like(to_cmp)
            to_rcv[...] = jnp.zeros_like(to_rcv)

            @pl.loop(half * HALF, (half + 1) * HALF)
            def _(block):
                fill_hot(index[block], ids, hot)
                rows, cmp_counts, rcv_counts = block_counts(hot)
                to_cmp[...] += cmp_counts
                to_rcv[...] += rcv_counts
                use_rows(block, left_over(rows))

            use_both(left_over(to_cmp[...]), left_over(to_rcv[...]))


def fetch_counts(refs, held, held_cmp, held_rcv, sems):
    *halves, cmp_1, cmp_2, rcv_1, rcv_2 = refs
    pieces = []
    for block in range(N_SHOT):
        start = block % HALF * SRC_G
        place = block % PARTS * SRC_G
        target = held.at[block // PARTS, place : place + SRC_G]
        pieces.append((halves[block // HALF].at[start : start + SRC_G], target))
    pieces += [(cmp_1, held_cmp.at[0]), (cmp_2, held_cmp.at[1])]
    pieces += [(rcv_1, held_rcv.at[0]), (rcv_2, held_rcv.at[1])]
    copies = [pltpu.make_async_copy(a, b, sems.at[k]) for k, (a, b) in enumerate(pieces)]
    for copy in copies[: 2 * PARTS]:
        copy.start()
    return copies


def next_chunk(copies, chunk):
    for copy in copies[chunk * PARTS : (chunk + 1) * PARTS]:
        copy.wait()
    if chunk + 2 < CHUNKS:
        last = len(copies) if chunk + 3 == CHUNKS else (chunk + 3) * PARTS
        for copy in copies[(chunk + 2) * PARTS : last]:
            copy.start()


def sum_halves(held):
    return (held[0].astype(F32) + held[1].astype(F32)).astype(BF16)


def load_halves(tab, rcv, own, shared):
    for tile in range(N_SHOT):
        own[:, tile * LANES : (tile + 1) * LANES] = split_rows(tab[at(tile)])
    shared[: 2 * SLICE, :LANES] = split_rows(tab[at(OFF_TILE)])
    for tile in range(RCV_TILES):
        shared[: 2 * SLICE, (1 + tile) * LANES : (2 + tile) * LANES] = split_rows(rcv[tile])
    for tile in range(CMP_TILE, LIVE_TILES):
        start = (tile - CMP_TILE) * LANES + OR
        shared[: 2 * SLICE, start : start + LANES] = split_rows(tab[at(tile)])


def normal_kernel(
    first, last, cmp_1, cmp_2, rcv_1, rcv_2, tab_in, rcv_in, diag_1, diag_2, most_1, most_2, index,
    tab, rcv, own_count, own, shared, to_shared, to_own,
    held, held_cmp, held_rcv, sems, hot, ids, exact_cmp, exact_rcv,
):
    counts = (first, last, cmp_1, cmp_2, rcv_1, rcv_2)
    copies = fetch_counts(counts, held, held_cmp, held_rcv, sems)
    top = 2 * SLICE
    load_halves(tab_in, rcv_in, own, shared)
    lanes = lax.broadcasted_iota(jnp.int32, (16, SHARED), 1)
    shared[top:] = jnp.where(lanes < LANES, 1.0, 0.0).astype(BF16)
    for chunk in range(CHUNKS):
        next_chunk(copies, chunk)
        span = slice(chunk * CHUNK_ROWS, (chunk + 1) * CHUNK_ROWS)
        sums = jnp.dot(own[:, span], held[chunk], preferred_element_type=F32)
        to_shared[...] = sums if chunk == 0 else to_shared[...] + sums
        to_own[:, span] = nt_dot(shared[...], held[chunk])

    def others(to_cmp, to_rcv):
        cmp_sums = jnp.dot(shared[:top, :OR], to_cmp, preferred_element_type=F32)
        to_shared[:, OR:] += cmp_sums
        to_shared[:, :OR] += nt_dot(shared[:top, OR:], to_cmp)
        rcv_sums = jnp.dot(shared[:top, :LANES], to_rcv, preferred_element_type=F32)
        to_shared[:, LANES:OR] += rcv_sums
        to_shared[:, :LANES] += nt_dot(shared[:top, LANES:OR], to_rcv)

    def use_rows(block, rows):
        span = pl.ds(pl.multiple_of(block * SRC_G, SRC_G), SRC_G)
        to_shared[...] += jnp.dot(own[:, span], rows, preferred_element_type=F32)
        to_own[:, span] += nt_dot(shared[...], rows)

    for copy in copies[-4:]:
        copy.wait()
    others(sum_halves(held_cmp), sum_halves(held_rcv))
    add_left_over(most_1, most_2, index, hot, ids, exact_cmp, exact_rcv, others, use_rows)
    diag = diag_1[...] + diag_2[...]
    for tile in range(N_SHOT):
        span = slice(tile * LANES, (tile + 1) * LANES)
        count = to_own[top : top + 1, span]
        own_count[tile : tile + 1] = count
        tab[at(tile)] = join_rows(to_own[:top, span]) + count * tab_in[at(tile)]
    tab[at(OFF_TILE)] = join_rows(to_shared[:, :LANES]) + diag[:, :LANES] * tab_in[at(OFF_TILE)]
    for tile in range(RCV_TILES):
        span = slice((1 + tile) * LANES, (2 + tile) * LANES)
        rcv[tile] = join_rows(to_shared[:, span]) + diag[:, span] * rcv_in[tile]
    for tile in range(CMP_TILE, LIVE_TILES):
        start = (tile - CMP_TILE) * LANES + OR
        span = slice(start, start + LANES)
        tab[at(tile)] = join_rows(to_shared[:, span]) + diag[:, span] * tab_in[at(tile)]
    tab[LIVE_ROWS:] = jnp.zeros((TAB_ROWS - LIVE_ROWS, LANES), F32)


def all_sum(values):
    return jnp.sum(values, axis=tuple(range(values.ndim)), keepdims=True).reshape(1, 1)


def fold(values):
    total = values[:, :LANES]
    for start in range(LANES, values.shape[1], LANES):
        total = total + values[:, start : start + LANES]
    return total


def norm_kernel(
    first, last, cmp_1, cmp_2, rcv_1, rcv_2,
    tab_b, rcv_b, tab_y, rcv_y, diag_1, diag_2, most_1, most_2, index, own_count,
    out, tab_z, rcv_z, own, shared, to_shared,
    held, held_cmp, held_rcv, sems, hot, ids, exact_cmp, exact_rcv,
):
    counts = (first, last, cmp_1, cmp_2, rcv_1, rcv_2)
    copies = fetch_counts(counts, held, held_cmp, held_rcv, sems)
    shared_b = tab_b[:LIVE_ROWS]
    shared_y = tab_y[:LIVE_ROWS]
    shift = all_sum(shared_b * shared_y) / all_sum(shared_b * shared_b)
    shared_z = shared_y - shift * shared_b
    own_b = rcv_b[...]
    own_z = rcv_y[...] - shift * own_b
    tab_z[...] = shared_z
    rcv_z[...] = own_z
    load_halves(tab_z, rcv_z, own, shared)
    for chunk in range(CHUNKS):
        next_chunk(copies, chunk)
        span = slice(chunk * CHUNK_ROWS, (chunk + 1) * CHUNK_ROWS)
        sums = jnp.dot(own[:, span], held[chunk], preferred_element_type=F32)
        to_shared[...] = sums if chunk == 0 else to_shared[...] + sums

    def whole(tabs, own):
        return all_sum(tabs) * (1.0 / N_RCV) + all_sum(own)

    def others(to_cmp, to_rcv):
        cmp_sums = jnp.dot(shared[:, :OR], to_cmp, preferred_element_type=F32)
        to_shared[:, OR:] += cmp_sums
        rcv_sums = jnp.dot(shared[:, :LANES], to_rcv, preferred_element_type=F32)
        to_shared[:, LANES:OR] += rcv_sums

    def use_rows(block, rows):
        span = pl.ds(pl.multiple_of(block * SRC_G, SRC_G), SRC_G)
        to_shared[...] += jnp.dot(own[:, span], rows, preferred_element_type=F32)

    for copy in copies[-4:]:
        copy.wait()
    others(sum_halves(held_cmp), sum_halves(held_rcv))
    add_left_over(most_1, most_2, index, hot, ids, exact_cmp, exact_rcv, others, use_rows)
    tiles = [tab_z[at(OFF_TILE)]] + [rcv_z[tile] for tile in range(RCV_TILES)]
    tiles += [tab_z[at(tile)] for tile in range(CMP_TILE, LIVE_TILES)]
    rest = jnp.concatenate(tiles, axis=1)
    diag = diag_1[...] + diag_2[...]
    total = fold(2.0 * rest * join_rows(to_shared[...]) + diag * rest * rest)
    for tile in range(N_SHOT):
        total = total + own_count[tile : tile + 1] * tab_z[at(tile)] * tab_z[at(tile)]
    sums = (
        whole(shared_b * shared_b, own_b * own_b),
        whole(shared_b * shared_z, own_b * own_z),
        whole(shared_z * shared_z, own_z * own_z),
        all_sum(total),
        shift,
    )
    lanes = lax.broadcasted_iota(jnp.int32, (1, LANES), 1)
    row = jnp.zeros((1, LANES), F32)
    for lane, value in enumerate(sums):
        row = jnp.where(lanes == lane, value, row)
    out[...] = row


def whole_spec(*shape):
    return pl.BlockSpec(shape, lambda c: (0,) * len(shape))


TAB = (TAB_ROWS, LANES)
RCV = (RCV_TILES, SLICE, LANES)
INDEX = (N_SHOT, INDEX_ROWS, LANES)
INDEX_SPEC = pl.BlockSpec((1, INDEX_ROWS, LANES), lambda c: (c, 0, 0))


def table_shapes():
    return [jax.ShapeDtypeStruct(TAB, F32), jax.ShapeDtypeStruct(RCV, F32)]


def hot_scratch():
    return [VMEM((ROWS, TR_DEV), FP8), VMEM((256, LANES), BF16)]


def adjoint_apply(data):
    return pl.pallas_call(
        adjoint_kernel,
        out_shape=table_shapes() + [jax.ShapeDtypeStruct(INDEX, jnp.int32)],
        scratch_shapes=[VMEM((4 * LANES, TR_DEV), BF16)] * 2 + [VMEM((256, LANES), BF16)],
        compiler_params=params(24),
        cost_estimate=cost(8),
        name="adjoint_apply",
    )(data)


COUNTS = (HALF * SRC_G, SHARED)
TO_CMP = (OR, SHARED - OR)
TO_RCV = (LANES, RCV_G)
IN_VMEM = pl.BlockSpec(memory_space=VMEM)


def count_call(index, first):
    rows = pl.BlockSpec((2 * SRC_G, SHARED), lambda c: (c, 0))
    small = [whole_spec(*TO_CMP), whole_spec(*TO_RCV), whole_spec(1, LANES), whole_spec(1, SHARED)]
    return pl.pallas_call(
        functools.partial(count_kernel, first=first),
        grid=(COUNT_STEPS,),
        in_specs=[whole_spec(*INDEX)],
        out_specs=[rows] + small,
        out_shape=[
            pltpu.HBM(COUNTS, BF16),
            pltpu.HBM(TO_CMP, jnp.int8),
            pltpu.HBM(TO_RCV, jnp.int8),
            jax.ShapeDtypeStruct((1, LANES), F32),
            jax.ShapeDtypeStruct((1, SHARED), F32),
        ],
        scratch_shapes=[VMEM((ROWS, TR_DEV), FP8)] * 2
        + [VMEM((256, LANES), BF16), VMEM(TO_CMP, F32), VMEM(TO_RCV, F32)],
        compiler_params=params(24),
        cost_estimate=cost(6),
        name="count_pairs",
    )(index)


def count_scratch(chunks):
    return (
        [
            VMEM((chunks, CHUNK_ROWS, SHARED), BF16),
            VMEM((2,) + TO_CMP, jnp.int8),
            VMEM((2,) + TO_RCV, jnp.int8),
            pltpu.SemaphoreType.DMA((N_SHOT + 4,)),
        ]
        + hot_scratch()
        + [VMEM(TO_CMP, F32), VMEM(TO_RCV, F32)]
    )


def count_operands(counts):
    big = in_hbm(*[array for pair in zip(counts[0][:3], counts[1][:3]) for array in pair])
    (most_1, diag_1), (most_2, diag_2) = counts[0][3:5], counts[1][3:5]
    return big, [diag_1, diag_2, most_1, most_2]


def normal_apply(tab, rcv, index, counts):
    big, small = count_operands(counts)
    return pl.pallas_call(
        normal_kernel,
        in_specs=[ANYWHERE] * 6 + [IN_VMEM] * 7,
        out_shape=table_shapes() + [jax.ShapeDtypeStruct((N_SHOT, LANES), F32)],
        scratch_shapes=[
            VMEM((2 * SLICE, N_SHOT * SRC_G), BF16),
            VMEM((2 * SLICE + 16, SHARED), BF16),
            VMEM((2 * SLICE, SHARED), F32),
            VMEM((2 * SLICE + 16, N_SHOT * SRC_G), F32),
        ]
        + count_scratch(CHUNKS),
        compiler_params=params(24),
        cost_estimate=cost(3),
        name="normal_apply",
    )(*big, tab, rcv, *small, index)


def norm_sums(tab_b, rcv_b, tab_y, rcv_y, own_count, index, counts):
    big, small = count_operands(counts)
    return pl.pallas_call(
        norm_kernel,
        in_specs=[ANYWHERE] * 6 + [IN_VMEM] * 10,
        out_shape=jax.ShapeDtypeStruct((1, LANES), F32),
        scratch_shapes=[
            VMEM((LIVE_ROWS, LANES), F32),
            VMEM(RCV, F32),
            VMEM((2 * SLICE, N_SHOT * SRC_G), BF16),
            VMEM((2 * SLICE, SHARED), BF16),
            VMEM((2 * SLICE, SHARED), F32),
        ]
        + count_scratch(CHUNKS),
        compiler_params=params(24),
        cost_estimate=cost(2),
        name="norm_sums",
    )(*big, tab_b, rcv_b, tab_y, rcv_y, *small, index, own_count)


def spread_kernel(parts, out):
    total = parts[0]
    for source in range(1, N_RCV):
        total = total + parts[source]
    for dest in range(N_RCV):
        out[dest] = total


def exchange(array, axis):
    return lax.all_to_all(array, axis, split_axis=0, concat_axis=0, tiled=True)


def spread_shares(arrived):
    shape = (N_RCV, SHARE, LANES)
    spread = pl.pallas_call(
        spread_kernel,
        out_shape=jax.ShapeDtypeStruct(shape, F32),
        compiler_params=params(24),
        cost_estimate=cost(1),
        name="sum_shares",
    )(arrived.reshape(shape))
    return spread.reshape(TAB)


def pack_kernel(tab, rcv, *refs, first):
    out, rows, sems = refs[-3:]
    lanes = lax.broadcasted_iota(jnp.int32, (SLICE, LANES), 1)
    half = SLICE // 2
    copies = []
    for dest in range(N_SHOT):
        rows[dest, :SLICE] = tab[at(dest)]
        rows[dest, SLICE : 2 * SLICE] = tab[at(OFF_TILE)]
        cmp_first = dest * CMP_G
        rcv_first = dest * (RCV_G // N_SHOT)
        bins = tab[at(CMP_TILE + cmp_first // LANES)]
        cmp_part = pltpu.roll(bins, (-cmp_first) % LANES, 1)
        rcv_part = pltpu.roll(rcv[rcv_first // LANES], (CMP_G - rcv_first) % LANES, 1)
        both = jnp.where(lanes < CMP_G, cmp_part, rcv_part)
        moved = pltpu.roll(both[half:], LANES // 2, 1)
        rows[dest, 2 * SLICE :] = jnp.where(lanes[:half] < LANES // 2, both[:half], moved)
        if dest % PACK == PACK - 1:
            group = dest // PACK
            span = slice(group * PACK, (group + 1) * PACK)
            place = out.at[span, first : first + OWN_ROWS]
            copies.append(pltpu.make_async_copy(rows.at[span], place, sems.at[group]))
            copies[-1].start()
    for copy in copies:
        copy.wait()


def pack_owned(tab, rcv, former=None):
    given = [] if former is None else in_hbm(former)
    return pl.pallas_call(
        functools.partial(pack_kernel, first=OWN_ROWS * len(given)),
        in_specs=[pl.BlockSpec(memory_space=VMEM)] * 2 + [ANYWHERE] * len(given),
        out_specs=ANYWHERE,
        out_shape=pltpu.HBM((N_SHOT, 2 * OWN_ROWS, LANES), F32),
        scratch_shapes=[
            VMEM((N_SHOT, OWN_ROWS, LANES), F32),
            pltpu.SemaphoreType.DMA((N_SHOT // PACK,)),
        ],
        input_output_aliases={2: 0} if given else {},
        compiler_params=params(24),
        cost_estimate=cost(1),
        name="pack_owned",
    )(tab, rcv, *given)


def swapped(value, axis, size, bit):
    return lax.ppermute(value, axis, [(s, s ^ bit) for s in range(size)])


def gather_sums(sums):
    for bit in (1, 2, 6):
        sums = sums + swapped(sums, "rcv", N_RCV, bit)
    here = jnp.arange(N_SHOT, dtype=jnp.int32)[:, None] == lax.axis_index("shot")
    rows = jnp.where(here, sums, 0.0)
    for bit in (1, 3, 4, 12):
        rows = rows + swapped(rows, "shot", N_SHOT, bit)
    return rows


def finish_kernel(sums, owned, source, receiver, offset, cmp):
    rows = sums[...]
    norm_b, cross, norm_z, norm_az, shift = (rows[:, lane : lane + 1] for lane in range(5))
    shift = shift * (1.0 / N_RCV)

    def total(values):
        return jnp.sum(values, axis=0, keepdims=True)

    total_b = total(norm_b)
    first = total(cross + shift * norm_b) / total_b
    off = shift - first
    zz = total(norm_z + 2.0 * off * cross + off * off * norm_b)
    zaz = total(
        norm_az
        + 2.0 * off * (norm_z + shift * cross)
        + off * off * (cross + shift * norm_b)
    )
    second = zaz / zz
    det = first * second - zz / total_b
    scale_b = (first + second) / det
    scale_y = 1.0 / det

    def combine(sender, start, stop):
        part_y = owned[sender, OWN_ROWS + start : OWN_ROWS + stop]
        return scale_b * owned[sender, start:stop] - scale_y * part_y

    def spread_halves(tile):
        return jnp.concatenate([tile, pltpu.roll(tile, LANES // 2, 1)], axis=0)

    per_tile = LANES // SLICE
    for group in range(N_SHOT // per_tile):
        span = slice(group * LANES, (group + 1) * LANES)
        senders = range(group * per_tile, (group + 1) * per_tile)
        source[:, span] = jnp.concatenate([combine(i, 0, SLICE) for i in senders], axis=0).T
        offset[:, span] = jnp.concatenate(
            [combine(i, SLICE, 2 * SLICE) for i in senders], axis=0
        ).T
        rest = jnp.concatenate(
            [spread_halves(combine(i, 2 * SLICE, OWN_ROWS)) for i in senders], axis=0
        ).T
        cmp[:, span] = rest[:CMP_G]
        receiver[0, :, span] = rest[CMP_G : CMP_G + RCV_G // N_SHOT]


def finish(sums, owned):
    return pl.pallas_call(
        finish_kernel,
        out_shape=[
            jax.ShapeDtypeStruct((SRC_G, FREQS), F32),
            jax.ShapeDtypeStruct((1, RCV_G // N_SHOT, FREQS), F32),
            jax.ShapeDtypeStruct((128, FREQS), F32),
            jax.ShapeDtypeStruct((CMP_G, FREQS), F32),
        ],
        compiler_params=params(),
        name="finish",
    )(sums, owned)


def per_device(basis, traces, src_index, rcv_index, off_index, send_rows, send_counts, recv_bins):
    data = log_spectra(
        traces, basis, send_rows[0], send_counts, recv_bins[0], src_index, rcv_index, off_index
    )
    data = exchange(data, "shot")

    tab_b, rcv_b, index = adjoint_apply(data)
    arrived = exchange(tab_b, "rcv")
    counts_1 = count_call(index, 0)
    arrived, index, counts_1 = lax.optimization_barrier((arrived, index, counts_1))
    spread = spread_shares(arrived)
    spread, index = lax.optimization_barrier((spread, index))
    tab_b = exchange(spread, "rcv")
    counts = (counts_1, count_call(index, HALF))

    tab_y, rcv_y, own_count = normal_apply(tab_b, rcv_b, index, counts)
    arrived = exchange(tab_y, "rcv")
    packed = pack_owned(tab_b, rcv_b)
    arrived, packed = lax.optimization_barrier((arrived, packed))
    tab_y = exchange(spread_shares(arrived), "rcv")
    packed = pack_owned(tab_y, rcv_y, packed)
    tab_y, packed = lax.optimization_barrier((tab_y, packed))
    owned = exchange(packed, "shot")
    sums = norm_sums(tab_b, rcv_b, tab_y, rcv_y, own_count, index, counts)
    return tuple(finish(gather_sums(sums), owned))


def solution(mesh):
    basis = fourier_rows()
    mapped = jax.shard_map(
        per_device,
        mesh=mesh,
        in_specs=(
            P(),
            P(("shot", "rcv"), None),
            P(("shot", "rcv")),
            P(("shot", "rcv")),
            P(("shot", "rcv")),
            P(("shot", "rcv"), None, None),
            P(("shot", "rcv"), None),
            P(("shot", "rcv"), None, None),
        ),
        out_specs=(P("shot", None), P("rcv", "shot", None), P(), P("shot", None)),
        check_vma=False,
    )

    def run(*args):
        return mapped(jnp.asarray(basis), *args)

    return run
```

```python
import functools

import ml_dtypes
import numpy as np

import jax
import jax.numpy as jnp
from jax import lax
from jax.experimental import pallas as pl
from jax.experimental.pallas import tpu as pltpu
from jax.sharding import PartitionSpec as P

SAMPLES = 1024
FREQS = 512
TR_DEV = 640
N_SHOT = 16
N_RCV = 8
DEVICES = 128
CAP = 80
SRC_G = 128
RCV_G = 256
CMP_G = 32
SLICE = FREQS // N_SHOT
LANES = 128
OFF_TILE = 16
CMP_TILE = 17
LIVE_TILES = 21
LIVE_ROWS = LIVE_TILES * SLICE
SHARE = -(-LIVE_ROWS // (8 * N_RCV)) * 8
TAB_ROWS = N_RCV * SHARE
RCV_TILES = 2
ROWS = SRC_G + RCV_G + 128 + 512
SHARED = ROWS - SRC_G
SO = 2 * LANES
SOR = SO + RCV_G
OR = LANES + RCV_G
HALF = N_SHOT // 2
COUNT_STEPS = HALF // 2
CHUNKS = 4
CHUNK_ROWS = N_SHOT * SRC_G // CHUNKS
TRACE_TILES = TR_DEV // LANES
BINS_AT = TRACE_TILES * SLICE
INDEX_AT = BINS_AT + N_SHOT
INDEX_ROWS = 24
DATA_ROWS = INDEX_AT + INDEX_ROWS
STEPS = 2
OWN_ROWS = 2 * SLICE + SLICE // 2
PACK = LANES // CMP_G

VMEM = pltpu.VMEM
F32 = jnp.float32
BF16 = jnp.bfloat16
FP8 = jnp.float8_e4m3fn


def fourier_rows():
    phase = np.arange(FREQS)[:, None] * np.arange(SAMPLES)[None, :] % SAMPLES
    angle = phase * (2.0 * np.pi / SAMPLES)
    waves = np.stack([np.cos(angle), np.sin(angle)]).reshape(2, STEPS, -1, SAMPLES)
    table = waves.transpose(1, 0, 2, 3).reshape(2 * FREQS, SAMPLES) / np.sqrt(SAMPLES)
    return table.astype(np.float32).astype(ml_dtypes.bfloat16)


def params(mib=48):
    return pltpu.CompilerParams(vmem_limit_bytes=mib * 2**20)


def cost(micros):
    return pl.CostEstimate(flops=int(micros * 1e9), bytes_accessed=int(micros * 3e6), transcendentals=0)


ANYWHERE = pl.BlockSpec(memory_space=pltpu.HBM)


def in_hbm(*arrays):
    return [pltpu.with_memory_space_constraint(array, pltpu.HBM) for array in arrays]


def nt_dot(left, right):
    return lax.dot_general(left, right, (((1,), (1,)), ((), ())), preferred_element_type=F32)


def split_rows(values):
    high = values.astype(BF16)
    low = (values - high.astype(F32)).astype(BF16)
    return jnp.concatenate([high, low], axis=0)


def at(tile):
    if isinstance(tile, int):
        return slice(tile * SLICE, (tile + 1) * SLICE)
    return pl.ds(pl.multiple_of(tile * SLICE, SLICE), SLICE)


def join_rows(both):
    half = both.shape[0] // 2
    return both[:half] + both[half:]


def flip(table):
    wide = jnp.concatenate(
        [table.astype(F32), jnp.zeros((N_SHOT, LANES - CAP), F32)], axis=1
    )
    return wide.T[:CAP].astype(jnp.int32)


def index_tiles(send_rows, send_counts, src, rcv, off):
    slots = lax.broadcasted_iota(jnp.int32, (CAP, N_SHOT), 0)
    targets = jnp.where(slots < send_counts[...], flip(send_rows[...]), -1)
    trace_ids = lax.broadcasted_iota(jnp.int32, (CAP, TR_DEV), 1)
    places = lax.broadcasted_iota(jnp.int32, (CAP, TR_DEV), 0)
    total = jnp.zeros((CAP, TR_DEV), jnp.int32)
    for owner in range(N_SHOT):
        hit = targets[:, owner : owner + 1] == trace_ids
        total = total + jnp.where(hit, places + owner * LANES, 0)
    slot_row = jnp.sum(total, axis=0, keepdims=True)
    rows = [src[...] & (SRC_G - 1), rcv[...] & (RCV_G - 1), off[...]]
    rows = [row.reshape(1, TR_DEV) for row in rows] + [slot_row]
    table = jnp.concatenate(rows, axis=0).astype(F32)
    tiles = [table[:, q * LANES : (q + 1) * LANES] for q in range(TRACE_TILES)]
    tiles.append(jnp.zeros((INDEX_ROWS - 4 * TRACE_TILES, LANES), F32))
    return jnp.concatenate(tiles, axis=0)


def spectra_kernel(traces, waves, *refs):
    given, out, own, basis, extra = refs[:6], refs[6], refs[7], refs[8], refs[9]
    small, sems, small_sems = refs[10:16], refs[16], refs[17]
    indices = [
        pltpu.make_async_copy(a, b, small_sems.at[k]) for k, (a, b) in enumerate(zip(given, small))
    ]
    for copy in indices:
        copy.start()
    pieces = []
    for k in range(TRACE_TILES):
        span = slice(k * LANES, (k + 1) * LANES)
        pieces.append((traces.at[span], own.at[span]))
    size = 2 * FREQS // STEPS // 2
    for k in range(2 * STEPS):
        span = slice(k * size, (k + 1) * size)
        pieces.append((waves.at[span], basis.at[span]))
    copies = [pltpu.make_async_copy(a, b, sems.at[k]) for k, (a, b) in enumerate(pieces)]
    early = TRACE_TILES + 2
    for copy in copies[:early]:
        copy.start()
    for copy in indices:
        copy.wait()
    send_rows, send_counts, bins, src, rcv, off = small
    pad = jnp.zeros((N_SHOT, LANES - CAP), F32)
    extra[:N_SHOT] = jnp.concatenate([bins[...].astype(F32), pad], axis=1)
    extra[N_SHOT:] = index_tiles(send_rows, send_counts, src, rcv, off)
    for part in range(N_SHOT):
        out[part, BINS_AT:, :] = extra[...]
    for copy in copies[:early]:
        copy.wait()
    for copy in copies[early:]:
        copy.start()
    half = FREQS // STEPS
    for step in range(STEPS):
        if step == 1:
            for copy in copies[early:]:
                copy.wait()
        parts = nt_dot(basis[2 * half * step : 2 * half * (step + 1)], own[...])
        logs = jnp.log1p(parts[:half] * parts[:half] + parts[half:] * parts[half:])
        for part in range(half // SLICE):
            for q in range(TRACE_TILES):
                out[step * (half // SLICE) + part, q * SLICE : (q + 1) * SLICE, :] = logs[
                    part * SLICE : (part + 1) * SLICE, q * LANES : (q + 1) * LANES
                ]


def log_spectra(traces, basis, *small):
    return pl.pallas_call(
        spectra_kernel,
        in_specs=[ANYWHERE] * (2 + len(small)),
        out_shape=jax.ShapeDtypeStruct((N_SHOT, DATA_ROWS, LANES), F32),
        scratch_shapes=[
            VMEM((TR_DEV, SAMPLES), BF16),
            VMEM((2 * FREQS, SAMPLES), BF16),
            VMEM((DATA_ROWS - BINS_AT, LANES), F32),
        ]
        + [VMEM(array.shape, jnp.int32) for array in small]
        + [
            pltpu.SemaphoreType.DMA((TRACE_TILES + 2 * STEPS,)),
            pltpu.SemaphoreType.DMA((len(small),)),
        ],
        compiler_params=params(24),
        cost_estimate=cost(5),
        name="spectra",
    )(*in_hbm(traces, basis, *small))


def fill_ids(ids):
    ids[...] = lax.broadcasted_iota(jnp.int32, ids.shape, 0).astype(F32).astype(BF16)


def fill_hot(tiles, ids, hot):
    one = jnp.ones((1, 1), BF16)
    zero = jnp.zeros((1, 1), BF16)
    values = tiles.astype(F32)
    for q in range(TRACE_TILES):
        span = slice(q * LANES, (q + 1) * LANES)
        first = 0
        for row, size, base in ((0, SRC_G, 0), (2, 128, 0), (1, RCV_G, 0), (3, 256, 0), (3, 256, 256)):
            wanted = (values[4 * q + row : 4 * q + row + 1] - base).astype(BF16)
            hits = jnp.where(ids[:size] == wanted, one, zero)
            hot[first : first + size, span] = hits.astype(hot.dtype)
            first += size


def resolve_bins(data, block):
    tiles = data[block, INDEX_AT:].astype(jnp.int32)
    rows = [data[owner, pl.ds(BINS_AT + block, 1)] for owner in range(N_SHOT)]
    table = jnp.concatenate(rows, axis=0)
    owners = lax.broadcasted_iota(jnp.int32, (N_SHOT, LANES), 0)
    resolved = []
    for q in range(TRACE_TILES):
        slot = tiles[4 * q + 3 : 4 * q + 4]
        place = jnp.broadcast_to(slot & (LANES - 1), (N_SHOT, LANES))
        found = jnp.take_along_axis(table, place, axis=1, mode="promise_in_bounds")
        found = jnp.where(owners == slot >> 7, found.astype(jnp.int32) + owners * CMP_G, 0)
        resolved += [tiles[4 * q : 4 * q + 3], jnp.sum(found, axis=0, keepdims=True)]
    resolved.append(jnp.zeros((INDEX_ROWS - 4 * TRACE_TILES, LANES), jnp.int32))
    return jnp.concatenate(resolved, axis=0)


def prepare_block(data, index, ids, hot, block):
    tiles = resolve_bins(data, block)
    index[block] = tiles
    one = jnp.ones((1, 1), BF16)
    zero = jnp.zeros((1, 1), BF16)
    for q in range(TRACE_TILES):
        for place, row in enumerate((0, 2, 1, 3)):
            lane = tiles[4 * q + row : 4 * q + row + 1] & (LANES - 1)
            hit = ids[:LANES] == lane.astype(F32).astype(BF16)
            span = slice(q * LANES, (q + 1) * LANES)
            hot[place * LANES : (place + 1) * LANES, span] = jnp.where(hit, one, zero)


def add_block(data, index, hot, tab, rcv, block):
    tiles = index[block]
    values = [data[block, q * SLICE : (q + 1) * SLICE] for q in range(TRACE_TILES)]

    both = split_rows(jnp.concatenate(values, axis=1))
    zero = jnp.zeros((1, 1), BF16)

    def of_tiles(row, count):
        place = [tiles[4 * q + row : 4 * q + row + 1] >> 7 for q in range(TRACE_TILES)]
        place = jnp.concatenate(place, axis=1).astype(F32).astype(BF16)
        return jnp.concatenate([jnp.where(place == tile, both, zero) for tile in range(count)], axis=0)

    plain = nt_dot(both, hot[: 2 * LANES])
    tab[at(block)] = join_rows(plain[:, :LANES])
    tab[at(OFF_TILE)] += join_rows(plain[:, LANES:])
    parts = of_tiles(1, RCV_TILES)
    sums = nt_dot(parts, hot[2 * LANES : 3 * LANES])
    for tile in range(RCV_TILES):
        rcv[tile] += join_rows(sums[tile * 2 * SLICE : (tile + 1) * 2 * SLICE])
    cmp_tiles = LIVE_TILES - CMP_TILE
    parts = of_tiles(3, cmp_tiles)
    sums = nt_dot(parts, hot[3 * LANES :])
    for tile in range(cmp_tiles):
        tab[at(CMP_TILE + tile)] += join_rows(sums[tile * 2 * SLICE : (tile + 1) * 2 * SLICE])


def adjoint_kernel(data, tab, rcv, index, hot_even, hot_odd, ids):
    tab[OFF_TILE * SLICE :] = jnp.zeros((TAB_ROWS - OFF_TILE * SLICE, LANES), F32)
    rcv[...] = jnp.zeros((RCV_TILES, SLICE, LANES), F32)
    fill_ids(ids)
    prepare_block(data, index, ids, hot_even, 0)

    @pl.loop(0, N_SHOT // 2)
    def _(pair):
        even = 2 * pair
        prepare_block(data, index, ids, hot_odd, even + 1)
        add_block(data, index, hot_even, tab, rcv, even)
        prepare_block(data, index, ids, hot_even, jnp.minimum(even + 2, N_SHOT - 1))
        add_block(data, index, hot_odd, tab, rcv, even + 1)


EXACT = 128


def kept_part(counts):
    return (counts.astype(jnp.int32) & (EXACT - 1)).astype(F32).astype(BF16)


def left_over(counts):
    whole = counts.astype(jnp.int32)
    return (whole - (whole & (EXACT - 1))).astype(F32).astype(BF16)


def peak(counts):
    top = jnp.max(counts, axis=0, keepdims=True)
    best = top[:, :LANES]
    for start in range(LANES, counts.shape[1], LANES):
        best = jnp.maximum(best, top[:, start : start + LANES])
    return best


def block_counts(hot):
    with_cmp = nt_dot(hot[:SOR], hot[SOR:])
    with_rcv = nt_dot(hot[:SO], hot[SO:SOR])
    with_off = nt_dot(hot[:SRC_G], hot[SRC_G:SO])
    rows = jnp.concatenate([with_off, with_rcv[:SRC_G], with_cmp[:SRC_G]], axis=1)
    return rows, with_cmp[SRC_G:], with_rcv[SRC_G:]


def count_kernel(
    index, kept, to_cmp_kept, to_rcv_kept, most, diag, hot_even, hot_odd, ids, to_cmp, to_rcv, *, first
):
    step = pl.program_id(0)
    even = first + 2 * step

    @pl.when(step == 0)
    def _():
        to_cmp[...] = jnp.zeros_like(to_cmp)
        to_rcv[...] = jnp.zeros_like(to_rcv)
        diag[...] = jnp.zeros_like(diag)
        most[...] = jnp.zeros_like(most)
        fill_ids(ids)
        fill_hot(index[even], ids, hot_even)

    def add(hot, place):
        rows, cmp_counts, rcv_counts = block_counts(hot)
        to_cmp[...] += cmp_counts
        to_rcv[...] += rcv_counts
        diag[...] += jnp.sum(rows, axis=0, keepdims=True)
        kept[place * SRC_G : (place + 1) * SRC_G] = kept_part(rows)
        most[...] = jnp.maximum(most[...], peak(rows))

    fill_hot(index[even + 1], ids, hot_odd)
    add(hot_even, 0)
    fill_hot(index[jnp.minimum(even + 2, N_SHOT - 1)], ids, hot_even)
    add(hot_odd, 1)

    @pl.when(step == COUNT_STEPS - 1)
    def _():
        to_cmp_kept[...] = (to_cmp[...].astype(jnp.int32) & (EXACT - 1)).astype(jnp.int8)
        to_rcv_kept[...] = (to_rcv[...].astype(jnp.int32) & (EXACT - 1)).astype(jnp.int8)
        most[...] = jnp.maximum(most[...], jnp.maximum(peak(to_cmp[...]), peak(to_rcv[...])))


def add_left_over(most_1, most_2, index, hot, ids, to_cmp, to_rcv, use_both, use_rows):
    top = jnp.maximum(jnp.max(most_1[...]), jnp.max(most_2[...]))

    @pl.when(top >= EXACT)
    def _():
        fill_ids(ids)
        for half in range(2):
            to_cmp[...] = jnp.zeros_like(to_cmp)
            to_rcv[...] = jnp.zeros_like(to_rcv)

            @pl.loop(half * HALF, (half + 1) * HALF)
            def _(block):
                fill_hot(index[block], ids, hot)
                rows, cmp_counts, rcv_counts = block_counts(hot)
                to_cmp[...] += cmp_counts
                to_rcv[...] += rcv_counts
                use_rows(block, left_over(rows))

            use_both(left_over(to_cmp[...]), left_over(to_rcv[...]))


def fetch_counts(refs, held, held_cmp, held_rcv, sems):
    *halves, cmp_1, cmp_2, rcv_1, rcv_2 = refs
    pieces = []
    for half, source in enumerate(halves):
        for chunk in range(CHUNKS // 2):
            start = chunk * CHUNK_ROWS
            place = held.at[half * (CHUNKS // 2) + chunk]
            pieces.append((source.at[start : start + CHUNK_ROWS], place))
    pieces += [(cmp_1, held_cmp.at[0]), (cmp_2, held_cmp.at[1])]
    pieces += [(rcv_1, held_rcv.at[0]), (rcv_2, held_rcv.at[1])]
    copies = [pltpu.make_async_copy(a, b, sems.at[k]) for k, (a, b) in enumerate(pieces)]
    for copy in copies:
        copy.start()
    return copies


def sum_halves(held):
    return (held[0].astype(F32) + held[1].astype(F32)).astype(BF16)


def load_halves(tab, rcv, own, shared):
    for tile in range(N_SHOT):
        own[:, tile * LANES : (tile + 1) * LANES] = split_rows(tab[at(tile)])
    shared[: 2 * SLICE, :LANES] = split_rows(tab[at(OFF_TILE)])
    for tile in range(RCV_TILES):
        shared[: 2 * SLICE, (1 + tile) * LANES : (2 + tile) * LANES] = split_rows(rcv[tile])
    for tile in range(CMP_TILE, LIVE_TILES):
        start = (tile - CMP_TILE) * LANES + OR
        shared[: 2 * SLICE, start : start + LANES] = split_rows(tab[at(tile)])


def normal_kernel(
    first, last, cmp_1, cmp_2, rcv_1, rcv_2, tab_in, rcv_in, diag_1, diag_2, most_1, most_2, index,
    tab, rcv, own_count, own, shared, to_shared, to_own,
    held, held_cmp, held_rcv, sems, hot, ids, exact_cmp, exact_rcv,
):
    counts = (first, last, cmp_1, cmp_2, rcv_1, rcv_2)
    copies = fetch_counts(counts, held, held_cmp, held_rcv, sems)
    top = 2 * SLICE
    load_halves(tab_in, rcv_in, own, shared)
    lanes = lax.broadcasted_iota(jnp.int32, (16, SHARED), 1)
    shared[top:] = jnp.where(lanes < LANES, 1.0, 0.0).astype(BF16)
    for chunk in range(CHUNKS):
        copies[chunk].wait()
        span = slice(chunk * CHUNK_ROWS, (chunk + 1) * CHUNK_ROWS)
        sums = jnp.dot(own[:, span], held[chunk], preferred_element_type=F32)
        to_shared[...] = sums if chunk == 0 else to_shared[...] + sums
        to_own[:, span] = nt_dot(shared[...], held[chunk])

    def others(to_cmp, to_rcv):
        cmp_sums = jnp.dot(shared[:top, :OR], to_cmp, preferred_element_type=F32)
        to_shared[:, OR:] += cmp_sums
        to_shared[:, :OR] += nt_dot(shared[:top, OR:], to_cmp)
        rcv_sums = jnp.dot(shared[:top, :LANES], to_rcv, preferred_element_type=F32)
        to_shared[:, LANES:OR] += rcv_sums
        to_shared[:, :LANES] += nt_dot(shared[:top, LANES:OR], to_rcv)

    def use_rows(block, rows):
        span = pl.ds(pl.multiple_of(block * SRC_G, SRC_G), SRC_G)
        to_shared[...] += jnp.dot(own[:, span], rows, preferred_element_type=F32)
        to_own[:, span] += nt_dot(shared[...], rows)

    for copy in copies[-4:]:
        copy.wait()
    others(sum_halves(held_cmp), sum_halves(held_rcv))
    add_left_over(most_1, most_2, index, hot, ids, exact_cmp, exact_rcv, others, use_rows)
    diag = diag_1[...] + diag_2[...]
    for tile in range(N_SHOT):
        span = slice(tile * LANES, (tile + 1) * LANES)
        count = to_own[top : top + 1, span]
        own_count[tile : tile + 1] = count
        tab[at(tile)] = join_rows(to_own[:top, span]) + count * tab_in[at(tile)]
    tab[at(OFF_TILE)] = join_rows(to_shared[:, :LANES]) + diag[:, :LANES] * tab_in[at(OFF_TILE)]
    for tile in range(RCV_TILES):
        span = slice((1 + tile) * LANES, (2 + tile) * LANES)
        rcv[tile] = join_rows(to_shared[:, span]) + diag[:, span] * rcv_in[tile]
    for tile in range(CMP_TILE, LIVE_TILES):
        start = (tile - CMP_TILE) * LANES + OR
        span = slice(start, start + LANES)
        tab[at(tile)] = join_rows(to_shared[:, span]) + diag[:, span] * tab_in[at(tile)]
    tab[LIVE_ROWS:] = jnp.zeros((TAB_ROWS - LIVE_ROWS, LANES), F32)


def all_sum(values):
    return jnp.sum(values, axis=tuple(range(values.ndim)), keepdims=True).reshape(1, 1)


def fold(values):
    total = values[:, :LANES]
    for start in range(LANES, values.shape[1], LANES):
        total = total + values[:, start : start + LANES]
    return total


def norm_kernel(
    first, last, cmp_1, cmp_2, rcv_1, rcv_2,
    tab_b, rcv_b, tab_y, rcv_y, diag_1, diag_2, most_1, most_2, index, own_count,
    out, tab_z, rcv_z, own, shared, to_shared,
    held, held_cmp, held_rcv, sems, hot, ids, exact_cmp, exact_rcv,
):
    counts = (first, last, cmp_1, cmp_2, rcv_1, rcv_2)
    copies = fetch_counts(counts, held, held_cmp, held_rcv, sems)
    shared_b = tab_b[:LIVE_ROWS]
    shared_y = tab_y[:LIVE_ROWS]
    shift = all_sum(shared_b * shared_y) / all_sum(shared_b * shared_b)
    shared_z = shared_y - shift * shared_b
    own_b = rcv_b[...]
    own_z = rcv_y[...] - shift * own_b
    tab_z[...] = shared_z
    rcv_z[...] = own_z
    load_halves(tab_z, rcv_z, own, shared)
    for chunk in range(CHUNKS):
        copies[chunk].wait()
        span = slice(chunk * CHUNK_ROWS, (chunk + 1) * CHUNK_ROWS)
        sums = jnp.dot(own[:, span], held[chunk], preferred_element_type=F32)
        to_shared[...] = sums if chunk == 0 else to_shared[...] + sums

    def whole(tabs, own):
        return all_sum(tabs) * (1.0 / N_RCV) + all_sum(own)

    def others(to_cmp, to_rcv):
        cmp_sums = jnp.dot(shared[:, :OR], to_cmp, preferred_element_type=F32)
        to_shared[:, OR:] += cmp_sums
        rcv_sums = jnp.dot(shared[:, :LANES], to_rcv, preferred_element_type=F32)
        to_shared[:, LANES:OR] += rcv_sums

    def use_rows(block, rows):
        span = pl.ds(pl.multiple_of(block * SRC_G, SRC_G), SRC_G)
        to_shared[...] += jnp.dot(own[:, span], rows, preferred_element_type=F32)

    for copy in copies[-4:]:
        copy.wait()
    others(sum_halves(held_cmp), sum_halves(held_rcv))
    add_left_over(most_1, most_2, index, hot, ids, exact_cmp, exact_rcv, others, use_rows)
    tiles = [tab_z[at(OFF_TILE)]] + [rcv_z[tile] for tile in range(RCV_TILES)]
    tiles += [tab_z[at(tile)] for tile in range(CMP_TILE, LIVE_TILES)]
    rest = jnp.concatenate(tiles, axis=1)
    diag = diag_1[...] + diag_2[...]
    total = fold(2.0 * rest * join_rows(to_shared[...]) + diag * rest * rest)
    for tile in range(N_SHOT):
        total = total + own_count[tile : tile + 1] * tab_z[at(tile)] * tab_z[at(tile)]
    sums = (
        whole(shared_b * shared_b, own_b * own_b),
        whole(shared_b * shared_z, own_b * own_z),
        whole(shared_z * shared_z, own_z * own_z),
        all_sum(total),
        shift,
    )
    lanes = lax.broadcasted_iota(jnp.int32, (1, LANES), 1)
    row = jnp.zeros((1, LANES), F32)
    for lane, value in enumerate(sums):
        row = jnp.where(lanes == lane, value, row)
    out[...] = row


def whole_spec(*shape):
    return pl.BlockSpec(shape, lambda c: (0,) * len(shape))


TAB = (TAB_ROWS, LANES)
RCV = (RCV_TILES, SLICE, LANES)
INDEX = (N_SHOT, INDEX_ROWS, LANES)
INDEX_SPEC = pl.BlockSpec((1, INDEX_ROWS, LANES), lambda c: (c, 0, 0))


def table_shapes():
    return [jax.ShapeDtypeStruct(TAB, F32), jax.ShapeDtypeStruct(RCV, F32)]


def hot_scratch():
    return [VMEM((ROWS, TR_DEV), FP8), VMEM((256, LANES), BF16)]


def adjoint_apply(data):
    return pl.pallas_call(
        adjoint_kernel,
        out_shape=table_shapes() + [jax.ShapeDtypeStruct(INDEX, jnp.int32)],
        scratch_shapes=[VMEM((4 * LANES, TR_DEV), BF16)] * 2 + [VMEM((256, LANES), BF16)],
        compiler_params=params(24),
        cost_estimate=cost(8),
        name="adjoint_apply",
    )(data)


COUNTS = (HALF * SRC_G, SHARED)
TO_CMP = (OR, SHARED - OR)
TO_RCV = (LANES, RCV_G)
IN_VMEM = pl.BlockSpec(memory_space=VMEM)


def count_call(index, first):
    rows = pl.BlockSpec((2 * SRC_G, SHARED), lambda c: (c, 0))
    small = [whole_spec(*TO_CMP), whole_spec(*TO_RCV), whole_spec(1, LANES), whole_spec(1, SHARED)]
    return pl.pallas_call(
        functools.partial(count_kernel, first=first),
        grid=(COUNT_STEPS,),
        in_specs=[whole_spec(*INDEX)],
        out_specs=[rows] + small,
        out_shape=[
            pltpu.HBM(COUNTS, BF16),
            pltpu.HBM(TO_CMP, jnp.int8),
            pltpu.HBM(TO_RCV, jnp.int8),
            jax.ShapeDtypeStruct((1, LANES), F32),
            jax.ShapeDtypeStruct((1, SHARED), F32),
        ],
        scratch_shapes=[VMEM((ROWS, TR_DEV), FP8)] * 2
        + [VMEM((256, LANES), BF16), VMEM(TO_CMP, F32), VMEM(TO_RCV, F32)],
        compiler_params=params(24),
        cost_estimate=cost(6),
        name="count_pairs",
    )(index)


def count_scratch(chunks):
    return (
        [
            VMEM((chunks, CHUNK_ROWS, SHARED), BF16),
            VMEM((2,) + TO_CMP, jnp.int8),
            VMEM((2,) + TO_RCV, jnp.int8),
            pltpu.SemaphoreType.DMA((chunks + 4,)),
        ]
        + hot_scratch()
        + [VMEM(TO_CMP, F32), VMEM(TO_RCV, F32)]
    )


def count_operands(counts):
    big = in_hbm(*[array for pair in zip(counts[0][:3], counts[1][:3]) for array in pair])
    (most_1, diag_1), (most_2, diag_2) = counts[0][3:5], counts[1][3:5]
    return big, [diag_1, diag_2, most_1, most_2]


def normal_apply(tab, rcv, index, counts):
    big, small = count_operands(counts)
    return pl.pallas_call(
        normal_kernel,
        in_specs=[ANYWHERE] * 6 + [IN_VMEM] * 7,
        out_shape=table_shapes() + [jax.ShapeDtypeStruct((N_SHOT, LANES), F32)],
        scratch_shapes=[
            VMEM((2 * SLICE, N_SHOT * SRC_G), BF16),
            VMEM((2 * SLICE + 16, SHARED), BF16),
            VMEM((2 * SLICE, SHARED), F32),
            VMEM((2 * SLICE + 16, N_SHOT * SRC_G), F32),
        ]
        + count_scratch(CHUNKS),
        compiler_params=params(24),
        cost_estimate=cost(3),
        name="normal_apply",
    )(*big, tab, rcv, *small, index)


def norm_sums(tab_b, rcv_b, tab_y, rcv_y, own_count, index, counts):
    big, small = count_operands(counts)
    return pl.pallas_call(
        norm_kernel,
        in_specs=[ANYWHERE] * 6 + [IN_VMEM] * 10,
        out_shape=jax.ShapeDtypeStruct((1, LANES), F32),
        scratch_shapes=[
            VMEM((LIVE_ROWS, LANES), F32),
            VMEM(RCV, F32),
            VMEM((2 * SLICE, N_SHOT * SRC_G), BF16),
            VMEM((2 * SLICE, SHARED), BF16),
            VMEM((2 * SLICE, SHARED), F32),
        ]
        + count_scratch(CHUNKS),
        compiler_params=params(24),
        cost_estimate=cost(2),
        name="norm_sums",
    )(*big, tab_b, rcv_b, tab_y, rcv_y, *small, index, own_count)


def spread_kernel(parts, out):
    total = parts[0]
    for source in range(1, N_RCV):
        total = total + parts[source]
    for dest in range(N_RCV):
        out[dest] = total


def exchange(array, axis):
    return lax.all_to_all(array, axis, split_axis=0, concat_axis=0, tiled=True)


def spread_shares(arrived):
    shape = (N_RCV, SHARE, LANES)
    spread = pl.pallas_call(
        spread_kernel,
        out_shape=jax.ShapeDtypeStruct(shape, F32),
        compiler_params=params(24),
        cost_estimate=cost(1),
        name="sum_shares",
    )(arrived.reshape(shape))
    return spread.reshape(TAB)


def pack_kernel(tab, rcv, *refs, first):
    out, rows, sems = refs[-3:]
    lanes = lax.broadcasted_iota(jnp.int32, (SLICE, LANES), 1)
    half = SLICE // 2
    copies = []
    for dest in range(N_SHOT):
        rows[dest, :SLICE] = tab[at(dest)]
        rows[dest, SLICE : 2 * SLICE] = tab[at(OFF_TILE)]
        cmp_first = dest * CMP_G
        rcv_first = dest * (RCV_G // N_SHOT)
        bins = tab[at(CMP_TILE + cmp_first // LANES)]
        cmp_part = pltpu.roll(bins, (-cmp_first) % LANES, 1)
        rcv_part = pltpu.roll(rcv[rcv_first // LANES], (CMP_G - rcv_first) % LANES, 1)
        both = jnp.where(lanes < CMP_G, cmp_part, rcv_part)
        moved = pltpu.roll(both[half:], LANES // 2, 1)
        rows[dest, 2 * SLICE :] = jnp.where(lanes[:half] < LANES // 2, both[:half], moved)
        if dest % PACK == PACK - 1:
            group = dest // PACK
            span = slice(group * PACK, (group + 1) * PACK)
            place = out.at[span, first : first + OWN_ROWS]
            copies.append(pltpu.make_async_copy(rows.at[span], place, sems.at[group]))
            copies[-1].start()
    for copy in copies:
        copy.wait()


def pack_owned(tab, rcv, former=None):
    given = [] if former is None else in_hbm(former)
    return pl.pallas_call(
        functools.partial(pack_kernel, first=OWN_ROWS * len(given)),
        in_specs=[pl.BlockSpec(memory_space=VMEM)] * 2 + [ANYWHERE] * len(given),
        out_specs=ANYWHERE,
        out_shape=pltpu.HBM((N_SHOT, 2 * OWN_ROWS, LANES), F32),
        scratch_shapes=[
            VMEM((N_SHOT, OWN_ROWS, LANES), F32),
            pltpu.SemaphoreType.DMA((N_SHOT // PACK,)),
        ],
        input_output_aliases={2: 0} if given else {},
        compiler_params=params(24),
        cost_estimate=cost(1),
        name="pack_owned",
    )(tab, rcv, *given)


def swapped(value, axis, size, bit):
    return lax.ppermute(value, axis, [(s, s ^ bit) for s in range(size)])


def sum_over_rcv(sums):
    for bit in (1, 2, 6):
        sums = sums + swapped(sums, "rcv", N_RCV, bit)
    return sums


def finish_kernel(sums, owned, source, receiver, offset, cmp):
    rows = sums[...].reshape(N_SHOT, LANES)
    norm_b, cross, norm_z, norm_az, shift = (rows[:, lane : lane + 1] for lane in range(5))
    shift = shift * (1.0 / N_RCV)

    def total(values):
        return jnp.sum(values, axis=0, keepdims=True)

    total_b = total(norm_b)
    first = total(cross + shift * norm_b) / total_b
    off = shift - first
    zz = total(norm_z + 2.0 * off * cross + off * off * norm_b)
    zaz = total(
        norm_az
        + 2.0 * off * (norm_z + shift * cross)
        + off * off * (cross + shift * norm_b)
    )
    second = zaz / zz
    det = first * second - zz / total_b
    scale_b = (first + second) / det
    scale_y = 1.0 / det

    def combine(sender, start, stop):
        part_y = owned[sender, OWN_ROWS + start : OWN_ROWS + stop]
        return scale_b * owned[sender, start:stop] - scale_y * part_y

    def spread_halves(tile):
        return jnp.concatenate([tile, pltpu.roll(tile, LANES // 2, 1)], axis=0)

    per_tile = LANES // SLICE
    for group in range(N_SHOT // per_tile):
        span = slice(group * LANES, (group + 1) * LANES)
        senders = range(group * per_tile, (group + 1) * per_tile)
        source[:, span] = jnp.concatenate([combine(i, 0, SLICE) for i in senders], axis=0).T
        offset[:, span] = jnp.concatenate(
            [combine(i, SLICE, 2 * SLICE) for i in senders], axis=0
        ).T
        rest = jnp.concatenate(
            [spread_halves(combine(i, 2 * SLICE, OWN_ROWS)) for i in senders], axis=0
        ).T
        cmp[:, span] = rest[:CMP_G]
        receiver[0, :, span] = rest[CMP_G : CMP_G + RCV_G // N_SHOT]


def finish(sums, owned):
    return pl.pallas_call(
        finish_kernel,
        out_shape=[
            jax.ShapeDtypeStruct((SRC_G, FREQS), F32),
            jax.ShapeDtypeStruct((1, RCV_G // N_SHOT, FREQS), F32),
            jax.ShapeDtypeStruct((128, FREQS), F32),
            jax.ShapeDtypeStruct((CMP_G, FREQS), F32),
        ],
        compiler_params=params(),
        name="finish",
    )(sums, owned)


def per_device(basis, traces, src_index, rcv_index, off_index, send_rows, send_counts, recv_bins):
    data = log_spectra(
        traces, basis, send_rows[0], send_counts, recv_bins[0], src_index, rcv_index, off_index
    )
    data = exchange(data, "shot")

    tab_b, rcv_b, index = adjoint_apply(data)
    arrived = exchange(tab_b, "rcv")
    counts_1 = count_call(index, 0)
    arrived, index, counts_1 = lax.optimization_barrier((arrived, index, counts_1))
    spread = spread_shares(arrived)
    spread, index = lax.optimization_barrier((spread, index))
    tab_b = exchange(spread, "rcv")
    counts = (counts_1, count_call(index, HALF))

    tab_y, rcv_y, own_count = normal_apply(tab_b, rcv_b, index, counts)
    arrived = exchange(tab_y, "rcv")
    packed = pack_owned(tab_b, rcv_b)
    arrived, packed = lax.optimization_barrier((arrived, packed))
    tab_y = exchange(spread_shares(arrived), "rcv")
    packed = pack_owned(tab_y, rcv_y, packed)
    tab_y, packed = lax.optimization_barrier((tab_y, packed))
    owned = exchange(packed, "shot")
    sums = sum_over_rcv(norm_sums(tab_b, rcv_b, tab_y, rcv_y, own_count, index, counts))
    owned, sums = lax.optimization_barrier((owned, sums))
    sums = exchange(jnp.broadcast_to(sums[None], (N_SHOT, 1, LANES)), "shot")
    return tuple(finish(sums, owned))


def solution(mesh):
    basis = fourier_rows()
    mapped = jax.shard_map(
        per_device,
        mesh=mesh,
        in_specs=(
            P(),
            P(("shot", "rcv"), None),
            P(("shot", "rcv")),
            P(("shot", "rcv")),
            P(("shot", "rcv")),
            P(("shot", "rcv"), None, None),
            P(("shot", "rcv"), None),
            P(("shot", "rcv"), None, None),
        ),
        out_specs=(P("shot", None), P("rcv", "shot", None), P(), P("shot", None)),
        check_vma=False,
    )

    def run(*args):
        return mapped(jnp.asarray(basis), *args)

    return run
```

```python
import functools

import ml_dtypes
import numpy as np

import jax
import jax.numpy as jnp
from jax import lax
from jax.experimental import pallas as pl
from jax.experimental.pallas import tpu as pltpu
from jax.sharding import PartitionSpec as P

SAMPLES = 1024
FREQS = 512
TR_DEV = 640
N_SHOT = 16
N_RCV = 8
DEVICES = 128
CAP = 80
SRC_G = 128
RCV_G = 256
CMP_G = 32
SLICE = FREQS // N_SHOT
LANES = 128
OFF_TILE = 16
CMP_TILE = 17
LIVE_TILES = 21
LIVE_ROWS = LIVE_TILES * SLICE
SHARE = -(-LIVE_ROWS // (8 * N_RCV)) * 8
TAB_ROWS = N_RCV * SHARE
RCV_TILES = 2
ROWS = SRC_G + RCV_G + 128 + 512
SHARED = ROWS - SRC_G
SO = 2 * LANES
SOR = SO + RCV_G
OR = LANES + RCV_G
HALF = N_SHOT // 2
COUNT_STEPS = HALF // 2
CHUNKS = 4
CHUNK_ROWS = N_SHOT * SRC_G // CHUNKS
TRACE_TILES = TR_DEV // LANES
BINS_AT = TRACE_TILES * SLICE
INDEX_AT = BINS_AT + N_SHOT
INDEX_ROWS = 24
DATA_ROWS = INDEX_AT + INDEX_ROWS
STEPS = 2
OWN_ROWS = 2 * SLICE + SLICE // 2
PACK = LANES // CMP_G

VMEM = pltpu.VMEM
F32 = jnp.float32
BF16 = jnp.bfloat16
FP8 = jnp.float8_e4m3fn


def fourier_rows():
    phase = np.arange(FREQS)[:, None] * np.arange(SAMPLES)[None, :] % SAMPLES
    angle = phase * (2.0 * np.pi / SAMPLES)
    waves = np.stack([np.cos(angle), np.sin(angle)]).reshape(2, STEPS, -1, SAMPLES)
    table = waves.transpose(1, 0, 2, 3).reshape(2 * FREQS, SAMPLES) / np.sqrt(SAMPLES)
    return table.astype(np.float32).astype(ml_dtypes.bfloat16)


def params(mib=48):
    return pltpu.CompilerParams(vmem_limit_bytes=mib * 2**20)


def cost(micros):
    return pl.CostEstimate(flops=int(micros * 1e9), bytes_accessed=int(micros * 3e6), transcendentals=0)


ANYWHERE = pl.BlockSpec(memory_space=pltpu.HBM)


def in_hbm(*arrays):
    return [pltpu.with_memory_space_constraint(array, pltpu.HBM) for array in arrays]


def nt_dot(left, right):
    return lax.dot_general(left, right, (((1,), (1,)), ((), ())), preferred_element_type=F32)


def split_rows(values):
    high = values.astype(BF16)
    low = (values - high.astype(F32)).astype(BF16)
    return jnp.concatenate([high, low], axis=0)


def at(tile):
    if isinstance(tile, int):
        return slice(tile * SLICE, (tile + 1) * SLICE)
    return pl.ds(pl.multiple_of(tile * SLICE, SLICE), SLICE)


def join_rows(both):
    half = both.shape[0] // 2
    return both[:half] + both[half:]


def flip(table):
    wide = jnp.concatenate(
        [table.astype(F32), jnp.zeros((N_SHOT, LANES - CAP), F32)], axis=1
    )
    return wide.T[:CAP].astype(jnp.int32)


def index_tiles(send_rows, send_counts, src, rcv, off):
    slots = lax.broadcasted_iota(jnp.int32, (CAP, N_SHOT), 0)
    targets = jnp.where(slots < send_counts[...], flip(send_rows[...]), -1)
    trace_ids = lax.broadcasted_iota(jnp.int32, (CAP, TR_DEV), 1)
    places = lax.broadcasted_iota(jnp.int32, (CAP, TR_DEV), 0)
    total = jnp.zeros((CAP, TR_DEV), jnp.int32)
    for owner in range(N_SHOT):
        hit = targets[:, owner : owner + 1] == trace_ids
        total = total + jnp.where(hit, places + owner * LANES, 0)
    slot_row = jnp.sum(total, axis=0, keepdims=True)
    rows = [src[...] & (SRC_G - 1), rcv[...] & (RCV_G - 1), off[...]]
    rows = [row.reshape(1, TR_DEV) for row in rows] + [slot_row]
    table = jnp.concatenate(rows, axis=0).astype(F32)
    tiles = [table[:, q * LANES : (q + 1) * LANES] for q in range(TRACE_TILES)]
    tiles.append(jnp.zeros((INDEX_ROWS - 4 * TRACE_TILES, LANES), F32))
    return jnp.concatenate(tiles, axis=0)


def spectra_kernel(traces, waves, *refs):
    given, out, own, basis, extra = refs[:6], refs[6], refs[7], refs[8], refs[9]
    small, sems, small_sems = refs[10:16], refs[16], refs[17]
    indices = [
        pltpu.make_async_copy(a, b, small_sems.at[k]) for k, (a, b) in enumerate(zip(given, small))
    ]
    for copy in indices:
        copy.start()
    pieces = []
    for k in range(TRACE_TILES):
        span = slice(k * LANES, (k + 1) * LANES)
        pieces.append((traces.at[span], own.at[span]))
    size = 2 * FREQS // STEPS // 2
    for k in range(2 * STEPS):
        span = slice(k * size, (k + 1) * size)
        pieces.append((waves.at[span], basis.at[span]))
    copies = [pltpu.make_async_copy(a, b, sems.at[k]) for k, (a, b) in enumerate(pieces)]
    early = TRACE_TILES + 2
    for copy in copies[:early]:
        copy.start()
    for copy in indices:
        copy.wait()
    send_rows, send_counts, bins, src, rcv, off = small
    pad = jnp.zeros((N_SHOT, LANES - CAP), F32)
    extra[:N_SHOT] = jnp.concatenate([bins[...].astype(F32), pad], axis=1)
    extra[N_SHOT:] = index_tiles(send_rows, send_counts, src, rcv, off)
    for part in range(N_SHOT):
        out[part, BINS_AT:, :] = extra[...]
    for copy in copies[:early]:
        copy.wait()
    for copy in copies[early:]:
        copy.start()
    half = FREQS // STEPS
    for step in range(STEPS):
        if step == 1:
            for copy in copies[early:]:
                copy.wait()
        parts = nt_dot(basis[2 * half * step : 2 * half * (step + 1)], own[...])
        logs = jnp.log1p(parts[:half] * parts[:half] + parts[half:] * parts[half:])
        for part in range(half // SLICE):
            for q in range(TRACE_TILES):
                out[step * (half // SLICE) + part, q * SLICE : (q + 1) * SLICE, :] = logs[
                    part * SLICE : (part + 1) * SLICE, q * LANES : (q + 1) * LANES
                ]


def log_spectra(traces, basis, *small):
    return pl.pallas_call(
        spectra_kernel,
        in_specs=[ANYWHERE] * (2 + len(small)),
        out_shape=jax.ShapeDtypeStruct((N_SHOT, DATA_ROWS, LANES), F32),
        scratch_shapes=[
            VMEM((TR_DEV, SAMPLES), BF16),
            VMEM((2 * FREQS, SAMPLES), BF16),
            VMEM((DATA_ROWS - BINS_AT, LANES), F32),
        ]
        + [VMEM(array.shape, jnp.int32) for array in small]
        + [
            pltpu.SemaphoreType.DMA((TRACE_TILES + 2 * STEPS,)),
            pltpu.SemaphoreType.DMA((len(small),)),
        ],
        compiler_params=params(24),
        cost_estimate=cost(5),
        name="spectra",
    )(*in_hbm(traces, basis, *small))


def fill_ids(ids):
    ids[...] = lax.broadcasted_iota(jnp.int32, ids.shape, 0).astype(F32).astype(BF16)


def fill_hot(tiles, ids, hot):
    one = jnp.ones((1, 1), BF16)
    zero = jnp.zeros((1, 1), BF16)
    values = tiles.astype(F32)
    for q in range(TRACE_TILES):
        span = slice(q * LANES, (q + 1) * LANES)
        first = 0
        for row, size, base in ((0, SRC_G, 0), (2, 128, 0), (1, RCV_G, 0), (3, 256, 0), (3, 256, 256)):
            wanted = (values[4 * q + row : 4 * q + row + 1] - base).astype(BF16)
            hits = jnp.where(ids[:size] == wanted, one, zero)
            hot[first : first + size, span] = hits.astype(hot.dtype)
            first += size


def resolve_bins(data, block):
    tiles = data[block, INDEX_AT:].astype(jnp.int32)
    rows = [data[owner, pl.ds(BINS_AT + block, 1)] for owner in range(N_SHOT)]
    table = jnp.concatenate(rows, axis=0)
    owners = lax.broadcasted_iota(jnp.int32, (N_SHOT, LANES), 0)
    resolved = []
    for q in range(TRACE_TILES):
        slot = tiles[4 * q + 3 : 4 * q + 4]
        place = jnp.broadcast_to(slot & (LANES - 1), (N_SHOT, LANES))
        found = jnp.take_along_axis(table, place, axis=1, mode="promise_in_bounds")
        found = jnp.where(owners == slot >> 7, found.astype(jnp.int32) + owners * CMP_G, 0)
        resolved += [tiles[4 * q : 4 * q + 3], jnp.sum(found, axis=0, keepdims=True)]
    resolved.append(jnp.zeros((INDEX_ROWS - 4 * TRACE_TILES, LANES), jnp.int32))
    return jnp.concatenate(resolved, axis=0)


def prepare_block(data, index, ids, hot, block):
    tiles = resolve_bins(data, block)
    index[block] = tiles
    one = jnp.ones((1, 1), BF16)
    zero = jnp.zeros((1, 1), BF16)
    for q in range(TRACE_TILES):
        for place, row in enumerate((0, 2, 1, 3)):
            lane = tiles[4 * q + row : 4 * q + row + 1] & (LANES - 1)
            hit = ids[:LANES] == lane.astype(F32).astype(BF16)
            span = slice(q * LANES, (q + 1) * LANES)
            hot[place * LANES : (place + 1) * LANES, span] = jnp.where(hit, one, zero)


def add_block(data, index, hot, tab, rcv, block):
    tiles = index[block]
    values = [data[block, q * SLICE : (q + 1) * SLICE] for q in range(TRACE_TILES)]

    both = split_rows(jnp.concatenate(values, axis=1))
    zero = jnp.zeros((1, 1), BF16)

    def of_tiles(row, count):
        place = [tiles[4 * q + row : 4 * q + row + 1] >> 7 for q in range(TRACE_TILES)]
        place = jnp.concatenate(place, axis=1).astype(F32).astype(BF16)
        return jnp.concatenate([jnp.where(place == tile, both, zero) for tile in range(count)], axis=0)

    plain = nt_dot(both, hot[: 2 * LANES])
    tab[at(block)] = join_rows(plain[:, :LANES])
    tab[at(OFF_TILE)] += join_rows(plain[:, LANES:])
    parts = of_tiles(1, RCV_TILES)
    sums = nt_dot(parts, hot[2 * LANES : 3 * LANES])
    for tile in range(RCV_TILES):
        rcv[tile] += join_rows(sums[tile * 2 * SLICE : (tile + 1) * 2 * SLICE])
    cmp_tiles = LIVE_TILES - CMP_TILE
    parts = of_tiles(3, cmp_tiles)
    sums = nt_dot(parts, hot[3 * LANES :])
    for tile in range(cmp_tiles):
        tab[at(CMP_TILE + tile)] += join_rows(sums[tile * 2 * SLICE : (tile + 1) * 2 * SLICE])


def adjoint_kernel(data, tab, rcv, index, hot_even, hot_odd, ids):
    tab[OFF_TILE * SLICE :] = jnp.zeros((TAB_ROWS - OFF_TILE * SLICE, LANES), F32)
    rcv[...] = jnp.zeros((RCV_TILES, SLICE, LANES), F32)
    fill_ids(ids)
    prepare_block(data, index, ids, hot_even, 0)

    @pl.loop(0, N_SHOT // 2)
    def _(pair):
        even = 2 * pair
        prepare_block(data, index, ids, hot_odd, even + 1)
        add_block(data, index, hot_even, tab, rcv, even)
        prepare_block(data, index, ids, hot_even, jnp.minimum(even + 2, N_SHOT - 1))
        add_block(data, index, hot_odd, tab, rcv, even + 1)


EXACT = 128


def kept_part(counts):
    return (counts.astype(jnp.int32) & (EXACT - 1)).astype(F32).astype(BF16)


def left_over(counts):
    whole = counts.astype(jnp.int32)
    return (whole - (whole & (EXACT - 1))).astype(F32).astype(BF16)


def peak(counts):
    top = jnp.max(counts, axis=0, keepdims=True)
    best = top[:, :LANES]
    for start in range(LANES, counts.shape[1], LANES):
        best = jnp.maximum(best, top[:, start : start + LANES])
    return best


def block_counts(hot):
    with_cmp = nt_dot(hot[:SOR], hot[SOR:])
    with_rcv = nt_dot(hot[:SO], hot[SO:SOR])
    with_off = nt_dot(hot[:SRC_G], hot[SRC_G:SO])
    rows = jnp.concatenate([with_off, with_rcv[:SRC_G], with_cmp[:SRC_G]], axis=1)
    return rows, with_cmp[SRC_G:], with_rcv[SRC_G:]


def count_kernel(
    index, kept, to_cmp_kept, to_rcv_kept, most, diag, hot_even, hot_odd, ids, to_cmp, to_rcv, *, first
):
    step = pl.program_id(0)
    even = first + 2 * step

    @pl.when(step == 0)
    def _():
        to_cmp[...] = jnp.zeros_like(to_cmp)
        to_rcv[...] = jnp.zeros_like(to_rcv)
        diag[...] = jnp.zeros_like(diag)
        most[...] = jnp.zeros_like(most)
        fill_ids(ids)
        fill_hot(index[even], ids, hot_even)

    def add(hot, place):
        rows, cmp_counts, rcv_counts = block_counts(hot)
        to_cmp[...] += cmp_counts
        to_rcv[...] += rcv_counts
        diag[...] += jnp.sum(rows, axis=0, keepdims=True)
        kept[place * SRC_G : (place + 1) * SRC_G] = kept_part(rows)
        most[...] = jnp.maximum(most[...], peak(rows))

    fill_hot(index[even + 1], ids, hot_odd)
    add(hot_even, 0)
    fill_hot(index[jnp.minimum(even + 2, N_SHOT - 1)], ids, hot_even)
    add(hot_odd, 1)

    @pl.when(step == COUNT_STEPS - 1)
    def _():
        to_cmp_kept[...] = (to_cmp[...].astype(jnp.int32) & (EXACT - 1)).astype(jnp.int8)
        to_rcv_kept[...] = (to_rcv[...].astype(jnp.int32) & (EXACT - 1)).astype(jnp.int8)
        most[...] = jnp.maximum(most[...], jnp.maximum(peak(to_cmp[...]), peak(to_rcv[...])))


def add_left_over(most_1, most_2, index, hot, ids, to_cmp, to_rcv, use_both, use_rows):
    top = jnp.maximum(jnp.max(most_1[...]), jnp.max(most_2[...]))

    @pl.when(top >= EXACT)
    def _():
        fill_ids(ids)
        for half in range(2):
            to_cmp[...] = jnp.zeros_like(to_cmp)
            to_rcv[...] = jnp.zeros_like(to_rcv)

            @pl.loop(half * HALF, (half + 1) * HALF)
            def _(block):
                fill_hot(index[block], ids, hot)
                rows, cmp_counts, rcv_counts = block_counts(hot)
                to_cmp[...] += cmp_counts
                to_rcv[...] += rcv_counts
                use_rows(block, left_over(rows))

            use_both(left_over(to_cmp[...]), left_over(to_rcv[...]))


def fetch_counts(refs, held, held_cmp, held_rcv, sems):
    *halves, cmp_1, cmp_2, rcv_1, rcv_2 = refs
    pieces = []
    for half, source in enumerate(halves):
        for chunk in range(CHUNKS // 2):
            start = chunk * CHUNK_ROWS
            place = held.at[half * (CHUNKS // 2) + chunk]
            pieces.append((source.at[start : start + CHUNK_ROWS], place))
    pieces += [(cmp_1, held_cmp.at[0]), (cmp_2, held_cmp.at[1])]
    pieces += [(rcv_1, held_rcv.at[0]), (rcv_2, held_rcv.at[1])]
    copies = [pltpu.make_async_copy(a, b, sems.at[k]) for k, (a, b) in enumerate(pieces)]
    for copy in copies:
        copy.start()
    return copies


def sum_halves(held):
    return (held[0].astype(F32) + held[1].astype(F32)).astype(BF16)


def load_halves(tab, rcv, own, shared):
    for tile in range(N_SHOT):
        own[:, tile * LANES : (tile + 1) * LANES] = split_rows(tab[at(tile)])
    shared[: 2 * SLICE, :LANES] = split_rows(tab[at(OFF_TILE)])
    for tile in range(RCV_TILES):
        shared[: 2 * SLICE, (1 + tile) * LANES : (2 + tile) * LANES] = split_rows(rcv[tile])
    for tile in range(CMP_TILE, LIVE_TILES):
        start = (tile - CMP_TILE) * LANES + OR
        shared[: 2 * SLICE, start : start + LANES] = split_rows(tab[at(tile)])


def normal_kernel(
    first, last, cmp_1, cmp_2, rcv_1, rcv_2, tab_in, rcv_in, diag_1, diag_2, most_1, most_2, index,
    tab, rcv, own_count, own, shared, to_shared, to_own,
    held, held_cmp, held_rcv, sems, hot, ids, exact_cmp, exact_rcv,
):
    counts = (first, last, cmp_1, cmp_2, rcv_1, rcv_2)
    copies = fetch_counts(counts, held, held_cmp, held_rcv, sems)
    top = 2 * SLICE
    load_halves(tab_in, rcv_in, own, shared)
    lanes = lax.broadcasted_iota(jnp.int32, (16, SHARED), 1)
    shared[top:] = jnp.where(lanes < LANES, 1.0, 0.0).astype(BF16)
    for chunk in range(CHUNKS):
        copies[chunk].wait()
        span = slice(chunk * CHUNK_ROWS, (chunk + 1) * CHUNK_ROWS)
        sums = jnp.dot(own[:, span], held[chunk], preferred_element_type=F32)
        to_shared[...] = sums if chunk == 0 else to_shared[...] + sums
        to_own[:, span] = nt_dot(shared[...], held[chunk])

    def others(to_cmp, to_rcv):
        cmp_sums = jnp.dot(shared[:top, :OR], to_cmp, preferred_element_type=F32)
        to_shared[:, OR:] += cmp_sums
        to_shared[:, :OR] += nt_dot(shared[:top, OR:], to_cmp)
        rcv_sums = jnp.dot(shared[:top, :LANES], to_rcv, preferred_element_type=F32)
        to_shared[:, LANES:OR] += rcv_sums
        to_shared[:, :LANES] += nt_dot(shared[:top, LANES:OR], to_rcv)

    def use_rows(block, rows):
        span = pl.ds(pl.multiple_of(block * SRC_G, SRC_G), SRC_G)
        to_shared[...] += jnp.dot(own[:, span], rows, preferred_element_type=F32)
        to_own[:, span] += nt_dot(shared[...], rows)

    for copy in copies[-4:]:
        copy.wait()
    others(sum_halves(held_cmp), sum_halves(held_rcv))
    add_left_over(most_1, most_2, index, hot, ids, exact_cmp, exact_rcv, others, use_rows)
    diag = diag_1[...] + diag_2[...]
    for tile in range(N_SHOT):
        span = slice(tile * LANES, (tile + 1) * LANES)
        count = to_own[top : top + 1, span]
        own_count[tile : tile + 1] = count
        tab[at(tile)] = join_rows(to_own[:top, span]) + count * tab_in[at(tile)]
    tab[at(OFF_TILE)] = join_rows(to_shared[:, :LANES]) + diag[:, :LANES] * tab_in[at(OFF_TILE)]
    for tile in range(RCV_TILES):
        span = slice((1 + tile) * LANES, (2 + tile) * LANES)
        rcv[tile] = join_rows(to_shared[:, span]) + diag[:, span] * rcv_in[tile]
    for tile in range(CMP_TILE, LIVE_TILES):
        start = (tile - CMP_TILE) * LANES + OR
        span = slice(start, start + LANES)
        tab[at(tile)] = join_rows(to_shared[:, span]) + diag[:, span] * tab_in[at(tile)]
    tab[LIVE_ROWS:] = jnp.zeros((TAB_ROWS - LIVE_ROWS, LANES), F32)


def all_sum(values):
    return jnp.sum(values, axis=tuple(range(values.ndim)), keepdims=True).reshape(1, 1)


def fold(values):
    total = values[:, :LANES]
    for start in range(LANES, values.shape[1], LANES):
        total = total + values[:, start : start + LANES]
    return total


def norm_kernel(
    first, last, cmp_1, cmp_2, rcv_1, rcv_2,
    tab_b, rcv_b, tab_y, rcv_y, diag_1, diag_2, most_1, most_2, index, own_count,
    out, tab_z, rcv_z, own, shared, to_shared,
    held, held_cmp, held_rcv, sems, hot, ids, exact_cmp, exact_rcv,
):
    counts = (first, last, cmp_1, cmp_2, rcv_1, rcv_2)
    copies = fetch_counts(counts, held, held_cmp, held_rcv, sems)
    shared_b = tab_b[:LIVE_ROWS]
    shared_y = tab_y[:LIVE_ROWS]
    shift = all_sum(shared_b * shared_y) / all_sum(shared_b * shared_b)
    shared_z = shared_y - shift * shared_b
    own_b = rcv_b[...]
    own_z = rcv_y[...] - shift * own_b
    tab_z[...] = shared_z
    rcv_z[...] = own_z
    load_halves(tab_z, rcv_z, own, shared)
    for chunk in range(CHUNKS):
        copies[chunk].wait()
        span = slice(chunk * CHUNK_ROWS, (chunk + 1) * CHUNK_ROWS)
        sums = jnp.dot(own[:, span], held[chunk], preferred_element_type=F32)
        to_shared[...] = sums if chunk == 0 else to_shared[...] + sums

    def whole(tabs, own):
        return all_sum(tabs) * (1.0 / N_RCV) + all_sum(own)

    def others(to_cmp, to_rcv):
        cmp_sums = jnp.dot(shared[:, :OR], to_cmp, preferred_element_type=F32)
        to_shared[:, OR:] += cmp_sums
        rcv_sums = jnp.dot(shared[:, :LANES], to_rcv, preferred_element_type=F32)
        to_shared[:, LANES:OR] += rcv_sums

    def use_rows(block, rows):
        span = pl.ds(pl.multiple_of(block * SRC_G, SRC_G), SRC_G)
        to_shared[...] += jnp.dot(own[:, span], rows, preferred_element_type=F32)

    for copy in copies[-4:]:
        copy.wait()
    others(sum_halves(held_cmp), sum_halves(held_rcv))
    add_left_over(most_1, most_2, index, hot, ids, exact_cmp, exact_rcv, others, use_rows)
    tiles = [tab_z[at(OFF_TILE)]] + [rcv_z[tile] for tile in range(RCV_TILES)]
    tiles += [tab_z[at(tile)] for tile in range(CMP_TILE, LIVE_TILES)]
    rest = jnp.concatenate(tiles, axis=1)
    diag = diag_1[...] + diag_2[...]
    total = fold(2.0 * rest * join_rows(to_shared[...]) + diag * rest * rest)
    for tile in range(N_SHOT):
        total = total + own_count[tile : tile + 1] * tab_z[at(tile)] * tab_z[at(tile)]
    sums = (
        whole(shared_b * shared_b, own_b * own_b),
        whole(shared_b * shared_z, own_b * own_z),
        whole(shared_z * shared_z, own_z * own_z),
        all_sum(total),
        shift,
    )
    lanes = lax.broadcasted_iota(jnp.int32, (1, LANES), 1)
    row = jnp.zeros((1, LANES), F32)
    for lane, value in enumerate(sums):
        row = jnp.where(lanes == lane, value, row)
    out[...] = row


def whole_spec(*shape):
    return pl.BlockSpec(shape, lambda c: (0,) * len(shape))


TAB = (TAB_ROWS, LANES)
RCV = (RCV_TILES, SLICE, LANES)
INDEX = (N_SHOT, INDEX_ROWS, LANES)
INDEX_SPEC = pl.BlockSpec((1, INDEX_ROWS, LANES), lambda c: (c, 0, 0))


def table_shapes():
    return [jax.ShapeDtypeStruct(TAB, F32), jax.ShapeDtypeStruct(RCV, F32)]


def hot_scratch():
    return [VMEM((ROWS, TR_DEV), FP8), VMEM((256, LANES), BF16)]


def adjoint_apply(data):
    return pl.pallas_call(
        adjoint_kernel,
        out_shape=table_shapes() + [jax.ShapeDtypeStruct(INDEX, jnp.int32)],
        scratch_shapes=[VMEM((4 * LANES, TR_DEV), BF16)] * 2 + [VMEM((256, LANES), BF16)],
        compiler_params=params(24),
        cost_estimate=cost(8),
        name="adjoint_apply",
    )(data)


COUNTS = (HALF * SRC_G, SHARED)
TO_CMP = (OR, SHARED - OR)
TO_RCV = (LANES, RCV_G)
IN_VMEM = pl.BlockSpec(memory_space=VMEM)


def count_call(index, first):
    rows = pl.BlockSpec((2 * SRC_G, SHARED), lambda c: (c, 0))
    small = [whole_spec(*TO_CMP), whole_spec(*TO_RCV), whole_spec(1, LANES), whole_spec(1, SHARED)]
    return pl.pallas_call(
        functools.partial(count_kernel, first=first),
        grid=(COUNT_STEPS,),
        in_specs=[whole_spec(*INDEX)],
        out_specs=[rows] + small,
        out_shape=[
            pltpu.HBM(COUNTS, BF16),
            pltpu.HBM(TO_CMP, jnp.int8),
            pltpu.HBM(TO_RCV, jnp.int8),
            jax.ShapeDtypeStruct((1, LANES), F32),
            jax.ShapeDtypeStruct((1, SHARED), F32),
        ],
        scratch_shapes=[VMEM((ROWS, TR_DEV), FP8)] * 2
        + [VMEM((256, LANES), BF16), VMEM(TO_CMP, F32), VMEM(TO_RCV, F32)],
        compiler_params=params(24),
        cost_estimate=cost(6),
        name="count_pairs",
    )(index)


def count_scratch(chunks):
    return (
        [
            VMEM((chunks, CHUNK_ROWS, SHARED), BF16),
            VMEM((2,) + TO_CMP, jnp.int8),
            VMEM((2,) + TO_RCV, jnp.int8),
            pltpu.SemaphoreType.DMA((chunks + 4,)),
        ]
        + hot_scratch()
        + [VMEM(TO_CMP, F32), VMEM(TO_RCV, F32)]
    )


def count_operands(counts):
    big = in_hbm(*[array for pair in zip(counts[0][:3], counts[1][:3]) for array in pair])
    (most_1, diag_1), (most_2, diag_2) = counts[0][3:5], counts[1][3:5]
    return big, [diag_1, diag_2, most_1, most_2]


def normal_apply(tab, rcv, index, counts):
    big, small = count_operands(counts)
    return pl.pallas_call(
        normal_kernel,
        in_specs=[ANYWHERE] * 6 + [IN_VMEM] * 7,
        out_shape=table_shapes() + [jax.ShapeDtypeStruct((N_SHOT, LANES), F32)],
        scratch_shapes=[
            VMEM((2 * SLICE, N_SHOT * SRC_G), BF16),
            VMEM((2 * SLICE + 16, SHARED), BF16),
            VMEM((2 * SLICE, SHARED), F32),
            VMEM((2 * SLICE + 16, N_SHOT * SRC_G), F32),
        ]
        + count_scratch(CHUNKS),
        compiler_params=params(24),
        cost_estimate=cost(3),
        name="normal_apply",
    )(*big, tab, rcv, *small, index)


def norm_sums(tab_b, rcv_b, tab_y, rcv_y, own_count, index, counts):
    big, small = count_operands(counts)
    return pl.pallas_call(
        norm_kernel,
        in_specs=[ANYWHERE] * 6 + [IN_VMEM] * 10,
        out_shape=jax.ShapeDtypeStruct((1, LANES), F32),
        scratch_shapes=[
            VMEM((LIVE_ROWS, LANES), F32),
            VMEM(RCV, F32),
            VMEM((2 * SLICE, N_SHOT * SRC_G), BF16),
            VMEM((2 * SLICE, SHARED), BF16),
            VMEM((2 * SLICE, SHARED), F32),
        ]
        + count_scratch(CHUNKS),
        compiler_params=params(24),
        cost_estimate=cost(2),
        name="norm_sums",
    )(*big, tab_b, rcv_b, tab_y, rcv_y, *small, index, own_count)


def spread_kernel(parts, out):
    total = parts[0]
    for source in range(1, N_RCV):
        total = total + parts[source]
    for dest in range(N_RCV):
        out[dest] = total


def exchange(array, axis):
    return lax.all_to_all(array, axis, split_axis=0, concat_axis=0, tiled=True)


def spread_shares(arrived):
    shape = (N_RCV, SHARE, LANES)
    spread = pl.pallas_call(
        spread_kernel,
        out_shape=jax.ShapeDtypeStruct(shape, F32),
        compiler_params=params(24),
        cost_estimate=cost(1),
        name="sum_shares",
    )(arrived.reshape(shape))
    return spread.reshape(TAB)


def pack_kernel(tab, rcv, *refs, first):
    out, rows, sems = refs[-3:]
    lanes = lax.broadcasted_iota(jnp.int32, (SLICE, LANES), 1)
    half = SLICE // 2
    copies = []
    for dest in range(N_SHOT):
        rows[dest, :SLICE] = tab[at(dest)]
        rows[dest, SLICE : 2 * SLICE] = tab[at(OFF_TILE)]
        cmp_first = dest * CMP_G
        rcv_first = dest * (RCV_G // N_SHOT)
        bins = tab[at(CMP_TILE + cmp_first // LANES)]
        cmp_part = pltpu.roll(bins, (-cmp_first) % LANES, 1)
        rcv_part = pltpu.roll(rcv[rcv_first // LANES], (CMP_G - rcv_first) % LANES, 1)
        both = jnp.where(lanes < CMP_G, cmp_part, rcv_part)
        moved = pltpu.roll(both[half:], LANES // 2, 1)
        rows[dest, 2 * SLICE :] = jnp.where(lanes[:half] < LANES // 2, both[:half], moved)
        if dest % PACK == PACK - 1:
            group = dest // PACK
            span = slice(group * PACK, (group + 1) * PACK)
            place = out.at[span, first : first + OWN_ROWS]
            copies.append(pltpu.make_async_copy(rows.at[span], place, sems.at[group]))
            copies[-1].start()
    for copy in copies:
        copy.wait()


def pack_owned(tab, rcv, former=None):
    given = [] if former is None else in_hbm(former)
    return pl.pallas_call(
        functools.partial(pack_kernel, first=OWN_ROWS * len(given)),
        in_specs=[pl.BlockSpec(memory_space=VMEM)] * 2 + [ANYWHERE] * len(given),
        out_specs=ANYWHERE,
        out_shape=pltpu.HBM((N_SHOT, 2 * OWN_ROWS, LANES), F32),
        scratch_shapes=[
            VMEM((N_SHOT, OWN_ROWS, LANES), F32),
            pltpu.SemaphoreType.DMA((N_SHOT // PACK,)),
        ],
        input_output_aliases={2: 0} if given else {},
        compiler_params=params(24),
        cost_estimate=cost(1),
        name="pack_owned",
    )(tab, rcv, *given)


def swapped(value, axis, size, bit):
    return lax.ppermute(value, axis, [(s, s ^ bit) for s in range(size)])


def gather_sums(sums):
    for bit in (1, 2, 6):
        sums = sums + swapped(sums, "rcv", N_RCV, bit)
    here = jnp.arange(N_SHOT, dtype=jnp.int32)[:, None] == lax.axis_index("shot")
    rows = jnp.where(here, sums, 0.0)
    for bit in (1, 3, 4, 12):
        rows = rows + swapped(rows, "shot", N_SHOT, bit)
    return rows


def finish_kernel(sums, owned, source, receiver, offset, cmp):
    rows = sums[...]
    norm_b, cross, norm_z, norm_az, shift = (rows[:, lane : lane + 1] for lane in range(5))
    shift = shift * (1.0 / N_RCV)

    def total(values):
        return jnp.sum(values, axis=0, keepdims=True)

    total_b = total(norm_b)
    first = total(cross + shift * norm_b) / total_b
    off = shift - first
    zz = total(norm_z + 2.0 * off * cross + off * off * norm_b)
    zaz = total(
        norm_az
        + 2.0 * off * (norm_z + shift * cross)
        + off * off * (cross + shift * norm_b)
    )
    second = zaz / zz
    det = first * second - zz / total_b
    scale_b = (first + second) / det
    scale_y = 1.0 / det

    def combine(sender, start, stop):
        part_y = owned[sender, OWN_ROWS + start : OWN_ROWS + stop]
        return scale_b * owned[sender, start:stop] - scale_y * part_y

    def spread_halves(tile):
        return jnp.concatenate([tile, pltpu.roll(tile, LANES // 2, 1)], axis=0)

    per_tile = LANES // SLICE
    for group in range(N_SHOT // per_tile):
        span = slice(group * LANES, (group + 1) * LANES)
        senders = range(group * per_tile, (group + 1) * per_tile)
        source[:, span] = jnp.concatenate([combine(i, 0, SLICE) for i in senders], axis=0).T
        offset[:, span] = jnp.concatenate(
            [combine(i, SLICE, 2 * SLICE) for i in senders], axis=0
        ).T
        rest = jnp.concatenate(
            [spread_halves(combine(i, 2 * SLICE, OWN_ROWS)) for i in senders], axis=0
        ).T
        cmp[:, span] = rest[:CMP_G]
        receiver[0, :, span] = rest[CMP_G : CMP_G + RCV_G // N_SHOT]


def finish(sums, owned):
    return pl.pallas_call(
        finish_kernel,
        out_shape=[
            jax.ShapeDtypeStruct((SRC_G, FREQS), F32),
            jax.ShapeDtypeStruct((1, RCV_G // N_SHOT, FREQS), F32),
            jax.ShapeDtypeStruct((128, FREQS), F32),
            jax.ShapeDtypeStruct((CMP_G, FREQS), F32),
        ],
        compiler_params=params(),
        name="finish",
    )(sums, owned)


def per_device(basis, traces, src_index, rcv_index, off_index, send_rows, send_counts, recv_bins):
    data = log_spectra(
        traces, basis, send_rows[0], send_counts, recv_bins[0], src_index, rcv_index, off_index
    )
    data = exchange(data, "shot")

    tab_b, rcv_b, index = adjoint_apply(data)
    arrived = exchange(tab_b, "rcv")
    counts_1 = count_call(index, 0)
    arrived, index, counts_1 = lax.optimization_barrier((arrived, index, counts_1))
    spread = spread_shares(arrived)
    spread, index = lax.optimization_barrier((spread, index))
    tab_b = exchange(spread, "rcv")
    counts = (counts_1, count_call(index, HALF))

    tab_y, rcv_y, own_count = normal_apply(tab_b, rcv_b, index, counts)
    arrived = exchange(tab_y, "rcv")
    packed = pack_owned(tab_b, rcv_b)
    arrived, packed = lax.optimization_barrier((arrived, packed))
    tab_y = exchange(spread_shares(arrived), "rcv")
    packed = pack_owned(tab_y, rcv_y, packed)
    tab_y, packed = lax.optimization_barrier((tab_y, packed))
    owned = exchange(packed, "shot")
    sums = norm_sums(tab_b, rcv_b, tab_y, rcv_y, own_count, index, counts)
    return tuple(finish(gather_sums(sums), owned))


def solution(mesh):
    basis = fourier_rows()
    mapped = jax.shard_map(
        per_device,
        mesh=mesh,
        in_specs=(
            P(),
            P(("shot", "rcv"), None),
            P(("shot", "rcv")),
            P(("shot", "rcv")),
            P(("shot", "rcv")),
            P(("shot", "rcv"), None, None),
            P(("shot", "rcv"), None),
            P(("shot", "rcv"), None, None),
        ),
        out_specs=(P("shot", None), P("rcv", "shot", None), P(), P("shot", None)),
        check_vma=False,
    )

    def run(*args):
        return mapped(jnp.asarray(basis), *args)

    return run
```

```python
import functools

import ml_dtypes
import numpy as np

import jax
import jax.numpy as jnp
from jax import lax
from jax.experimental import pallas as pl
from jax.experimental.pallas import tpu as pltpu
from jax.sharding import PartitionSpec as P

SAMPLES = 1024
FREQS = 512
TR_DEV = 640
N_SHOT = 16
N_RCV = 8
DEVICES = 128
CAP = 80
SRC_G = 128
RCV_G = 256
CMP_G = 32
SLICE = FREQS // N_SHOT
LANES = 128
OFF_TILE = 16
CMP_TILE = 17
LIVE_TILES = 21
LIVE_ROWS = LIVE_TILES * SLICE
SHARE = -(-LIVE_ROWS // (8 * N_RCV)) * 8
TAB_ROWS = N_RCV * SHARE
RCV_TILES = 2
ROWS = SRC_G + RCV_G + 128 + 512
SHARED = ROWS - SRC_G
SO = 2 * LANES
SOR = SO + RCV_G
OR = LANES + RCV_G
HALF = N_SHOT // 2
COUNT_STEPS = HALF // 2
CHUNKS = 4
CHUNK_ROWS = N_SHOT * SRC_G // CHUNKS
TRACE_TILES = TR_DEV // LANES
BINS_AT = TRACE_TILES * SLICE
INDEX_AT = BINS_AT + N_SHOT
INDEX_ROWS = 24
DATA_ROWS = INDEX_AT + INDEX_ROWS
STEPS = 2
OWN_ROWS = 2 * SLICE + SLICE // 2
PACK = LANES // CMP_G

VMEM = pltpu.VMEM
F32 = jnp.float32
BF16 = jnp.bfloat16
FP8 = jnp.float8_e4m3fn


def fourier_rows():
    phase = np.arange(FREQS)[:, None] * np.arange(SAMPLES)[None, :] % SAMPLES
    angle = phase * (2.0 * np.pi / SAMPLES)
    waves = np.stack([np.cos(angle), np.sin(angle)]).reshape(2, STEPS, -1, SAMPLES)
    table = waves.transpose(1, 0, 2, 3).reshape(2 * FREQS, SAMPLES) / np.sqrt(SAMPLES)
    return table.astype(np.float32).astype(ml_dtypes.bfloat16)


def params(mib=48):
    return pltpu.CompilerParams(vmem_limit_bytes=mib * 2**20)


def cost(micros):
    return pl.CostEstimate(flops=int(micros * 1e9), bytes_accessed=int(micros * 3e6), transcendentals=0)


ANYWHERE = pl.BlockSpec(memory_space=pltpu.HBM)


def in_hbm(*arrays):
    return [pltpu.with_memory_space_constraint(array, pltpu.HBM) for array in arrays]


def nt_dot(left, right):
    return lax.dot_general(left, right, (((1,), (1,)), ((), ())), preferred_element_type=F32)


def split_rows(values):
    high = values.astype(BF16)
    low = (values - high.astype(F32)).astype(BF16)
    return jnp.concatenate([high, low], axis=0)


def at(tile):
    if isinstance(tile, int):
        return slice(tile * SLICE, (tile + 1) * SLICE)
    return pl.ds(pl.multiple_of(tile * SLICE, SLICE), SLICE)


def join_rows(both):
    half = both.shape[0] // 2
    return both[:half] + both[half:]


def flip(table):
    wide = jnp.concatenate(
        [table.astype(F32), jnp.zeros((N_SHOT, LANES - CAP), F32)], axis=1
    )
    return wide.T[:CAP].astype(jnp.int32)


def index_tiles(send_rows, send_counts, src, rcv, off):
    slots = lax.broadcasted_iota(jnp.int32, (CAP, N_SHOT), 0)
    targets = jnp.where(slots < send_counts[...], flip(send_rows[...]), -1)
    trace_ids = lax.broadcasted_iota(jnp.int32, (CAP, TR_DEV), 1)
    places = lax.broadcasted_iota(jnp.int32, (CAP, TR_DEV), 0)
    total = jnp.zeros((CAP, TR_DEV), jnp.int32)
    for owner in range(N_SHOT):
        hit = targets[:, owner : owner + 1] == trace_ids
        total = total + jnp.where(hit, places + owner * LANES, 0)
    slot_row = jnp.sum(total, axis=0, keepdims=True)
    rows = [src[...] & (SRC_G - 1), rcv[...] & (RCV_G - 1), off[...]]
    rows = [row.reshape(1, TR_DEV) for row in rows] + [slot_row]
    table = jnp.concatenate(rows, axis=0).astype(F32)
    tiles = [table[:, q * LANES : (q + 1) * LANES] for q in range(TRACE_TILES)]
    tiles.append(jnp.zeros((INDEX_ROWS - 4 * TRACE_TILES, LANES), F32))
    return jnp.concatenate(tiles, axis=0)


def spectra_kernel(traces, waves, *refs):
    given, out, own, basis, extra = refs[:6], refs[6], refs[7], refs[8], refs[9]
    small, sems, small_sems = refs[10:16], refs[16], refs[17]
    indices = [
        pltpu.make_async_copy(a, b, small_sems.at[k]) for k, (a, b) in enumerate(zip(given, small))
    ]
    for copy in indices:
        copy.start()
    pieces = []
    for k in range(TRACE_TILES):
        span = slice(k * LANES, (k + 1) * LANES)
        pieces.append((traces.at[span], own.at[span]))
    size = 2 * FREQS // STEPS // 2
    for k in range(2 * STEPS):
        span = slice(k * size, (k + 1) * size)
        pieces.append((waves.at[span], basis.at[span]))
    copies = [pltpu.make_async_copy(a, b, sems.at[k]) for k, (a, b) in enumerate(pieces)]
    early = TRACE_TILES + 2
    for copy in copies[:early]:
        copy.start()
    for copy in indices:
        copy.wait()
    send_rows, send_counts, bins, src, rcv, off = small
    pad = jnp.zeros((N_SHOT, LANES - CAP), F32)
    extra[:N_SHOT] = jnp.concatenate([bins[...].astype(F32), pad], axis=1)
    extra[N_SHOT:] = index_tiles(send_rows, send_counts, src, rcv, off)
    for part in range(N_SHOT):
        out[part, BINS_AT:, :] = extra[...]
    for copy in copies[:early]:
        copy.wait()
    for copy in copies[early:]:
        copy.start()
    half = FREQS // STEPS
    for step in range(STEPS):
        if step == 1:
            for copy in copies[early:]:
                copy.wait()
        parts = nt_dot(basis[2 * half * step : 2 * half * (step + 1)], own[...])
        logs = jnp.log1p(parts[:half] * parts[:half] + parts[half:] * parts[half:])
        for part in range(half // SLICE):
            for q in range(TRACE_TILES):
                out[step * (half // SLICE) + part, q * SLICE : (q + 1) * SLICE, :] = logs[
                    part * SLICE : (part + 1) * SLICE, q * LANES : (q + 1) * LANES
                ]


def log_spectra(traces, basis, *small):
    return pl.pallas_call(
        spectra_kernel,
        in_specs=[ANYWHERE] * (2 + len(small)),
        out_shape=jax.ShapeDtypeStruct((N_SHOT, DATA_ROWS, LANES), F32),
        scratch_shapes=[
            VMEM((TR_DEV, SAMPLES), BF16),
            VMEM((2 * FREQS, SAMPLES), BF16),
            VMEM((DATA_ROWS - BINS_AT, LANES), F32),
        ]
        + [VMEM(array.shape, jnp.int32) for array in small]
        + [
            pltpu.SemaphoreType.DMA((TRACE_TILES + 2 * STEPS,)),
            pltpu.SemaphoreType.DMA((len(small),)),
        ],
        compiler_params=params(24),
        cost_estimate=cost(5),
        name="spectra",
    )(*in_hbm(traces, basis, *small))


def fill_ids(ids):
    ids[...] = lax.broadcasted_iota(jnp.int32, ids.shape, 0).astype(F32).astype(BF16)


def fill_hot(tiles, ids, hot):
    one = jnp.ones((1, 1), BF16)
    zero = jnp.zeros((1, 1), BF16)
    values = tiles.astype(F32)
    for q in range(TRACE_TILES):
        span = slice(q * LANES, (q + 1) * LANES)
        first = 0
        for row, size, base in ((0, SRC_G, 0), (2, 128, 0), (1, RCV_G, 0), (3, 256, 0), (3, 256, 256)):
            wanted = (values[4 * q + row : 4 * q + row + 1] - base).astype(BF16)
            hits = jnp.where(ids[:size] == wanted, one, zero)
            hot[first : first + size, span] = hits.astype(hot.dtype)
            first += size


def resolve_bins(data, block):
    tiles = data[block, INDEX_AT:].astype(jnp.int32)
    rows = [data[owner, pl.ds(BINS_AT + block, 1)] for owner in range(N_SHOT)]
    table = jnp.concatenate(rows, axis=0)
    owners = lax.broadcasted_iota(jnp.int32, (N_SHOT, LANES), 0)
    resolved = []
    for q in range(TRACE_TILES):
        slot = tiles[4 * q + 3 : 4 * q + 4]
        place = jnp.broadcast_to(slot & (LANES - 1), (N_SHOT, LANES))
        found = jnp.take_along_axis(table, place, axis=1, mode="promise_in_bounds")
        found = jnp.where(owners == slot >> 7, found.astype(jnp.int32) + owners * CMP_G, 0)
        resolved += [tiles[4 * q : 4 * q + 3], jnp.sum(found, axis=0, keepdims=True)]
    resolved.append(jnp.zeros((INDEX_ROWS - 4 * TRACE_TILES, LANES), jnp.int32))
    return jnp.concatenate(resolved, axis=0)


def prepare_block(data, index, ids, hot, block):
    tiles = resolve_bins(data, block)
    index[block] = tiles
    one = jnp.ones((1, 1), BF16)
    zero = jnp.zeros((1, 1), BF16)
    for q in range(TRACE_TILES):
        for place, row in enumerate((0, 2, 1, 3)):
            lane = tiles[4 * q + row : 4 * q + row + 1] & (LANES - 1)
            hit = ids[:LANES] == lane.astype(F32).astype(BF16)
            span = slice(q * LANES, (q + 1) * LANES)
            hot[place * LANES : (place + 1) * LANES, span] = jnp.where(hit, one, zero)


def add_block(data, index, hot, tab, rcv, block):
    tiles = index[block]
    values = [data[block, q * SLICE : (q + 1) * SLICE] for q in range(TRACE_TILES)]

    both = split_rows(jnp.concatenate(values, axis=1))
    zero = jnp.zeros((1, 1), BF16)

    def of_tiles(row, count):
        place = [tiles[4 * q + row : 4 * q + row + 1] >> 7 for q in range(TRACE_TILES)]
        place = jnp.concatenate(place, axis=1).astype(F32).astype(BF16)
        return jnp.concatenate([jnp.where(place == tile, both, zero) for tile in range(count)], axis=0)

    plain = nt_dot(both, hot[: 2 * LANES])
    tab[at(block)] = join_rows(plain[:, :LANES])
    tab[at(OFF_TILE)] += join_rows(plain[:, LANES:])
    parts = of_tiles(1, RCV_TILES)
    sums = nt_dot(parts, hot[2 * LANES : 3 * LANES])
    for tile in range(RCV_TILES):
        rcv[tile] += join_rows(sums[tile * 2 * SLICE : (tile + 1) * 2 * SLICE])
    cmp_tiles = LIVE_TILES - CMP_TILE
    parts = of_tiles(3, cmp_tiles)
    sums = nt_dot(parts, hot[3 * LANES :])
    for tile in range(cmp_tiles):
        tab[at(CMP_TILE + tile)] += join_rows(sums[tile * 2 * SLICE : (tile + 1) * 2 * SLICE])


def adjoint_kernel(data, tab, rcv, index, hot_even, hot_odd, ids):
    tab[OFF_TILE * SLICE :] = jnp.zeros((TAB_ROWS - OFF_TILE * SLICE, LANES), F32)
    rcv[...] = jnp.zeros((RCV_TILES, SLICE, LANES), F32)
    fill_ids(ids)
    prepare_block(data, index, ids, hot_even, 0)

    @pl.loop(0, N_SHOT // 2)
    def _(pair):
        even = 2 * pair
        prepare_block(data, index, ids, hot_odd, even + 1)
        add_block(data, index, hot_even, tab, rcv, even)
        prepare_block(data, index, ids, hot_even, jnp.minimum(even + 2, N_SHOT - 1))
        add_block(data, index, hot_odd, tab, rcv, even + 1)


EXACT = 128


ROW_EXACT = 16


def kept_part(counts):
    return (counts.astype(jnp.int32) & (ROW_EXACT - 1)).astype(F32).astype(FP8)


def left_over(counts, exact):
    whole = counts.astype(jnp.int32)
    return (whole - (whole & (exact - 1))).astype(F32).astype(BF16)


def peak(counts):
    top = jnp.max(counts, axis=0, keepdims=True)
    best = top[:, :LANES]
    for start in range(LANES, counts.shape[1], LANES):
        best = jnp.maximum(best, top[:, start : start + LANES])
    return best


def block_counts(hot):
    with_cmp = nt_dot(hot[:SOR], hot[SOR:])
    with_rcv = nt_dot(hot[:SO], hot[SO:SOR])
    with_off = nt_dot(hot[:SRC_G], hot[SRC_G:SO])
    rows = jnp.concatenate([with_off, with_rcv[:SRC_G], with_cmp[:SRC_G]], axis=1)
    return rows, with_cmp[SRC_G:], with_rcv[SRC_G:]


def count_kernel(
    index, kept, to_cmp_kept, to_rcv_kept, most, diag, hot_even, hot_odd, ids, to_cmp, to_rcv, *, first
):
    step = pl.program_id(0)
    even = first + 2 * step

    @pl.when(step == 0)
    def _():
        to_cmp[...] = jnp.zeros_like(to_cmp)
        to_rcv[...] = jnp.zeros_like(to_rcv)
        diag[...] = jnp.zeros_like(diag)
        most[...] = jnp.zeros_like(most)
        fill_ids(ids)
        fill_hot(index[even], ids, hot_even)

    def add(hot, place):
        rows, cmp_counts, rcv_counts = block_counts(hot)
        to_cmp[...] += cmp_counts
        to_rcv[...] += rcv_counts
        diag[...] += jnp.sum(rows, axis=0, keepdims=True)
        kept[place * SRC_G : (place + 1) * SRC_G] = kept_part(rows)
        most[...] = jnp.maximum(most[...], peak(rows) * (EXACT / ROW_EXACT))

    fill_hot(index[even + 1], ids, hot_odd)
    add(hot_even, 0)
    fill_hot(index[jnp.minimum(even + 2, N_SHOT - 1)], ids, hot_even)
    add(hot_odd, 1)

    @pl.when(step == COUNT_STEPS - 1)
    def _():
        to_cmp_kept[...] = (to_cmp[...].astype(jnp.int32) & (EXACT - 1)).astype(jnp.int8)
        to_rcv_kept[...] = (to_rcv[...].astype(jnp.int32) & (EXACT - 1)).astype(jnp.int8)
        most[...] = jnp.maximum(most[...], jnp.maximum(peak(to_cmp[...]), peak(to_rcv[...])))


def add_left_over(most_1, most_2, index, hot, ids, to_cmp, to_rcv, use_both, use_rows):
    top = jnp.maximum(jnp.max(most_1[...]), jnp.max(most_2[...]))

    @pl.when(top >= EXACT)
    def _():
        fill_ids(ids)
        for half in range(2):
            to_cmp[...] = jnp.zeros_like(to_cmp)
            to_rcv[...] = jnp.zeros_like(to_rcv)

            @pl.loop(half * HALF, (half + 1) * HALF)
            def _(block):
                fill_hot(index[block], ids, hot)
                rows, cmp_counts, rcv_counts = block_counts(hot)
                to_cmp[...] += cmp_counts
                to_rcv[...] += rcv_counts
                use_rows(block, left_over(rows, ROW_EXACT))

            use_both(left_over(to_cmp[...], EXACT), left_over(to_rcv[...], EXACT))


def fetch_counts(refs, held, held_cmp, held_rcv, sems):
    *halves, cmp_1, cmp_2, rcv_1, rcv_2 = refs
    pieces = []
    for half, source in enumerate(halves):
        for chunk in range(CHUNKS // 2):
            start = chunk * CHUNK_ROWS
            place = held.at[half * (CHUNKS // 2) + chunk]
            pieces.append((source.at[start : start + CHUNK_ROWS], place))
    pieces += [(cmp_1, held_cmp.at[0]), (cmp_2, held_cmp.at[1])]
    pieces += [(rcv_1, held_rcv.at[0]), (rcv_2, held_rcv.at[1])]
    copies = [pltpu.make_async_copy(a, b, sems.at[k]) for k, (a, b) in enumerate(pieces)]
    for copy in copies:
        copy.start()
    return copies


def sum_halves(held):
    return (held[0].astype(F32) + held[1].astype(F32)).astype(BF16)


def load_halves(tab, rcv, own, shared):
    for tile in range(N_SHOT):
        own[:, tile * LANES : (tile + 1) * LANES] = split_rows(tab[at(tile)])
    shared[: 2 * SLICE, :LANES] = split_rows(tab[at(OFF_TILE)])
    for tile in range(RCV_TILES):
        shared[: 2 * SLICE, (1 + tile) * LANES : (2 + tile) * LANES] = split_rows(rcv[tile])
    for tile in range(CMP_TILE, LIVE_TILES):
        start = (tile - CMP_TILE) * LANES + OR
        shared[: 2 * SLICE, start : start + LANES] = split_rows(tab[at(tile)])


def normal_kernel(
    first, last, cmp_1, cmp_2, rcv_1, rcv_2, tab_in, rcv_in, diag_1, diag_2, most_1, most_2, index,
    tab, rcv, own_count, own, shared, to_shared, to_own,
    held, held_cmp, held_rcv, sems, hot, ids, exact_cmp, exact_rcv,
):
    counts = (first, last, cmp_1, cmp_2, rcv_1, rcv_2)
    copies = fetch_counts(counts, held, held_cmp, held_rcv, sems)
    top = 2 * SLICE
    load_halves(tab_in, rcv_in, own, shared)
    lanes = lax.broadcasted_iota(jnp.int32, (16, SHARED), 1)
    shared[top:] = jnp.where(lanes < LANES, 1.0, 0.0).astype(BF16)
    for chunk in range(CHUNKS):
        copies[chunk].wait()
        rows = held[chunk].astype(BF16)
        span = slice(chunk * CHUNK_ROWS, (chunk + 1) * CHUNK_ROWS)
        sums = jnp.dot(own[:, span], rows, preferred_element_type=F32)
        to_shared[...] = sums if chunk == 0 else to_shared[...] + sums
        to_own[:, span] = nt_dot(shared[...], rows)

    def others(to_cmp, to_rcv):
        cmp_sums = jnp.dot(shared[:top, :OR], to_cmp, preferred_element_type=F32)
        to_shared[:, OR:] += cmp_sums
        to_shared[:, :OR] += nt_dot(shared[:top, OR:], to_cmp)
        rcv_sums = jnp.dot(shared[:top, :LANES], to_rcv, preferred_element_type=F32)
        to_shared[:, LANES:OR] += rcv_sums
        to_shared[:, :LANES] += nt_dot(shared[:top, LANES:OR], to_rcv)

    def use_rows(block, rows):
        span = pl.ds(pl.multiple_of(block * SRC_G, SRC_G), SRC_G)
        to_shared[...] += jnp.dot(own[:, span], rows, preferred_element_type=F32)
        to_own[:, span] += nt_dot(shared[...], rows)

    for copy in copies[-4:]:
        copy.wait()
    others(sum_halves(held_cmp), sum_halves(held_rcv))
    add_left_over(most_1, most_2, index, hot, ids, exact_cmp, exact_rcv, others, use_rows)
    diag = diag_1[...] + diag_2[...]
    for tile in range(N_SHOT):
        span = slice(tile * LANES, (tile + 1) * LANES)
        count = to_own[top : top + 1, span]
        own_count[tile : tile + 1] = count
        tab[at(tile)] = join_rows(to_own[:top, span]) + count * tab_in[at(tile)]
    tab[at(OFF_TILE)] = join_rows(to_shared[:, :LANES]) + diag[:, :LANES] * tab_in[at(OFF_TILE)]
    for tile in range(RCV_TILES):
        span = slice((1 + tile) * LANES, (2 + tile) * LANES)
        rcv[tile] = join_rows(to_shared[:, span]) + diag[:, span] * rcv_in[tile]
    for tile in range(CMP_TILE, LIVE_TILES):
        start = (tile - CMP_TILE) * LANES + OR
        span = slice(start, start + LANES)
        tab[at(tile)] = join_rows(to_shared[:, span]) + diag[:, span] * tab_in[at(tile)]
    tab[LIVE_ROWS:] = jnp.zeros((TAB_ROWS - LIVE_ROWS, LANES), F32)


def all_sum(values):
    return jnp.sum(values, axis=tuple(range(values.ndim)), keepdims=True).reshape(1, 1)


def fold(values):
    total = values[:, :LANES]
    for start in range(LANES, values.shape[1], LANES):
        total = total + values[:, start : start + LANES]
    return total


def norm_kernel(
    first, last, cmp_1, cmp_2, rcv_1, rcv_2,
    tab_b, rcv_b, tab_y, rcv_y, diag_1, diag_2, most_1, most_2, index, own_count,
    out, tab_z, rcv_z, own, shared, to_shared,
    held, held_cmp, held_rcv, sems, hot, ids, exact_cmp, exact_rcv,
):
    counts = (first, last, cmp_1, cmp_2, rcv_1, rcv_2)
    copies = fetch_counts(counts, held, held_cmp, held_rcv, sems)
    shared_b = tab_b[:LIVE_ROWS]
    shared_y = tab_y[:LIVE_ROWS]
    shift = all_sum(shared_b * shared_y) / all_sum(shared_b * shared_b)
    shared_z = shared_y - shift * shared_b
    own_b = rcv_b[...]
    own_z = rcv_y[...] - shift * own_b
    tab_z[...] = shared_z
    rcv_z[...] = own_z
    load_halves(tab_z, rcv_z, own, shared)
    for chunk in range(CHUNKS):
        copies[chunk].wait()
        rows = held[chunk].astype(BF16)
        span = slice(chunk * CHUNK_ROWS, (chunk + 1) * CHUNK_ROWS)
        sums = jnp.dot(own[:, span], rows, preferred_element_type=F32)
        to_shared[...] = sums if chunk == 0 else to_shared[...] + sums

    def whole(tabs, own):
        return all_sum(tabs) * (1.0 / N_RCV) + all_sum(own)

    def others(to_cmp, to_rcv):
        cmp_sums = jnp.dot(shared[:, :OR], to_cmp, preferred_element_type=F32)
        to_shared[:, OR:] += cmp_sums
        rcv_sums = jnp.dot(shared[:, :LANES], to_rcv, preferred_element_type=F32)
        to_shared[:, LANES:OR] += rcv_sums

    def use_rows(block, rows):
        span = pl.ds(pl.multiple_of(block * SRC_G, SRC_G), SRC_G)
        to_shared[...] += jnp.dot(own[:, span], rows, preferred_element_type=F32)

    for copy in copies[-4:]:
        copy.wait()
    others(sum_halves(held_cmp), sum_halves(held_rcv))
    add_left_over(most_1, most_2, index, hot, ids, exact_cmp, exact_rcv, others, use_rows)
    tiles = [tab_z[at(OFF_TILE)]] + [rcv_z[tile] for tile in range(RCV_TILES)]
    tiles += [tab_z[at(tile)] for tile in range(CMP_TILE, LIVE_TILES)]
    rest = jnp.concatenate(tiles, axis=1)
    diag = diag_1[...] + diag_2[...]
    total = fold(2.0 * rest * join_rows(to_shared[...]) + diag * rest * rest)
    for tile in range(N_SHOT):
        total = total + own_count[tile : tile + 1] * tab_z[at(tile)] * tab_z[at(tile)]
    sums = (
        whole(shared_b * shared_b, own_b * own_b),
        whole(shared_b * shared_z, own_b * own_z),
        whole(shared_z * shared_z, own_z * own_z),
        all_sum(total),
        shift,
    )
    lanes = lax.broadcasted_iota(jnp.int32, (1, LANES), 1)
    row = jnp.zeros((1, LANES), F32)
    for lane, value in enumerate(sums):
        row = jnp.where(lanes == lane, value, row)
    out[...] = row


def whole_spec(*shape):
    return pl.BlockSpec(shape, lambda c: (0,) * len(shape))


TAB = (TAB_ROWS, LANES)
RCV = (RCV_TILES, SLICE, LANES)
INDEX = (N_SHOT, INDEX_ROWS, LANES)
INDEX_SPEC = pl.BlockSpec((1, INDEX_ROWS, LANES), lambda c: (c, 0, 0))


def table_shapes():
    return [jax.ShapeDtypeStruct(TAB, F32), jax.ShapeDtypeStruct(RCV, F32)]


def hot_scratch():
    return [VMEM((ROWS, TR_DEV), FP8), VMEM((256, LANES), BF16)]


def adjoint_apply(data):
    return pl.pallas_call(
        adjoint_kernel,
        out_shape=table_shapes() + [jax.ShapeDtypeStruct(INDEX, jnp.int32)],
        scratch_shapes=[VMEM((4 * LANES, TR_DEV), BF16)] * 2 + [VMEM((256, LANES), BF16)],
        compiler_params=params(24),
        cost_estimate=cost(8),
        name="adjoint_apply",
    )(data)


COUNTS = (HALF * SRC_G, SHARED)
TO_CMP = (OR, SHARED - OR)
TO_RCV = (LANES, RCV_G)
IN_VMEM = pl.BlockSpec(memory_space=VMEM)


def count_call(index, first):
    rows = pl.BlockSpec((2 * SRC_G, SHARED), lambda c: (c, 0))
    small = [whole_spec(*TO_CMP), whole_spec(*TO_RCV), whole_spec(1, LANES), whole_spec(1, SHARED)]
    return pl.pallas_call(
        functools.partial(count_kernel, first=first),
        grid=(COUNT_STEPS,),
        in_specs=[whole_spec(*INDEX)],
        out_specs=[rows] + small,
        out_shape=[
            pltpu.HBM(COUNTS, FP8),
            pltpu.HBM(TO_CMP, jnp.int8),
            pltpu.HBM(TO_RCV, jnp.int8),
            jax.ShapeDtypeStruct((1, LANES), F32),
            jax.ShapeDtypeStruct((1, SHARED), F32),
        ],
        scratch_shapes=[VMEM((ROWS, TR_DEV), FP8)] * 2
        + [VMEM((256, LANES), BF16), VMEM(TO_CMP, F32), VMEM(TO_RCV, F32)],
        compiler_params=params(24),
        cost_estimate=cost(6),
        name="count_pairs",
    )(index)


def count_scratch(chunks):
    return (
        [
            VMEM((chunks, CHUNK_ROWS, SHARED), FP8),
            VMEM((2,) + TO_CMP, jnp.int8),
            VMEM((2,) + TO_RCV, jnp.int8),
            pltpu.SemaphoreType.DMA((chunks + 4,)),
        ]
        + hot_scratch()
        + [VMEM(TO_CMP, F32), VMEM(TO_RCV, F32)]
    )


def count_operands(counts):
    big = in_hbm(*[array for pair in zip(counts[0][:3], counts[1][:3]) for array in pair])
    (most_1, diag_1), (most_2, diag_2) = counts[0][3:5], counts[1][3:5]
    return big, [diag_1, diag_2, most_1, most_2]


def normal_apply(tab, rcv, index, counts):
    big, small = count_operands(counts)
    return pl.pallas_call(
        normal_kernel,
        in_specs=[ANYWHERE] * 6 + [IN_VMEM] * 7,
        out_shape=table_shapes() + [jax.ShapeDtypeStruct((N_SHOT, LANES), F32)],
        scratch_shapes=[
            VMEM((2 * SLICE, N_SHOT * SRC_G), BF16),
            VMEM((2 * SLICE + 16, SHARED), BF16),
            VMEM((2 * SLICE, SHARED), F32),
            VMEM((2 * SLICE + 16, N_SHOT * SRC_G), F32),
        ]
        + count_scratch(CHUNKS),
        compiler_params=params(24),
        cost_estimate=cost(3),
        name="normal_apply",
    )(*big, tab, rcv, *small, index)


def norm_sums(tab_b, rcv_b, tab_y, rcv_y, own_count, index, counts):
    big, small = count_operands(counts)
    return pl.pallas_call(
        norm_kernel,
        in_specs=[ANYWHERE] * 6 + [IN_VMEM] * 10,
        out_shape=jax.ShapeDtypeStruct((1, LANES), F32),
        scratch_shapes=[
            VMEM((LIVE_ROWS, LANES), F32),
            VMEM(RCV, F32),
            VMEM((2 * SLICE, N_SHOT * SRC_G), BF16),
            VMEM((2 * SLICE, SHARED), BF16),
            VMEM((2 * SLICE, SHARED), F32),
        ]
        + count_scratch(CHUNKS),
        compiler_params=params(24),
        cost_estimate=cost(2),
        name="norm_sums",
    )(*big, tab_b, rcv_b, tab_y, rcv_y, *small, index, own_count)


def spread_kernel(parts, out):
    total = parts[0]
    for source in range(1, N_RCV):
        total = total + parts[source]
    for dest in range(N_RCV):
        out[dest] = total


def exchange(array, axis):
    return lax.all_to_all(array, axis, split_axis=0, concat_axis=0, tiled=True)


def spread_shares(arrived):
    shape = (N_RCV, SHARE, LANES)
    spread = pl.pallas_call(
        spread_kernel,
        out_shape=jax.ShapeDtypeStruct(shape, F32),
        compiler_params=params(24),
        cost_estimate=cost(1),
        name="sum_shares",
    )(arrived.reshape(shape))
    return spread.reshape(TAB)


def pack_kernel(tab, rcv, *refs, first):
    out, rows, sems = refs[-3:]
    lanes = lax.broadcasted_iota(jnp.int32, (SLICE, LANES), 1)
    half = SLICE // 2
    copies = []
    for dest in range(N_SHOT):
        rows[dest, :SLICE] = tab[at(dest)]
        rows[dest, SLICE : 2 * SLICE] = tab[at(OFF_TILE)]
        cmp_first = dest * CMP_G
        rcv_first = dest * (RCV_G // N_SHOT)
        bins = tab[at(CMP_TILE + cmp_first // LANES)]
        cmp_part = pltpu.roll(bins, (-cmp_first) % LANES, 1)
        rcv_part = pltpu.roll(rcv[rcv_first // LANES], (CMP_G - rcv_first) % LANES, 1)
        both = jnp.where(lanes < CMP_G, cmp_part, rcv_part)
        moved = pltpu.roll(both[half:], LANES // 2, 1)
        rows[dest, 2 * SLICE :] = jnp.where(lanes[:half] < LANES // 2, both[:half], moved)
        if dest % PACK == PACK - 1:
            group = dest // PACK
            span = slice(group * PACK, (group + 1) * PACK)
            place = out.at[span, first : first + OWN_ROWS]
            copies.append(pltpu.make_async_copy(rows.at[span], place, sems.at[group]))
            copies[-1].start()
    for copy in copies:
        copy.wait()


def pack_owned(tab, rcv, former=None):
    given = [] if former is None else in_hbm(former)
    return pl.pallas_call(
        functools.partial(pack_kernel, first=OWN_ROWS * len(given)),
        in_specs=[pl.BlockSpec(memory_space=VMEM)] * 2 + [ANYWHERE] * len(given),
        out_specs=ANYWHERE,
        out_shape=pltpu.HBM((N_SHOT, 2 * OWN_ROWS, LANES), F32),
        scratch_shapes=[
            VMEM((N_SHOT, OWN_ROWS, LANES), F32),
            pltpu.SemaphoreType.DMA((N_SHOT // PACK,)),
        ],
        input_output_aliases={2: 0} if given else {},
        compiler_params=params(24),
        cost_estimate=cost(1),
        name="pack_owned",
    )(tab, rcv, *given)


def swapped(value, axis, size, bit):
    return lax.ppermute(value, axis, [(s, s ^ bit) for s in range(size)])


def gather_sums(sums):
    for bit in (1, 2, 6):
        sums = sums + swapped(sums, "rcv", N_RCV, bit)
    here = jnp.arange(N_SHOT, dtype=jnp.int32)[:, None] == lax.axis_index("shot")
    rows = jnp.where(here, sums, 0.0)
    for bit in (1, 3, 4, 12):
        rows = rows + swapped(rows, "shot", N_SHOT, bit)
    return rows


def finish_kernel(sums, owned, source, receiver, offset, cmp):
    rows = sums[...]
    norm_b, cross, norm_z, norm_az, shift = (rows[:, lane : lane + 1] for lane in range(5))
    shift = shift * (1.0 / N_RCV)

    def total(values):
        return jnp.sum(values, axis=0, keepdims=True)

    total_b = total(norm_b)
    first = total(cross + shift * norm_b) / total_b
    off = shift - first
    zz = total(norm_z + 2.0 * off * cross + off * off * norm_b)
    zaz = total(
        norm_az
        + 2.0 * off * (norm_z + shift * cross)
        + off * off * (cross + shift * norm_b)
    )
    second = zaz / zz
    det = first * second - zz / total_b
    scale_b = (first + second) / det
    scale_y = 1.0 / det

    def combine(sender, start, stop):
        part_y = owned[sender, OWN_ROWS + start : OWN_ROWS + stop]
        return scale_b * owned[sender, start:stop] - scale_y * part_y

    def spread_halves(tile):
        return jnp.concatenate([tile, pltpu.roll(tile, LANES // 2, 1)], axis=0)

    per_tile = LANES // SLICE
    for group in range(N_SHOT // per_tile):
        span = slice(group * LANES, (group + 1) * LANES)
        senders = range(group * per_tile, (group + 1) * per_tile)
        source[:, span] = jnp.concatenate([combine(i, 0, SLICE) for i in senders], axis=0).T
        offset[:, span] = jnp.concatenate(
            [combine(i, SLICE, 2 * SLICE) for i in senders], axis=0
        ).T
        rest = jnp.concatenate(
            [spread_halves(combine(i, 2 * SLICE, OWN_ROWS)) for i in senders], axis=0
        ).T
        cmp[:, span] = rest[:CMP_G]
        receiver[0, :, span] = rest[CMP_G : CMP_G + RCV_G // N_SHOT]


def finish(sums, owned):
    return pl.pallas_call(
        finish_kernel,
        out_shape=[
            jax.ShapeDtypeStruct((SRC_G, FREQS), F32),
            jax.ShapeDtypeStruct((1, RCV_G // N_SHOT, FREQS), F32),
            jax.ShapeDtypeStruct((128, FREQS), F32),
            jax.ShapeDtypeStruct((CMP_G, FREQS), F32),
        ],
        compiler_params=params(),
        name="finish",
    )(sums, owned)


def per_device(basis, traces, src_index, rcv_index, off_index, send_rows, send_counts, recv_bins):
    data = log_spectra(
        traces, basis, send_rows[0], send_counts, recv_bins[0], src_index, rcv_index, off_index
    )
    data = exchange(data, "shot")

    tab_b, rcv_b, index = adjoint_apply(data)
    arrived = exchange(tab_b, "rcv")
    counts_1 = count_call(index, 0)
    arrived, index, counts_1 = lax.optimization_barrier((arrived, index, counts_1))
    spread = spread_shares(arrived)
    spread, index = lax.optimization_barrier((spread, index))
    tab_b = exchange(spread, "rcv")
    counts = (counts_1, count_call(index, HALF))

    tab_y, rcv_y, own_count = normal_apply(tab_b, rcv_b, index, counts)
    arrived = exchange(tab_y, "rcv")
    packed = pack_owned(tab_b, rcv_b)
    arrived, packed = lax.optimization_barrier((arrived, packed))
    tab_y = exchange(spread_shares(arrived), "rcv")
    packed = pack_owned(tab_y, rcv_y, packed)
    tab_y, packed = lax.optimization_barrier((tab_y, packed))
    owned = exchange(packed, "shot")
    sums = norm_sums(tab_b, rcv_b, tab_y, rcv_y, own_count, index, counts)
    return tuple(finish(gather_sums(sums), owned))


def solution(mesh):
    basis = fourier_rows()
    mapped = jax.shard_map(
        per_device,
        mesh=mesh,
        in_specs=(
            P(),
            P(("shot", "rcv"), None),
            P(("shot", "rcv")),
            P(("shot", "rcv")),
            P(("shot", "rcv")),
            P(("shot", "rcv"), None, None),
            P(("shot", "rcv"), None),
            P(("shot", "rcv"), None, None),
        ),
        out_specs=(P("shot", None), P("rcv", "shot", None), P(), P("shot", None)),
        check_vma=False,
    )

    def run(*args):
        return mapped(jnp.asarray(basis), *args)

    return run
```

```python
import functools

import ml_dtypes
import numpy as np

import jax
import jax.numpy as jnp
from jax import lax
from jax.experimental import pallas as pl
from jax.experimental.pallas import tpu as pltpu
from jax.sharding import PartitionSpec as P

SAMPLES = 1024
FREQS = 512
TR_DEV = 640
N_SHOT = 16
N_RCV = 8
DEVICES = 128
CAP = 80
SRC_G = 128
RCV_G = 256
CMP_G = 32
SLICE = FREQS // N_SHOT
LANES = 128
OFF_TILE = 16
CMP_TILE = 17
LIVE_TILES = 21
LIVE_ROWS = LIVE_TILES * SLICE
SHARE = -(-LIVE_ROWS // (8 * N_RCV)) * 8
TAB_ROWS = N_RCV * SHARE
RCV_TILES = 2
ROWS = SRC_G + RCV_G + 128 + 512
SHARED = ROWS - SRC_G
SO = 2 * LANES
SOR = SO + RCV_G
OR = LANES + RCV_G
HALF = N_SHOT // 2
COUNT_STEPS = HALF // 2
CHUNKS = 4
CHUNK_ROWS = N_SHOT * SRC_G // CHUNKS
TRACE_TILES = TR_DEV // LANES
BINS_AT = TRACE_TILES * SLICE
INDEX_AT = BINS_AT + N_SHOT
INDEX_ROWS = 24
DATA_ROWS = INDEX_AT + INDEX_ROWS
STEPS = 2
OWN_ROWS = 2 * SLICE + SLICE // 2
PACK = LANES // CMP_G

VMEM = pltpu.VMEM
F32 = jnp.float32
BF16 = jnp.bfloat16
FP8 = jnp.float8_e4m3fn


def fourier_rows():
    phase = np.arange(FREQS)[:, None] * np.arange(SAMPLES)[None, :] % SAMPLES
    angle = phase * (2.0 * np.pi / SAMPLES)
    waves = np.stack([np.cos(angle), np.sin(angle)]).reshape(2, STEPS, -1, SAMPLES)
    table = waves.transpose(1, 0, 2, 3).reshape(2 * FREQS, SAMPLES) / np.sqrt(SAMPLES)
    return table.astype(np.float32).astype(ml_dtypes.bfloat16)


def params(mib=48):
    return pltpu.CompilerParams(vmem_limit_bytes=mib * 2**20)


def cost(micros):
    return pl.CostEstimate(flops=int(micros * 1e9), bytes_accessed=int(micros * 3e6), transcendentals=0)


ANYWHERE = pl.BlockSpec(memory_space=pltpu.HBM)


def in_hbm(*arrays):
    return [pltpu.with_memory_space_constraint(array, pltpu.HBM) for array in arrays]


def nt_dot(left, right):
    return lax.dot_general(left, right, (((1,), (1,)), ((), ())), preferred_element_type=F32)


def split_rows(values):
    high = values.astype(BF16)
    low = (values - high.astype(F32)).astype(BF16)
    return jnp.concatenate([high, low], axis=0)


def at(tile):
    if isinstance(tile, int):
        return slice(tile * SLICE, (tile + 1) * SLICE)
    return pl.ds(pl.multiple_of(tile * SLICE, SLICE), SLICE)


def join_rows(both):
    half = both.shape[0] // 2
    return both[:half] + both[half:]


def flip(table):
    wide = jnp.concatenate(
        [table.astype(F32), jnp.zeros((N_SHOT, LANES - CAP), F32)], axis=1
    )
    return wide.T[:CAP].astype(jnp.int32)


def index_tiles(send_rows, send_counts, src, rcv, off):
    slots = lax.broadcasted_iota(jnp.int32, (CAP, N_SHOT), 0)
    targets = jnp.where(slots < send_counts[...], flip(send_rows[...]), -1)
    trace_ids = lax.broadcasted_iota(jnp.int32, (CAP, TR_DEV), 1)
    places = lax.broadcasted_iota(jnp.int32, (CAP, TR_DEV), 0)
    total = jnp.zeros((CAP, TR_DEV), jnp.int32)
    for owner in range(N_SHOT):
        hit = targets[:, owner : owner + 1] == trace_ids
        total = total + jnp.where(hit, places + owner * LANES, 0)
    slot_row = jnp.sum(total, axis=0, keepdims=True)
    rows = [src[...] & (SRC_G - 1), rcv[...] & (RCV_G - 1), off[...]]
    rows = [row.reshape(1, TR_DEV) for row in rows] + [slot_row]
    table = jnp.concatenate(rows, axis=0).astype(F32)
    tiles = [table[:, q * LANES : (q + 1) * LANES] for q in range(TRACE_TILES)]
    tiles.append(jnp.zeros((INDEX_ROWS - 4 * TRACE_TILES, LANES), F32))
    return jnp.concatenate(tiles, axis=0)


def spectra_kernel(traces, waves, *refs):
    given, out, own, basis, extra = refs[:6], refs[6], refs[7], refs[8], refs[9]
    small, sems, small_sems = refs[10:16], refs[16], refs[17]
    indices = [
        pltpu.make_async_copy(a, b, small_sems.at[k]) for k, (a, b) in enumerate(zip(given, small))
    ]
    for copy in indices:
        copy.start()
    pieces = []
    for k in range(TRACE_TILES):
        span = slice(k * LANES, (k + 1) * LANES)
        pieces.append((traces.at[span], own.at[span]))
    size = 2 * FREQS // STEPS // 2
    for k in range(2 * STEPS):
        span = slice(k * size, (k + 1) * size)
        pieces.append((waves.at[span], basis.at[span]))
    copies = [pltpu.make_async_copy(a, b, sems.at[k]) for k, (a, b) in enumerate(pieces)]
    early = TRACE_TILES + 2
    for copy in copies[:early]:
        copy.start()
    for copy in indices:
        copy.wait()
    send_rows, send_counts, bins, src, rcv, off = small
    pad = jnp.zeros((N_SHOT, LANES - CAP), F32)
    extra[:N_SHOT] = jnp.concatenate([bins[...].astype(F32), pad], axis=1)
    extra[N_SHOT:] = index_tiles(send_rows, send_counts, src, rcv, off)
    for part in range(N_SHOT):
        out[part, BINS_AT:, :] = extra[...]
    for copy in copies[:early]:
        copy.wait()
    for copy in copies[early:]:
        copy.start()
    half = FREQS // STEPS
    for step in range(STEPS):
        if step == 1:
            for copy in copies[early:]:
                copy.wait()
        parts = nt_dot(basis[2 * half * step : 2 * half * (step + 1)], own[...])
        logs = jnp.log1p(parts[:half] * parts[:half] + parts[half:] * parts[half:])
        for part in range(half // SLICE):
            for q in range(TRACE_TILES):
                out[step * (half // SLICE) + part, q * SLICE : (q + 1) * SLICE, :] = logs[
                    part * SLICE : (part + 1) * SLICE, q * LANES : (q + 1) * LANES
                ]


def log_spectra(traces, basis, *small):
    return pl.pallas_call(
        spectra_kernel,
        in_specs=[ANYWHERE] * (2 + len(small)),
        out_shape=jax.ShapeDtypeStruct((N_SHOT, DATA_ROWS, LANES), F32),
        scratch_shapes=[
            VMEM((TR_DEV, SAMPLES), BF16),
            VMEM((2 * FREQS, SAMPLES), BF16),
            VMEM((DATA_ROWS - BINS_AT, LANES), F32),
        ]
        + [VMEM(array.shape, jnp.int32) for array in small]
        + [
            pltpu.SemaphoreType.DMA((TRACE_TILES + 2 * STEPS,)),
            pltpu.SemaphoreType.DMA((len(small),)),
        ],
        compiler_params=params(24),
        cost_estimate=cost(5),
        name="spectra",
    )(*in_hbm(traces, basis, *small))


def fill_ids(ids):
    ids[...] = lax.broadcasted_iota(jnp.int32, ids.shape, 0).astype(F32).astype(BF16)


def fill_hot(tiles, ids, hot):
    one = jnp.ones((1, 1), BF16)
    zero = jnp.zeros((1, 1), BF16)
    values = tiles.astype(F32)
    for q in range(TRACE_TILES):
        span = slice(q * LANES, (q + 1) * LANES)
        first = 0
        for row, size, base in ((0, SRC_G, 0), (2, 128, 0), (1, RCV_G, 0), (3, 256, 0), (3, 256, 256)):
            wanted = (values[4 * q + row : 4 * q + row + 1] - base).astype(BF16)
            hits = jnp.where(ids[:size] == wanted, one, zero)
            hot[first : first + size, span] = hits.astype(hot.dtype)
            first += size


def resolve_bins(data, block):
    tiles = data[block, INDEX_AT:].astype(jnp.int32)
    rows = [data[owner, pl.ds(BINS_AT + block, 1)] for owner in range(N_SHOT)]
    table = jnp.concatenate(rows, axis=0)
    owners = lax.broadcasted_iota(jnp.int32, (N_SHOT, LANES), 0)
    resolved = []
    for q in range(TRACE_TILES):
        slot = tiles[4 * q + 3 : 4 * q + 4]
        place = jnp.broadcast_to(slot & (LANES - 1), (N_SHOT, LANES))
        found = jnp.take_along_axis(table, place, axis=1, mode="promise_in_bounds")
        found = jnp.where(owners == slot >> 7, found.astype(jnp.int32) + owners * CMP_G, 0)
        resolved += [tiles[4 * q : 4 * q + 3], jnp.sum(found, axis=0, keepdims=True)]
    resolved.append(jnp.zeros((INDEX_ROWS - 4 * TRACE_TILES, LANES), jnp.int32))
    return jnp.concatenate(resolved, axis=0)


def prepare_block(data, index, ids, hot, block):
    tiles = resolve_bins(data, block)
    index[block] = tiles
    one = jnp.ones((1, 1), BF16)
    zero = jnp.zeros((1, 1), BF16)
    for q in range(TRACE_TILES):
        for place, row in enumerate((0, 2, 1, 3)):
            lane = tiles[4 * q + row : 4 * q + row + 1] & (LANES - 1)
            hit = ids[:LANES] == lane.astype(F32).astype(BF16)
            span = slice(q * LANES, (q + 1) * LANES)
            hot[place * LANES : (place + 1) * LANES, span] = jnp.where(hit, one, zero)


def add_block(data, index, hot, tab, rcv, block):
    tiles = index[block]
    values = [data[block, q * SLICE : (q + 1) * SLICE] for q in range(TRACE_TILES)]

    both = split_rows(jnp.concatenate(values, axis=1))
    zero = jnp.zeros((1, 1), BF16)

    def of_tiles(row, count):
        place = [tiles[4 * q + row : 4 * q + row + 1] >> 7 for q in range(TRACE_TILES)]
        place = jnp.concatenate(place, axis=1).astype(F32).astype(BF16)
        return jnp.concatenate([jnp.where(place == tile, both, zero) for tile in range(count)], axis=0)

    plain = nt_dot(both, hot[: 2 * LANES])
    tab[at(block)] = join_rows(plain[:, :LANES])
    tab[at(OFF_TILE)] += join_rows(plain[:, LANES:])
    parts = of_tiles(1, RCV_TILES)
    sums = nt_dot(parts, hot[2 * LANES : 3 * LANES])
    for tile in range(RCV_TILES):
        rcv[tile] += join_rows(sums[tile * 2 * SLICE : (tile + 1) * 2 * SLICE])
    cmp_tiles = LIVE_TILES - CMP_TILE
    parts = of_tiles(3, cmp_tiles)
    sums = nt_dot(parts, hot[3 * LANES :])
    for tile in range(cmp_tiles):
        tab[at(CMP_TILE + tile)] += join_rows(sums[tile * 2 * SLICE : (tile + 1) * 2 * SLICE])


def adjoint_kernel(data, tab, rcv, index, hot_even, hot_odd, ids):
    tab[OFF_TILE * SLICE :] = jnp.zeros((TAB_ROWS - OFF_TILE * SLICE, LANES), F32)
    rcv[...] = jnp.zeros((RCV_TILES, SLICE, LANES), F32)
    fill_ids(ids)
    prepare_block(data, index, ids, hot_even, 0)

    @pl.loop(0, N_SHOT // 2, unroll=2)
    def _(pair):
        even = 2 * pair
        prepare_block(data, index, ids, hot_odd, even + 1)
        add_block(data, index, hot_even, tab, rcv, even)
        prepare_block(data, index, ids, hot_even, jnp.minimum(even + 2, N_SHOT - 1))
        add_block(data, index, hot_odd, tab, rcv, even + 1)


EXACT = 128


def kept_part(counts):
    return (counts.astype(jnp.int32) & (EXACT - 1)).astype(F32).astype(BF16)


def left_over(counts):
    whole = counts.astype(jnp.int32)
    return (whole - (whole & (EXACT - 1))).astype(F32).astype(BF16)


def peak(counts):
    top = jnp.max(counts, axis=0, keepdims=True)
    best = top[:, :LANES]
    for start in range(LANES, counts.shape[1], LANES):
        best = jnp.maximum(best, top[:, start : start + LANES])
    return best


def block_counts(hot):
    with_cmp = nt_dot(hot[:SOR], hot[SOR:])
    with_rcv = nt_dot(hot[:SO], hot[SO:SOR])
    with_off = nt_dot(hot[:SRC_G], hot[SRC_G:SO])
    rows = jnp.concatenate([with_off, with_rcv[:SRC_G], with_cmp[:SRC_G]], axis=1)
    return rows, with_cmp[SRC_G:], with_rcv[SRC_G:]


def count_kernel(
    index, kept, to_cmp_kept, to_rcv_kept, most, diag, hot_even, hot_odd, ids, to_cmp, to_rcv, *, first
):
    step = pl.program_id(0)
    even = first + 2 * step

    @pl.when(step == 0)
    def _():
        to_cmp[...] = jnp.zeros_like(to_cmp)
        to_rcv[...] = jnp.zeros_like(to_rcv)
        diag[...] = jnp.zeros_like(diag)
        most[...] = jnp.zeros_like(most)
        fill_ids(ids)
        fill_hot(index[even], ids, hot_even)

    def add(hot, place):
        rows, cmp_counts, rcv_counts = block_counts(hot)
        to_cmp[...] += cmp_counts
        to_rcv[...] += rcv_counts
        diag[...] += jnp.sum(rows, axis=0, keepdims=True)
        kept[place * SRC_G : (place + 1) * SRC_G] = kept_part(rows)
        most[...] = jnp.maximum(most[...], peak(rows))

    fill_hot(index[even + 1], ids, hot_odd)
    add(hot_even, 0)
    fill_hot(index[jnp.minimum(even + 2, N_SHOT - 1)], ids, hot_even)
    add(hot_odd, 1)

    @pl.when(step == COUNT_STEPS - 1)
    def _():
        to_cmp_kept[...] = (to_cmp[...].astype(jnp.int32) & (EXACT - 1)).astype(jnp.int8)
        to_rcv_kept[...] = (to_rcv[...].astype(jnp.int32) & (EXACT - 1)).astype(jnp.int8)
        most[...] = jnp.maximum(most[...], jnp.maximum(peak(to_cmp[...]), peak(to_rcv[...])))


def add_left_over(most_1, most_2, index, hot, ids, to_cmp, to_rcv, use_both, use_rows):
    top = jnp.maximum(jnp.max(most_1[...]), jnp.max(most_2[...]))

    @pl.when(top >= EXACT)
    def _():
        fill_ids(ids)
        for half in range(2):
            to_cmp[...] = jnp.zeros_like(to_cmp)
            to_rcv[...] = jnp.zeros_like(to_rcv)

            @pl.loop(half * HALF, (half + 1) * HALF)
            def _(block):
                fill_hot(index[block], ids, hot)
                rows, cmp_counts, rcv_counts = block_counts(hot)
                to_cmp[...] += cmp_counts
                to_rcv[...] += rcv_counts
                use_rows(block, left_over(rows))

            use_both(left_over(to_cmp[...]), left_over(to_rcv[...]))


def fetch_counts(refs, held, held_cmp, held_rcv, sems):
    *halves, cmp_1, cmp_2, rcv_1, rcv_2 = refs
    pieces = []
    for half, source in enumerate(halves):
        for chunk in range(CHUNKS // 2):
            start = chunk * CHUNK_ROWS
            place = held.at[half * (CHUNKS // 2) + chunk]
            pieces.append((source.at[start : start + CHUNK_ROWS], place))
    pieces += [(cmp_1, held_cmp.at[0]), (cmp_2, held_cmp.at[1])]
    pieces += [(rcv_1, held_rcv.at[0]), (rcv_2, held_rcv.at[1])]
    copies = [pltpu.make_async_copy(a, b, sems.at[k]) for k, (a, b) in enumerate(pieces)]
    for copy in copies:
        copy.start()
    return copies


def sum_halves(held):
    return (held[0].astype(F32) + held[1].astype(F32)).astype(BF16)


def load_halves(tab, rcv, own, shared):
    for tile in range(N_SHOT):
        own[:, tile * LANES : (tile + 1) * LANES] = split_rows(tab[at(tile)])
    shared[: 2 * SLICE, :LANES] = split_rows(tab[at(OFF_TILE)])
    for tile in range(RCV_TILES):
        shared[: 2 * SLICE, (1 + tile) * LANES : (2 + tile) * LANES] = split_rows(rcv[tile])
    for tile in range(CMP_TILE, LIVE_TILES):
        start = (tile - CMP_TILE) * LANES + OR
        shared[: 2 * SLICE, start : start + LANES] = split_rows(tab[at(tile)])


def normal_kernel(
    first, last, cmp_1, cmp_2, rcv_1, rcv_2, tab_in, rcv_in, diag_1, diag_2, most_1, most_2, index,
    tab, rcv, own_count, own, shared, to_shared, to_own,
    held, held_cmp, held_rcv, sems, hot, ids, exact_cmp, exact_rcv,
):
    counts = (first, last, cmp_1, cmp_2, rcv_1, rcv_2)
    copies = fetch_counts(counts, held, held_cmp, held_rcv, sems)
    top = 2 * SLICE
    load_halves(tab_in, rcv_in, own, shared)
    lanes = lax.broadcasted_iota(jnp.int32, (16, SHARED), 1)
    shared[top:] = jnp.where(lanes < LANES, 1.0, 0.0).astype(BF16)
    for chunk in range(CHUNKS):
        copies[chunk].wait()
        span = slice(chunk * CHUNK_ROWS, (chunk + 1) * CHUNK_ROWS)
        sums = jnp.dot(own[:, span], held[chunk], preferred_element_type=F32)
        to_shared[...] = sums if chunk == 0 else to_shared[...] + sums
        to_own[:, span] = nt_dot(shared[...], held[chunk])

    def others(to_cmp, to_rcv):
        cmp_sums = jnp.dot(shared[:top, :OR], to_cmp, preferred_element_type=F32)
        to_shared[:, OR:] += cmp_sums
        to_shared[:, :OR] += nt_dot(shared[:top, OR:], to_cmp)
        rcv_sums = jnp.dot(shared[:top, :LANES], to_rcv, preferred_element_type=F32)
        to_shared[:, LANES:OR] += rcv_sums
        to_shared[:, :LANES] += nt_dot(shared[:top, LANES:OR], to_rcv)

    def use_rows(block, rows):
        span = pl.ds(pl.multiple_of(block * SRC_G, SRC_G), SRC_G)
        to_shared[...] += jnp.dot(own[:, span], rows, preferred_element_type=F32)
        to_own[:, span] += nt_dot(shared[...], rows)

    for copy in copies[-4:]:
        copy.wait()
    others(sum_halves(held_cmp), sum_halves(held_rcv))
    add_left_over(most_1, most_2, index, hot, ids, exact_cmp, exact_rcv, others, use_rows)
    diag = diag_1[...] + diag_2[...]
    for tile in range(N_SHOT):
        span = slice(tile * LANES, (tile + 1) * LANES)
        count = to_own[top : top + 1, span]
        own_count[tile : tile + 1] = count
        tab[at(tile)] = join_rows(to_own[:top, span]) + count * tab_in[at(tile)]
    tab[at(OFF_TILE)] = join_rows(to_shared[:, :LANES]) + diag[:, :LANES] * tab_in[at(OFF_TILE)]
    for tile in range(RCV_TILES):
        span = slice((1 + tile) * LANES, (2 + tile) * LANES)
        rcv[tile] = join_rows(to_shared[:, span]) + diag[:, span] * rcv_in[tile]
    for tile in range(CMP_TILE, LIVE_TILES):
        start = (tile - CMP_TILE) * LANES + OR
        span = slice(start, start + LANES)
        tab[at(tile)] = join_rows(to_shared[:, span]) + diag[:, span] * tab_in[at(tile)]
    tab[LIVE_ROWS:] = jnp.zeros((TAB_ROWS - LIVE_ROWS, LANES), F32)


def all_sum(values):
    return jnp.sum(values, axis=tuple(range(values.ndim)), keepdims=True).reshape(1, 1)


def fold(values):
    total = values[:, :LANES]
    for start in range(LANES, values.shape[1], LANES):
        total = total + values[:, start : start + LANES]
    return total


def norm_kernel(
    first, last, cmp_1, cmp_2, rcv_1, rcv_2,
    tab_b, rcv_b, tab_y, rcv_y, diag_1, diag_2, most_1, most_2, index, own_count,
    out, tab_z, rcv_z, own, shared, to_shared,
    held, held_cmp, held_rcv, sems, hot, ids, exact_cmp, exact_rcv,
):
    counts = (first, last, cmp_1, cmp_2, rcv_1, rcv_2)
    copies = fetch_counts(counts, held, held_cmp, held_rcv, sems)
    shared_b = tab_b[:LIVE_ROWS]
    shared_y = tab_y[:LIVE_ROWS]
    shift = all_sum(shared_b * shared_y) / all_sum(shared_b * shared_b)
    shared_z = shared_y - shift * shared_b
    own_b = rcv_b[...]
    own_z = rcv_y[...] - shift * own_b
    tab_z[...] = shared_z
    rcv_z[...] = own_z
    load_halves(tab_z, rcv_z, own, shared)
    for chunk in range(CHUNKS):
        copies[chunk].wait()
        span = slice(chunk * CHUNK_ROWS, (chunk + 1) * CHUNK_ROWS)
        sums = jnp.dot(own[:, span], held[chunk], preferred_element_type=F32)
        to_shared[...] = sums if chunk == 0 else to_shared[...] + sums

    def whole(tabs, own):
        return all_sum(tabs) * (1.0 / N_RCV) + all_sum(own)

    def others(to_cmp, to_rcv):
        cmp_sums = jnp.dot(shared[:, :OR], to_cmp, preferred_element_type=F32)
        to_shared[:, OR:] += cmp_sums
        rcv_sums = jnp.dot(shared[:, :LANES], to_rcv, preferred_element_type=F32)
        to_shared[:, LANES:OR] += rcv_sums

    def use_rows(block, rows):
        span = pl.ds(pl.multiple_of(block * SRC_G, SRC_G), SRC_G)
        to_shared[...] += jnp.dot(own[:, span], rows, preferred_element_type=F32)

    for copy in copies[-4:]:
        copy.wait()
    others(sum_halves(held_cmp), sum_halves(held_rcv))
    add_left_over(most_1, most_2, index, hot, ids, exact_cmp, exact_rcv, others, use_rows)
    tiles = [tab_z[at(OFF_TILE)]] + [rcv_z[tile] for tile in range(RCV_TILES)]
    tiles += [tab_z[at(tile)] for tile in range(CMP_TILE, LIVE_TILES)]
    rest = jnp.concatenate(tiles, axis=1)
    diag = diag_1[...] + diag_2[...]
    total = fold(2.0 * rest * join_rows(to_shared[...]) + diag * rest * rest)
    for tile in range(N_SHOT):
        total = total + own_count[tile : tile + 1] * tab_z[at(tile)] * tab_z[at(tile)]
    sums = (
        whole(shared_b * shared_b, own_b * own_b),
        whole(shared_b * shared_z, own_b * own_z),
        whole(shared_z * shared_z, own_z * own_z),
        all_sum(total),
        shift,
    )
    lanes = lax.broadcasted_iota(jnp.int32, (1, LANES), 1)
    row = jnp.zeros((1, LANES), F32)
    for lane, value in enumerate(sums):
        row = jnp.where(lanes == lane, value, row)
    out[...] = row


def whole_spec(*shape):
    return pl.BlockSpec(shape, lambda c: (0,) * len(shape))


TAB = (TAB_ROWS, LANES)
RCV = (RCV_TILES, SLICE, LANES)
INDEX = (N_SHOT, INDEX_ROWS, LANES)
INDEX_SPEC = pl.BlockSpec((1, INDEX_ROWS, LANES), lambda c: (c, 0, 0))


def table_shapes():
    return [jax.ShapeDtypeStruct(TAB, F32), jax.ShapeDtypeStruct(RCV, F32)]


def hot_scratch():
    return [VMEM((ROWS, TR_DEV), FP8), VMEM((256, LANES), BF16)]


def adjoint_apply(data):
    return pl.pallas_call(
        adjoint_kernel,
        out_shape=table_shapes() + [jax.ShapeDtypeStruct(INDEX, jnp.int32)],
        scratch_shapes=[VMEM((4 * LANES, TR_DEV), BF16)] * 2 + [VMEM((256, LANES), BF16)],
        compiler_params=params(24),
        cost_estimate=cost(8),
        name="adjoint_apply",
    )(data)


COUNTS = (HALF * SRC_G, SHARED)
TO_CMP = (OR, SHARED - OR)
TO_RCV = (LANES, RCV_G)
IN_VMEM = pl.BlockSpec(memory_space=VMEM)


def count_call(index, first):
    rows = pl.BlockSpec((2 * SRC_G, SHARED), lambda c: (c, 0))
    small = [whole_spec(*TO_CMP), whole_spec(*TO_RCV), whole_spec(1, LANES), whole_spec(1, SHARED)]
    return pl.pallas_call(
        functools.partial(count_kernel, first=first),
        grid=(COUNT_STEPS,),
        in_specs=[whole_spec(*INDEX)],
        out_specs=[rows] + small,
        out_shape=[
            pltpu.HBM(COUNTS, BF16),
            pltpu.HBM(TO_CMP, jnp.int8),
            pltpu.HBM(TO_RCV, jnp.int8),
            jax.ShapeDtypeStruct((1, LANES), F32),
            jax.ShapeDtypeStruct((1, SHARED), F32),
        ],
        scratch_shapes=[VMEM((ROWS, TR_DEV), FP8)] * 2
        + [VMEM((256, LANES), BF16), VMEM(TO_CMP, F32), VMEM(TO_RCV, F32)],
        compiler_params=params(24),
        cost_estimate=cost(6),
        name="count_pairs",
    )(index)


def count_scratch(chunks):
    return (
        [
            VMEM((chunks, CHUNK_ROWS, SHARED), BF16),
            VMEM((2,) + TO_CMP, jnp.int8),
            VMEM((2,) + TO_RCV, jnp.int8),
            pltpu.SemaphoreType.DMA((chunks + 4,)),
        ]
        + hot_scratch()
        + [VMEM(TO_CMP, F32), VMEM(TO_RCV, F32)]
    )


def count_operands(counts):
    big = in_hbm(*[array for pair in zip(counts[0][:3], counts[1][:3]) for array in pair])
    (most_1, diag_1), (most_2, diag_2) = counts[0][3:5], counts[1][3:5]
    return big, [diag_1, diag_2, most_1, most_2]


def normal_apply(tab, rcv, index, counts):
    big, small = count_operands(counts)
    return pl.pallas_call(
        normal_kernel,
        in_specs=[ANYWHERE] * 6 + [IN_VMEM] * 7,
        out_shape=table_shapes() + [jax.ShapeDtypeStruct((N_SHOT, LANES), F32)],
        scratch_shapes=[
            VMEM((2 * SLICE, N_SHOT * SRC_G), BF16),
            VMEM((2 * SLICE + 16, SHARED), BF16),
            VMEM((2 * SLICE, SHARED), F32),
            VMEM((2 * SLICE + 16, N_SHOT * SRC_G), F32),
        ]
        + count_scratch(CHUNKS),
        compiler_params=params(24),
        cost_estimate=cost(3),
        name="normal_apply",
    )(*big, tab, rcv, *small, index)


def norm_sums(tab_b, rcv_b, tab_y, rcv_y, own_count, index, counts):
    big, small = count_operands(counts)
    return pl.pallas_call(
        norm_kernel,
        in_specs=[ANYWHERE] * 6 + [IN_VMEM] * 10,
        out_shape=jax.ShapeDtypeStruct((1, LANES), F32),
        scratch_shapes=[
            VMEM((LIVE_ROWS, LANES), F32),
            VMEM(RCV, F32),
            VMEM((2 * SLICE, N_SHOT * SRC_G), BF16),
            VMEM((2 * SLICE, SHARED), BF16),
            VMEM((2 * SLICE, SHARED), F32),
        ]
        + count_scratch(CHUNKS),
        compiler_params=params(24),
        cost_estimate=cost(2),
        name="norm_sums",
    )(*big, tab_b, rcv_b, tab_y, rcv_y, *small, index, own_count)


def spread_kernel(parts, out):
    total = parts[0]
    for source in range(1, N_RCV):
        total = total + parts[source]
    for dest in range(N_RCV):
        out[dest] = total


def exchange(array, axis):
    return lax.all_to_all(array, axis, split_axis=0, concat_axis=0, tiled=True)


def spread_shares(arrived):
    shape = (N_RCV, SHARE, LANES)
    spread = pl.pallas_call(
        spread_kernel,
        out_shape=jax.ShapeDtypeStruct(shape, F32),
        compiler_params=params(24),
        cost_estimate=cost(1),
        name="sum_shares",
    )(arrived.reshape(shape))
    return spread.reshape(TAB)


def pack_kernel(tab, rcv, *refs, first):
    out, rows, sems = refs[-3:]
    lanes = lax.broadcasted_iota(jnp.int32, (SLICE, LANES), 1)
    half = SLICE // 2
    copies = []
    for dest in range(N_SHOT):
        rows[dest, :SLICE] = tab[at(dest)]
        rows[dest, SLICE : 2 * SLICE] = tab[at(OFF_TILE)]
        cmp_first = dest * CMP_G
        rcv_first = dest * (RCV_G // N_SHOT)
        bins = tab[at(CMP_TILE + cmp_first // LANES)]
        cmp_part = pltpu.roll(bins, (-cmp_first) % LANES, 1)
        rcv_part = pltpu.roll(rcv[rcv_first // LANES], (CMP_G - rcv_first) % LANES, 1)
        both = jnp.where(lanes < CMP_G, cmp_part, rcv_part)
        moved = pltpu.roll(both[half:], LANES // 2, 1)
        rows[dest, 2 * SLICE :] = jnp.where(lanes[:half] < LANES // 2, both[:half], moved)
        if dest % PACK == PACK - 1:
            group = dest // PACK
            span = slice(group * PACK, (group + 1) * PACK)
            place = out.at[span, first : first + OWN_ROWS]
            copies.append(pltpu.make_async_copy(rows.at[span], place, sems.at[group]))
            copies[-1].start()
    for copy in copies:
        copy.wait()


def pack_owned(tab, rcv, former=None):
    given = [] if former is None else in_hbm(former)
    return pl.pallas_call(
        functools.partial(pack_kernel, first=OWN_ROWS * len(given)),
        in_specs=[pl.BlockSpec(memory_space=VMEM)] * 2 + [ANYWHERE] * len(given),
        out_specs=ANYWHERE,
        out_shape=pltpu.HBM((N_SHOT, 2 * OWN_ROWS, LANES), F32),
        scratch_shapes=[
            VMEM((N_SHOT, OWN_ROWS, LANES), F32),
            pltpu.SemaphoreType.DMA((N_SHOT // PACK,)),
        ],
        input_output_aliases={2: 0} if given else {},
        compiler_params=params(24),
        cost_estimate=cost(1),
        name="pack_owned",
    )(tab, rcv, *given)


def swapped(value, axis, size, bit):
    return lax.ppermute(value, axis, [(s, s ^ bit) for s in range(size)])


def gather_sums(sums):
    for bit in (1, 2, 6):
        sums = sums + swapped(sums, "rcv", N_RCV, bit)
    here = jnp.arange(N_SHOT, dtype=jnp.int32)[:, None] == lax.axis_index("shot")
    rows = jnp.where(here, sums, 0.0)
    for bit in (1, 3, 4, 12):
        rows = rows + swapped(rows, "shot", N_SHOT, bit)
    return rows


def finish_kernel(sums, owned, source, receiver, offset, cmp):
    rows = sums[...]
    norm_b, cross, norm_z, norm_az, shift = (rows[:, lane : lane + 1] for lane in range(5))
    shift = shift * (1.0 / N_RCV)

    def total(values):
        return jnp.sum(values, axis=0, keepdims=True)

    total_b = total(norm_b)
    first = total(cross + shift * norm_b) / total_b
    off = shift - first
    zz = total(norm_z + 2.0 * off * cross + off * off * norm_b)
    zaz = total(
        norm_az
        + 2.0 * off * (norm_z + shift * cross)
        + off * off * (cross + shift * norm_b)
    )
    second = zaz / zz
    det = first * second - zz / total_b
    scale_b = (first + second) / det
    scale_y = 1.0 / det

    def combine(sender, start, stop):
        part_y = owned[sender, OWN_ROWS + start : OWN_ROWS + stop]
        return scale_b * owned[sender, start:stop] - scale_y * part_y

    def spread_halves(tile):
        return jnp.concatenate([tile, pltpu.roll(tile, LANES // 2, 1)], axis=0)

    per_tile = LANES // SLICE
    for group in range(N_SHOT // per_tile):
        span = slice(group * LANES, (group + 1) * LANES)
        senders = range(group * per_tile, (group + 1) * per_tile)
        source[:, span] = jnp.concatenate([combine(i, 0, SLICE) for i in senders], axis=0).T
        offset[:, span] = jnp.concatenate(
            [combine(i, SLICE, 2 * SLICE) for i in senders], axis=0
        ).T
        rest = jnp.concatenate(
            [spread_halves(combine(i, 2 * SLICE, OWN_ROWS)) for i in senders], axis=0
        ).T
        cmp[:, span] = rest[:CMP_G]
        receiver[0, :, span] = rest[CMP_G : CMP_G + RCV_G // N_SHOT]


def finish(sums, owned):
    return pl.pallas_call(
        finish_kernel,
        out_shape=[
            jax.ShapeDtypeStruct((SRC_G, FREQS), F32),
            jax.ShapeDtypeStruct((1, RCV_G // N_SHOT, FREQS), F32),
            jax.ShapeDtypeStruct((128, FREQS), F32),
            jax.ShapeDtypeStruct((CMP_G, FREQS), F32),
        ],
        compiler_params=params(),
        name="finish",
    )(sums, owned)


def per_device(basis, traces, src_index, rcv_index, off_index, send_rows, send_counts, recv_bins):
    data = log_spectra(
        traces, basis, send_rows[0], send_counts, recv_bins[0], src_index, rcv_index, off_index
    )
    data = exchange(data, "shot")

    tab_b, rcv_b, index = adjoint_apply(data)
    arrived = exchange(tab_b, "rcv")
    counts_1 = count_call(index, 0)
    arrived, index, counts_1 = lax.optimization_barrier((arrived, index, counts_1))
    spread = spread_shares(arrived)
    spread, index = lax.optimization_barrier((spread, index))
    tab_b = exchange(spread, "rcv")
    counts = (counts_1, count_call(index, HALF))

    tab_y, rcv_y, own_count = normal_apply(tab_b, rcv_b, index, counts)
    arrived = exchange(tab_y, "rcv")
    packed = pack_owned(tab_b, rcv_b)
    arrived, packed = lax.optimization_barrier((arrived, packed))
    tab_y = exchange(spread_shares(arrived), "rcv")
    packed = pack_owned(tab_y, rcv_y, packed)
    tab_y, packed = lax.optimization_barrier((tab_y, packed))
    owned = exchange(packed, "shot")
    sums = norm_sums(tab_b, rcv_b, tab_y, rcv_y, own_count, index, counts)
    return tuple(finish(gather_sums(sums), owned))


def solution(mesh):
    basis = fourier_rows()
    mapped = jax.shard_map(
        per_device,
        mesh=mesh,
        in_specs=(
            P(),
            P(("shot", "rcv"), None),
            P(("shot", "rcv")),
            P(("shot", "rcv")),
            P(("shot", "rcv")),
            P(("shot", "rcv"), None, None),
            P(("shot", "rcv"), None),
            P(("shot", "rcv"), None, None),
        ),
        out_specs=(P("shot", None), P("rcv", "shot", None), P(), P("shot", None)),
        check_vma=False,
    )

    def run(*args):
        return mapped(jnp.asarray(basis), *args)

    return run
```
